32 devices in a mesh: dp: 8 (over y, x, core), head: 4 (over z).
Axes of the slice: x: 2, y: 2, z: 4, core: 2. Of those that a mesh axis runs over, the one named last changes fastest.
Arguments:
- hidden_in: bfloat16 [12288, 768], P('dp'), may hold values from -6 to 6
- seq_lengths: int32 [24], P('dp'), may hold values from 64 to 512, as said below
- layer_map: int32 [2], replicated, may hold values from 0 to 3, as said below
- teacher_states: bfloat16 [4, 12288, 768], P(None, 'dp', 'head'), may hold values from -6 to 6
- out_cotangent: bfloat16 [12288, 768], P('dp'), may hold values from -6 to 6
- query_weight: bfloat16 [2, 768, 768], P(None, None, 'head'), may hold values from -0.21875 to 0.21875
- key_weight: bfloat16 [2, 768, 768], P(None, None, 'head'), may hold values from -0.21875 to 0.21875
- value_weight: bfloat16 [2, 768, 768], P(None, None, 'head'), may hold values from -0.21875 to 0.21875
- query_value_bias: float32 [2, 2, 768], P(None, None, 'head'), may hold values from -0.3 to 0.3
- output_weight: bfloat16 [2, 768, 768], P(None, 'head'), may hold values from -2.5 to 2.5
- branch_bias: float32 [2, 2, 768], replicated, may hold values from -0.15 to 0.15
- norm_gain: float32 [2, 2, 768], replicated, may hold values from 0.5 to 1.5
- norm_shift: float32 [2, 2, 768], replicated, may hold values from -0.15 to 0.15
- inner_weight: bfloat16 [2, 768, 3072], P(None, None, 'head'), may hold values from -0.21875 to 0.21875
- inner_bias: float32 [2, 3072], P(None, 'head'), may hold values from -3 to 3
- outer_weight: bfloat16 [2, 3072, 768], P(None, 'head'), may hold values from -0.21875 to 0.21875
- head_alpha: float32 [2, 12], P(None, 'head'), may hold values from -3 to 3
- head_noise: float32 [2, 12], P(None, 'head'), may hold values from -1.5 to 1.5
- unit_alpha: float32 [2, 3072], P(None, 'head'), may hold values from -3 to 3
- unit_noise: float32 [2, 3072], P(None, 'head'), may hold values from -1.5 to 1.5
- map_weight: bfloat16 [768, 768], P(None, 'head'), may hold values from -0.21875 to 0.21875
Outputs:
- block_out: bfloat16 [12288, 768], P('dp')
- grad_hidden: float32 [12288, 768], P('dp')
- distill_loss: float32 [], replicated
- grad_query: float32 [2, 768, 768], P(None, 'dp', 'head')
- grad_key: float32 [2, 768, 768], P(None, 'dp', 'head')
- grad_value: float32 [2, 768, 768], P(None, 'dp', 'head')
- grad_query_value_bias: float32 [2, 2, 768], P(None, None, ('head', 'dp'))
- grad_output: float32 [2, 768, 768], P(None, 'head', 'dp')
- grad_branch_bias: float32 [2, 2, 768], P(None, None, 'dp')
- grad_norm_gain: float32 [2, 2, 768], P(None, None, 'dp')
- grad_norm_shift: float32 [2, 2, 768], P(None, None, 'dp')
- grad_inner: float32 [2, 768, 3072], P(None, 'dp', 'head')
- grad_inner_bias: float32 [2, 3072], P(None, ('head', 'dp'))
- grad_outer: float32 [2, 3072, 768], P(None, 'head', 'dp')
- grad_head_alpha: float32 [2, 12], P(None, 'head')
- grad_unit_alpha: float32 [2, 3072], P(None, ('head', 'dp'))
- grad_map: float32 [768, 768], P('dp', 'head')
The draws below stay inside these ranges and needn't reach their ends.
Inputs may be any that keep to these rules, and one draw needn't show every extreme that they name: Each sequence uses its first seq_lengths slots; some sequence uses all 512, some only 64. `layer_map`: the last student layer matches teacher layer 3; the entries differ.
All inputs are finite; a program needn't handle non-finite values.
Results may differ from the reference program's by a relative error of at most 0.03.
Values may be sent and summed in bfloat16 or wider, within the bound.
A program may use at most 256 MiB of HBM per device.

```python
import jax
import jax.numpy as jnp
from jax import lax

D = 768
H = 12
HD = 64
FF = 3072
MAXLEN = 512
LAYERS = 2
TEACH = 4
SEQ_DEV = 3
SEQS = 24
TOKENS = 12288
N_HEAD = 4


def draw_seq_lengths(key, part):
    key = jax.random.fold_in(key, 7)
    first, second, third = jax.random.split(key, 3)
    places = jnp.arange(SEQS)
    owner = places // SEQ_DEV
    last_owner = SEQS // SEQ_DEV - 1
    shortest = MAXLEN // 8
    cap = shortest + (MAXLEN - shortest) * owner // max(last_owner, 1)
    spans = jax.random.randint(first, (SEQS,), 0, 1 << 20)
    drawn = shortest + spans % (cap - shortest + 1)
    top_slot = SEQS - 1 - jax.random.randint(second, (), 0, SEQ_DEV)
    low_slot = jax.random.randint(third, (), 0, SEQ_DEV)
    drawn = jnp.where(places == top_slot, MAXLEN, drawn)
    drawn = jnp.where(places == low_slot, shortest, drawn)
    return drawn.astype(jnp.int32)


def draw_layer_map(key, part):
    key = jax.random.fold_in(key, 11)
    picks = jax.random.randint(key, (LAYERS,), 0, TEACH - 1)
    places = jnp.arange(LAYERS)
    spread = (picks + places) % (TEACH - 1)
    drawn = jnp.where(places == LAYERS - 1, TEACH - 1, spread)
    return drawn.astype(jnp.int32)


def normal_field(key, shape, scale, bound):
    values = jax.random.normal(key, shape, jnp.float32) * scale
    return jnp.clip(values, -bound * scale, bound * scale)


def draw_query_value_bias(key, part):
    key = jax.random.fold_in(key, 13)
    return normal_field(key, (LAYERS, 2, D), 0.1, 3.0)


def draw_branch_bias(key, part):
    key = jax.random.fold_in(key, 17)
    return normal_field(key, (LAYERS, 2, D), 0.05, 3.0)


def draw_norm_shift(key, part):
    key = jax.random.fold_in(key, 19)
    return normal_field(key, (LAYERS, 2, D), 0.05, 3.0)


def block_levels(rng, shape, pieces, least, high):
    def one(dim, blocks):
        steps = jax.random.uniform(jax.random.fold_in(jax.random.fold_in(rng, 6), dim), (blocks,), jnp.float32, least / len(pieces), high / len(pieces))
        return jnp.repeat(jnp.exp(steps), shape[dim] // blocks).reshape((-1,) + (1,) * (len(shape) - dim - 1))

    level = one(*pieces[0])
    for cut in pieces[1:]:
        level = level * one(*cut)
    return level


def bell_draw(stream_key, dims, scale, most, pieces=(), kind=jnp.bfloat16):
    level = block_levels(stream_key, dims, pieces, -0.22, 0.18) if pieces else 1.0
    values = jax.random.normal(stream_key, dims, jnp.float32) * scale * level
    return jnp.minimum(jnp.maximum(values, -most), most).astype(kind)


def setup_inputs(seed: int = 0) -> dict:
    keys = jax.random.split(jax.random.key(seed), 22)
    hidden_in = bell_draw(keys[0], (TOKENS, D), 1.0, 6.0, ((0, 8),))
    seq_lengths = draw_seq_lengths(jax.random.fold_in(keys[21], 71), 0)
    layer_map = draw_layer_map(jax.random.fold_in(keys[21], 71), 0)
    teacher_states = bell_draw(keys[3], (TEACH, TOKENS, D), 1.0, 6.0, ((1, 8), (2, 4)))
    out_cotangent = bell_draw(keys[4], (TOKENS, D), 1.0, 6.0, ((0, 8),))
    query_weight = bell_draw(keys[5], (LAYERS, D, D), D ** -0.5, 0.21875, ((2, 4),))
    key_weight = bell_draw(keys[6], (LAYERS, D, D), D ** -0.5, 0.21875, ((2, 4),))
    value_weight = bell_draw(keys[7], (LAYERS, D, D), D ** -0.5, 0.21875, ((2, 4),))
    query_value_bias = draw_query_value_bias(jax.random.fold_in(keys[21], 71), 0)
    output_weight = bell_draw(keys[9], (LAYERS, D, D), (D // 128) ** -0.5, 2.5, ((1, 4),))
    branch_bias = draw_branch_bias(jax.random.fold_in(keys[21], 71), 0)
    norm_gain = jnp.clip(1.0 + 0.1 * jax.random.normal(keys[11], (LAYERS, 2, D), jnp.float32), 0.5, 1.5)
    norm_shift = draw_norm_shift(jax.random.fold_in(keys[21], 71), 0)
    inner_weight = bell_draw(keys[13], (LAYERS, D, FF), D ** -0.5, 0.21875, ((2, 4),))
    inner_bias = bell_draw(keys[14], (LAYERS, FF), 0.5, 3.0, ((1, 4),), jnp.float32)
    outer_weight = bell_draw(keys[15], (LAYERS, FF, D), (FF // 4) ** -0.5, 0.21875, ((1, 4),))
    head_alpha = bell_draw(keys[16], (LAYERS, H), 0.8, 3.0, ((1, 4),), jnp.float32)
    head_noise = jnp.clip(jax.random.uniform(keys[17], (LAYERS, H), jnp.float32, -1.5, 1.5) * block_levels(keys[17], (LAYERS, H), ((1, 4),), -0.4, 0.0), -1.5, 1.5)
    unit_alpha = bell_draw(keys[18], (LAYERS, FF), 0.8, 3.0, ((1, 4),), jnp.float32)
    unit_noise = jnp.clip(jax.random.uniform(keys[19], (LAYERS, FF), jnp.float32, -1.5, 1.5) * block_levels(keys[19], (LAYERS, FF), ((1, 4),), -0.4, 0.0), -1.5, 1.5)
    map_weight = bell_draw(keys[20], (D, D), D ** -0.5, 0.21875, ((1, 4),))
    return {"hidden_in": hidden_in, "seq_lengths": seq_lengths, "layer_map": layer_map, "teacher_states": teacher_states, "out_cotangent": out_cotangent, "query_weight": query_weight, "key_weight": key_weight, "value_weight": value_weight, "query_value_bias": query_value_bias, "output_weight": output_weight, "branch_bias": branch_bias, "norm_gain": norm_gain, "norm_shift": norm_shift, "inner_weight": inner_weight, "inner_bias": inner_bias, "outer_weight": outer_weight, "head_alpha": head_alpha, "head_noise": head_noise, "unit_alpha": unit_alpha, "unit_noise": unit_noise, "map_weight": map_weight}


HIGH = lax.Precision.HIGHEST
BETA = 2.0 / 3.0
EPS = 1e-05

@jax.custom_vjp
def low(v):
    return lax.optimization_barrier(v.astype(jnp.bfloat16)).astype(jnp.float32)

@jax.custom_vjp
def low_back(v):
    return v

def low_keep(v):
    return (low(v), None)

def low_pass(kept, grad):
    return (grad,)

def back_keep(v):
    return (v, None)

def back_low(kept, grad):
    return (low(grad),)
low.defvjp(low_keep, low_pass)
low_back.defvjp(back_keep, back_low)

def layer_norm(before, gain, shift):
    center = before - lax.optimization_barrier(jnp.mean(before, -1, keepdims=True))
    spread = lax.optimization_barrier(jnp.mean(center * center, -1, keepdims=True))
    return center * lax.rsqrt(spread + EPS) * gain + shift

def gate_open(noise, alpha):
    return jnp.clip(jax.nn.sigmoid((noise + alpha) / BETA) * 1.2 - 0.1, 0.0, 1.0)

def matmul(left, right):
    return jnp.dot(left, right, precision=HIGH)

def attend_one(packed):
    query_rows, key_rows, value_rows, length = packed
    scores = jnp.einsum('qhd,khd->hqk', query_rows, key_rows, precision=HIGH) * 0.125
    scores = low_back(scores)
    usable = jnp.arange(MAXLEN) < length
    scores = jnp.where(usable[None, None, :], scores, -1e+30)
    largest = lax.optimization_barrier(jnp.max(scores, -1, keepdims=True))
    powers = jnp.exp(scores - largest)
    chances = powers / lax.optimization_barrier(jnp.sum(powers, -1, keepdims=True))
    return jnp.einsum('hqk,khd->qhd', low(chances), value_rows, precision=HIGH)

def encoder_layer(layer, current, copies, params, seq_lengths, head_noise, unit_noise):
    query_weight, key_weight, value_weight, query_value_bias, output_weight, branch_bias, norm_gain, norm_shift, inner_weight, inner_bias, outer_weight, head_alpha, unit_alpha = params
    width = D // N_HEAD
    heads_dev = H // N_HEAD
    inner = FF // N_HEAD
    branches = []
    for group in range(N_HEAD):
        cols = slice(group * width, (group + 1) * width)
        heads = slice(group * heads_dev, (group + 1) * heads_dev)
        query_rows = low(low_back(matmul(copies[group], query_weight[layer][:, cols]) + query_value_bias[layer, 0, cols]))
        key_rows = low(low_back(matmul(copies[group], key_weight[layer][:, cols])))
        value_rows = low(low_back(matmul(copies[group], value_weight[layer][:, cols]) + query_value_bias[layer, 1, cols]))
        shape_four = (SEQS, MAXLEN, heads_dev, HD)
        context = lax.map(jax.checkpoint(attend_one), (query_rows.reshape(shape_four), key_rows.reshape(shape_four), value_rows.reshape(shape_four), seq_lengths))
        context = low_back(context.reshape(TOKENS, width))
        opened = gate_open(head_noise[layer, heads], head_alpha[layer, heads])
        gated = low((context.reshape(TOKENS, heads_dev, HD) * opened[None, :, None]).reshape(TOKENS, width))
        branches.append(low(low_back(matmul(gated, output_weight[layer][cols, :]))))
    before_one = current + sum(branches) + branch_bias[layer, 0]
    middle = layer_norm(before_one, norm_gain[layer, 0], norm_shift[layer, 0])
    middle_low = low(middle)
    feeds = []
    for group in range(N_HEAD):
        units = slice(group * inner, (group + 1) * inner)
        unit_in = low_back(matmul(low_back(middle_low), inner_weight[layer][:, units]) + inner_bias[layer, units])
        active = low(jax.nn.gelu(unit_in) * gate_open(unit_noise[layer, units], unit_alpha[layer, units]))
        feeds.append(low(low_back(matmul(active, outer_weight[layer][units, :]))))
    before_two = middle + sum(feeds) + branch_bias[layer, 1]
    return layer_norm(before_two, norm_gain[layer, 1], norm_shift[layer, 1])

def reference(hidden_in, seq_lengths, layer_map, teacher_states, out_cotangent, query_weight, key_weight, value_weight, query_value_bias, output_weight, branch_bias, norm_gain, norm_shift, inner_weight, inner_bias, outer_weight, head_alpha, head_noise, unit_alpha, unit_noise, map_weight):
    teacher = teacher_states.astype(jnp.float32)
    count = jnp.sum(seq_lengths).astype(jnp.float32)
    row_ok = (jnp.arange(TOKENS) % MAXLEN < jnp.repeat(seq_lengths, MAXLEN, total_repeat_length=TOKENS)).astype(jnp.float32)[:, None]
    head_noise32 = head_noise.astype(jnp.float32)
    unit_noise32 = unit_noise.astype(jnp.float32)
    width = D // N_HEAD

    def forward(hidden, qw, kw, vw, qvb, ow, bb, ng, ns, iw, ib, uw, ha, ua, mw):
        params = (qw, kw, vw, qvb, ow, bb, ng, ns, iw, ib, uw, ha, ua)
        rounded = low(hidden)
        copies = [low_back(rounded) for group in range(N_HEAD)]
        current = hidden
        error_sum = jnp.zeros((), jnp.float32)
        for layer in range(LAYERS):
            current = encoder_layer(layer, current, copies, params, seq_lengths, head_noise32, unit_noise32)
            rounded = low(current)
            copies = [low_back(rounded) for group in range(N_HEAD)]
            target = teacher[layer_map[layer]]
            for group in range(N_HEAD):
                cols = slice(group * width, (group + 1) * width)
                mapped = low_back(matmul(copies[group], mw[:, cols]))
                miss = (mapped - target[:, cols]) * row_ok
                error_sum = error_sum + jnp.sum(miss * miss)
        objective = 0.5 * (TOKENS / count) * error_sum
        return ((current, objective), error_sum)
    primals = tuple((array.astype(jnp.float32) for array in (hidden_in, query_weight, key_weight, value_weight, query_value_bias, output_weight, branch_bias, norm_gain, norm_shift, inner_weight, inner_bias, outer_weight, head_alpha, unit_alpha, map_weight)))
    outputs, pullback, error_sum = jax.vjp(forward, *primals, has_aux=True)
    grads = pullback((out_cotangent.astype(jnp.float32), jnp.ones((), jnp.float32)))
    distill_loss = error_sum / (count * D * LAYERS)
    return (outputs[0].astype(jnp.bfloat16), grads[0], distill_loss, grads[1], grads[2], grads[3], grads[4], grads[5], grads[6], grads[7], grads[8], grads[9], grads[10], grads[11], grads[12], grads[13], grads[14])
```

```python
from functools import partial

import jax
import jax.numpy as jnp
from jax import lax
from jax.experimental import pallas as pl
from jax.experimental.pallas import tpu as pltpu
from jax.sharding import PartitionSpec as P

BETA = 2.0 / 3.0
EPS = 1e-05
LOW = jnp.bfloat16
F32 = jnp.float32
GELU_C = 0.7978845608028654
GELU_K = 0.044715
VMEM_LIMIT = 56 * 1024 * 1024


def gate_open(noise, alpha):
    return jnp.clip(jax.nn.sigmoid((noise + alpha) / BETA) * 1.2 - 0.1, 0.0, 1.0)


def product(left, right, dims):
    return lax.dot_general(left, right, ((dims[:1], dims[1:]), ((), ())), preferred_element_type=F32)


def nn(left, right):
    return product(left, right, (1, 0))


def nt(left, right):
    return product(left, right, (1, 1))


def tn(left, right):
    return product(left, right, (0, 0))


def full(array):
    shape = array.shape
    return pl.BlockSpec(shape, lambda r, info: (0,) * len(shape))


def by_group(shape):
    return pl.BlockSpec((1,) + shape[1:], lambda r, info: (r,) + (0,) * (len(shape) - 1))


def run(body, groups, info, inputs, outputs, scratch, flops, name):
    specs = {
        "full": full,
        "group": lambda a: by_group(a.shape),
        "any": lambda a: pl.BlockSpec(memory_space=pl.ANY),
    }
    out_shape = [jax.ShapeDtypeStruct(shape, dtype) for shape, dtype, _ in outputs]
    moved = sum(a.size * a.dtype.itemsize for a, _ in inputs)
    return pl.pallas_call(
        body,
        name=name,
        grid_spec=pltpu.PrefetchScalarGridSpec(
            num_scalar_prefetch=1,
            grid=(groups,),
            in_specs=[specs[kind](a) for a, kind in inputs],
            out_specs=[specs[kind](o) for o, (_, _, kind) in zip(out_shape, outputs)],
            scratch_shapes=scratch,
        ),
        out_shape=out_shape,
        compiler_params=pltpu.CompilerParams(vmem_limit_bytes=VMEM_LIMIT),
        cost_estimate=pl.CostEstimate(flops=int(flops), bytes_accessed=int(moved), transcendentals=0),
    )(info, *[a for a, _ in inputs])


class Stream:
    def __init__(self, own, parts, col, width, buf, sems):
        self.own, self.parts, self.col, self.width, self.buf, self.sems = own, parts, col, width, buf, sems

    def first(self):
        return [
            pltpu.make_async_copy(
                self.own.at[:, pl.ds(self.col, self.width)], self.buf.at[0], self.sems.at[0, 0]
            )
        ]

    def later(self, index, slot):
        copies, row = [], 0
        for number, part in enumerate(self.parts):
            rows = part.shape[1]
            copies.append(
                pltpu.make_async_copy(
                    part.at[index - 1, :, pl.ds(self.col, self.width)],
                    self.buf.at[slot, pl.ds(row, rows), :],
                    self.sems.at[slot, number],
                )
            )
            row += rows
        return copies


def turn(streams, r, groups):
    slot = lax.rem(r, 2)

    @pl.when(r == 0)
    def _():
        for stream in streams:
            for copy in stream.first():
                copy.start()
        for stream in streams:
            for copy in stream.later(1, 1):
                copy.start()
        for stream in streams:
            for copy in stream.first():
                copy.wait()

    @pl.when((r > 0) & (r < groups - 1))
    def _():
        for stream in streams:
            for copy in stream.later(r + 1, 1 - slot):
                copy.start()

    @pl.when(r > 0)
    def _():
        for stream in streams:
            for copy in stream.later(r, slot):
                copy.wait()

    return slot


class Gathered:
    def __init__(self, own, parts, col=0, width=None):
        self.own, self.parts, self.col = own, parts, col
        self.width = own.shape[1] if width is None else width

    def columns(self, col, width):
        return Gathered(self.own, self.parts, col, width)

    def operands(self):
        return [(self.own, "any")] + [(part, "any") for part in self.parts]

    def scratch(self):
        return [
            pltpu.VMEM((2, self.own.shape[0], self.width), LOW),
            pltpu.SemaphoreType.DMA((2, len(self.parts))),
        ]

    def stream(self, refs, buf, sems):
        return Stream(refs[0], refs[1:], self.col, self.width, buf, sems)


def norm_forward(before, gain, shift):
    center = before - jnp.mean(before, -1, keepdims=True)
    spread = jnp.mean(center * center, -1, keepdims=True)
    return center * lax.rsqrt(spread + EPS) * gain + shift


def norm_backward(before, gain, grad):
    center = before - jnp.mean(before, -1, keepdims=True)
    rate = lax.rsqrt(jnp.mean(center * center, -1, keepdims=True) + EPS)
    hat = center * rate
    grad_hat = grad * gain
    mean_one = jnp.mean(grad_hat, -1, keepdims=True)
    mean_two = jnp.mean(grad_hat * hat, -1, keepdims=True)
    grad_before = rate * (grad_hat - mean_one - hat * mean_two)
    return (
        grad_before,
        jnp.sum(grad * hat, 0, keepdims=True),
        jnp.sum(grad, 0, keepdims=True),
        jnp.sum(grad_before, 0, keepdims=True),
    )


BIAS_ONE, BIAS_TWO, GAIN_ONE, GAIN_TWO, SHIFT_ONE, SHIFT_TWO = range(6)
OWN, PAIR, MID, MID_ROW, LOC, LENGTH = 0, 1, 2, 3, 4, 8


def attention_forward(size, layer, first, left, right, info, *refs):
    seq_len, block, heads, head_size = size
    refs = list(refs)
    xwin, small, vec = refs[:3]
    refs = refs[3:]
    resid = None if first else refs.pop(0)
    left_refs = [refs.pop(0) for _ in left.operands()]
    right_refs = [refs.pop(0) for _ in right.operands()]
    kv_out, q_out, ctx_out, lse_out, gated_out, before_out, h_out, hb_out = refs[:8]
    left_buf, left_sems, right_buf, right_sems, total = refs[8:]
    r, groups = pl.program_id(0), pl.num_programs(0)
    slot = turn(
        [left.stream(left_refs, left_buf, left_sems), right.stream(right_refs, right_buf, right_sems)], r, groups
    )
    width = heads * head_size
    rows = total.shape[0]
    row = small[0, 4 * layer + 2 : 4 * layer + 3, :]
    kv = nn(xwin[...], left_buf[slot]) + row[:, 2 * width :]
    kv_out[0] = kv.astype(LOW)
    own = pl.multiple_of(info[OWN], block)
    query = (nn(xwin[pl.ds(own, rows), :], right_buf[slot, :, :width]) + row[:, :width]).astype(LOW)
    q_out[0] = query
    scaled = query * jnp.asarray(0.125, LOW)
    for piece in range(rows // block):
        here = slice(piece * block, (piece + 1) * block)
        loc = info[LOC + piece]
        length = info[LENGTH + loc]
        keys = pl.ds(pl.multiple_of(loc * seq_len, seq_len), seq_len)
        usable = lax.broadcasted_iota(jnp.int32, (block, seq_len), 1) < length
        for head in range(heads):
            lanes = slice(head * head_size, (head + 1) * head_size)
            scores = nt(scaled[here, lanes], kv_out[0, keys, lanes])
            scores = jnp.where(usable, scores, -1e30)
            largest = jnp.max(scores, -1, keepdims=True)
            powers = jnp.exp(scores - largest)
            sums = jnp.sum(powers, -1, keepdims=True)
            value = kv_out[0, keys, width + head * head_size : width + (head + 1) * head_size]
            context = nn(powers.astype(LOW), value) / sums
            ctx_out[0, here, lanes] = context
            lse_out[0, here, head : head + 1] = largest + jnp.log(sums)
    gated = (ctx_out[0] * row[:, width : 2 * width]).astype(LOW)
    gated_out[0] = gated
    part = nt(gated, right_buf[slot, :, width:])

    @pl.when(r == 0)
    def _():
        total[...] = part

    @pl.when(r > 0)
    def _():
        total[...] += part

    @pl.when(r == groups - 1)
    def _():
        base = 6 * layer
        if first:
            current = xwin[pl.ds(own, rows), :].astype(F32)
        else:
            current = resid[...]
        before = current + total[...] + vec[base + BIAS_ONE : base + BIAS_ONE + 1, :]
        middle = norm_forward(
            before,
            vec[base + GAIN_ONE : base + GAIN_ONE + 1, :],
            vec[base + SHIFT_ONE : base + SHIFT_ONE + 1, :],
        )
        before_out[...] = before
        h_out[...] = middle
        hb_out[...] = middle.astype(LOW)


def gelu_parts(unit):
    square = unit * unit
    bent = jnp.tanh(GELU_C * unit * (1.0 + GELU_K * square))
    half = 0.5 * (1.0 + bent)
    slope = half + 0.5 * unit * (1.0 - bent * bent) * (GELU_C * (1.0 + 3.0 * GELU_K * square))
    return unit * half, slope


def feed_forward(layer, left, right, info, *refs):
    refs = list(refs)
    middle, middle_low, small, vec = refs[:4]
    refs = refs[4:]
    left_refs = [refs.pop(0) for _ in left.operands()]
    right_refs = [refs.pop(0) for _ in right.operands()]
    unit_out, before_out, x_out, xb_out = refs[:4]
    left_buf, left_sems, right_buf, right_sems, total = refs[4:]
    r, groups = pl.program_id(0), pl.num_programs(0)
    slot = turn(
        [left.stream(left_refs, left_buf, left_sems), right.stream(right_refs, right_buf, right_sems)], r, groups
    )
    unit = nn(middle_low[...], left_buf[slot]) + small[0, 4 * layer + 1 : 4 * layer + 2, :]
    unit_out[0] = unit.astype(LOW)
    bent = jnp.tanh(GELU_C * unit * (1.0 + GELU_K * (unit * unit)))
    active = (0.5 * unit * (1.0 + bent) * small[0, 4 * layer : 4 * layer + 1, :]).astype(LOW)
    part = nt(active, right_buf[slot])

    @pl.when(r == 0)
    def _():
        total[...] = part

    @pl.when(r > 0)
    def _():
        total[...] += part

    @pl.when(r == groups - 1)
    def _():
        base = 6 * layer
        before = middle[...] + total[...] + vec[base + BIAS_TWO : base + BIAS_TWO + 1, :]
        current = norm_forward(
            before,
            vec[base + GAIN_TWO : base + GAIN_TWO + 1, :],
            vec[base + SHIFT_TWO : base + SHIFT_TWO + 1, :],
        )
        before_out[...] = before
        x_out[...] = current
        xb_out[...] = current.astype(LOW)


def match_teacher(layers, weight, info, *refs):
    refs = list(refs)
    states = [refs.pop(0) for _ in range(layers)]
    target, row_ok, factor = refs[:3]
    refs = refs[3:]
    weight_refs = [refs.pop(0) for _ in weight.operands()]
    back_out, loss_out, keep_out, send_out = refs[:4]
    buf, sems = refs[4:]
    r, groups = pl.program_id(0), pl.num_programs(0)
    slot = turn([weight.stream(weight_refs, buf, sems)], r, groups)

    @pl.when(r == 0)
    def _():
        loss_out[...] = jnp.zeros_like(loss_out)
        back_out[...] = jnp.zeros_like(back_out)

    total = None
    for layer in range(layers):
        miss = (nn(states[layer][...], buf[slot]) - target[0, layer].astype(F32)) * row_ok[:, :1]
        loss_out[:1, : miss.shape[1]] += jnp.sum(miss * miss, 0, keepdims=True)
        low = (factor[0, 0] * miss).astype(LOW)
        back_out[layer] += nt(low, buf[slot])
        grad = tn(states[layer][...], low)
        total = grad if total is None else total + grad
    half = keep_out.shape[1]
    keep_out[0] = total[:half].astype(LOW)
    send_out[0] = total[half:].astype(LOW)


def feed_backward(layer, last, left, right, info, *refs):
    refs = list(refs)
    before_two, before_one, middle_low, unit_in, small, vec = refs[:6]
    refs = refs[6:]
    if last:
        grad_refs = refs[:2]
        refs = refs[2:]
    else:
        grad_refs = refs[:3]
        refs = refs[3:]
    left_refs = [refs.pop(0) for _ in left.operands()]
    right_refs = [refs.pop(0) for _ in right.operands()]
    inner_keep, inner_send, outer_keep, outer_send, attn_out, grad_out, vec_out, unit_vec = refs[:8]
    left_buf, left_sems, right_buf, right_sems, total, feed = refs[8:]
    r, groups = pl.program_id(0), pl.num_programs(0)
    slot = turn(
        [left.stream(left_refs, left_buf, left_sems), right.stream(right_refs, right_buf, right_sems)], r, groups
    )
    base = 6 * layer

    @pl.when(r == 0)
    def _():
        if last:
            cotangent, back = grad_refs
            grad = cotangent[...].astype(F32) + back[...]
        else:
            mine, pair, mid = grad_refs
            total[...] = mine[...] + pair[...].astype(F32)
            here = pl.ds(pl.multiple_of(info[MID_ROW], mid.shape[0] // 2), mid.shape[0])
            total[here, :] += mid[...].astype(F32)
            grad = total[...]
        grad_before, grad_gain, grad_shift, grad_bias = norm_backward(
            before_two[...], vec[base + GAIN_TWO : base + GAIN_TWO + 1, :], grad
        )
        vec_out[BIAS_TWO : BIAS_TWO + 1, :] = grad_bias
        vec_out[GAIN_TWO : GAIN_TWO + 1, :] = grad_gain
        vec_out[SHIFT_TWO : SHIFT_TWO + 1, :] = grad_shift
        feed[...] = grad_before.astype(LOW)
        total[...] = grad_before

    grad_active = nn(feed[...], right_buf[slot])
    value, slope = gelu_parts(unit_in[0].astype(F32))
    opened = small[0, 4 * layer : 4 * layer + 1, :]
    grad_unit = (grad_active * (slope * opened)).astype(LOW)
    unit_vec[0, 0:1, :] = jnp.sum(grad_unit.astype(F32), 0, keepdims=True)
    unit_vec[0, 1:2, :] = jnp.sum(grad_active * value, 0, keepdims=True)
    active = (value * opened).astype(LOW)
    half = inner_keep.shape[1]
    total[...] += nt(grad_unit, left_buf[slot])
    inner_keep[0] = tn(middle_low[:, :half], grad_unit).astype(LOW)
    inner_send[0] = tn(middle_low[:, half:], grad_unit).astype(LOW)
    outer_keep[0] = tn(feed[:, :half], active).astype(LOW)
    outer_send[0] = tn(feed[:, half:], active).astype(LOW)

    @pl.when(r == groups - 1)
    def _():
        grad_before, grad_gain, grad_shift, grad_bias = norm_backward(
            before_one[...], vec[base + GAIN_ONE : base + GAIN_ONE + 1, :], total[...]
        )
        vec_out[BIAS_ONE : BIAS_ONE + 1, :] = grad_bias
        vec_out[GAIN_ONE : GAIN_ONE + 1, :] = grad_gain
        vec_out[SHIFT_ONE : SHIFT_ONE + 1, :] = grad_shift
        grad_out[...] = grad_before
        attn_out[...] = grad_before.astype(LOW)


def attention_backward(size, layer, extra, left, right, info, *refs):
    seq_len, block, heads, head_size = size
    refs = list(refs)
    attn, grad_before, xwin, query_in, kv, ctx, lse, gated, small = refs[:9]
    refs = refs[9:]
    back = refs.pop(0) if extra else None
    left_refs = [refs.pop(0) for _ in left.operands()]
    right_refs = [refs.pop(0) for _ in right.operands()]
    left_keep, left_send, right_keep, right_send, mine_out, pair_out, mid_out, head_vec = refs[:8]
    left_buf, left_sems, right_buf, right_sems, grad_kv, grad_q, window, mine = refs[8:]
    r, groups = pl.program_id(0), pl.num_programs(0)
    slot = turn(
        [left.stream(left_refs, left_buf, left_sems), right.stream(right_refs, right_buf, right_sems)], r, groups
    )
    width = heads * head_size
    rows = mine.shape[0]
    row = small[0, 4 * layer + 2 : 4 * layer + 3, :]
    opened = row[:, width : 2 * width]
    grad_gated = nn(attn[...], right_buf[slot, :, width:])
    shared = grad_gated * ctx[0]
    grad_ctx = (grad_gated * opened).astype(LOW)
    pulled = shared * opened
    scaled = query_in[0] * jnp.asarray(0.125, LOW)
    grad_kv[...] = jnp.zeros_like(grad_kv)
    for piece in range(rows // block):
        here = slice(piece * block, (piece + 1) * block)
        loc = info[LOC + piece]
        length = info[LENGTH + loc]
        keys = pl.ds(pl.multiple_of(loc * seq_len, seq_len), seq_len)
        usable = lax.broadcasted_iota(jnp.int32, (block, seq_len), 1) < length
        for head in range(heads):
            lanes = slice(head * head_size, (head + 1) * head_size)
            later = slice(width + head * head_size, width + (head + 1) * head_size)
            key = kv[0, keys, lanes]
            scores = nt(scaled[here, lanes], key)
            chances = jnp.where(usable, jnp.exp(scores - lse[0, here, head : head + 1]), 0.0)
            grad_chances = nt(grad_ctx[here, lanes], kv[0, keys, later])
            delta = jnp.sum(pulled[here, lanes], -1, keepdims=True)
            grad_scores = (chances * (grad_chances - delta)).astype(LOW)
            grad_q[here, lanes] = nn(grad_scores, key) * 0.125
            grad_kv[keys, lanes] += tn(grad_scores, scaled[here, lanes])
            grad_kv[keys, later] += tn(chances.astype(LOW), grad_ctx[here, lanes])
    query_low = grad_q[...].astype(LOW)
    kv_low = grad_kv[...].astype(LOW)
    head_vec[0, 0:1, :width] = jnp.sum(query_low.astype(F32), 0, keepdims=True)
    head_vec[0, 0:1, 2 * width :] = jnp.sum(kv_low.astype(F32), 0, keepdims=True)
    head_vec[0, 1:2, :width] = jnp.sum(shared, 0, keepdims=True)
    own = pl.multiple_of(info[OWN], block)

    @pl.when(r == 0)
    def _():
        window[...] = jnp.zeros_like(window)
        if extra:
            mine[...] = grad_before[...] + back[0]
        else:
            mine[...] = grad_before[...]

    window[...] += nt(kv_low, left_buf[slot])
    mine[...] += nt(query_low, right_buf[slot, :, :width])
    half = left_keep.shape[1]
    left_keep[0] = tn(xwin[:, :half], kv_low).astype(LOW)
    left_send[0] = tn(xwin[:, half:], kv_low).astype(LOW)
    here = pl.ds(own, rows)
    right_keep[0, :, :width] = tn(xwin[here, :half], query_low).astype(LOW)
    right_send[0, :, :width] = tn(xwin[here, half:], query_low).astype(LOW)
    right_keep[0, :, width:] = tn(attn[:, :half], gated[0]).astype(LOW)
    right_send[0, :, width:] = tn(attn[:, half:], gated[0]).astype(LOW)

    @pl.when(r == groups - 1)
    def _():
        mine_out[...] = mine[...] + window[here, :]
        pair_out[...] = window[pl.ds(pl.multiple_of(info[PAIR], block), rows), :].astype(LOW)
        mid_out[...] = window[pl.ds(pl.multiple_of(info[MID], block), mid_out.shape[0]), :].astype(LOW)


def place_rows(groups, info, *refs):
    pieces, matrix, out = refs[:groups], refs[groups], refs[groups + 1]
    r = pl.program_id(0)
    for group in range(groups):

        @pl.when(r == group)
        def _(group=group):
            out[...] = nn(pieces[group][...], matrix[...]).astype(out.dtype)


def factor_pair(count):
    side = 1
    for trial in range(1, count + 1):
        if count % trial == 0 and trial * trial <= count:
            side = trial
    return side, count // side


def after(value, *others):
    return lax.optimization_barrier((value,) + others)[0]


def on_device(
    ndp,
    groups,
    hidden_in,
    seq_lengths,
    layer_map,
    teacher_states,
    out_cotangent,
    query_weight,
    key_weight,
    value_weight,
    query_value_bias,
    output_weight,
    branch_bias,
    norm_gain,
    norm_shift,
    inner_weight,
    inner_bias,
    outer_weight,
    head_alpha,
    head_noise,
    unit_alpha,
    unit_noise,
    map_weight,
):
    tokens_dev, model = hidden_in.shape
    seqs_dev = seq_lengths.shape[0]
    seq_len = tokens_dev // seqs_dev
    width = query_weight.shape[2]
    units = inner_weight.shape[2]
    layers, heads = head_alpha.shape
    head_size = width // heads
    rows = tokens_dev // groups
    block = seq_len // groups
    blocks = rows // block
    mid_rows = 2 * block
    feats = model // ndp
    size_y, size_x = factor_pair(ndp // 2)
    chips = size_y * size_x
    half = chips * feats
    size = (seq_len, block, heads, head_size)
    dp = lax.axis_index("dp")
    h = lax.axis_index("head")
    my_c, my_x, my_y = dp % 2, (dp // 2) % size_x, dp // (2 * size_x)

    def relative(index, c, y, x):
        core, ix, iy = index % 2, (index // 2) % size_x, index // (2 * size_x)
        return (((iy + y) % size_y) * size_x + (ix + x) % size_x) * 2 + (core ^ c)

    def pull(value, c=0, y=0, x=0):
        return lax.ppermute(value, "dp", [(relative(i, c, y, x), i) for i in range(ndp)])

    def push(value, c=0, y=0, x=0):
        return lax.ppermute(value, "dp", [(i, relative(i, c, y, x)) for i in range(ndp)])

    def pull_group(value, r):
        return lax.ppermute(value, "head", [((i + r) % groups, i) for i in range(groups)])

    def push_group(value, r):
        return lax.ppermute(value, "head", [(i, (i + r) % groups) for i in range(groups)])

    def sum_plane(value):
        for axis, count in (("c", 2), ("y", size_y), ("x", size_x)):
            step = 1
            while step < count:
                stride = {"c": 1, "x": 2, "y": 2 * size_x}[axis] * step
                value = value + lax.ppermute(value, "dp", [(i, i ^ stride) for i in range(ndp)])
                step *= 2
        return value

    def sum_groups(value):
        step = 1
        while step < groups:
            value = value + lax.ppermute(value, "head", [(i, i ^ step) for i in range(groups)])
            step *= 2
        return value

    position = jnp.arange(ndp)
    pos_c, pos_y, pos_x = position // chips, (position // size_x) % size_y, position % size_x
    order = (((my_y + pos_y) % size_y) * size_x + (my_x + pos_x) % size_x) * 2 + (my_c ^ pos_c)
    place = (my_c ^ (position % 2)) * chips
    place = place + ((position // (2 * size_x) - my_y) % size_y) * size_x
    place = place + ((position // 2) % size_x - my_x) % size_x
    source = (order[:, None] * feats + jnp.arange(feats)[None, :]).reshape(model)
    matrix = (source[:, None] == jnp.arange(model)[None, :]).astype(LOW)

    def reorder(value):
        return product(matrix, value, (1, 0)).astype(LOW)

    def reorder_turned(value):
        return product(matrix, value, (1, 1)).astype(LOW)

    def gather(own, dep, y_first):
        mine = own[:feats]
        if dep is not None:
            mine = after(mine, dep)
        got = [pull_group(mine, r) for r in range(1, groups)]
        token = got[0]
        start = jnp.stack(got)
        found = {(0, 0): start}
        if y_first:
            for y in range(1, size_y):
                found[y, 0] = pull(start, y=y)
            for y in range(size_y):
                for x in range(1, size_x):
                    found[y, x] = pull(found[y, 0], x=x)
        else:
            for x in range(1, size_x):
                found[0, x] = pull(start, x=x)
            for x in range(size_x):
                for y in range(1, size_y):
                    found[y, x] = pull(found[0, x], y=y)
        pieces = [found[y, x] for y in range(size_y) for x in range(size_x)]
        if feats % 16:
            pieces = [jnp.concatenate(pieces, 1)]
        return Gathered(own, pieces + [pull(piece, c=1) for piece in pieces]), token

    def scatter(keep, send, y_first):
        terms = [keep, pull(send, c=1)]
        terms = [term.reshape(groups, size_y, size_x, feats, term.shape[-1]) for term in terms]

        def total(items):
            out = items[0].astype(F32)
            for item in items[1:]:
                out = out + item.astype(F32)
            return out

        for axis, count in (("y", size_y), ("x", size_x)) if y_first else (("x", size_x), ("y", size_y)):
            dim = 1 if axis == "y" else terms[0].ndim - 3

            def part(index):
                return [lax.index_in_dim(term, index, dim, keepdims=False) for term in terms]

            arrived = [push(total(part(i)).astype(LOW), **{axis: i}) for i in range(1, count)]
            terms = part(0) + arrived
        final = [term[0] for term in terms]
        for r in range(1, groups):
            final.append(push_group(total([term[r] for term in terms]).astype(LOW), r))
        return total(final)

    dep = None
    attn_weights, feed_weights = [], []
    for layer in range(layers):
        key_value = reorder(jnp.concatenate([key_weight[layer], value_weight[layer]], 1))
        query_output = jnp.concatenate(
            [reorder(query_weight[layer]), reorder_turned(output_weight[layer])], 1
        )
        inner = reorder(inner_weight[layer])
        outer = reorder_turned(outer_weight[layer])
        if layer == 0:
            left, dep = gather(key_value, dep, False)
            right, _ = gather(query_output, None, True)
            attn_weights.append((left, right))
            left, next_dep = gather(inner, dep, False)
            right, _ = gather(outer, dep, True)
            feed_weights.append((left, right))
            dep = next_dep
        else:
            left, next_dep = gather(jnp.concatenate([key_value, inner], 1), dep, False)
            right, _ = gather(jnp.concatenate([query_output, outer], 1), dep, True)
            attn_weights.append((left.columns(0, 2 * width), right.columns(0, 2 * width)))
            feed_weights.append((left.columns(2 * width, units), right.columns(2 * width, units)))
            dep = next_dep
    map_gathered, dep = gather(reorder(map_weight), dep, False)

    open_unit, unit_back = jax.vjp(partial(gate_open, unit_noise), unit_alpha)
    open_head, head_back = jax.vjp(partial(gate_open, head_noise), head_alpha)
    (unit_slope,) = unit_back(jnp.ones_like(open_unit))
    (head_slope,) = head_back(jnp.ones_like(open_head))
    mixed = jnp.concatenate(
        [
            query_value_bias[:, 0],
            jnp.repeat(open_head, head_size, axis=1),
            jnp.zeros((layers, width), F32),
            query_value_bias[:, 1],
        ],
        1,
    )
    empty = jnp.zeros((layers, units), F32)
    small_own = jnp.stack([open_unit, inner_bias, mixed, empty], 1).reshape(4 * layers, units)
    small = jnp.stack([small_own] + [pull_group(small_own, r) for r in range(1, groups)])
    vec = jnp.concatenate([branch_bias, norm_gain, norm_shift], 1).reshape(6 * layers, ndp, feats)
    vec = jnp.take(vec, order, axis=1).reshape(6 * layers, model)
    vec = jnp.concatenate([vec, jnp.zeros((16 - 6 * layers, model), F32)])

    win = jnp.minimum(h * rows // seq_len, seqs_dev - 2)
    base = win * seq_len
    pair_index = h ^ 1
    piece = jnp.arange(blocks)
    locs = (h * blocks + piece) * block // seq_len - win
    mid_row = jnp.where(h == 1, block, 0)
    lengths = lax.dynamic_slice(seq_lengths, (win,), (2,))
    info = jnp.concatenate(
        [
            jnp.stack([h * rows - base, pair_index * rows - base, jnp.where(h == 1, 2 * rows, 0), mid_row]),
            locs,
            jnp.zeros((LENGTH - LOC - blocks,), jnp.int32),
            lengths,
        ]
    ).astype(jnp.int32)
    spot = (h * rows + jnp.arange(rows)) % seq_len
    own_lengths = jnp.repeat(jnp.take(lengths, locs), block, total_repeat_length=rows)
    row_ok = jnp.broadcast_to((spot < own_lengths).astype(F32)[:, None], (rows, 128))
    count_all = sum_plane(jnp.sum(seq_lengths).astype(F32).reshape(1, 1))
    factor = (tokens_dev * ndp) / count_all

    hidden = product(lax.dynamic_slice(hidden_in, (base, 0), (2 * seq_len, model)), matrix, (1, 1)).astype(LOW)
    cotangent = product(
        lax.dynamic_slice(out_cotangent, (h * rows, 0), (rows, model)), matrix, (1, 1)
    ).astype(LOW)
    chosen = jnp.take(teacher_states, layer_map, axis=0)

    def teacher_rows(r):
        return lax.dynamic_slice(
            chosen, (0, ((h - r) % groups) * rows, 0), (layers, rows, width)
        )

    target = jnp.stack(
        [teacher_rows(0)] + [pull_group(after(teacher_rows(r), dep), r) for r in range(1, groups)]
    )

    xwin, resid = hidden, None
    records = []
    lows = []
    for layer in range(layers):
        left, right = attn_weights[layer]
        inputs = [(xwin, "full"), (small, "group"), (vec, "full")]
        if layer:
            inputs.append((resid, "full"))
        kv, query, ctx, lse, gated, before_one, middle, middle_low = run(
            partial(attention_forward, size, layer, layer == 0, left, right),
            groups,
            info,
            inputs + left.operands() + right.operands(),
            [
                ((groups, 2 * seq_len, 2 * width), LOW, "group"),
                ((groups, rows, width), LOW, "group"),
                ((groups, rows, width), F32, "group"),
                ((groups, rows, 128), F32, "group"),
                ((groups, rows, width), LOW, "group"),
                ((rows, model), F32, "full"),
                ((rows, model), F32, "full"),
                ((rows, model), LOW, "full"),
            ],
            left.scratch() + right.scratch() + [pltpu.VMEM((rows, model), F32)],
            8e9,
            "attention_forward",
        )
        left, right = feed_weights[layer]
        unit_in, before_two, resid, low = run(
            partial(feed_forward, layer, left, right),
            groups,
            info,
            [(middle, "full"), (middle_low, "full"), (small, "group"), (vec, "full")]
            + left.operands()
            + right.operands(),
            [
                ((groups, rows, units), LOW, "group"),
                ((rows, model), F32, "full"),
                ((rows, model), F32, "full"),
                ((rows, model), LOW, "full"),
            ],
            left.scratch() + right.scratch() + [pltpu.VMEM((rows, model), F32)],
            5e9,
            "feed_forward",
        )
        records.append((xwin, kv, query, ctx, lse, gated, before_one, middle_low, unit_in, before_two))
        lows.append(low)
        if layer + 1 < layers:
            pair = lax.ppermute(low, "head", [(i, i ^ 1) for i in range(groups)])
            mid = lax.ppermute(
                lax.dynamic_slice(low, (mid_row, 0), (mid_rows, model)), "head", [(1, 2), (2, 1)]
            )
            odd = h % 2 == 1
            ahead = jnp.where(odd, pair, low)
            behind = jnp.where(odd, low, pair)
            xwin = jnp.where(
                h < 2, jnp.concatenate([ahead, behind, mid]), jnp.concatenate([mid, ahead, behind])
            )
    back, loss, map_keep, map_send = run(
        partial(match_teacher, layers, map_gathered),
        groups,
        info,
        [(low, "full") for low in lows]
        + [(target, "group"), (row_ok, "full"), (factor, "full")]
        + map_gathered.operands(),
        [
            ((layers, rows, model), F32, "full"),
            ((8, 256), F32, "full"),
            ((groups, half, width), LOW, "group"),
            ((groups, half, width), LOW, "group"),
        ],
        map_gathered.scratch(),
        4e9,
        "match_teacher",
    )
    info_place = jnp.stack([h]).astype(jnp.int32)

    def place_all(value, dtype):
        pieces = [value] + [pull_group(value, r) for r in range(1, groups)]
        return pl.pallas_call(
            partial(place_rows, groups),
            name="place_rows",
            grid_spec=pltpu.PrefetchScalarGridSpec(
                num_scalar_prefetch=1,
                grid=(groups,),
                in_specs=[full(piece) for piece in pieces] + [full(matrix)],
                out_specs=pl.BlockSpec((rows, model), lambda r, info: (lax.rem(info[0] + r, groups), 0)),
            ),
            out_shape=jax.ShapeDtypeStruct((tokens_dev, model), dtype),
            compiler_params=pltpu.CompilerParams(vmem_limit_bytes=VMEM_LIMIT),
            cost_estimate=pl.CostEstimate(
                flops=2 * tokens_dev * model * model, bytes_accessed=8 * tokens_dev * model, transcendentals=0
            ),
        )(info_place, *pieces, matrix)

    block_out = place_all(lows[-1], LOW)

    grads = [(cotangent, "full"), (back[layers - 1], "full")]
    results = [None] * layers
    for layer in reversed(range(layers)):
        xwin, kv, query, ctx, lse, gated, before_one, middle_low, unit_in, before_two = records[layer]
        left, right = feed_weights[layer]
        inner_keep, inner_send, outer_keep, outer_send, attn, grad_before, vec_out, unit_vec = run(
            partial(feed_backward, layer, layer == layers - 1, left, right),
            groups,
            info,
            [
                (before_two, "full"),
                (before_one, "full"),
                (middle_low, "full"),
                (unit_in, "group"),
                (small, "group"),
                (vec, "full"),
            ]
            + grads
            + left.operands()
            + right.operands(),
            [((groups, half, units), LOW, "group")] * 4
            + [
                ((rows, model), LOW, "full"),
                ((rows, model), F32, "full"),
                ((8, model), F32, "full"),
                ((groups, 8, units), F32, "group"),
            ],
            left.scratch() + right.scratch() + [pltpu.VMEM((rows, model), F32), pltpu.VMEM((rows, model), LOW)],
            10e9,
            "feed_backward",
        )
        grad_inner = scatter(inner_keep, inner_send, False)
        grad_outer = scatter(outer_keep, outer_send, True)
        left, right = attn_weights[layer]
        extra = [(back[layer - 1 : layer], "full")] if layer else []
        left_keep, left_send, right_keep, right_send, mine, to_pair, to_mid, head_vec = run(
            partial(attention_backward, size, layer, bool(layer), left, right),
            groups,
            info,
            [
                (attn, "full"),
                (grad_before, "full"),
                (xwin, "full"),
                (query, "group"),
                (kv, "group"),
                (ctx, "group"),
                (lse, "group"),
                (gated, "group"),
                (small, "group"),
            ]
            + extra
            + left.operands()
            + right.operands(),
            [((groups, half, 2 * width), LOW, "group")] * 4
            + [
                ((rows, model), F32, "full"),
                ((rows, model), LOW, "full"),
                ((mid_rows, model), LOW, "full"),
                ((groups, 8, units), F32, "group"),
            ],
            left.scratch()
            + right.scratch()
            + [
                pltpu.VMEM((2 * seq_len, 2 * width), F32),
                pltpu.VMEM((rows, width), F32),
                pltpu.VMEM((2 * seq_len, model), F32),
                pltpu.VMEM((rows, model), F32),
            ],
            12e9,
            "attention_backward",
        )
        from_pair = lax.ppermute(to_pair, "head", [(i, i ^ 1) for i in range(groups)])
        from_mid = lax.ppermute(to_mid, "head", [(1, 2), (2, 1)])
        grads = [(mine, "full"), (from_pair, "full"), (from_mid, "full")]
        grad_kv = scatter(left_keep, left_send, False)
        grad_qo = scatter(right_keep, right_send, True)
        results[layer] = (grad_inner, grad_outer, grad_kv, grad_qo, vec_out, unit_vec, head_vec)
    grad_map = scatter(map_keep, map_send, False)
    grad_in = mine + from_pair.astype(F32)
    patch = lax.dynamic_slice(grad_in, (mid_row, 0), (mid_rows, model)) + from_mid.astype(F32)
    grad_in = lax.dynamic_update_slice(grad_in, patch, (mid_row, 0)).astype(LOW)
    grad_hidden = place_all(grad_in, F32)

    by_feature = jnp.concatenate([results[layer][4][:6] for layer in range(layers)])
    by_feature = jnp.take(by_feature.reshape(6 * layers, ndp, feats), place, axis=1)
    by_feature = by_feature.reshape(6 * layers, model)
    loss_row = jnp.concatenate([loss[:1], jnp.zeros((1, model - loss.shape[1]), F32)], 1)
    by_feature = sum_groups(jnp.concatenate([by_feature, loss_row]))
    by_unit = jnp.concatenate(
        [jnp.concatenate([results[layer][5][:, :2], results[layer][6][:, :2]], 1) for layer in range(layers)], 1
    )
    summed = by_unit[0]
    for r in range(1, groups):
        summed = summed + push_group(by_unit[r], r)
    everything = sum_plane(jnp.concatenate([by_feature, summed]))
    distill_loss = jnp.sum(everything[6 * layers]) / (count_all[0, 0] * model * layers)
    by_unit = everything[6 * layers + 1 :].reshape(layers, 4, units)
    mine_feats = lax.dynamic_slice(
        everything[: 6 * layers].reshape(layers, 3, 2, model), (0, 0, 0, dp * feats), (layers, 3, 2, feats)
    )
    unit_count = units // ndp
    mine_units = lax.dynamic_slice(by_unit[:, :2], (0, 0, dp * unit_count), (layers, 2, unit_count))
    own_slope = lax.dynamic_slice(unit_slope, (0, dp * unit_count), (layers, unit_count))
    qv_cols = width // ndp
    both = jnp.stack([by_unit[:, 2, :width], by_unit[:, 2, 3 * width : 4 * width]], 1)
    grad_qv_bias = lax.dynamic_slice(both, (0, 0, dp * qv_cols), (layers, 2, qv_cols))
    head_sums = jnp.sum(by_unit[:, 3, :width].reshape(layers, heads, head_size), -1)

    def stacked(member, cols, turned=False):
        arrays = [results[layer][member][:, cols] for layer in range(layers)]
        return jnp.stack([array.T if turned else array for array in arrays])

    front, rear, whole = slice(0, width), slice(width, 2 * width), slice(None)
    return (
        block_out,
        grad_hidden,
        distill_loss,
        stacked(3, front),
        stacked(2, front),
        stacked(2, rear),
        grad_qv_bias,
        stacked(3, rear, True),
        mine_feats[:, 0],
        mine_feats[:, 1],
        mine_feats[:, 2],
        stacked(0, whole),
        mine_units[:, 0],
        stacked(1, whole, True),
        head_sums * head_slope,
        mine_units[:, 1] * own_slope,
        grad_map,
    )


def solution(mesh):
    in_specs = (
        P("dp", None),
        P("dp"),
        P(),
        P(None, "dp", "head"),
        P("dp", None),
        P(None, None, "head"),
        P(None, None, "head"),
        P(None, None, "head"),
        P(None, None, "head"),
        P(None, "head", None),
        P(),
        P(),
        P(),
        P(None, None, "head"),
        P(None, "head"),
        P(None, "head", None),
        P(None, "head"),
        P(None, "head"),
        P(None, "head"),
        P(None, "head"),
        P(None, "head"),
    )
    out_specs = (
        P("dp", None),
        P("dp", None),
        P(),
        P(None, "dp", "head"),
        P(None, "dp", "head"),
        P(None, "dp", "head"),
        P(None, None, ("head", "dp")),
        P(None, "head", "dp"),
        P(None, None, "dp"),
        P(None, None, "dp"),
        P(None, None, "dp"),
        P(None, "dp", "head"),
        P(None, ("head", "dp")),
        P(None, "head", "dp"),
        P(None, "head"),
        P(None, ("head", "dp")),
        P("dp", "head"),
    )
    return jax.shard_map(
        partial(on_device, mesh.shape["dp"], mesh.shape["head"]),
        mesh=mesh,
        in_specs=in_specs,
        out_specs=out_specs,
        check_vma=False,
    )
```

```python
from functools import partial

import jax
import jax.numpy as jnp
from jax import lax
from jax.experimental import pallas as pl
from jax.experimental.pallas import tpu as pltpu
from jax.sharding import PartitionSpec as P

BETA = 2.0 / 3.0
EPS = 1e-05
LOW = jnp.bfloat16
F32 = jnp.float32
GELU_C = 0.7978845608028654
GELU_K = 0.044715
VMEM_LIMIT = 56 * 1024 * 1024
ATTN_CUTS = (128, 256)
FEED_CUTS = (256, 256, 256)


def gate_open(noise, alpha):
    return jnp.clip(jax.nn.sigmoid((noise + alpha) / BETA) * 1.2 - 0.1, 0.0, 1.0)


def product(left, right, dims):
    return lax.dot_general(left, right, ((dims[:1], dims[1:]), ((), ())), preferred_element_type=F32)


def nn(left, right):
    return product(left, right, (1, 0))


def nt(left, right):
    return product(left, right, (1, 1))


def tn(left, right):
    return product(left, right, (0, 0))


def full(array):
    shape = array.shape
    return pl.BlockSpec(shape, lambda r: (0,) * len(shape))


def by_group(array):
    shape = array.shape
    return pl.BlockSpec((1,) + shape[1:], lambda r: (r,) + (0,) * (len(shape) - 1))


SPECS = {
    "full": full,
    "group": by_group,
    "any": lambda a: pl.BlockSpec(memory_space=pl.ANY),
    "smem": lambda a: pl.BlockSpec(memory_space=pltpu.SMEM),
}


def run(body, groups, inputs, outputs, scratch, flops, name, riders=(), points=1, number=None):
    count = len(inputs)
    sizes = []
    inputs, outputs, scratch = list(inputs), list(outputs), list(scratch)
    n_out, n_scratch = len(outputs), len(scratch)
    for rider in riders:
        sizes.append((len(rider.inputs), len(rider.outputs), len(rider.scratch)))
        inputs += rider.inputs
        outputs += rider.outputs
        scratch += rider.scratch
    out_shape = [jax.ShapeDtypeStruct(shape, dtype) for shape, dtype, _ in outputs]
    moved = sum(a.size * a.dtype.itemsize for a, kind in inputs if kind != "any")

    def whole(*refs):
        refs = list(refs)
        ins, outs, tmps = refs[: len(inputs)], refs[len(inputs) : len(inputs) + len(outputs)], refs[len(inputs) + len(outputs) :]
        at = [count, n_out, n_scratch]
        tasks = []
        for rider, size in zip(riders, sizes):
            tasks.append(rider.tasks(*[part[i : i + n] for part, i, n in zip((ins, outs, tmps), at, size)]))
            at = [i + n for i, n in zip(at, size)]
        merged = []
        longest = max([len(t) for t in tasks], default=0)
        for index in range(longest):
            merged += [t[index] for t in tasks if index < len(t)]
        slots = groups * points
        r = pl.program_id(0)
        chosen = [[] for _ in range(slots)]
        for index, task in enumerate(merged):
            chosen[round(index * (slots - 1) / max(1, len(merged) - 1))].append(task)

        def point(spot):
            for step in range(groups):
                if chosen[step * points + spot]:

                    @pl.when(r == step)
                    def _(step=step):
                        if step == 0 and spot == 0:
                            riders[0].geo.greet()
                        for task in chosen[step * points + spot]:
                            task()

        body(point, *ins[:count], *outs[:n_out], *tmps[:n_scratch])

    params = {"vmem_limit_bytes": VMEM_LIMIT}
    if riders:
        params.update(collective_id=number, has_side_effects=True)
    return pl.pallas_call(
        whole,
        name=name,
        grid=(groups,),
        in_specs=[SPECS[kind](a) for a, kind in inputs],
        out_specs=[SPECS[kind](o) for o, (_, _, kind) in zip(out_shape, outputs)],
        scratch_shapes=scratch,
        out_shape=out_shape,
        compiler_params=pltpu.CompilerParams(**params),
        cost_estimate=pl.CostEstimate(flops=int(flops), bytes_accessed=int(moved), transcendentals=0),
    )(*[a for a, _ in inputs])


class Geometry:
    def __init__(self, ndp, groups):
        self.ndp, self.groups = ndp, groups
        self.size_y, self.size_x = factor_pair(ndp // 2)
        self.chips = self.size_y * self.size_x

    def here(self):
        dp, h = lax.axis_index("dp"), lax.axis_index("head")
        return lax.rem(dp, 2), lax.rem(lax.div(dp, 2), self.size_x), lax.div(dp, 2 * self.size_x), h

    def device(self, c=0, y=0, x=0, z=0):
        core, ix, iy, h = self.here()
        core = 1 - core if c else core
        iy = lax.rem(iy + y + self.size_y, self.size_y) if y else iy
        ix = lax.rem(ix + x + self.size_x, self.size_x) if x else ix
        h = lax.rem(h + z + self.groups, self.groups) if z else h
        return ((iy * self.size_x + ix) * 2 + core, h)

    def peers(self):
        out = [dict(c=1)]
        out += [dict(y=y) for y in range(1, self.size_y)]
        out += [dict(x=x) for x in range(1, self.size_x)]
        return out + [dict(z=z) for z in range(1, self.groups)]

    def greet(self):
        barrier = pltpu.get_barrier_semaphore()
        for peer in self.peers():
            pl.semaphore_signal(barrier, inc=1, device_id=self.device(**peer), device_id_type=pl.DeviceIdType.MESH)
        pl.semaphore_wait(barrier, len(self.peers()))


class Mover:
    def __init__(self, geo, send, recv):
        self.geo, self.send, self.recv, self.ids, self.copies = geo, send, recv, {}, []

    def __call__(self, key, src, dst, **to):
        index = self.ids.setdefault(key, len(self.ids))
        return pltpu.make_async_remote_copy(
            src_ref=src,
            dst_ref=dst,
            send_sem=self.send.at[index],
            recv_sem=self.recv.at[index],
            device_id=self.geo.device(**to),
            device_id_type=pl.DeviceIdType.MESH,
        )


class Gather:
    def __init__(self, geo, owns, chunks):
        self.geo, self.chunks = geo, chunks
        self.inputs = [(own, "any") for own in owns]
        self.outputs = [((geo.groups,) + own.shape, LOW, "any") for own in owns]
        halves = sum(len(chunk) for chunk in chunks)
        each = geo.groups - 1 + 2 * geo.chips
        sems = pltpu.SemaphoreType.DMA((halves * each,))
        self.scratch = [sems, sems, pltpu.SemaphoreType.DMA((len(owns),))]

    def tasks(self, owns, outs, scratch):
        geo, send, recv, local = self.geo, *scratch
        move = Mover(geo, send, recv)
        groups, sx, sy = geo.groups, geo.size_x, geo.size_y
        others = pl.ds(1, groups - 1)

        def spot(y, x, c=0):
            return c * geo.chips + y * sx + x

        def along(chunk, half, r):
            m, col, cols, _ = self.chunks[chunk][half]
            return move(
                ("z", chunk, half, r),
                owns[m].at[0, :, pl.ds(col, cols)],
                outs[m].at[r, 0, :, pl.ds(col, cols)],
                z=-r,
            )

        def plane(chunk, half, at_y, at_x, **to):
            m, col, cols, _ = self.chunks[chunk][half]
            land = spot(at_y + to.get("y", 0), at_x + to.get("x", 0), to.get("c", 0))
            return move(
                ("p", chunk, half, land),
                outs[m].at[others, spot(at_y, at_x), :, pl.ds(col, cols)],
                outs[m].at[others, land, :, pl.ds(col, cols)],
                **{key: -value if key != "c" else value for key, value in to.items()},
            )

        def own_copy(m):
            return pltpu.make_async_copy(owns[m], outs[m].at[0], local.at[m])

        def halves(chunk):
            return range(len(self.chunks[chunk]))

        def firsts(chunk):
            out = []
            for half in halves(chunk):
                out += [plane(chunk, half, 0, 0, x=x) for x in range(1, sx)]
                out += [plane(chunk, half, 0, 0, y=y) for y in range(1, sy)]
            return out

        def seconds(chunk):
            out = []
            for half in halves(chunk):
                if self.chunks[chunk][half][3]:
                    out += [plane(chunk, half, y, 0, x=x) for y in range(1, sy) for x in range(1, sx)]
                else:
                    out += [plane(chunk, half, 0, x, y=y) for x in range(1, sx) for y in range(1, sy)]
            return out

        def cores(chunk, places):
            return [plane(chunk, half, y, x, c=1) for half in halves(chunk) for y, x in places]

        axes = [(0, x) for x in range(1, sx)] + [(y, 0) for y in range(1, sy)]
        corners = [(y, x) for y in range(1, sy) for x in range(1, sx)]

        def alongs(chunk):
            return [along(chunk, half, r) for half in halves(chunk) for r in range(1, groups)]

        def start(copies):
            for copy in copies:
                copy.start()

        def arrive(copies):
            for copy in copies:
                copy.wait_recv()

        count = len(self.chunks)

        def begin():
            start(alongs(0))
            if count > 1:
                start(alongs(1))
            for m in range(len(owns)):
                own_copy(m).start()

        def level_one(chunk):
            arrive(alongs(chunk))
            start(firsts(chunk))
            start(cores(chunk, [(0, 0)]))
            if chunk + 2 < count:
                start(alongs(chunk + 2))

        def level_two(chunk):
            arrive(firsts(chunk))
            start(seconds(chunk))
            start(cores(chunk, axes))

        def level_three(chunk):
            arrive(seconds(chunk))
            start(cores(chunk, corners))

        def end():
            for m in range(len(owns)):
                own_copy(m).wait()
            for chunk in range(count):
                arrive(cores(chunk, [(0, 0)] + axes + corners))
                for copy in alongs(chunk) + firsts(chunk) + seconds(chunk) + cores(chunk, [(0, 0)] + axes + corners):
                    copy.wait_send()

        out = [begin]
        for time in range(count + 2):
            for level, late in ((level_one, 0), (level_two, 1), (level_three, 2)):
                if 0 <= time - late < count:
                    out.append(partial(level, time - late))
        return out + [end]


class Scatter:
    def __init__(self, geo, grads, chunks):
        self.geo, self.chunks = geo, chunks
        self.inputs = [(grad, "any") for grad in grads]
        self.outputs = [(grad.shape[4:], F32, "full") for grad in grads]
        self.feats = grads[0].shape[4]
        halves = [half for chunk in chunks for half in chunk]
        each = 1 + (geo.size_x - 1) + (geo.size_y - 1) + geo.groups - 1
        sems = pltpu.SemaphoreType.DMA((len(halves) * each,))
        self.scratch = [sems, sems, pltpu.SemaphoreType.DMA((len(halves),))]
        for _, _, cols, y_first in halves:
            self.scratch += [pltpu.VMEM(shape, LOW) for shape in self.shapes(cols, y_first)]

    def shapes(self, cols, y_first):
        geo, feats = self.geo, self.feats
        near, far = (geo.size_y, geo.size_x) if y_first else (geo.size_x, geo.size_y)
        return [
            (geo.groups, geo.size_y, geo.size_x, feats, cols),
            (geo.groups, geo.size_y, geo.size_x, feats, cols),
            (near - 1, geo.groups, far, feats, cols),
            (far - 1, geo.groups, feats, cols),
            (geo.groups - 1, feats, cols),
        ]

    def tasks(self, grads, outs, scratch):
        geo, (send, recv, local), buffers = self.geo, scratch[:3], scratch[3:]
        move = Mover(geo, send, recv)
        groups, sx, sy = geo.groups, geo.size_x, geo.size_y
        index = {}
        for chunk, halves in enumerate(self.chunks):
            for half in range(len(halves)):
                index[chunk, half] = len(index)

        def parts(chunk, half):
            number = index[chunk, half]
            return self.chunks[chunk][half], number, buffers[5 * number : 5 * number + 5]

        def load(chunk, half):
            (m, col, cols, _), number, bufs = parts(chunk, half)
            return pltpu.make_async_copy(
                grads[m].at[:, 0, :, :, :, pl.ds(col, cols)], bufs[0], local.at[number]
            )

        def core(chunk, half):
            (m, col, cols, y_first), number, bufs = parts(chunk, half)
            return move(("c", chunk, half), grads[m].at[:, 1, :, :, :, pl.ds(col, cols)], bufs[1], c=1)

        def near(chunk, half):
            (m, col, cols, y_first), number, bufs = parts(chunk, half)
            if y_first:
                return [
                    move(("n", chunk, half, y), bufs[0].at[:, y], bufs[2].at[y - 1], y=y) for y in range(1, sy)
                ]
            return [
                move(("n", chunk, half, x), bufs[0].at[:, :, x], bufs[2].at[x - 1], x=x) for x in range(1, sx)
            ]

        def far(chunk, half):
            (m, col, cols, y_first), number, bufs = parts(chunk, half)
            if y_first:
                return [
                    move(("f", chunk, half, x), bufs[0].at[:, 0, x], bufs[3].at[x - 1], x=x) for x in range(1, sx)
                ]
            return [
                move(("f", chunk, half, y), bufs[0].at[:, y, 0], bufs[3].at[y - 1], y=y) for y in range(1, sy)
            ]

        def along(chunk, half):
            (m, col, cols, y_first), number, bufs = parts(chunk, half)
            return [
                move(("z", chunk, half, r), bufs[0].at[r, 0, 0], bufs[4].at[r - 1], z=r) for r in range(1, groups)
            ]

        def each(chunk):
            return range(len(self.chunks[chunk]))

        def start(copies):
            for copy in copies:
                copy.start()

        def arrive(copies):
            for copy in copies:
                copy.wait_recv()

        def begin_one(chunk):
            for half in each(chunk):
                core(chunk, half).start()
                load(chunk, half).start()

        count = len(self.chunks)

        def begin():
            begin_one(0)
            if count > 1:
                begin_one(1)

        def level_one(chunk):
            for half in each(chunk):
                _, _, bufs = parts(chunk, half)
                load(chunk, half).wait()
                core(chunk, half).wait_recv()
                for r in range(groups):
                    bufs[0][r] = (bufs[0][r].astype(F32) + bufs[1][r].astype(F32)).astype(LOW)
                start(near(chunk, half))
            if chunk + 2 < count:
                begin_one(chunk + 2)

        def level_two(chunk):
            for half in each(chunk):
                (m, col, cols, y_first), _, bufs = parts(chunk, half)
                arrive(near(chunk, half))
                for r in range(groups):
                    keep = (r, 0) if y_first else (r, slice(None), 0)
                    total = bufs[0][keep].astype(F32)
                    for other in range(bufs[2].shape[0]):
                        total = total + bufs[2][other, r].astype(F32)
                    bufs[0][keep] = total.astype(LOW)
                start(far(chunk, half))

        def level_three(chunk):
            for half in each(chunk):
                _, _, bufs = parts(chunk, half)
                arrive(far(chunk, half))
                for r in range(groups):
                    total = bufs[0][r, 0, 0].astype(F32)
                    for other in range(bufs[3].shape[0]):
                        total = total + bufs[3][other, r].astype(F32)
                    bufs[0][r, 0, 0] = total.astype(LOW)
                start(along(chunk, half))

        def level_four(chunk):
            for half in each(chunk):
                (m, col, cols, y_first), _, bufs = parts(chunk, half)
                arrive(along(chunk, half))
                total = bufs[0][0, 0, 0].astype(F32)
                for r in range(1, groups):
                    total = total + bufs[4][r - 1].astype(F32)
                outs[m][:, col : col + cols] = total

        def end():
            for chunk in range(count):
                for half in each(chunk):
                    for copy in [core(chunk, half)] + near(chunk, half) + far(chunk, half) + along(chunk, half):
                        copy.wait_send()

        out = [begin]
        for time in range(count + 3):
            for level, late in ((level_one, 0), (level_two, 1), (level_three, 2), (level_four, 3)):
                if 0 <= time - late < count:
                    out.append(partial(level, time - late))
        return out + [end]


def only_move(point):
    point(0)


def norm_forward(before, gain, shift):
    center = before - jnp.mean(before, -1, keepdims=True)
    spread = jnp.mean(center * center, -1, keepdims=True)
    return center * lax.rsqrt(spread + EPS) * gain + shift


def norm_backward(before, gain, grad):
    center = before - jnp.mean(before, -1, keepdims=True)
    rate = lax.rsqrt(jnp.mean(center * center, -1, keepdims=True) + EPS)
    hat = center * rate
    grad_hat = grad * gain
    mean_one = jnp.mean(grad_hat, -1, keepdims=True)
    mean_two = jnp.mean(grad_hat * hat, -1, keepdims=True)
    grad_before = rate * (grad_hat - mean_one - hat * mean_two)
    return (
        grad_before,
        jnp.sum(grad * hat, 0, keepdims=True),
        jnp.sum(grad, 0, keepdims=True),
        jnp.sum(grad_before, 0, keepdims=True),
    )


BIAS_ONE, BIAS_TWO, GAIN_ONE, GAIN_TWO, SHIFT_ONE, SHIFT_TWO = range(6)


class Window:
    def __init__(self, seqs, seq_len, rows, groups):
        self.seq_len, self.rows, self.groups = seq_len, rows, groups
        self.block = seq_len // groups
        self.seqs = seqs
        h = lax.axis_index("head")
        self.first = lax.div(h * (seqs - 1), groups)
        self.h = h
        self.base = self.first * seq_len
        self.own = h * rows - self.base
        self.pair = (h + 1 - 2 * lax.rem(h, 2)) * rows - self.base
        self.mid = lax.rem(h, 2) * (2 * rows)
        self.mid_row = lax.rem(h, 2) * self.block

    def at(self, start, rows):
        return pl.ds(pl.multiple_of(start, self.block), rows)

    def loc(self, piece):
        return lax.div((self.h * (self.rows // self.block) + piece) * self.block, self.seq_len) - self.first

    def keys(self, piece):
        return pl.ds(pl.multiple_of(self.loc(piece) * self.seq_len, self.seq_len), self.seq_len)


def attention_forward(size, layer, first, point, *refs):
    seqs, seq_len, heads, head_size = size
    refs = list(refs)
    xwin, small, vec, lengths, left, right = refs[:6]
    refs = refs[6:]
    resid = None if first else refs.pop(0)
    kv_out, q_out, ctx_out, lse_out, gated_out, before_out, h_out, hb_out, total = refs
    r, groups = pl.program_id(0), pl.num_programs(0)
    width = heads * head_size
    rows = total.shape[0]
    window = Window(seqs, seq_len, rows, total.shape[1] // width)
    block = window.block
    row = small[0, 4 * layer + 2 : 4 * layer + 3, :]
    point(0)
    kv = nn(xwin[...], left[0]) + row[:, 2 * width :]
    kv_out[0] = kv.astype(LOW)
    here = window.at(window.own, rows)
    query = (nn(xwin[here, :], right[0, :, :width]) + row[:, :width]).astype(LOW)
    q_out[0] = query
    scaled = query * jnp.asarray(0.125, LOW)
    for piece in range(rows // block):
        mine = slice(piece * block, (piece + 1) * block)
        keys = window.keys(piece)
        usable = lax.broadcasted_iota(jnp.int32, (block, seq_len), 1) < lengths[window.loc(piece)]
        for head in range(heads):
            lanes = slice(head * head_size, (head + 1) * head_size)
            scores = nt(scaled[mine, lanes], kv_out[0, keys, lanes])
            scores = jnp.where(usable, scores, -1e30)
            largest = jnp.max(scores, -1, keepdims=True)
            powers = jnp.exp(scores - largest)
            sums = jnp.sum(powers, -1, keepdims=True)
            value = kv_out[0, keys, width + head * head_size : width + (head + 1) * head_size]
            context = nn(powers.astype(LOW), value) / sums
            ctx_out[0, mine, lanes] = context
            lse_out[0, mine, head : head + 1] = largest + jnp.log(sums)
            point(1 + piece * heads + head)
    gated = (ctx_out[0] * row[:, width : 2 * width]).astype(LOW)
    gated_out[0] = gated
    part = nt(gated, right[0, :, width:])

    @pl.when(r == 0)
    def _():
        total[...] = part

    @pl.when(r > 0)
    def _():
        total[...] += part

    @pl.when(r == groups - 1)
    def _():
        base = 6 * layer
        if first:
            current = xwin[here, :].astype(F32)
        else:
            current = resid[...]
        before = current + total[...] + vec[base + BIAS_ONE : base + BIAS_ONE + 1, :]
        middle = norm_forward(
            before,
            vec[base + GAIN_ONE : base + GAIN_ONE + 1, :],
            vec[base + SHIFT_ONE : base + SHIFT_ONE + 1, :],
        )
        before_out[...] = before
        h_out[...] = middle
        hb_out[...] = middle.astype(LOW)

    point(1 + rows // block * heads)


def gelu_parts(unit):
    square = unit * unit
    bent = jnp.tanh(GELU_C * unit * (1.0 + GELU_K * square))
    half = 0.5 * (1.0 + bent)
    slope = half + 0.5 * unit * (1.0 - bent * bent) * (GELU_C * (1.0 + 3.0 * GELU_K * square))
    return unit * half, slope


def feed_forward(layer, point, *refs):
    middle, middle_low, small, vec, left, right = refs[:6]
    unit_out, before_out, x_out, xb_out, total = refs[6:]
    r, groups = pl.program_id(0), pl.num_programs(0)
    point(0)
    unit = nn(middle_low[...], left[0]) + small[0, 4 * layer + 1 : 4 * layer + 2, :]
    unit_out[0] = unit.astype(LOW)
    point(1)
    bent = jnp.tanh(GELU_C * unit * (1.0 + GELU_K * (unit * unit)))
    active = (0.5 * unit * (1.0 + bent) * small[0, 4 * layer : 4 * layer + 1, :]).astype(LOW)
    point(2)
    part = nt(active, right[0])

    @pl.when(r == 0)
    def _():
        total[...] = part

    @pl.when(r > 0)
    def _():
        total[...] += part

    @pl.when(r == groups - 1)
    def _():
        base = 6 * layer
        before = middle[...] + total[...] + vec[base + BIAS_TWO : base + BIAS_TWO + 1, :]
        current = norm_forward(
            before,
            vec[base + GAIN_TWO : base + GAIN_TWO + 1, :],
            vec[base + SHIFT_TWO : base + SHIFT_TWO + 1, :],
        )
        before_out[...] = before
        x_out[...] = current
        xb_out[...] = current.astype(LOW)

    point(3)


def match_teacher(layers, point, *refs):
    refs = list(refs)
    states = [refs.pop(0) for _ in range(layers)]
    target, row_ok, factor, weight = refs[:4]
    back_out, loss_out, grad_out = refs[4:]
    r = pl.program_id(0)

    @pl.when(r == 0)
    def _():
        loss_out[...] = jnp.zeros_like(loss_out)
        back_out[...] = jnp.zeros_like(back_out)

    total = None
    for layer in range(layers):
        miss = (nn(states[layer][...], weight[0]) - target[0, layer].astype(F32)) * row_ok[:, :1]
        loss_out[:1, : miss.shape[1]] += jnp.sum(miss * miss, 0, keepdims=True)
        low = (factor[...] * miss).astype(LOW)
        back_out[layer] += nt(low, weight[0])
        grad = tn(states[layer][...], low)
        total = grad if total is None else total + grad
    grad_out[0] = total.astype(LOW)


def feed_backward(size, layer, last, point, *refs):
    seqs, seq_len, heads, head_size = size
    refs = list(refs)
    before_two, before_one, middle_low, unit_in, small, vec, left, right = refs[:8]
    refs = refs[8:]
    if last:
        grad_refs = refs[:2]
        refs = refs[2:]
    else:
        grad_refs = refs[:3]
        refs = refs[3:]
    inner_out, outer_out, attn_out, grad_out, vec_out, unit_vec, total, feed = refs
    r, groups = pl.program_id(0), pl.num_programs(0)
    base = 6 * layer
    point(0)

    @pl.when(r == 0)
    def _():
        if last:
            cotangent, back = grad_refs
            grad = cotangent[...].astype(F32) + back[0]
        else:
            mine, pair, mid = grad_refs
            rows, model = mine.shape
            window = Window(seqs, seq_len, rows, model // (heads * head_size))
            total[...] = mine[...] + pair[...].astype(F32)
            total[window.at(window.mid_row, mid.shape[0]), :] += mid[...].astype(F32)
            grad = total[...]
        grad_before, grad_gain, grad_shift, grad_bias = norm_backward(
            before_two[...], vec[base + GAIN_TWO : base + GAIN_TWO + 1, :], grad
        )
        vec_out[BIAS_TWO : BIAS_TWO + 1, :] = grad_bias
        vec_out[GAIN_TWO : GAIN_TWO + 1, :] = grad_gain
        vec_out[SHIFT_TWO : SHIFT_TWO + 1, :] = grad_shift
        feed[...] = grad_before.astype(LOW)
        total[...] = grad_before

    grad_active = nn(feed[...], right[0])
    point(1)
    value, slope = gelu_parts(unit_in[0].astype(F32))
    opened = small[0, 4 * layer : 4 * layer + 1, :]
    grad_unit = (grad_active * (slope * opened)).astype(LOW)
    unit_vec[0, 0:1, :] = jnp.sum(grad_unit.astype(F32), 0, keepdims=True)
    unit_vec[0, 1:2, :] = jnp.sum(grad_active * value, 0, keepdims=True)
    active = (value * opened).astype(LOW)
    point(2)
    total[...] += nt(grad_unit, left[0])
    point(3)
    inner_out[0] = tn(middle_low[...], grad_unit).astype(LOW)
    point(4)
    outer_out[0] = tn(feed[...], active).astype(LOW)
    point(5)

    @pl.when(r == groups - 1)
    def _():
        grad_before, grad_gain, grad_shift, grad_bias = norm_backward(
            before_one[...], vec[base + GAIN_ONE : base + GAIN_ONE + 1, :], total[...]
        )
        vec_out[BIAS_ONE : BIAS_ONE + 1, :] = grad_bias
        vec_out[GAIN_ONE : GAIN_ONE + 1, :] = grad_gain
        vec_out[SHIFT_ONE : SHIFT_ONE + 1, :] = grad_shift
        grad_out[...] = grad_before
        attn_out[...] = grad_before.astype(LOW)

    point(6)


def attention_backward(size, layer, extra, point, *refs):
    seqs, seq_len, heads, head_size = size
    refs = list(refs)
    attn, grad_before, xwin, query_in, kv, ctx, lse, gated, small, lengths, left, right = refs[:12]
    refs = refs[12:]
    back = refs.pop(0) if extra else None
    left_out, right_out, mine_out, pair_out, mid_out, head_vec = refs[:6]
    grad_kv, grad_q, spread, mine = refs[6:]
    r, groups = pl.program_id(0), pl.num_programs(0)
    width = heads * head_size
    rows = mine.shape[0]
    window = Window(seqs, seq_len, rows, mine.shape[1] // width)
    block = window.block
    row = small[0, 4 * layer + 2 : 4 * layer + 3, :]
    opened = row[:, width : 2 * width]
    point(0)
    grad_gated = nn(attn[...], right[0, :, width:])
    shared = grad_gated * ctx[0]
    grad_ctx = (grad_gated * opened).astype(LOW)
    pulled = shared * opened
    scaled = query_in[0] * jnp.asarray(0.125, LOW)
    grad_kv[...] = jnp.zeros_like(grad_kv)
    for piece in range(rows // block):
        here = slice(piece * block, (piece + 1) * block)
        keys = window.keys(piece)
        usable = lax.broadcasted_iota(jnp.int32, (block, seq_len), 1) < lengths[window.loc(piece)]
        for head in range(heads):
            lanes = slice(head * head_size, (head + 1) * head_size)
            later = slice(width + head * head_size, width + (head + 1) * head_size)
            key = kv[0, keys, lanes]
            scores = nt(scaled[here, lanes], key)
            chances = jnp.where(usable, jnp.exp(scores - lse[0, here, head : head + 1]), 0.0)
            grad_chances = nt(grad_ctx[here, lanes], kv[0, keys, later])
            delta = jnp.sum(pulled[here, lanes], -1, keepdims=True)
            grad_scores = (chances * (grad_chances - delta)).astype(LOW)
            grad_q[here, lanes] = nn(grad_scores, key) * 0.125
            grad_kv[keys, lanes] += tn(grad_scores, scaled[here, lanes])
            grad_kv[keys, later] += tn(chances.astype(LOW), grad_ctx[here, lanes])
            point(1 + piece * heads + head)
    spot = 1 + rows // block * heads
    query_low = grad_q[...].astype(LOW)
    kv_low = grad_kv[...].astype(LOW)
    head_vec[0, 0:1, :width] = jnp.sum(query_low.astype(F32), 0, keepdims=True)
    head_vec[0, 0:1, 2 * width :] = jnp.sum(kv_low.astype(F32), 0, keepdims=True)
    head_vec[0, 1:2, :width] = jnp.sum(shared, 0, keepdims=True)

    @pl.when(r == 0)
    def _():
        spread[...] = jnp.zeros_like(spread)
        if extra:
            mine[...] = grad_before[...] + back[0]
        else:
            mine[...] = grad_before[...]

    spread[...] += nt(kv_low, left[0])
    mine[...] += nt(query_low, right[0, :, :width])
    point(spot)
    left_out[0] = tn(xwin[...], kv_low).astype(LOW)
    point(spot + 1)
    here = window.at(window.own, rows)
    right_out[0, :, :width] = tn(xwin[here, :], query_low).astype(LOW)
    right_out[0, :, width:] = tn(attn[...], gated[0]).astype(LOW)

    @pl.when(r == groups - 1)
    def _():
        mine_out[...] = mine[...] + spread[here, :]
        pair_out[...] = spread[window.at(window.pair, rows), :].astype(LOW)
        mid_out[...] = spread[window.at(window.mid, mid_out.shape[0]), :].astype(LOW)

    point(spot + 2)


def place_rows(groups, info, *refs):
    pieces, matrix, out = refs[:groups], refs[groups], refs[groups + 1]
    r = pl.program_id(0)
    for group in range(groups):

        @pl.when(r == group)
        def _(group=group):
            out[...] = nn(pieces[group][...], matrix[...]).astype(out.dtype)


def factor_pair(count):
    side = 1
    for trial in range(1, count + 1):
        if count % trial == 0 and trial * trial <= count:
            side = trial
    return side, count // side


def after(value, *others):
    return lax.optimization_barrier((value,) + others)[0]


def on_device(
    ndp,
    groups,
    hidden_in,
    seq_lengths,
    layer_map,
    teacher_states,
    out_cotangent,
    query_weight,
    key_weight,
    value_weight,
    query_value_bias,
    output_weight,
    branch_bias,
    norm_gain,
    norm_shift,
    inner_weight,
    inner_bias,
    outer_weight,
    head_alpha,
    head_noise,
    unit_alpha,
    unit_noise,
    map_weight,
):
    tokens_dev, model = hidden_in.shape
    seqs_dev = seq_lengths.shape[0]
    seq_len = tokens_dev // seqs_dev
    width = query_weight.shape[2]
    units = inner_weight.shape[2]
    layers, heads = head_alpha.shape
    head_size = width // heads
    rows = tokens_dev // groups
    feats = model // ndp
    geo = Geometry(ndp, groups)
    size_y, size_x, chips = geo.size_y, geo.size_x, geo.chips
    size = (seqs_dev, seq_len, heads, head_size)
    dp = lax.axis_index("dp")
    h = lax.axis_index("head")
    my_c, my_x, my_y, _ = geo.here()

    def pull_group(value, r):
        return lax.ppermute(value, "head", [((i + r) % groups, i) for i in range(groups)])

    def push_group(value, r):
        return lax.ppermute(value, "head", [(i, (i + r) % groups) for i in range(groups)])

    def sum_plane(value):
        for axis, count in (("c", 2), ("y", size_y), ("x", size_x)):
            step = 1
            while step < count:
                stride = {"c": 1, "x": 2, "y": 2 * size_x}[axis] * step
                value = value + lax.ppermute(value, "dp", [(i, i ^ stride) for i in range(ndp)])
                step *= 2
        return value

    def sum_groups(value):
        step = 1
        while step < groups:
            value = value + lax.ppermute(value, "head", [(i, i ^ step) for i in range(groups)])
            step *= 2
        return value

    position = jnp.arange(ndp)
    pos_c, pos_y, pos_x = position // chips, (position // size_x) % size_y, position % size_x
    order = (((my_y + pos_y) % size_y) * size_x + (my_x + pos_x) % size_x) * 2 + (my_c ^ pos_c)
    place = (my_c ^ (position % 2)) * chips
    place = place + ((position // (2 * size_x) - my_y) % size_y) * size_x
    place = place + ((position // 2) % size_x - my_x) % size_x
    source = (order[:, None] * feats + jnp.arange(feats)[None, :]).reshape(model)
    matrix = (source[:, None] == jnp.arange(model)[None, :]).astype(LOW)

    def reorder(value):
        return product(matrix, value, (1, 0)).astype(LOW)

    def reorder_turned(value):
        return product(matrix, value, (1, 1)).astype(LOW)

    kinds = []
    for layer in range(layers):
        kinds.append(reorder(jnp.concatenate([key_weight[layer], value_weight[layer]], 1)))
        kinds.append(
            jnp.concatenate([reorder(query_weight[layer]), reorder_turned(output_weight[layer])], 1)
        )
        kinds.append(reorder(inner_weight[layer]))
        kinds.append(reorder_turned(outer_weight[layer]))
    kinds.append(reorder(map_weight))
    kinds = [kind.reshape(ndp, feats, kind.shape[1]) for kind in kinds]

    def cuts(cols, steps):
        out, start = [], 0
        for step in steps:
            out.append((start, step))
            start += step
        return out if start == cols else [(0, cols)]

    def pairs(cols, steps):
        return [[(0, col, count, False), (1, col, count, True)] for col, count in cuts(cols, steps)]

    attn_pairs, feed_pairs = pairs(2 * width, ATTN_CUTS), pairs(units, FEED_CUTS)

    def attn_gather(layer):
        return Gather(geo, kinds[4 * layer : 4 * layer + 2], attn_pairs)

    def feed_gather(layer):
        return Gather(geo, kinds[4 * layer + 2 : 4 * layer + 4], feed_pairs)

    def matrices(arrays):
        return [(array.reshape(groups, model, array.shape[-1]), "group") for array in arrays]

    def parts(grad):
        return grad.reshape(groups, 2, size_y, size_x, feats, grad.shape[-1])

    open_unit, unit_back = jax.vjp(partial(gate_open, unit_noise), unit_alpha)
    open_head, head_back = jax.vjp(partial(gate_open, head_noise), head_alpha)
    (unit_slope,) = unit_back(jnp.ones_like(open_unit))
    (head_slope,) = head_back(jnp.ones_like(open_head))
    mixed = jnp.concatenate(
        [
            query_value_bias[:, 0],
            jnp.repeat(open_head, head_size, axis=1),
            jnp.zeros((layers, width), F32),
            query_value_bias[:, 1],
        ],
        1,
    )
    empty = jnp.zeros((layers, units), F32)
    small_own = jnp.stack([open_unit, inner_bias, mixed, empty], 1).reshape(4 * layers, units)
    small = jnp.stack([small_own] + [pull_group(small_own, r) for r in range(1, groups)])
    vec = jnp.concatenate([branch_bias, norm_gain, norm_shift], 1).reshape(6 * layers, ndp, feats)
    vec = jnp.take(vec, order, axis=1).reshape(6 * layers, model)
    vec = jnp.concatenate([vec, jnp.zeros((16 - 6 * layers, model), F32)])

    window = Window(seqs_dev, seq_len, rows, groups)
    block, mid_rows = window.block, 2 * window.block
    blocks = rows // block
    win, base, mid_row = window.first, window.base, window.mid_row
    locs = jnp.stack([window.loc(piece) for piece in range(blocks)])
    lengths = lax.dynamic_slice(seq_lengths, (win,), (2,))
    spot = (h * rows + jnp.arange(rows)) % seq_len
    own_lengths = jnp.repeat(jnp.take(lengths, locs), block, total_repeat_length=rows)
    row_ok = jnp.broadcast_to((spot < own_lengths).astype(F32)[:, None], (rows, 128))
    count_all = sum_plane(jnp.sum(seq_lengths).astype(F32).reshape(1, 1))
    factor = (tokens_dev * ndp) / count_all

    hidden = product(lax.dynamic_slice(hidden_in, (base, 0), (2 * seq_len, model)), matrix, (1, 1)).astype(LOW)
    cotangent = product(
        lax.dynamic_slice(out_cotangent, (h * rows, 0), (rows, model)), matrix, (1, 1)
    ).astype(LOW)
    chosen = jnp.take(teacher_states, layer_map, axis=0)

    def teacher_rows(r):
        return lax.dynamic_slice(
            chosen, (0, ((h - r) % groups) * rows, 0), (layers, rows, width)
        )

    target = jnp.stack(
        [teacher_rows(0)] + [pull_group(teacher_rows(r), r) for r in range(1, groups)]
    )

    weights = matrices(run(only_move, 1, [], [], [], 0, "gather_first", [attn_gather(0)], 1, 1))
    xwin, resid = hidden, None
    records = []
    lows = []
    for layer in range(layers):
        inputs = [(xwin, "full"), (small, "group"), (vec, "full"), (lengths, "smem")] + weights
        if layer:
            inputs.append((resid, "full"))
        attn_weights = weights
        kv, query, ctx, lse, gated, before_one, middle, middle_low, *got = run(
            partial(attention_forward, size, layer, layer == 0),
            groups,
            inputs,
            [
                ((groups, 2 * seq_len, 2 * width), LOW, "group"),
                ((groups, rows, width), LOW, "group"),
                ((groups, rows, width), F32, "group"),
                ((groups, rows, 128), F32, "group"),
                ((groups, rows, width), LOW, "group"),
                ((rows, model), F32, "full"),
                ((rows, model), F32, "full"),
                ((rows, model), LOW, "full"),
            ],
            [pltpu.VMEM((rows, model), F32)],
            8e9,
            "attention_forward",
            [feed_gather(layer)],
            2 + blocks * heads,
            2 + 2 * layer,
        )
        feed_weights = matrices(got)
        ahead = attn_gather(layer + 1) if layer + 1 < layers else Gather(geo, kinds[-1:], [[(0, 0, width, False)]])
        unit_in, before_two, resid, low, *got = run(
            partial(feed_forward, layer),
            groups,
            [(middle, "full"), (middle_low, "full"), (small, "group"), (vec, "full")] + feed_weights,
            [
                ((groups, rows, units), LOW, "group"),
                ((rows, model), F32, "full"),
                ((rows, model), F32, "full"),
                ((rows, model), LOW, "full"),
            ],
            [pltpu.VMEM((rows, model), F32)],
            5e9,
            "feed_forward",
            [ahead],
            4,
            3 + 2 * layer,
        )
        weights = matrices(got)
        records.append(
            (xwin, kv, query, ctx, lse, gated, before_one, middle_low, unit_in, before_two, attn_weights, feed_weights)
        )
        lows.append(low)
        if layer + 1 < layers:
            pair = lax.ppermute(low, "head", [(i, i ^ 1) for i in range(groups)])
            mid = lax.ppermute(
                lax.dynamic_slice(low, (mid_row, 0), (mid_rows, model)), "head", [(1, 2), (2, 1)]
            )
            odd = h % 2 == 1
            ahead = jnp.where(odd, pair, low)
            behind = jnp.where(odd, low, pair)
            xwin = jnp.where(
                h < 2, jnp.concatenate([ahead, behind, mid]), jnp.concatenate([mid, ahead, behind])
            )
    back, loss, grad_map = run(
        partial(match_teacher, layers),
        groups,
        [(low, "full") for low in lows] + [(target, "group"), (row_ok, "full"), (factor, "full")] + weights,
        [
            ((layers, rows, model), F32, "full"),
            ((8, 256), F32, "full"),
            ((groups, model, width), LOW, "group"),
        ],
        [],
        4e9,
        "match_teacher",
    )
    info_place = jnp.stack([h]).astype(jnp.int32)

    def place_all(value, dtype):
        pieces = [value] + [pull_group(value, r) for r in range(1, groups)]
        return pl.pallas_call(
            partial(place_rows, groups),
            name="place_rows",
            grid_spec=pltpu.PrefetchScalarGridSpec(
                num_scalar_prefetch=1,
                grid=(groups,),
                in_specs=[pl.BlockSpec(a.shape, lambda r, info: (0, 0)) for a in pieces + [matrix]],
                out_specs=pl.BlockSpec((rows, model), lambda r, info: (lax.rem(info[0] + r, groups), 0)),
            ),
            out_shape=jax.ShapeDtypeStruct((tokens_dev, model), dtype),
            compiler_params=pltpu.CompilerParams(vmem_limit_bytes=VMEM_LIMIT),
            cost_estimate=pl.CostEstimate(
                flops=2 * tokens_dev * model * model, bytes_accessed=8 * tokens_dev * model, transcendentals=0
            ),
        )(info_place, *pieces, matrix)

    block_out = place_all(lows[-1], LOW)

    grads = [(cotangent, "full"), (back[layers - 1 :], "full")]
    results = [None] * layers
    riders, waiting = [], []
    number = 2 + 2 * layers

    def settle(got):
        for (layer, name), value in zip(waiting, got):
            results[layer][name] = value

    map_rider = Scatter(geo, [parts(grad_map)], [[(0, 0, width, False)]])
    for layer in reversed(range(layers)):
        results[layer] = {}
        xwin, kv, query, ctx, lse, gated, before_one, middle_low, unit_in, before_two, attn_weights, feed_weights = records[layer]
        inner, outer, attn, grad_before, vec_out, unit_vec, *got = run(
            partial(feed_backward, size, layer, layer == layers - 1),
            groups,
            [
                (before_two, "full"),
                (before_one, "full"),
                (middle_low, "full"),
                (unit_in, "group"),
                (small, "group"),
                (vec, "full"),
            ]
            + feed_weights
            + grads,
            [((groups, model, units), LOW, "group")] * 2
            + [
                ((rows, model), LOW, "full"),
                ((rows, model), F32, "full"),
                ((8, model), F32, "full"),
                ((groups, 8, units), F32, "group"),
            ],
            [pltpu.VMEM((rows, model), F32), pltpu.VMEM((rows, model), LOW)],
            10e9,
            "feed_backward",
            riders,
            7,
            number,
        )
        number += 1
        settle(got)
        riders = [Scatter(geo, [parts(inner), parts(outer)], feed_pairs)]
        waiting = [(layer, "inner"), (layer, "outer")]
        if layer == layers - 1:
            riders.append(map_rider)
            waiting.append((layer, "map"))
        extra = [(back[layer - 1 : layer], "full")] if layer else []
        left, right, mine, to_pair, to_mid, head_vec, *got = run(
            partial(attention_backward, size, layer, bool(layer)),
            groups,
            [
                (attn, "full"),
                (grad_before, "full"),
                (xwin, "full"),
                (query, "group"),
                (kv, "group"),
                (ctx, "group"),
                (lse, "group"),
                (gated, "group"),
                (small, "group"),
                (lengths, "smem"),
            ]
            + attn_weights
            + extra,
            [((groups, model, 2 * width), LOW, "group")] * 2
            + [
                ((rows, model), F32, "full"),
                ((rows, model), LOW, "full"),
                ((mid_rows, model), LOW, "full"),
                ((groups, 8, units), F32, "group"),
            ],
            [
                pltpu.VMEM((2 * seq_len, 2 * width), F32),
                pltpu.VMEM((rows, width), F32),
                pltpu.VMEM((2 * seq_len, model), F32),
                pltpu.VMEM((rows, model), F32),
            ],
            12e9,
            "attention_backward",
            riders,
            4 + blocks * heads,
            number,
        )
        number += 1
        settle(got)
        riders = [Scatter(geo, [parts(left), parts(right)], attn_pairs)]
        waiting = [(layer, "kv"), (layer, "qo")]
        from_pair = lax.ppermute(to_pair, "head", [(i, i ^ 1) for i in range(groups)])
        from_mid = lax.ppermute(to_mid, "head", [(1, 2), (2, 1)])
        grads = [(mine, "full"), (from_pair, "full"), (from_mid, "full")]
        results[layer].update(vec=vec_out, unit=unit_vec, head=head_vec)
    settle(run(only_move, 1, [], [], [], 0, "scatter_last", riders, 1, number))
    grad_map = results[layers - 1]["map"]
    grad_in = mine + from_pair.astype(F32)
    patch = lax.dynamic_slice(grad_in, (mid_row, 0), (mid_rows, model)) + from_mid.astype(F32)
    grad_in = lax.dynamic_update_slice(grad_in, patch, (mid_row, 0)).astype(LOW)
    grad_hidden = place_all(grad_in, F32)

    by_feature = jnp.concatenate([results[layer]["vec"][:6] for layer in range(layers)])
    by_feature = jnp.take(by_feature.reshape(6 * layers, ndp, feats), place, axis=1)
    by_feature = by_feature.reshape(6 * layers, model)
    loss_row = jnp.concatenate([loss[:1], jnp.zeros((1, model - loss.shape[1]), F32)], 1)
    by_feature = sum_groups(jnp.concatenate([by_feature, loss_row]))
    by_unit = jnp.concatenate(
        [jnp.concatenate([results[layer]["unit"][:, :2], results[layer]["head"][:, :2]], 1) for layer in range(layers)], 1
    )
    summed = by_unit[0]
    for r in range(1, groups):
        summed = summed + push_group(by_unit[r], r)
    everything = sum_plane(jnp.concatenate([by_feature, summed]))
    distill_loss = jnp.sum(everything[6 * layers]) / (count_all[0, 0] * model * layers)
    by_unit = everything[6 * layers + 1 :].reshape(layers, 4, units)
    mine_feats = lax.dynamic_slice(
        everything[: 6 * layers].reshape(layers, 3, 2, model), (0, 0, 0, dp * feats), (layers, 3, 2, feats)
    )
    unit_count = units // ndp
    mine_units = lax.dynamic_slice(by_unit[:, :2], (0, 0, dp * unit_count), (layers, 2, unit_count))
    own_slope = lax.dynamic_slice(unit_slope, (0, dp * unit_count), (layers, unit_count))
    qv_cols = width // ndp
    both = jnp.stack([by_unit[:, 2, :width], by_unit[:, 2, 3 * width : 4 * width]], 1)
    grad_qv_bias = lax.dynamic_slice(both, (0, 0, dp * qv_cols), (layers, 2, qv_cols))
    head_sums = jnp.sum(by_unit[:, 3, :width].reshape(layers, heads, head_size), -1)

    def stacked(member, cols, turned=False):
        arrays = [results[layer][member][:, cols] for layer in range(layers)]
        return jnp.stack([array.T if turned else array for array in arrays])

    front, rear, whole = slice(0, width), slice(width, 2 * width), slice(None)
    return (
        block_out,
        grad_hidden,
        distill_loss,
        stacked("qo", front),
        stacked("kv", front),
        stacked("kv", rear),
        grad_qv_bias,
        stacked("qo", rear, True),
        mine_feats[:, 0],
        mine_feats[:, 1],
        mine_feats[:, 2],
        stacked("inner", whole),
        mine_units[:, 0],
        stacked("outer", whole, True),
        head_sums * head_slope,
        mine_units[:, 1] * own_slope,
        grad_map,
    )


def solution(mesh):
    in_specs = (
        P("dp", None),
        P("dp"),
        P(),
        P(None, "dp", "head"),
        P("dp", None),
        P(None, None, "head"),
        P(None, None, "head"),
        P(None, None, "head"),
        P(None, None, "head"),
        P(None, "head", None),
        P(),
        P(),
        P(),
        P(None, None, "head"),
        P(None, "head"),
        P(None, "head", None),
        P(None, "head"),
        P(None, "head"),
        P(None, "head"),
        P(None, "head"),
        P(None, "head"),
    )
    out_specs = (
        P("dp", None),
        P("dp", None),
        P(),
        P(None, "dp", "head"),
        P(None, "dp", "head"),
        P(None, "dp", "head"),
        P(None, None, ("head", "dp")),
        P(None, "head", "dp"),
        P(None, None, "dp"),
        P(None, None, "dp"),
        P(None, None, "dp"),
        P(None, "dp", "head"),
        P(None, ("head", "dp")),
        P(None, "head", "dp"),
        P(None, "head"),
        P(None, ("head", "dp")),
        P("dp", "head"),
    )
    return jax.shard_map(
        partial(on_device, mesh.shape["dp"], mesh.shape["head"]),
        mesh=mesh,
        in_specs=in_specs,
        out_specs=out_specs,
        check_vma=False,
    )
```

```python
from functools import partial

import jax
import jax.numpy as jnp
from jax import lax
from jax.experimental import pallas as pl
from jax.experimental.pallas import tpu as pltpu
from jax.sharding import PartitionSpec as P

BETA = 2.0 / 3.0
EPS = 1e-05
LOW = jnp.bfloat16
F32 = jnp.float32
GELU_C = 0.7978845608028654
GELU_K = 0.044715
VMEM_LIMIT = 56 * 1024 * 1024
ATTN_CUTS = (128, 256)
FEED_CUTS = (128, 128, 256, 256)
BACK_CUTS = (128,) * 6
LAST_CUTS = (128, 128, 128)
MESH = pl.DeviceIdType.MESH


def gate_open(noise, alpha):
    return jnp.clip(jax.nn.sigmoid((noise + alpha) / BETA) * 1.2 - 0.1, 0.0, 1.0)


def product(left, right, dims):
    return lax.dot_general(left, right, ((dims[:1], dims[1:]), ((), ())), preferred_element_type=F32)


def nn(left, right):
    return product(left, right, (1, 0))


def nt(left, right):
    return product(left, right, (1, 1))


def tn(left, right):
    return product(left, right, (0, 0))


def factor_pair(count):
    side = 1
    for trial in range(1, count + 1):
        if count % trial == 0 and trial * trial <= count:
            side = trial
    return side, count // side


def block_of(shape, place):
    if place == "full":
        return pl.BlockSpec(shape, lambda r: (0,) * len(shape))
    return pl.BlockSpec((1,) + tuple(shape[1:]), lambda r: (place(r),) + (0,) * (len(shape) - 1))


def spec_of(array, kind):
    if kind == "any":
        return pl.BlockSpec(memory_space=pl.ANY)
    if kind == "smem":
        return pl.BlockSpec(memory_space=pltpu.SMEM)
    if kind == "group":
        return block_of(array.shape, lambda r: r)
    return block_of(array.shape, kind)


def run(body, steps, inputs, outputs, scratch, flops, name, riders=(), points=1, number=None):
    inputs, outputs, scratch = list(inputs), list(outputs), list(scratch)
    at = [len(inputs), len(outputs), len(scratch)]
    starts, sizes = [], []
    for rider in riders:
        starts.append((len(inputs), len(outputs), len(scratch)))
        inputs += rider.inputs
        outputs += rider.outputs
        scratch += rider.scratch
        sizes.append((len(rider.inputs), len(rider.outputs), len(rider.scratch)))
    out_shape = [jax.ShapeDtypeStruct(shape, dtype) for shape, dtype, _ in outputs]
    moved = sum(a.size * a.dtype.itemsize for a, kind in inputs if kind != "any")
    n_in, n_out = len(inputs), len(outputs)
    peers = []
    for rider in riders:
        peers += [peer for peer in rider.peers if peer not in peers]

    def whole(*refs):
        kinds = refs[:n_in], refs[n_in : n_in + n_out], refs[n_in + n_out :]
        slots = steps * points
        listed = []
        for number, (rider, start, size) in enumerate(zip(riders, starts, sizes)):
            tasks = rider.tasks(*[part[i : i + n] for part, i, n in zip(kinds, start, size)])
            for index, task in enumerate(tasks):
                listed.append((index / max(1, len(tasks) - 1), number, index, task))
        chosen = [[] for _ in range(slots)]
        for share, _, _, task in sorted(listed, key=lambda item: item[:3]):
            chosen[round(share * (slots - 1))].append(task)
        r = pl.program_id(0)

        def point(spot, span=range(steps)):
            for step in span:
                if chosen[step * points + spot]:

                    @pl.when(r == step)
                    def _(step=step):
                        if step == 0 and spot == 0:
                            riders[0].geo.greet(peers)
                        for task in chosen[step * points + spot]:
                            task()

        body(point, *[ref for part, n in zip(kinds, at) for ref in part[:n]])

    params = {"vmem_limit_bytes": VMEM_LIMIT}
    if riders:
        params.update(collective_id=number, has_side_effects=True)
    return pl.pallas_call(
        whole,
        name=name,
        grid=(steps,),
        in_specs=[spec_of(a, kind) for a, kind in inputs],
        out_specs=[spec_of(o, kind) for o, (_, _, kind) in zip(out_shape, outputs)],
        scratch_shapes=scratch,
        out_shape=out_shape,
        compiler_params=pltpu.CompilerParams(**params),
        cost_estimate=pl.CostEstimate(flops=int(flops), bytes_accessed=int(moved), transcendentals=0),
    )(*[a for a, _ in inputs])


def only_move(point):
    point(0)


class Geometry:
    def __init__(self, ndp, groups):
        self.ndp, self.groups = ndp, groups
        self.size_y, self.size_x = factor_pair(ndp // 2)

    def here(self):
        dp, h = lax.axis_index("dp"), lax.axis_index("head")
        return lax.rem(dp, 2), lax.rem(lax.div(dp, 2), self.size_x), lax.div(dp, 2 * self.size_x), h

    def place(self, c=0, y=0, x=0, z=0):
        core, ix, iy, h = self.here()
        core = 1 - core if c else core
        iy = lax.rem(iy + (y + self.size_y), self.size_y) if y else iy
        ix = lax.rem(ix + (x + self.size_x), self.size_x) if x else ix
        h = lax.rem(h + (z + self.groups), self.groups) if z else h
        return iy, ix, core, h

    def device(self, **to):
        iy, ix, core, h = self.place(**to)
        return ((iy * self.size_x + ix) * 2 + core, h)

    def axes(self):
        out = [dict(c=1)]
        out += [dict(y=y) for y in range(1, self.size_y)]
        out += [dict(x=x) for x in range(1, self.size_x)]
        return out + self.column()

    def column(self):
        return [dict(z=z) for z in range(1, self.groups)]

    def plane(self):
        out = []
        for c in range(2):
            for y in range(self.size_y):
                for x in range(self.size_x):
                    to = {key: value for key, value in (("c", c), ("y", y), ("x", x)) if value}
                    if to:
                        out.append(to)
        return out

    def greet(self, peers):
        barrier = pltpu.get_barrier_semaphore()
        for peer in peers:
            pl.semaphore_signal(barrier, inc=1, device_id=self.device(**peer), device_id_type=MESH)
        pl.semaphore_wait(barrier, len(peers))


class Mover:
    def __init__(self, geo, send, recv):
        self.geo, self.send, self.recv, self.ids = geo, send, recv, {}

    def __call__(self, key, src, dst, **to):
        index = self.ids.setdefault(key, len(self.ids))
        return pltpu.make_async_remote_copy(
            src_ref=src,
            dst_ref=dst,
            send_sem=self.send.at[index],
            recv_sem=self.recv.at[index],
            device_id=self.geo.device(**to),
            device_id_type=MESH,
        )


def back(to):
    return {key: value if key == "c" else -value for key, value in to.items()}


def start(copies):
    for copy in copies:
        copy.start()


def arrive(copies):
    for copy in copies:
        copy.wait_recv()


def leave(copies):
    for copy in copies:
        copy.wait_send()


class Gather:
    def __init__(self, geo, owns, chunks):
        self.geo, self.chunks, self.peers = geo, chunks, geo.axes()
        self.layers = [layer for _, layer in owns]
        self.inputs = [(own, "any") for own, _ in owns]
        self.outputs = [((geo.groups,) + own.shape[1:], LOW, "any") for own, _ in owns]
        halves = sum(len(chunk) for chunk in chunks)
        each = geo.groups - 1 + 2 * geo.size_x * geo.size_y
        sems = pltpu.SemaphoreType.DMA((halves * each,))
        self.scratch = [sems, sems, pltpu.SemaphoreType.DMA((2, len(owns)))]
        self.scratch += [pltpu.VMEM(own.shape[1:], LOW) for own, _ in owns]

    def tasks(self, owns, outs, scratch):
        geo, (send, recv, local), stages = self.geo, scratch[:3], scratch[3:]
        move = Mover(geo, send, recv)
        groups, sx, sy = geo.groups, geo.size_x, geo.size_y
        others = pl.ds(1, groups - 1)
        owns = [own.at[layer] for own, layer in zip(owns, self.layers)]

        def columns(chunk, half):
            m, col, cols, _ = self.chunks[chunk][half]
            return m, pl.ds(col, cols)

        def along(chunk, half, r):
            m, cols = columns(chunk, half)
            iy, ix, core, _ = geo.place()
            return move(
                ("z", chunk, half, r), owns[m].at[iy, ix, core, :, cols], outs[m].at[r, iy, ix, core, :, cols], z=-r
            )

        def hop(chunk, half, block, to):
            m, cols = columns(chunk, half)
            iy, ix, core, _ = geo.place(**block)
            part = outs[m].at[others, iy, ix, core, :, cols]
            return move(("p", chunk, half, str(block), str(to)), part, part, **back(to))

        def into(m):
            return pltpu.make_async_copy(owns[m], stages[m], local.at[0, m])

        def out_of(m):
            return pltpu.make_async_copy(stages[m], outs[m].at[0], local.at[1, m])

        ways_x = [dict(x=x) for x in range(1, sx)]
        ways_y = [dict(y=y) for y in range(1, sy)]
        corners = [dict(x=x, y=y) for x in range(1, sx) for y in range(1, sy)]

        def halves(chunk):
            return range(len(self.chunks[chunk]))

        def alongs(chunk):
            return [along(chunk, half, r) for half in halves(chunk) for r in range(1, groups)]

        def firsts(chunk):
            return [hop(chunk, half, {}, to) for half in halves(chunk) for to in ways_x + ways_y]

        def seconds(chunk):
            out = []
            for half in halves(chunk):
                near, far = (ways_y, ways_x) if self.chunks[chunk][half][3] else (ways_x, ways_y)
                out += [hop(chunk, half, block, to) for block in near for to in far]
            return out

        def cores(chunk, blocks):
            return [hop(chunk, half, block, dict(c=1)) for half in halves(chunk) for block in blocks]

        count = len(self.chunks)

        def begin():
            start(alongs(0))
            if count > 1:
                start(alongs(1))
            for m in range(len(owns)):
                into(m).start()

        def level_one(chunk):
            arrive(alongs(chunk))
            start(firsts(chunk))
            start(cores(chunk, [{}]))
            if chunk + 2 < count:
                start(alongs(chunk + 2))

        def level_two(chunk):
            arrive(firsts(chunk))
            start(seconds(chunk))
            start(cores(chunk, ways_x + ways_y))
            if chunk == 0:
                for m in range(len(owns)):
                    into(m).wait()
                    out_of(m).start()

        def level_three(chunk):
            arrive(seconds(chunk))
            start(cores(chunk, corners))

        def end():
            for m in range(len(owns)):
                out_of(m).wait()
            for chunk in range(count):
                last = cores(chunk, [{}] + ways_x + ways_y + corners)
                arrive(last)
                leave(alongs(chunk) + firsts(chunk) + seconds(chunk) + last)

        out = [begin]
        for time in range(count + 2):
            for level, late in ((level_one, 0), (level_two, 1), (level_three, 2)):
                if 0 <= time - late < count:
                    out.append(partial(level, time - late))
        return out + [end]


class Scatter:
    def __init__(self, geo, grads, chunks):
        self.geo, self.chunks, self.peers = geo, chunks, geo.axes()
        self.inputs = [(grad, "any") for grad in grads]
        self.outputs = [(grad.shape[4:], F32, "full") for grad in grads]
        feats = grads[0].shape[4]
        halves = [half for chunk in chunks for half in chunk]
        each = 1 + (geo.size_x - 1) + (geo.size_y - 1) + geo.groups - 1
        sems = pltpu.SemaphoreType.DMA((len(halves) * each,))
        self.scratch = [sems, sems, pltpu.SemaphoreType.DMA((len(halves),))]
        for _, _, cols, y_first in halves:
            near, far = (geo.size_y, geo.size_x) if y_first else (geo.size_x, geo.size_y)
            self.scratch += [
                pltpu.VMEM(shape, LOW)
                for shape in (
                    (geo.groups, geo.size_y, geo.size_x, feats, cols),
                    (geo.groups, geo.size_y, geo.size_x, feats, cols),
                    (near - 1, geo.groups, far, feats, cols),
                    (far - 1, geo.groups, feats, cols),
                    (geo.groups - 1, feats, cols),
                )
            ]

    def tasks(self, grads, outs, scratch):
        geo, (send, recv, local), buffers = self.geo, scratch[:3], scratch[3:]
        move = Mover(geo, send, recv)
        groups, sx, sy = geo.groups, geo.size_x, geo.size_y
        index = {}
        for chunk, halves in enumerate(self.chunks):
            for half in range(len(halves)):
                index[chunk, half] = len(index)

        def parts(chunk, half):
            m, col, cols, y_first = self.chunks[chunk][half]
            number = index[chunk, half]
            return grads[m], pl.ds(col, cols), y_first, buffers[5 * number : 5 * number + 5]

        def load(chunk, half):
            grad, cols, _, bufs = parts(chunk, half)
            _, _, core, _ = geo.place()
            return pltpu.make_async_copy(
                grad.at[:, :, :, core, :, cols], bufs[0], local.at[index[chunk, half]]
            )

        def cross(chunk, half):
            grad, cols, _, bufs = parts(chunk, half)
            _, _, core, _ = geo.place(c=1)
            return move(("c", chunk, half), grad.at[:, :, :, core, :, cols], bufs[1], c=1)

        def near(chunk, half):
            _, _, y_first, bufs = parts(chunk, half)
            out = []
            for step in range(1, sy if y_first else sx):
                to = dict(y=step) if y_first else dict(x=step)
                iy, ix, _, _ = geo.place(**to)
                part = bufs[0].at[:, iy] if y_first else bufs[0].at[:, :, ix]
                out.append(move(("n", chunk, half, step), part, bufs[2].at[step - 1], **to))
            return out

        def far(chunk, half):
            _, _, y_first, bufs = parts(chunk, half)
            out = []
            for step in range(1, sx if y_first else sy):
                to = dict(x=step) if y_first else dict(y=step)
                iy, ix, _, _ = geo.place(**to)
                out.append(move(("f", chunk, half, step), bufs[0].at[:, iy, ix], bufs[3].at[step - 1], **to))
            return out

        def along(chunk, half):
            _, _, _, bufs = parts(chunk, half)
            iy, ix, _, _ = geo.place()
            return [
                move(("z", chunk, half, r), bufs[0].at[r, iy, ix], bufs[4].at[r - 1], z=r) for r in range(1, groups)
            ]

        def each(chunk):
            return range(len(self.chunks[chunk]))

        def begin_one(chunk):
            for half in each(chunk):
                cross(chunk, half).start()
                load(chunk, half).start()

        count = len(self.chunks)

        def begin():
            for chunk in range(min(2, count)):
                begin_one(chunk)

        def level_one(chunk):
            for half in each(chunk):
                _, _, _, bufs = parts(chunk, half)
                load(chunk, half).wait()
                cross(chunk, half).wait_recv()
                for r in range(groups):
                    bufs[0][r] = (bufs[0][r].astype(F32) + bufs[1][r].astype(F32)).astype(LOW)
                start(near(chunk, half))
            if chunk + 2 < count:
                begin_one(chunk + 2)

        def level_two(chunk):
            iy, ix, _, _ = geo.place()
            for half in each(chunk):
                _, _, y_first, bufs = parts(chunk, half)
                arrive(near(chunk, half))
                for r in range(groups):
                    total = (bufs[0][r, iy] if y_first else bufs[0][r, :, ix]).astype(F32)
                    for other in range(bufs[2].shape[0]):
                        total = total + bufs[2][other, r].astype(F32)
                    if y_first:
                        bufs[0][r, iy] = total.astype(LOW)
                    else:
                        bufs[0][r, :, ix] = total.astype(LOW)
                start(far(chunk, half))

        def level_three(chunk):
            iy, ix, _, _ = geo.place()
            for half in each(chunk):
                _, _, _, bufs = parts(chunk, half)
                arrive(far(chunk, half))
                for r in range(groups):
                    total = bufs[0][r, iy, ix].astype(F32)
                    for other in range(bufs[3].shape[0]):
                        total = total + bufs[3][other, r].astype(F32)
                    bufs[0][r, iy, ix] = total.astype(LOW)
                start(along(chunk, half))

        def level_four(chunk):
            iy, ix, _, _ = geo.place()
            for half in each(chunk):
                m, col, cols, _ = self.chunks[chunk][half]
                _, _, _, bufs = parts(chunk, half)
                arrive(along(chunk, half))
                total = bufs[0][0, iy, ix].astype(F32)
                for r in range(1, groups):
                    total = total + bufs[4][r - 1].astype(F32)
                outs[m][:, col : col + cols] = total

        def end():
            for chunk in range(count):
                for half in each(chunk):
                    leave([cross(chunk, half)] + near(chunk, half) + far(chunk, half) + along(chunk, half))

        out = [begin]
        for time in range(count + 3):
            for level, late in ((level_one, 0), (level_two, 1), (level_three, 2), (level_four, 3)):
                if 0 <= time - late < count:
                    out.append(partial(level, time - late))
        return out + [end]


class Spread:
    def __init__(self, geo, value, plane=False, absolute=True):
        self.geo, self.plane, self.absolute = geo, plane, absolute
        self.peers = geo.plane() if plane else geo.column()
        self.inputs = [(value, "full")]
        self.outputs = [((len(self.peers) + 1,) + value.shape, value.dtype, "any")]
        sems = pltpu.SemaphoreType.DMA((len(self.peers),))
        self.scratch = [sems, sems, pltpu.SemaphoreType.DMA]

    def tasks(self, values, outs, scratch):
        geo, (value,), (out,), (send, recv, local) = self.geo, values, outs, scratch
        move = Mover(geo, send, recv)
        own = 0
        if self.absolute:
            own = geo.device()[0] if self.plane else geo.device()[1]
        copies = []
        for to in self.peers:
            slot = own if self.absolute else to["z"]
            copies.append(move(str(to), value, out.at[slot], **back(to)))
        mine = pltpu.make_async_copy(value, out.at[own], local)

        def begin():
            start(copies)
            mine.start()

        def end():
            mine.wait()
            arrive(copies)
            leave(copies)

        return [begin, end]


class Deal:
    def __init__(self, geo, value):
        self.geo, self.peers = geo, geo.column()
        self.rows = value.shape[1] // geo.groups
        self.inputs = [(value, "any")]
        shape = (geo.groups - 1, value.shape[0], self.rows, value.shape[2])
        self.outputs = [(shape, value.dtype, "any")]
        sems = pltpu.SemaphoreType.DMA((geo.groups - 1,))
        self.scratch = [sems, sems]

    def tasks(self, values, outs, scratch):
        geo = self.geo
        move = Mover(geo, *scratch)
        copies = []
        for r in range(1, geo.groups):
            first = pl.multiple_of(geo.place(z=-r)[3] * self.rows, self.rows)
            copies.append(move(r, values[0].at[:, pl.ds(first, self.rows), :], outs[0].at[r - 1], z=-r))

        def end():
            arrive(copies)
            leave(copies)

        return [lambda: start(copies), end]


class Fold:
    def __init__(self, geo, items):
        self.geo, self.peers = geo, geo.plane() + geo.column()
        self.inputs = [(item[0], "full") for item in items]
        self.picks = [item[1:] for item in items]
        rows = sum(stop - first for _, (first, stop), _ in self.picks)
        self.rows = -(-rows // 8) * 8
        self.outputs = [((self.rows, 128), F32, "full")]
        near, far = pltpu.SemaphoreType.DMA((geo.ndp - 1,)), pltpu.SemaphoreType.DMA((geo.groups - 1,))
        wide = pltpu.VMEM((geo.ndp, geo.groups, self.rows, 128), F32)
        slim = pltpu.VMEM((geo.groups, self.rows, 128), F32)
        self.scratch = [near, near, far, far, wide, wide, slim, slim]

    def tasks(self, values, outs, scratch):
        geo = self.geo
        near_send, near_recv, far_send, far_recv, packed, landed, middle, last = scratch
        groups, ndp = geo.groups, geo.ndp
        to_plane, to_column = Mover(geo, near_send, near_recv), Mover(geo, far_send, far_recv)
        dp, h = geo.device()
        near, far = [], []
        for to in geo.plane():
            there, _ = geo.device(**to)
            near.append(to_plane(str(to), packed.at[there], landed.at[dp], **to))
        for r in range(1, groups):
            far.append(to_column(r, middle.at[r], last.at[h], z=r))

        def begin():
            packed[...] = jnp.zeros_like(packed)
            row = 0
            for value, (grouped, (low, high), (first, stride, cols)) in zip(values, self.picks):
                for r in range(groups):
                    for d in range(ndp):
                        lanes = slice(first + d * stride, first + d * stride + cols)
                        part = value[r, low:high, lanes] if grouped else value[low:high, lanes]
                        packed[d, r, row : row + high - low, :cols] = part
                row += high - low
            start(near)

        def fold():
            landed[dp] = packed[dp]
            arrive(near)
            total = landed[0]
            for d in range(1, ndp):
                total = total + landed[d]
            middle[...] = total
            start(far)

        def end():
            last[h] = middle[0]
            arrive(far)
            total = last[0]
            for z in range(1, groups):
                total = total + last[z]
            outs[0][...] = total
            leave(near)
            leave(far)

        return [begin, fold, end]


def norm_forward(before, gain, shift):
    center = before - jnp.mean(before, -1, keepdims=True)
    spread = jnp.mean(center * center, -1, keepdims=True)
    return center * lax.rsqrt(spread + EPS) * gain + shift


def norm_backward(before, gain, grad):
    center = before - jnp.mean(before, -1, keepdims=True)
    rate = lax.rsqrt(jnp.mean(center * center, -1, keepdims=True) + EPS)
    hat = center * rate
    grad_hat = grad * gain
    mean_one = jnp.mean(grad_hat, -1, keepdims=True)
    mean_two = jnp.mean(grad_hat * hat, -1, keepdims=True)
    grad_before = rate * (grad_hat - mean_one - hat * mean_two)
    return (
        grad_before,
        jnp.sum(grad * hat, 0, keepdims=True),
        jnp.sum(grad, 0, keepdims=True),
        jnp.sum(grad_before, 0, keepdims=True),
    )


BIAS_ONE, BIAS_TWO, GAIN_ONE, GAIN_TWO, SHIFT_ONE, SHIFT_TWO = range(6)


class Window:
    def __init__(self, size, rows, groups):
        self.seqs, self.seq_len, self.heads, self.head_size = size
        self.rows, self.groups = rows, groups
        self.block = self.seq_len // groups
        self.mid_rows = 2 * self.block
        h = lax.axis_index("head")
        self.h = h
        self.first = lax.div(h * (self.seqs - 1), groups)
        self.base = self.first * self.seq_len
        self.own = h * rows - self.base
        pair = h + 1 - 2 * lax.rem(h, 2)
        self.pair = pair * rows - self.base
        self.mid = lax.rem(h, 2) * (2 * rows)
        self.mid_row = lax.rem(h, 2) * self.block
        self.middle = (h > 0) & (h < groups - 1)
        dp = lax.axis_index("dp")
        self.to_pair = (dp, pair)
        self.to_mid = (dp, groups - 1 - h)

    def at(self, begin, rows):
        return pl.ds(pl.multiple_of(begin, self.block), rows)

    def loc(self, piece):
        return lax.div((self.h * (self.rows // self.block) + piece) * self.block, self.seq_len) - self.first

    def keys(self, piece):
        return pl.ds(pl.multiple_of(self.loc(piece) * self.seq_len, self.seq_len), self.seq_len)


def remote(src, dst, sems, to):
    return pltpu.make_async_remote_copy(
        src_ref=src, dst_ref=dst, send_sem=sems.at[0], recv_sem=sems.at[1], device_id=to, device_id_type=MESH
    )


def add_up(r, total, part):
    @pl.when(r == 0)
    def _():
        total[...] = part

    @pl.when(r > 0)
    def _():
        total[...] += part


def attention_forward(size, layer, first, point, *refs):
    seqs, seq_len, heads, head_size = size
    refs = list(refs)
    xwin, small, vec, lengths, left, right = refs[:6]
    refs = refs[6:]
    resid = None if first else refs.pop(0)
    kv_out, q_out, ctx_out, lse_out, gated_out, before_out, h_out, hb_out, total = refs
    r, groups = pl.program_id(0), pl.num_programs(0)
    width = heads * head_size
    rows = total.shape[0]
    window = Window(size, rows, total.shape[1] // width)
    block = window.block
    offset = window.base if first else 0
    row = small[0, 4 * layer + 2 : 4 * layer + 3, :]
    point(0)
    kv = nn(xwin[window.at(offset, 2 * seq_len), :], left[0]) + row[:, 2 * width :]
    kv_out[0] = kv.astype(LOW)
    here = window.at(offset + window.own, rows)
    query = (nn(xwin[here, :], right[0, :, :width]) + row[:, :width]).astype(LOW)
    q_out[0] = query
    scaled = query * jnp.asarray(0.125, LOW)
    for piece in range(rows // block):
        mine = slice(piece * block, (piece + 1) * block)
        keys = window.keys(piece)
        usable = lax.broadcasted_iota(jnp.int32, (block, seq_len), 1) < lengths[window.loc(piece)]
        for head in range(heads):
            lanes = slice(head * head_size, (head + 1) * head_size)
            scores = nt(scaled[mine, lanes], kv_out[0, keys, lanes])
            scores = jnp.where(usable, scores, -1e30)
            largest = jnp.max(scores, -1, keepdims=True)
            powers = jnp.exp(scores - largest)
            sums = jnp.sum(powers, -1, keepdims=True)
            value = kv_out[0, keys, width + head * head_size : width + (head + 1) * head_size]
            context = nn(powers.astype(LOW), value) / sums
            ctx_out[0, mine, lanes] = context
            lse_out[0, mine, head : head + 1] = largest + jnp.log(sums)
            point(1 + piece * heads + head)
    gated = (ctx_out[0] * row[:, width : 2 * width]).astype(LOW)
    gated_out[0] = gated
    add_up(r, total, nt(gated, right[0, :, width:]))

    @pl.when(r == groups - 1)
    def _():
        base = 6 * layer
        if first:
            current = xwin[here, :].astype(F32)
        else:
            current = resid[...]
        before = current + total[...] + vec[base + BIAS_ONE : base + BIAS_ONE + 1, :]
        middle = norm_forward(
            before,
            vec[base + GAIN_ONE : base + GAIN_ONE + 1, :],
            vec[base + SHIFT_ONE : base + SHIFT_ONE + 1, :],
        )
        before_out[...] = before
        h_out[...] = middle
        hb_out[...] = middle.astype(LOW)

    point(1 + rows // block * heads)


def gelu_parts(unit):
    square = unit * unit
    bent = jnp.tanh(GELU_C * unit * (1.0 + GELU_K * square))
    half = 0.5 * (1.0 + bent)
    slope = half + 0.5 * unit * (1.0 - bent * bent) * (GELU_C * (1.0 + 3.0 * GELU_K * square))
    return unit * half, slope


def feed_forward(size, layer, halo, point, *refs):
    refs = list(refs)
    middle, middle_low, small, vec, left, right = refs[:6]
    refs = refs[6:]
    unit_out, before_out, x_out, xb_out = refs[:4]
    refs = refs[4:]
    win_out = refs.pop(0) if halo else None
    total = refs.pop(0)
    r, groups = pl.program_id(0), pl.num_programs(0)
    point(0)
    unit = nn(middle_low[...], left[0]) + small[0, 4 * layer + 1 : 4 * layer + 2, :]
    unit_out[0] = unit.astype(LOW)
    point(1)
    bent = jnp.tanh(GELU_C * unit * (1.0 + GELU_K * (unit * unit)))
    active = (0.5 * unit * (1.0 + bent) * small[0, 4 * layer : 4 * layer + 1, :]).astype(LOW)
    point(2)
    add_up(r, total, nn(active, right[0]))
    if halo:
        low, zero, pair_sems, mid_sems, local = refs
        rows = total.shape[0]
        window = Window(size, rows, win_out.shape[1] // (size[2] * size[3]))
        groups_all, mid_rows = window.groups, window.mid_rows
        own = win_out.at[window.at(window.own, rows)]
        to_pair = remote(low, own, pair_sems, window.to_pair)
        to_mid = remote(
            low.at[window.at(window.mid_row, mid_rows)],
            win_out.at[window.at((1 - lax.rem(window.h, 2)) * 2 * rows, mid_rows)],
            mid_sems,
            window.to_mid,
        )
        mine = pltpu.make_async_copy(low, own, local.at[0])
        empty = pltpu.make_async_copy(
            zero, win_out.at[window.at(lax.rem(window.h + 1, 2) * 2 * rows, mid_rows)], local.at[1]
        )

    @pl.when(r == groups - 1)
    def _():
        base = 6 * layer
        before = middle[...] + total[...] + vec[base + BIAS_TWO : base + BIAS_TWO + 1, :]
        current = norm_forward(
            before,
            vec[base + GAIN_TWO : base + GAIN_TWO + 1, :],
            vec[base + SHIFT_TWO : base + SHIFT_TWO + 1, :],
        )
        before_out[...] = before
        x_out[...] = current
        xb_out[...] = current.astype(LOW)
        if halo:
            low[...] = current.astype(LOW)
            to_pair.start()

            @pl.when(window.middle)
            def _():
                to_mid.start()

            mine.start()

            @pl.when(jnp.logical_not(window.middle))
            def _():
                zero[...] = jnp.zeros_like(zero)
                empty.start()

    point(3)
    if halo:

        @pl.when(r == groups - 1)
        def _():
            mine.wait()
            to_pair.wait()

            @pl.when(window.middle)
            def _():
                to_mid.wait()

            @pl.when(jnp.logical_not(window.middle))
            def _():
                empty.wait()


def match_teacher(layers, tokens, point, *refs):
    refs = list(refs)
    states = [refs.pop(0) for _ in range(layers)]
    target, chosen, row_ok, counts, weight = refs[:5]
    back_out, loss_out, grad_out = refs[5:]
    r = pl.program_id(0)
    rows = states[0].shape[0]

    @pl.when(r == 0)
    def _():
        loss_out[...] = jnp.zeros_like(loss_out)
        back_out[...] = jnp.zeros_like(back_out)

    count = jnp.sum(counts[...][:, 0:1, 0:1], 0)
    factor = tokens / count
    mine = pl.ds(pl.multiple_of(lax.axis_index("head") * rows, rows), rows)
    total = None
    for layer in range(layers):
        goal = jnp.where(r == 0, chosen[layer, mine, :], target[0, layer]).astype(F32)
        miss = (nn(states[layer][...], weight[0]) - goal) * row_ok[:, :1]
        loss_out[:1, :1] += jnp.sum(jnp.sum(miss * miss, 0, keepdims=True), 1, keepdims=True)
        low = (factor * miss).astype(LOW)
        back_out[layer] += nt(low, weight[0])
        grad = tn(states[layer][...], low)
        total = grad if total is None else total + grad
    grad_out[0] = total.astype(LOW)


def feed_backward(layer, last, point, *refs):
    refs = list(refs)
    before_two, before_one, middle_low, unit_in, small, vec, left, right = refs[:8]
    refs = refs[8:]
    grad_refs = [refs.pop(0) for _ in range(2 if last else 1)]
    inner_out, outer_out, attn_out, grad_out, vec_out, unit_vec, total, feed = refs
    r, groups = pl.program_id(0), pl.num_programs(0)
    base = 6 * layer
    point(0)

    @pl.when(r == 0)
    def _():
        if last:
            cotangent, spread = grad_refs
            rows = total.shape[0]
            mine = pl.ds(pl.multiple_of(lax.axis_index("head") * rows, rows), rows)
            grad = cotangent[mine, :].astype(F32) + spread[0]
        else:
            grad = grad_refs[0][...]
        grad_before, grad_gain, grad_shift, grad_bias = norm_backward(
            before_two[...], vec[base + GAIN_TWO : base + GAIN_TWO + 1, :], grad
        )
        vec_out[BIAS_TWO : BIAS_TWO + 1, :] = grad_bias
        vec_out[GAIN_TWO : GAIN_TWO + 1, :] = grad_gain
        vec_out[SHIFT_TWO : SHIFT_TWO + 1, :] = grad_shift
        feed[...] = grad_before.astype(LOW)
        total[...] = grad_before

    grad_active = nt(feed[...], right[0])
    point(1)
    value, slope = gelu_parts(unit_in[0].astype(F32))
    opened = small[0, 4 * layer : 4 * layer + 1, :]
    grad_unit = (grad_active * (slope * opened)).astype(LOW)
    unit_vec[0, 0:1, :] = jnp.sum(grad_unit.astype(F32), 0, keepdims=True)
    unit_vec[0, 1:2, :] = jnp.sum(grad_active * value, 0, keepdims=True)
    active = (value * opened).astype(LOW)
    point(2)
    total[...] += nt(grad_unit, left[0])
    point(3)
    inner_out[0] = tn(middle_low[...], grad_unit).astype(LOW)
    point(4)
    outer_out[0] = tn(feed[...], active).astype(LOW)
    point(5)

    @pl.when(r == groups - 1)
    def _():
        grad_before, grad_gain, grad_shift, grad_bias = norm_backward(
            before_one[...], vec[base + GAIN_ONE : base + GAIN_ONE + 1, :], total[...]
        )
        vec_out[BIAS_ONE : BIAS_ONE + 1, :] = grad_bias
        vec_out[GAIN_ONE : GAIN_ONE + 1, :] = grad_gain
        vec_out[SHIFT_ONE : SHIFT_ONE + 1, :] = grad_shift
        grad_out[...] = grad_before
        attn_out[...] = grad_before.astype(LOW)

    point(6)


def attention_backward(size, layer, first, point, *refs):
    seqs, seq_len, heads, head_size = size
    refs = list(refs)
    attn, grad_before, xwin, query_in, kv, ctx, lse, gated, small, lengths, left, right = refs[:12]
    refs = refs[12:]
    extra = None if first else refs.pop(0)
    left_out, right_out, grad_out, head_vec = refs[:4]
    (grad_kv, grad_q, kv_all, q_all, spread, mine, pair_low, pair_got, mid_low, mid_got, pair_sems, mid_sems) = refs[4:]
    step, groups = pl.program_id(0), pl.num_programs(0) // 2
    width = heads * head_size
    rows = mine.shape[0]
    group_count = mine.shape[1] // width
    window = Window(size, rows, group_count)
    block, mid_rows = window.block, window.mid_rows
    blocks = rows // block
    offset = window.base if first else 0
    here = window.at(offset + window.own, rows)
    row = small[0, 4 * layer + 2 : 4 * layer + 3, :]
    to_pair = remote(pair_low, pair_got, pair_sems, window.to_pair)
    to_mid = remote(mid_low, mid_got, mid_sems, window.to_mid)
    ahead, behind = range(group_count), range(group_count, 2 * group_count)

    @pl.when(step < groups)
    def _():
        point(0, ahead)
        opened = row[:, width : 2 * width]
        grad_gated = nn(attn[...], right[0, :, width:])
        shared = grad_gated * ctx[0]
        grad_ctx = (grad_gated * opened).astype(LOW)
        pulled = shared * opened
        scaled = query_in[0] * jnp.asarray(0.125, LOW)
        grad_kv[...] = jnp.zeros_like(grad_kv)
        for piece in range(blocks):
            part = slice(piece * block, (piece + 1) * block)
            keys = window.keys(piece)
            usable = lax.broadcasted_iota(jnp.int32, (block, seq_len), 1) < lengths[window.loc(piece)]
            for head in range(heads):
                lanes = slice(head * head_size, (head + 1) * head_size)
                later = slice(width + head * head_size, width + (head + 1) * head_size)
                key = kv[0, keys, lanes]
                scores = nt(scaled[part, lanes], key)
                chances = jnp.where(usable, jnp.exp(scores - lse[0, part, head : head + 1]), 0.0)
                grad_chances = nt(grad_ctx[part, lanes], kv[0, keys, later])
                delta = jnp.sum(pulled[part, lanes], -1, keepdims=True)
                grad_scores = (chances * (grad_chances - delta)).astype(LOW)
                grad_q[part, lanes] = nn(grad_scores, key) * 0.125
                grad_kv[keys, lanes] += tn(grad_scores, scaled[part, lanes])
                grad_kv[keys, later] += tn(chances.astype(LOW), grad_ctx[part, lanes])
                point(1 + piece * heads + head, ahead)
        query_low = grad_q[...].astype(LOW)
        kv_low = grad_kv[...].astype(LOW)
        q_all[step] = query_low
        kv_all[step] = kv_low
        head_vec[0, 0:1, :width] = jnp.sum(query_low.astype(F32), 0, keepdims=True)
        head_vec[0, 0:1, 2 * width :] = jnp.sum(kv_low.astype(F32), 0, keepdims=True)
        shared_sum = jnp.sum(shared, 0, keepdims=True)
        lane = lax.broadcasted_iota(jnp.int32, (1, 128), 1)
        by_head = jnp.zeros((1, 128), F32)
        for head in range(heads):
            one = jnp.sum(shared_sum[:, head * head_size : (head + 1) * head_size], 1, keepdims=True)
            by_head = jnp.where(lane == head, one, by_head)
        head_vec[0, 1:2, :128] = by_head

        @pl.when(step == 0)
        def _():
            spread[...] = jnp.zeros_like(spread)
            mine[...] = grad_before[...] if first else grad_before[...] + extra[0]

        spread[...] += nt(kv_low, left[0])
        mine[...] += nt(query_low, right[0, :, :width])
        point(1 + blocks * heads, ahead)

        @pl.when(step == groups - 1)
        def _():
            pair_low[...] = spread[window.at(window.pair, rows), :].astype(LOW)
            to_pair.start()

            @pl.when(window.middle)
            def _():
                mid_low[...] = spread[window.at(window.mid, mid_rows), :].astype(LOW)
                to_mid.start()

    @pl.when(step >= groups)
    def _():
        for spot in range(1 + blocks * heads):
            if spot % 3 == 0:
                point(spot, behind)
        r = step - groups
        left_out[0] = tn(xwin[window.at(offset, 2 * seq_len), :], kv_all[r]).astype(LOW)
        for spot in range(1 + blocks * heads):
            if spot % 3 == 1:
                point(spot, behind)
        right_out[0, :, :width] = tn(xwin[here, :], q_all[r]).astype(LOW)
        for spot in range(1 + blocks * heads):
            if spot % 3 == 2:
                point(spot, behind)
        right_out[0, :, width:] = tn(attn[...], gated[0]).astype(LOW)

        @pl.when(step == 2 * groups - 1)
        def _():
            to_pair.wait()
            mine[...] += spread[window.at(window.own, rows), :] + pair_got[...].astype(F32)

            @pl.when(window.middle)
            def _():
                to_mid.wait()
                mine[window.at(window.mid_row, mid_rows), :] += mid_got[...].astype(F32)

            grad_out[...] = mine[...].astype(grad_out.dtype)

        point(1 + blocks * heads, behind)


def on_device(
    ndp,
    groups,
    hidden_in,
    seq_lengths,
    layer_map,
    teacher_states,
    out_cotangent,
    query_weight,
    key_weight,
    value_weight,
    query_value_bias,
    output_weight,
    branch_bias,
    norm_gain,
    norm_shift,
    inner_weight,
    inner_bias,
    outer_weight,
    head_alpha,
    head_noise,
    unit_alpha,
    unit_noise,
    map_weight,
):
    tokens_dev, model = hidden_in.shape
    seqs_dev = seq_lengths.shape[0]
    seq_len = tokens_dev // seqs_dev
    width = query_weight.shape[2]
    units = inner_weight.shape[2]
    layers, heads = head_alpha.shape
    head_size = width // heads
    rows = tokens_dev // groups
    feats = model // ndp
    geo = Geometry(ndp, groups)
    size = (seqs_dev, seq_len, heads, head_size)
    window = Window(size, rows, groups)
    blocks = rows // window.block
    dp = lax.axis_index("dp")

    def slices(array):
        return array.reshape(array.shape[0], geo.size_y, geo.size_x, 2, feats, array.shape[-1])

    def matrices(arrays):
        return [(array.reshape(groups, model, array.shape[-1]), "group") for array in arrays]

    def pairs(cols, steps):
        out, begin = [], 0
        for step in steps:
            out.append([(0, begin, step, False), (1, begin, step, True)])
            begin += step
        return out if begin == cols else [[(0, 0, cols, False), (1, 0, cols, True)]]

    key_value = slices(jnp.concatenate([key_weight, value_weight], 2))
    query_output = slices(jnp.concatenate([query_weight, jnp.swapaxes(output_weight, 1, 2)], 2))
    inner, outer = slices(inner_weight), slices(outer_weight)

    def attn_gather(layer):
        return Gather(geo, [(key_value, layer), (query_output, layer)], pairs(2 * width, ATTN_CUTS))

    def feed_gather(layer):
        return Gather(geo, [(inner, layer), (outer, layer)], pairs(units, FEED_CUTS))

    open_unit, unit_back = jax.vjp(partial(gate_open, unit_noise), unit_alpha)
    open_head, head_back = jax.vjp(partial(gate_open, head_noise), head_alpha)
    (unit_slope,) = unit_back(jnp.ones_like(open_unit))
    (head_slope,) = head_back(jnp.ones_like(open_head))
    mixed = jnp.concatenate(
        [
            query_value_bias[:, 0],
            jnp.repeat(open_head, head_size, axis=1),
            jnp.zeros((layers, width), F32),
            query_value_bias[:, 1],
        ],
        1,
    )
    small = jnp.stack([open_unit, inner_bias, mixed, mixed], 1).reshape(4 * layers, units)
    vec = jnp.concatenate([branch_bias, norm_gain, norm_shift], 1).reshape(6 * layers, model)
    lengths = lax.dynamic_slice(seq_lengths, (window.first,), (2,))
    spot = jnp.arange(tokens_dev)
    row_ok = (spot % seq_len < jnp.repeat(seq_lengths, seq_len, total_repeat_length=tokens_dev)).astype(F32)
    row_ok = lax.dynamic_slice(row_ok, (window.h * rows,), (rows,))
    row_ok = jnp.broadcast_to(row_ok[:, None], (rows, 128))
    count = jnp.broadcast_to(jnp.sum(seq_lengths).astype(F32), (8, 128))
    chosen = jnp.take(teacher_states, layer_map, axis=0)

    *weights, small, counts = run(
        only_move,
        1,
        [],
        [],
        [],
        0,
        "gather_first",
        [attn_gather(0), Spread(geo, small, absolute=False), Spread(geo, count, plane=True)],
        1,
        1,
    )
    weights = matrices(weights)
    xwin, resid = hidden_in, None
    records, lows = [], []
    row_block = pltpu.VMEM((rows, model), F32)
    low_block = pltpu.VMEM((rows, model), LOW)
    mid_block = pltpu.VMEM((window.mid_rows, model), LOW)
    two = pltpu.SemaphoreType.DMA((2,))
    for layer in range(layers):
        ending = layer == layers - 1
        inputs = [(xwin, "full"), (small, "group"), (vec, "full"), (lengths, "smem")] + weights
        if layer:
            inputs.append((resid, "full"))
        attn_weights = weights
        kv, query, ctx, lse, gated, before_one, middle, middle_low, *got = run(
            partial(attention_forward, size, layer, layer == 0),
            groups,
            inputs,
            [
                ((groups, 2 * seq_len, 2 * width), LOW, "group"),
                ((groups, rows, width), LOW, "group"),
                ((groups, rows, width), F32, "group"),
                ((groups, rows, 128), F32, "group"),
                ((groups, rows, width), LOW, "group"),
                ((rows, model), F32, "full"),
                ((rows, model), F32, "full"),
                ((rows, model), LOW, "full"),
            ],
            [row_block],
            8e9,
            "attention_forward",
            [feed_gather(layer)],
            2 + blocks * heads,
            2 + 2 * layer,
        )
        feed_weights = matrices(got)
        outputs = [
            ((groups, rows, units), LOW, "group"),
            ((rows, model), F32, "full"),
            ((rows, model), F32, "full"),
            ((rows, model), LOW, "full"),
        ]
        scratch = [row_block]
        if ending:
            riders = [Gather(geo, [(slices(map_weight[None]), 0)], [[(0, 0, width, False)]]), Deal(geo, chosen)]
        else:
            riders = [attn_gather(layer + 1)]
            outputs.append(((2 * seq_len, model), LOW, "any"))
            scratch += [low_block, mid_block, two, two, two]
        unit_in, before_two, resid, low, *got = run(
            partial(feed_forward, size, layer, not ending),
            groups,
            [(middle, "full"), (middle_low, "full"), (small, "group"), (vec, "full")] + feed_weights,
            outputs,
            scratch,
            5e9,
            "feed_forward",
            riders,
            4,
            3 + 2 * layer,
        )
        records.append(
            (xwin, kv, query, ctx, lse, gated, before_one, middle_low, unit_in, before_two, attn_weights, feed_weights)
        )
        lows.append(low)
        if not ending:
            xwin, *got = got
            weights = matrices(got)
    weights, target = matrices(got[:1]), got[1]
    spread, loss, grad_map = run(
        partial(match_teacher, layers, float(tokens_dev * ndp)),
        groups,
        [(low, "full") for low in lows]
        + [(target, lambda r: jnp.maximum(r - 1, 0)), (chosen, "full"), (row_ok, "full"), (counts, "full")]
        + weights,
        [
            ((layers, rows, model), F32, "full"),
            ((8, 128), F32, "full"),
            ((groups, model, width), LOW, "group"),
        ],
        [],
        4e9,
        "match_teacher",
    )

    def parts(grad):
        return slices(grad)

    grads = [(out_cotangent, "full"), (spread[layers - 1 :], "full")]
    results = [{} for _ in range(layers)]
    riders, waiting = [Spread(geo, lows[-1])], [(0, "block_out")]
    number = 2 + 2 * layers

    def settle(got):
        for (layer, name), value in zip(waiting, got):
            results[layer][name] = value

    early, late = (lambda s: jnp.minimum(s, groups - 1)), (lambda s: jnp.maximum(s - groups, 0))
    for layer in reversed(range(layers)):
        xwin, kv, query, ctx, lse, gated, before_one, middle_low, unit_in, before_two, attn_weights, feed_weights = records[layer]
        inner_grad, outer_grad, attn, grad_before, vec_out, unit_vec, *got = run(
            partial(feed_backward, layer, layer == layers - 1),
            groups,
            [
                (before_two, "full"),
                (before_one, "full"),
                (middle_low, "full"),
                (unit_in, "group"),
                (small, "group"),
                (vec, "full"),
            ]
            + feed_weights
            + grads,
            [((groups, model, units), LOW, "group")] * 2
            + [
                ((rows, model), LOW, "full"),
                ((rows, model), F32, "full"),
                ((8, model), F32, "full"),
                ((groups, 8, units), F32, "group"),
            ],
            [row_block, low_block],
            10e9,
            "feed_backward",
            riders,
            7,
            number,
        )
        number += 1
        settle(got)
        riders = [Scatter(geo, [parts(inner_grad), parts(outer_grad)], pairs(units, BACK_CUTS))]
        waiting = [(layer, "inner"), (layer, "outer")]
        if layer == layers - 1:
            riders.append(Scatter(geo, [parts(grad_map)], [[(0, 0, width, False)]]))
            waiting.append((0, "map"))
        left, right, grad, head_vec, *got = run(
            partial(attention_backward, size, layer, layer == 0),
            2 * groups,
            [
                (attn, "full"),
                (grad_before, "full"),
                (xwin, "full"),
                (query, early),
                (kv, early),
                (ctx, early),
                (lse, early),
                (gated, late),
                (small, early),
                (lengths, "smem"),
            ]
            + [(array, early) for array, _ in attn_weights]
            + ([(spread[layer - 1 : layer], "full")] if layer else []),
            [((groups, model, 2 * width), LOW, late)] * 2
            + [
                ((rows, model), F32 if layer else LOW, "full"),
                ((groups, 8, units), F32, early),
            ],
            [
                pltpu.VMEM((2 * seq_len, 2 * width), F32),
                pltpu.VMEM((rows, width), F32),
                pltpu.VMEM((groups, 2 * seq_len, 2 * width), LOW),
                pltpu.VMEM((groups, rows, width), LOW),
                pltpu.VMEM((2 * seq_len, model), F32),
                row_block,
                low_block,
                low_block,
                mid_block,
                mid_block,
                two,
                two,
            ],
            12e9,
            "attention_backward",
            riders,
            2 + blocks * heads,
            number,
        )
        number += 1
        settle(got)
        riders = [Scatter(geo, [parts(left), parts(right)], pairs(2 * width, LAST_CUTS if layer == 0 else ATTN_CUTS))]
        waiting = [(layer, "kv"), (layer, "qo")]
        grads = [(grad, "full")]
        results[layer].update(vec=vec_out, unit=unit_vec, head=head_vec)

    everywhere = (0, feats, feats)
    unit_count, qv_cols = units // ndp, width // ndp
    items = [(results[layer]["vec"], False, (0, 6), everywhere) for layer in range(layers)]
    items += [(results[layer]["unit"], True, (0, 2), (0, unit_count, unit_count)) for layer in range(layers)]
    for layer in range(layers):
        items += [(results[layer]["head"], True, (0, 1), (0, qv_cols, qv_cols))]
        items += [(results[layer]["head"], True, (0, 1), (3 * width, qv_cols, qv_cols))]
    items += [(results[layer]["head"], True, (1, 2), (0, 0, 128)) for layer in range(layers)]
    items += [(loss, False, (0, 1), (0, 0, 128))]
    riders += [Fold(geo, items), Spread(geo, grad)]
    waiting += [(0, "sums"), (0, "grad_hidden")]
    settle(run(only_move, 1, [], [], [], 0, "scatter_last", riders, 1, number))
    sums = results[0]["sums"]
    by_feature = sums[: 6 * layers, :feats].reshape(layers, 3, 2, feats)
    by_unit = sums[6 * layers : 8 * layers, :unit_count].reshape(layers, 2, unit_count)
    by_column = sums[8 * layers : 10 * layers, :qv_cols].reshape(layers, 2, qv_cols)
    by_head = sums[10 * layers : 11 * layers, :heads]
    distill_loss = sums[11 * layers, 0] / (jnp.sum(counts[:, 0, 0]) * model * layers)
    own_slope = lax.dynamic_slice(unit_slope, (0, dp * unit_count), (layers, unit_count))

    def stacked(member, cols, turned=False):
        arrays = [results[layer][member][:, cols] for layer in range(layers)]
        return jnp.stack([array.T if turned else array for array in arrays])

    front, rear, whole = slice(0, width), slice(width, 2 * width), slice(None)
    return (
        results[0]["block_out"].reshape(tokens_dev, model),
        results[0]["grad_hidden"].reshape(tokens_dev, model).astype(F32),
        distill_loss,
        stacked("qo", front),
        stacked("kv", front),
        stacked("kv", rear),
        by_column,
        stacked("qo", rear, True),
        by_feature[:, 0],
        by_feature[:, 1],
        by_feature[:, 2],
        stacked("inner", whole),
        by_unit[:, 0],
        stacked("outer", whole, True),
        by_head * head_slope,
        by_unit[:, 1] * own_slope,
        results[0]["map"],
    )


def solution(mesh):
    in_specs = (
        P("dp", None),
        P("dp"),
        P(),
        P(None, "dp", "head"),
        P("dp", None),
        P(None, None, "head"),
        P(None, None, "head"),
        P(None, None, "head"),
        P(None, None, "head"),
        P(None, "head", None),
        P(),
        P(),
        P(),
        P(None, None, "head"),
        P(None, "head"),
        P(None, "head", None),
        P(None, "head"),
        P(None, "head"),
        P(None, "head"),
        P(None, "head"),
        P(None, "head"),
    )
    out_specs = (
        P("dp", None),
        P("dp", None),
        P(),
        P(None, "dp", "head"),
        P(None, "dp", "head"),
        P(None, "dp", "head"),
        P(None, None, ("head", "dp")),
        P(None, "head", "dp"),
        P(None, None, "dp"),
        P(None, None, "dp"),
        P(None, None, "dp"),
        P(None, "dp", "head"),
        P(None, ("head", "dp")),
        P(None, "head", "dp"),
        P(None, "head"),
        P(None, ("head", "dp")),
        P("dp", "head"),
    )
    return jax.shard_map(
        partial(on_device, mesh.shape["dp"], mesh.shape["head"]),
        mesh=mesh,
        in_specs=in_specs,
        out_specs=out_specs,
        check_vma=False,
    )
```

```python
from functools import partial

import jax
import jax.numpy as jnp
from jax import lax
from jax.experimental import pallas as pl
from jax.experimental.pallas import tpu as pltpu
from jax.sharding import PartitionSpec as P

BETA = 2.0 / 3.0
EPS = 1e-05
LOW = jnp.bfloat16
F32 = jnp.float32
GELU_C = 0.7978845608028654
GELU_K = 0.044715
VMEM_LIMIT = 56 * 1024 * 1024
ATTN_CUTS = (128, 256)
FEED_CUTS = (128, 128, 256, 256)
BACK_CUTS = (128,) * 6
LAST_CUTS = (128, 128, 128)
MESH = pl.DeviceIdType.MESH


def gate_open(noise, alpha):
    return jnp.clip(jax.nn.sigmoid((noise + alpha) / BETA) * 1.2 - 0.1, 0.0, 1.0)


def product(left, right, dims):
    return lax.dot_general(left, right, ((dims[:1], dims[1:]), ((), ())), preferred_element_type=F32)


def nn(left, right):
    return product(left, right, (1, 0))


def nt(left, right):
    return product(left, right, (1, 1))


def tn(left, right):
    return product(left, right, (0, 0))


def factor_pair(count):
    side = 1
    for trial in range(1, count + 1):
        if count % trial == 0 and trial * trial <= count:
            side = trial
    return side, count // side


def block_of(shape, place):
    if place == "full":
        return pl.BlockSpec(shape, lambda r: (0,) * len(shape))
    return pl.BlockSpec((1,) + tuple(shape[1:]), lambda r: (place(r),) + (0,) * (len(shape) - 1))


def spec_of(array, kind):
    if kind == "any":
        return pl.BlockSpec(memory_space=pl.ANY)
    if kind == "smem":
        return pl.BlockSpec(memory_space=pltpu.SMEM)
    if kind == "group":
        return block_of(array.shape, lambda r: r)
    return block_of(array.shape, kind)


class Plan:
    def __init__(self, spots):
        self.spots = spots
        self.slots = [(step, spot) for step, count in enumerate(spots) for spot in range(count)]
        self.chosen = {slot: [] for slot in self.slots}

    def slot(self, step, spot):
        return self.slots.index((step, spot % self.spots[step]))

    def spread(self, tasks, first, last):
        for share, _, task in sorted(tasks, key=lambda item: item[:2]):
            self.chosen[self.slots[first + round(share * (last - first))]].append(task)

    def even(self, tasks, first, last):
        count = len(tasks)
        self.spread([((index + 1) / count, index, task) for index, task in enumerate(tasks)], first, last)

    def point(self, r, spot, span):
        for step in span:
            tasks = self.chosen.get((step, spot), ())
            if tasks:

                @pl.when(r == step)
                def _(tasks=tasks):
                    for task in tasks:
                        task()


def run(body, steps, inputs, outputs, scratch, flops, name, riders=(), points=1, number=None, placed=False):
    inputs, outputs, scratch = list(inputs), list(outputs), list(scratch)
    at = [len(inputs), len(outputs), len(scratch)]
    starts, sizes = [], []
    for rider in riders:
        starts.append((len(inputs), len(outputs), len(scratch)))
        inputs += rider.inputs
        outputs += rider.outputs
        scratch += rider.scratch
        sizes.append((len(rider.inputs), len(rider.outputs), len(rider.scratch)))
    out_shape = [jax.ShapeDtypeStruct(shape, dtype) for shape, dtype, _ in outputs]
    moved = sum(a.size * a.dtype.itemsize for a, kind in inputs if kind != "any")
    n_in, n_out = len(inputs), len(outputs)
    peers = []
    for rider in riders:
        peers += [peer for peer in rider.peers if peer not in peers]

    def whole(*refs):
        kinds = refs[:n_in], refs[n_in : n_in + n_out], refs[n_in + n_out :]
        own = [ref for part, n in zip(kinds, at) for ref in part[:n]]
        lists = [
            rider.tasks(*[part[i : i + n] for part, i, n in zip(kinds, start, size)])
            for rider, start, size in zip(riders, starts, sizes)
        ]
        r = pl.program_id(0)
        if riders:

            @pl.when(r == 0)
            def _():
                riders[0].geo.greet(peers)

        if placed:
            body(lists, *own)
            return
        plan = Plan([points] * steps)
        listed = []
        for number, tasks in enumerate(lists):
            for index, task in enumerate(tasks):
                listed.append((index / max(1, len(tasks) - 1), (number, index), task))
        plan.spread(listed, 0, len(plan.slots) - 1)
        body(lambda spot, span=range(steps): plan.point(r, spot, span), *own)

    params = {"vmem_limit_bytes": VMEM_LIMIT}
    if riders:
        params.update(collective_id=number, has_side_effects=True)
    return pl.pallas_call(
        whole,
        name=name,
        grid=(steps,),
        in_specs=[spec_of(a, kind) for a, kind in inputs],
        out_specs=[spec_of(o, kind) for o, (_, _, kind) in zip(out_shape, outputs)],
        scratch_shapes=scratch,
        out_shape=out_shape,
        compiler_params=pltpu.CompilerParams(**params),
        cost_estimate=pl.CostEstimate(flops=int(flops), bytes_accessed=int(moved), transcendentals=0),
    )(*[a for a, _ in inputs])


def only_move(point):
    point(0)


class Geometry:
    def __init__(self, ndp, groups):
        self.ndp, self.groups = ndp, groups
        self.size_y, self.size_x = factor_pair(ndp // 2)

    def here(self):
        dp, h = lax.axis_index("dp"), lax.axis_index("head")
        return lax.rem(dp, 2), lax.rem(lax.div(dp, 2), self.size_x), lax.div(dp, 2 * self.size_x), h

    def place(self, c=0, y=0, x=0, z=0):
        core, ix, iy, h = self.here()
        core = 1 - core if c else core
        iy = lax.rem(iy + (y + self.size_y), self.size_y) if y else iy
        ix = lax.rem(ix + (x + self.size_x), self.size_x) if x else ix
        h = lax.rem(h + (z + self.groups), self.groups) if z else h
        return iy, ix, core, h

    def device(self, **to):
        iy, ix, core, h = self.place(**to)
        return ((iy * self.size_x + ix) * 2 + core, h)

    def axes(self):
        out = [dict(c=1)]
        out += [dict(y=y) for y in range(1, self.size_y)]
        out += [dict(x=x) for x in range(1, self.size_x)]
        return out + self.column()

    def column(self):
        return [dict(z=z) for z in range(1, self.groups)]

    def plane(self):
        out = []
        for c in range(2):
            for y in range(self.size_y):
                for x in range(self.size_x):
                    to = {key: value for key, value in (("c", c), ("y", y), ("x", x)) if value}
                    if to:
                        out.append(to)
        return out

    def greet(self, peers):
        barrier = pltpu.get_barrier_semaphore()
        for peer in peers:
            pl.semaphore_signal(barrier, inc=1, device_id=self.device(**peer), device_id_type=MESH)
        pl.semaphore_wait(barrier, len(peers))


class Mover:
    def __init__(self, geo, send, recv):
        self.geo, self.send, self.recv, self.ids = geo, send, recv, {}

    def __call__(self, key, src, dst, **to):
        index = self.ids.setdefault(key, len(self.ids))
        return pltpu.make_async_remote_copy(
            src_ref=src,
            dst_ref=dst,
            send_sem=self.send.at[index],
            recv_sem=self.recv.at[index],
            device_id=self.geo.device(**to),
            device_id_type=MESH,
        )


def back(to):
    return {key: value if key == "c" else -value for key, value in to.items()}


def start(copies):
    for copy in copies:
        copy.start()


def arrive(copies):
    for copy in copies:
        copy.wait_recv()


def leave(copies):
    for copy in copies:
        copy.wait_send()


class Gather:
    def __init__(self, geo, owns, chunks):
        self.geo, self.chunks, self.peers = geo, chunks, geo.axes()
        self.layers = [layer for _, layer in owns]
        self.inputs = [(own, "any") for own, _ in owns]
        self.outputs = [((geo.groups,) + own.shape[1:], LOW, "any") for own, _ in owns]
        halves = sum(len(chunk) for chunk in chunks)
        each = geo.groups - 1 + 2 * geo.size_x * geo.size_y
        sems = pltpu.SemaphoreType.DMA((halves * each,))
        self.scratch = [sems, sems]

    def tasks(self, owns, outs, scratch):
        self.outs = outs
        geo = self.geo
        move = Mover(geo, *scratch)
        groups, sx, sy = geo.groups, geo.size_x, geo.size_y
        others = pl.ds(1, groups - 1)
        owns = [own.at[layer] for own, layer in zip(owns, self.layers)]

        def columns(chunk, half):
            m, col, cols, _ = self.chunks[chunk][half]
            return m, pl.ds(col, cols)

        def along(chunk, half, r):
            m, cols = columns(chunk, half)
            iy, ix, core, _ = geo.place()
            return move(
                ("z", chunk, half, r), owns[m].at[iy, ix, core, :, cols], outs[m].at[r, iy, ix, core, :, cols], z=-r
            )

        def hop(chunk, half, block, to):
            m, cols = columns(chunk, half)
            iy, ix, core, _ = geo.place(**block)
            part = outs[m].at[others, iy, ix, core, :, cols]
            return move(("p", chunk, half, str(block), str(to)), part, part, **back(to))

        ways_x = [dict(x=x) for x in range(1, sx)]
        ways_y = [dict(y=y) for y in range(1, sy)]
        corners = [dict(x=x, y=y) for x in range(1, sx) for y in range(1, sy)]

        def halves(chunk):
            return range(len(self.chunks[chunk]))

        def alongs(chunk):
            return [along(chunk, half, r) for half in halves(chunk) for r in range(1, groups)]

        def firsts(chunk):
            return [hop(chunk, half, {}, to) for half in halves(chunk) for to in ways_x + ways_y]

        def seconds(chunk):
            out = []
            for half in halves(chunk):
                near, far = (ways_y, ways_x) if self.chunks[chunk][half][3] else (ways_x, ways_y)
                out += [hop(chunk, half, block, to) for block in near for to in far]
            return out

        def cores(chunk, blocks):
            return [hop(chunk, half, block, dict(c=1)) for half in halves(chunk) for block in blocks]

        count = len(self.chunks)

        def begin():
            start(alongs(0))
            if count > 1:
                start(alongs(1))

        def level_one(chunk):
            arrive(alongs(chunk))
            start(firsts(chunk))
            start(cores(chunk, [{}]))
            if chunk + 2 < count:
                start(alongs(chunk + 2))

        def level_two(chunk):
            arrive(firsts(chunk))
            start(seconds(chunk))
            start(cores(chunk, ways_x + ways_y))

        def level_three(chunk):
            arrive(seconds(chunk))
            start(cores(chunk, corners))

        def level_four(chunk):
            arrive(cores(chunk, [{}] + ways_x + ways_y + corners))

        def end():
            for chunk in range(count):
                leave(alongs(chunk) + firsts(chunk) + seconds(chunk) + cores(chunk, [{}] + ways_x + ways_y + corners))

        out = [begin]
        self.done = []
        for time in range(count + 3):
            for level, late in ((level_one, 0), (level_two, 1), (level_three, 2), (level_four, 3)):
                if 0 <= time - late < count:
                    out.append(partial(level, time - late))
            if time >= 3:
                self.done.append(len(out))
        return out + [end]


class Lend:
    def __init__(self, geo, rider):
        self.geo, self.rider, self.peers = geo, rider, []
        self.inputs, self.outputs, self.scratch = [], [], []

    def tasks(self, owns, outs, scratch):
        return [self.rider.outs]


class Scatter:
    def __init__(self, geo, grads, chunks):
        self.geo, self.chunks, self.peers = geo, chunks, geo.axes()
        self.inputs = [(grad, "any") for grad in grads]
        self.outputs = [(grad.shape[4:], F32, "full") for grad in grads]
        feats = grads[0].shape[4]
        halves = [half for chunk in chunks for half in chunk]
        each = 1 + (geo.size_x - 1) + (geo.size_y - 1) + geo.groups - 1
        sems = pltpu.SemaphoreType.DMA((len(halves) * each,))
        self.scratch = [sems, sems, pltpu.SemaphoreType.DMA((len(halves),))]
        for _, _, cols, y_first in halves:
            near, far = (geo.size_y, geo.size_x) if y_first else (geo.size_x, geo.size_y)
            self.scratch += [
                pltpu.VMEM(shape, LOW)
                for shape in (
                    (geo.groups, geo.size_y, geo.size_x, feats, cols),
                    (geo.groups, geo.size_y, geo.size_x, feats, cols),
                    (near - 1, geo.groups, far, feats, cols),
                    (far - 1, geo.groups, feats, cols),
                    (geo.groups - 1, feats, cols),
                )
            ]

    def tasks(self, grads, outs, scratch):
        geo, (send, recv, local), buffers = self.geo, scratch[:3], scratch[3:]
        move = Mover(geo, send, recv)
        groups, sx, sy = geo.groups, geo.size_x, geo.size_y
        index = {}
        for chunk, halves in enumerate(self.chunks):
            for half in range(len(halves)):
                index[chunk, half] = len(index)

        def parts(chunk, half):
            m, col, cols, y_first = self.chunks[chunk][half]
            number = index[chunk, half]
            return grads[m], pl.ds(col, cols), y_first, buffers[5 * number : 5 * number + 5]

        def load(chunk, half):
            grad, cols, _, bufs = parts(chunk, half)
            _, _, core, _ = geo.place()
            return pltpu.make_async_copy(
                grad.at[:, :, :, core, :, cols], bufs[0], local.at[index[chunk, half]]
            )

        def cross(chunk, half):
            grad, cols, _, bufs = parts(chunk, half)
            _, _, core, _ = geo.place(c=1)
            return move(("c", chunk, half), grad.at[:, :, :, core, :, cols], bufs[1], c=1)

        def near(chunk, half):
            _, _, y_first, bufs = parts(chunk, half)
            out = []
            for step in range(1, sy if y_first else sx):
                to = dict(y=step) if y_first else dict(x=step)
                iy, ix, _, _ = geo.place(**to)
                part = bufs[0].at[:, iy] if y_first else bufs[0].at[:, :, ix]
                out.append(move(("n", chunk, half, step), part, bufs[2].at[step - 1], **to))
            return out

        def far(chunk, half):
            _, _, y_first, bufs = parts(chunk, half)
            out = []
            for step in range(1, sx if y_first else sy):
                to = dict(x=step) if y_first else dict(y=step)
                iy, ix, _, _ = geo.place(**to)
                out.append(move(("f", chunk, half, step), bufs[0].at[:, iy, ix], bufs[3].at[step - 1], **to))
            return out

        def along(chunk, half):
            _, _, _, bufs = parts(chunk, half)
            iy, ix, _, _ = geo.place()
            return [
                move(("z", chunk, half, r), bufs[0].at[r, iy, ix], bufs[4].at[r - 1], z=r) for r in range(1, groups)
            ]

        def each(chunk):
            return range(len(self.chunks[chunk]))

        def begin_one(chunk):
            for half in each(chunk):
                cross(chunk, half).start()
                load(chunk, half).start()

        count = len(self.chunks)

        def begin():
            for chunk in range(min(2, count)):
                begin_one(chunk)

        def level_one(chunk):
            for half in each(chunk):
                _, _, _, bufs = parts(chunk, half)
                load(chunk, half).wait()
                cross(chunk, half).wait_recv()
                for r in range(groups):
                    bufs[0][r] = (bufs[0][r].astype(F32) + bufs[1][r].astype(F32)).astype(LOW)
                start(near(chunk, half))
            if chunk + 2 < count:
                begin_one(chunk + 2)

        def level_two(chunk):
            iy, ix, _, _ = geo.place()
            for half in each(chunk):
                _, _, y_first, bufs = parts(chunk, half)
                arrive(near(chunk, half))
                for r in range(groups):
                    total = (bufs[0][r, iy] if y_first else bufs[0][r, :, ix]).astype(F32)
                    for other in range(bufs[2].shape[0]):
                        total = total + bufs[2][other, r].astype(F32)
                    if y_first:
                        bufs[0][r, iy] = total.astype(LOW)
                    else:
                        bufs[0][r, :, ix] = total.astype(LOW)
                start(far(chunk, half))

        def level_three(chunk):
            iy, ix, _, _ = geo.place()
            for half in each(chunk):
                _, _, _, bufs = parts(chunk, half)
                arrive(far(chunk, half))
                for r in range(groups):
                    total = bufs[0][r, iy, ix].astype(F32)
                    for other in range(bufs[3].shape[0]):
                        total = total + bufs[3][other, r].astype(F32)
                    bufs[0][r, iy, ix] = total.astype(LOW)
                start(along(chunk, half))

        def level_four(chunk):
            iy, ix, _, _ = geo.place()
            for half in each(chunk):
                m, col, cols, _ = self.chunks[chunk][half]
                _, _, _, bufs = parts(chunk, half)
                arrive(along(chunk, half))
                total = bufs[0][0, iy, ix].astype(F32)
                for r in range(1, groups):
                    total = total + bufs[4][r - 1].astype(F32)
                outs[m][:, col : col + cols] = total

        def end():
            for chunk in range(count):
                for half in each(chunk):
                    leave([cross(chunk, half)] + near(chunk, half) + far(chunk, half) + along(chunk, half))

        out = [begin]
        for time in range(count + 3):
            for level, late in ((level_one, 0), (level_two, 1), (level_three, 2), (level_four, 3)):
                if 0 <= time - late < count:
                    out.append(partial(level, time - late))
        return out + [end]


class Spread:
    def __init__(self, geo, value, plane=False, absolute=True):
        self.geo, self.plane, self.absolute = geo, plane, absolute
        self.peers = geo.plane() if plane else geo.column()
        self.inputs = [(value, "full")]
        self.outputs = [((len(self.peers) + 1,) + value.shape, value.dtype, "any")]
        sems = pltpu.SemaphoreType.DMA((len(self.peers),))
        self.scratch = [sems, sems, pltpu.SemaphoreType.DMA]

    def tasks(self, values, outs, scratch):
        geo, (value,), (out,), (send, recv, local) = self.geo, values, outs, scratch
        move = Mover(geo, send, recv)
        own = 0
        if self.absolute:
            own = geo.device()[0] if self.plane else geo.device()[1]
        copies = []
        for to in self.peers:
            slot = own if self.absolute else to["z"]
            copies.append(move(str(to), value, out.at[slot], **back(to)))
        mine = pltpu.make_async_copy(value, out.at[own], local)

        def begin():
            start(copies)
            mine.start()

        def end():
            mine.wait()
            arrive(copies)
            leave(copies)

        return [begin, end]


class Deal:
    def __init__(self, geo, value):
        self.geo, self.peers = geo, geo.column()
        self.rows = value.shape[1] // geo.groups
        self.inputs = [(value, "any")]
        shape = (geo.groups - 1, value.shape[0], self.rows, value.shape[2])
        self.outputs = [(shape, value.dtype, "any")]
        sems = pltpu.SemaphoreType.DMA((geo.groups - 1,))
        self.scratch = [sems, sems]

    def tasks(self, values, outs, scratch):
        geo = self.geo
        move = Mover(geo, *scratch)
        copies = []
        for r in range(1, geo.groups):
            first = pl.multiple_of(geo.place(z=-r)[3] * self.rows, self.rows)
            copies.append(move(r, values[0].at[:, pl.ds(first, self.rows), :], outs[0].at[r - 1], z=-r))

        def end():
            arrive(copies)
            leave(copies)

        return [lambda: start(copies), end]


class Fold:
    def __init__(self, geo, items):
        self.geo, self.peers = geo, geo.plane() + geo.column()
        self.inputs = [(item[0], "full") for item in items]
        self.picks = [item[1:] for item in items]
        rows = sum(stop - first for _, (first, stop), _ in self.picks)
        self.rows = -(-rows // 8) * 8
        self.outputs = [((self.rows, 128), F32, "full")]
        near, far = pltpu.SemaphoreType.DMA((geo.ndp - 1,)), pltpu.SemaphoreType.DMA((geo.groups - 1,))
        wide = pltpu.VMEM((geo.ndp, geo.groups, self.rows, 128), F32)
        slim = pltpu.VMEM((geo.groups, self.rows, 128), F32)
        self.scratch = [near, near, far, far, wide, wide, slim, slim]

    def tasks(self, values, outs, scratch):
        geo = self.geo
        near_send, near_recv, far_send, far_recv, packed, landed, middle, last = scratch
        groups, ndp = geo.groups, geo.ndp
        to_plane, to_column = Mover(geo, near_send, near_recv), Mover(geo, far_send, far_recv)
        dp, h = geo.device()
        near, far = [], []
        for to in geo.plane():
            there, _ = geo.device(**to)
            near.append(to_plane(str(to), packed.at[there], landed.at[dp], **to))
        for r in range(1, groups):
            far.append(to_column(r, middle.at[r], last.at[h], z=r))

        def begin():
            packed[...] = jnp.zeros_like(packed)
            row = 0
            for value, (grouped, (low, high), (first, stride, cols)) in zip(values, self.picks):
                for r in range(groups):
                    for d in range(ndp):
                        lanes = slice(first + d * stride, first + d * stride + cols)
                        part = value[r, low:high, lanes] if grouped else value[low:high, lanes]
                        packed[d, r, row : row + high - low, :cols] = part
                row += high - low
            start(near)

        def fold():
            landed[dp] = packed[dp]
            arrive(near)
            total = landed[0]
            for d in range(1, ndp):
                total = total + landed[d]
            middle[...] = total
            start(far)

        def end():
            last[h] = middle[0]
            arrive(far)
            total = last[0]
            for z in range(1, groups):
                total = total + last[z]
            outs[0][...] = total
            leave(near)
            leave(far)

        return [begin, fold, end]


def norm_forward(before, gain, shift):
    center = before - jnp.mean(before, -1, keepdims=True)
    spread = jnp.mean(center * center, -1, keepdims=True)
    return center * lax.rsqrt(spread + EPS) * gain + shift


def norm_backward(before, gain, grad):
    center = before - jnp.mean(before, -1, keepdims=True)
    rate = lax.rsqrt(jnp.mean(center * center, -1, keepdims=True) + EPS)
    hat = center * rate
    grad_hat = grad * gain
    mean_one = jnp.mean(grad_hat, -1, keepdims=True)
    mean_two = jnp.mean(grad_hat * hat, -1, keepdims=True)
    grad_before = rate * (grad_hat - mean_one - hat * mean_two)
    return (
        grad_before,
        jnp.sum(grad * hat, 0, keepdims=True),
        jnp.sum(grad, 0, keepdims=True),
        jnp.sum(grad_before, 0, keepdims=True),
    )


BIAS_ONE, BIAS_TWO, GAIN_ONE, GAIN_TWO, SHIFT_ONE, SHIFT_TWO = range(6)


class Window:
    def __init__(self, size, rows, groups):
        self.seqs, self.seq_len, self.heads, self.head_size = size
        self.rows, self.groups = rows, groups
        self.block = self.seq_len // groups
        self.mid_rows = 2 * self.block
        h = lax.axis_index("head")
        self.h = h
        self.first = lax.div(h * (self.seqs - 1), groups)
        self.base = self.first * self.seq_len
        self.own = h * rows - self.base
        pair = h + 1 - 2 * lax.rem(h, 2)
        self.pair = pair * rows - self.base
        self.mid = lax.rem(h, 2) * (2 * rows)
        self.mid_row = lax.rem(h, 2) * self.block
        self.middle = (h > 0) & (h < groups - 1)
        dp = lax.axis_index("dp")
        self.to_pair = (dp, pair)
        self.to_mid = (dp, groups - 1 - h)

    def at(self, begin, rows):
        return pl.ds(pl.multiple_of(begin, self.block), rows)

    def loc(self, piece):
        return lax.div((self.h * (self.rows // self.block) + piece) * self.block, self.seq_len) - self.first

    def keys(self, piece):
        return pl.ds(pl.multiple_of(self.loc(piece) * self.seq_len, self.seq_len), self.seq_len)


def remote(src, dst, sems, to):
    return pltpu.make_async_remote_copy(
        src_ref=src, dst_ref=dst, send_sem=sems.at[0], recv_sem=sems.at[1], device_id=to, device_id_type=MESH
    )


def add_up(r, total, part):
    @pl.when(r == 0)
    def _():
        total[...] = part

    @pl.when(r > 0)
    def _():
        total[...] += part


def gelu_parts(unit):
    square = unit * unit
    bent = jnp.tanh(GELU_C * unit * (1.0 + GELU_K * square))
    half = 0.5 * (1.0 + bent)
    slope = half + 0.5 * unit * (1.0 - bent * bent) * (GELU_C * (1.0 + 3.0 * GELU_K * square))
    return unit * half, slope


def vector(vec, layer, which):
    return vec[6 * layer + which : 6 * layer + which + 1, :]


def attend(window, layer, xin, offset, row, lengths, left, right, outs, total, r, point):
    kv_out, q_out, ctx_out, lse_out, gated_out = outs
    seq_len, heads, head_size, block, rows = (
        window.seq_len,
        window.heads,
        window.head_size,
        window.block,
        window.rows,
    )
    width = heads * head_size
    point(0)
    kv = nn(xin[window.at(offset, 2 * seq_len), :], left) + row[:, 2 * width :]
    kv_out[0] = kv.astype(LOW)
    query = (nn(xin[window.at(offset + window.own, rows), :], right[:, :width]) + row[:, :width]).astype(LOW)
    q_out[0] = query
    scaled = query * jnp.asarray(0.125, LOW)
    for piece in range(rows // block):
        mine = slice(piece * block, (piece + 1) * block)
        keys = window.keys(piece)
        usable = lax.broadcasted_iota(jnp.int32, (block, seq_len), 1) < lengths[window.loc(piece)]
        for head in range(heads):
            lanes = slice(head * head_size, (head + 1) * head_size)
            scores = nt(scaled[mine, lanes], kv_out[0, keys, lanes])
            scores = jnp.where(usable, scores, -1e30)
            largest = jnp.max(scores, -1, keepdims=True)
            powers = jnp.exp(scores - largest)
            sums = jnp.sum(powers, -1, keepdims=True)
            value = kv_out[0, keys, width + head * head_size : width + (head + 1) * head_size]
            context = nn(powers.astype(LOW), value) / sums
            ctx_out[0, mine, lanes] = context
            lse_out[0, mine, head : head + 1] = largest + jnp.log(sums)
            point(1 + piece * heads + head)
    gated = (ctx_out[0] * row[:, width : 2 * width]).astype(LOW)
    gated_out[0] = gated
    add_up(r, total, nt(gated, right[:, width:]))


def forward(size, layers, geo, gather, lists, *refs):
    seqs, seq_len, heads, head_size = size
    refs = list(refs)
    take = lambda n: [refs.pop(0) for _ in range(n)]
    hidden, small_own, vec, lengths, key_value, query_output, inner, outer, map_own = take(9)
    saved = [take(10) for _ in range(layers)]
    win_out, small_out = take(2)
    left_buf, right_buf, inner_buf, outer_buf, load_sems, back_sems = take(6)
    total, middle, current, low, xwin, small, small_send, small_recv, map_stage = take(9)
    pair_sems, mid_sems, local = take(3)
    gather_tasks, count_tasks, deal_tasks, (weights,) = lists
    groups = geo.groups
    rows, model = total.shape
    window = Window(size, rows, groups)
    mid_rows, width = window.mid_rows, heads * head_size
    s = pl.program_id(0)
    r = lax.rem(s, groups)
    slot = lax.rem(r, 2)
    spots_attn, spots_feed = 2 + rows // window.block * heads, 4
    plan = Plan(([spots_attn] * groups + [spots_feed] * groups) * layers)

    move = Mover(geo, small_send, small_recv)
    small_copies = [move(i, small_own, small.at[i], z=-i) for i in range(1, groups)]
    keep_small = pltpu.make_async_copy(small, small_out, local.at[2])

    def small_begin():
        start(small_copies)

    def small_end():
        arrive(small_copies)
        leave(small_copies)
        keep_small.start()

    into_stage = pltpu.make_async_copy(map_own.at[0], map_stage, local.at[3])
    out_of_stage = pltpu.make_async_copy(map_stage, weights[-1].at[0], local.at[4])

    def stage_begin():
        into_stage.start()

    def stage_end():
        into_stage.wait()
        out_of_stage.start()

    phases = 2 * layers
    plan.even([small_begin] + [count_tasks[0]], 0, 0)
    ends, done = [], 0
    for phase in range(phases):
        for chunk, halves in enumerate(gather.chunks):
            if halves[0][0] // 2 == phase:
                done = gather.done[chunk]
        ends.append(done)
    first, begun = 0, 0
    for phase in range(phases):
        last = plan.slot(phase * groups, -1)
        plan.even(gather_tasks[begun : ends[phase]], first, last)
        first, begun = last, ends[phase]
        if phase == 0:
            plan.even([small_end, stage_begin], last, last)
            plan.even([count_tasks[1]], plan.slot(groups, 0), plan.slot(groups, 0))
            plan.even([stage_end], plan.slot(groups, 1), plan.slot(groups, 1))
        if phase == 2:
            plan.even([deal_tasks[0]], last, last)
    closing = len(plan.slots) - 1
    plan.even(gather_tasks[begun:], first, closing)
    plan.even([deal_tasks[1]], closing, closing)

    kinds = [(left_buf, right_buf), (inner_buf, outer_buf)]
    sources = [(key_value, query_output), (inner, outer)]

    def own_loads(phase):
        layer, kind = phase // 2, phase % 2
        return [
            pltpu.make_async_copy(src.at[layer], buf.at[0], load_sems.at[kind, side, 0])
            for side, (src, buf) in enumerate(zip(sources[kind], kinds[kind]))
        ]

    def own_backs(phase):
        kind = phase % 2
        return [
            pltpu.make_async_copy(buf.at[0], weights[2 * phase + side].at[0], back_sems.at[kind, side])
            for side, buf in enumerate(kinds[kind])
        ]

    def loads(phase, group, into):
        kind = phase % 2
        return [
            pltpu.make_async_copy(weights[2 * phase + side].at[group], buf.at[into], load_sems.at[kind, side, into])
            for side, buf in enumerate(kinds[kind])
        ]

    @pl.when(s == 0)
    def _():
        small[0] = small_own[...]
        start(own_loads(0))

    def before(phase):
        @pl.when(r == 0)
        def _():
            if phase + 1 < phases:
                start(own_loads(phase + 1))
            for copy in own_loads(phase):
                copy.wait()
            start(own_backs(phase))

        @pl.when(r > 0)
        def _():
            for copy in loads(phase, r, slot):
                copy.wait()

        @pl.when((r > 0) & (r < groups - 1))
        def _():
            start(loads(phase, r + 1, 1 - slot))

    def behind(phase):
        @pl.when(r == 0)
        def _():
            for copy in own_backs(phase):
                copy.wait()
            start(loads(phase, 1, 1))

    def flat(buf):
        value = buf[slot]
        return value.reshape(model, value.shape[-1])

    own_place = xwin.at[window.at(window.own, rows)]
    to_pair = remote(low, own_place, pair_sems, window.to_pair)
    to_mid = remote(
        low.at[window.at(window.mid_row, mid_rows)],
        xwin.at[window.at((1 - lax.rem(window.h, 2)) * 2 * rows, mid_rows)],
        mid_sems,
        window.to_mid,
    )
    keep_win = pltpu.make_async_copy(xwin, win_out, local.at[0])

    for phase in range(phases):
        layer, kind = phase // 2, phase % 2
        kv_out, q_out, ctx_out, lse_out, gated_out, before_one, middle_low, unit_out, before_two, low_out = saved[layer]
        span = range(phase * groups, (phase + 1) * groups)

        def point(spot, span=span):
            plan.point(s, spot, span)

        @pl.when(lax.div(s, groups) == phase)
        def _():
            if kind == 0:
                if layer:

                    @pl.when(r == 0)
                    def _():
                        to_pair.wait()

                        @pl.when(window.middle)
                        def _():
                            to_mid.wait()

                        keep_win.start()

                before(phase)
                xin, offset = (xwin, 0) if layer else (hidden, window.base)
                row = small[r, 4 * layer + 2 : 4 * layer + 3, :]
                outs = (kv_out, q_out, ctx_out, lse_out, gated_out)
                attend(window, layer, xin, offset, row, lengths, flat(left_buf), flat(right_buf), outs, total, r, point)

                @pl.when(r == groups - 1)
                def _():
                    if layer:
                        resid = current[...]
                    else:
                        resid = hidden[window.at(offset + window.own, rows), :].astype(F32)
                    value = resid + total[...] + vector(vec, layer, BIAS_ONE)
                    normed = norm_forward(value, vector(vec, layer, GAIN_ONE), vector(vec, layer, SHIFT_ONE))
                    before_one[...] = value
                    middle[...] = normed
                    middle_low[...] = normed.astype(LOW)

                point(spots_attn - 1)
                behind(phase)
            else:
                before(phase)
                point(0)
                unit = nn(middle_low[...], flat(inner_buf)) + small[r, 4 * layer + 1 : 4 * layer + 2, :]
                unit_out[0] = unit.astype(LOW)
                point(1)
                bent = jnp.tanh(GELU_C * unit * (1.0 + GELU_K * (unit * unit)))
                active = (0.5 * unit * (1.0 + bent) * small[r, 4 * layer : 4 * layer + 1, :]).astype(LOW)
                point(2)
                add_up(r, total, nn(active, flat(outer_buf)))

                @pl.when(r == groups - 1)
                def _():
                    value = middle[...] + total[...] + vector(vec, layer, BIAS_TWO)
                    normed = norm_forward(value, vector(vec, layer, GAIN_TWO), vector(vec, layer, SHIFT_TWO))
                    before_two[...] = value
                    low_out[...] = normed.astype(LOW)
                    if layer + 1 < layers:
                        current[...] = normed
                        low[...] = normed.astype(LOW)
                        to_pair.start()

                        @pl.when(window.middle)
                        def _():
                            to_mid.start()

                        xwin[window.at(window.own, rows), :] = normed.astype(LOW)

                        @pl.when(jnp.logical_not(window.middle))
                        def _():
                            empty = window.at(lax.rem(window.h + 1, 2) * 2 * rows, mid_rows)
                            xwin[empty, :] = jnp.zeros((mid_rows, model), LOW)

                point(spots_feed - 1)
                behind(phase)

    @pl.when(s == phases * groups - 1)
    def _():
        keep_win.wait()
        keep_small.wait()
        out_of_stage.wait()


def match_teacher(layers, tokens, point, *refs):
    refs = list(refs)
    states = [refs.pop(0) for _ in range(layers)]
    target, chosen, row_ok, counts, weight = refs[:5]
    back_out, loss_out, grad_out = refs[5:]
    r = pl.program_id(0)
    rows = states[0].shape[0]

    @pl.when(r == 0)
    def _():
        loss_out[...] = jnp.zeros_like(loss_out)
        back_out[...] = jnp.zeros_like(back_out)

    count = jnp.sum(counts[...][:, 0:1, 0:1], 0)
    factor = tokens / count
    mine = pl.ds(pl.multiple_of(lax.axis_index("head") * rows, rows), rows)
    total = None
    for layer in range(layers):
        goal = jnp.where(r == 0, chosen[layer, mine, :], target[0, layer]).astype(F32)
        miss = (nn(states[layer][...], weight[0]) - goal) * row_ok[:, :1]
        loss_out[:1, :1] += jnp.sum(jnp.sum(miss * miss, 0, keepdims=True), 1, keepdims=True)
        low = (factor * miss).astype(LOW)
        back_out[layer] += nt(low, weight[0])
        grad = tn(states[layer][...], low)
        total = grad if total is None else total + grad
    grad_out[0] = total.astype(LOW)


def feed_backward(layer, last, point, *refs):
    refs = list(refs)
    before_two, before_one, middle_low, unit_in, small, vec, left, right = refs[:8]
    refs = refs[8:]
    grad_refs = [refs.pop(0) for _ in range(2 if last else 1)]
    inner_out, outer_out, attn_out, grad_out, vec_out, unit_vec, total, feed = refs
    r, groups = pl.program_id(0), pl.num_programs(0)
    base = 6 * layer
    point(0)

    @pl.when(r == 0)
    def _():
        if last:
            cotangent, spread = grad_refs
            rows = total.shape[0]
            mine = pl.ds(pl.multiple_of(lax.axis_index("head") * rows, rows), rows)
            grad = cotangent[mine, :].astype(F32) + spread[0]
        else:
            grad = grad_refs[0][...]
        grad_before, grad_gain, grad_shift, grad_bias = norm_backward(
            before_two[...], vec[base + GAIN_TWO : base + GAIN_TWO + 1, :], grad
        )
        vec_out[BIAS_TWO : BIAS_TWO + 1, :] = grad_bias
        vec_out[GAIN_TWO : GAIN_TWO + 1, :] = grad_gain
        vec_out[SHIFT_TWO : SHIFT_TWO + 1, :] = grad_shift
        feed[...] = grad_before.astype(LOW)
        total[...] = grad_before

    grad_active = nt(feed[...], right[0])
    point(1)
    value, slope = gelu_parts(unit_in[0].astype(F32))
    opened = small[0, 4 * layer : 4 * layer + 1, :]
    grad_unit = (grad_active * (slope * opened)).astype(LOW)
    unit_vec[0, 0:1, :] = jnp.sum(grad_unit.astype(F32), 0, keepdims=True)
    unit_vec[0, 1:2, :] = jnp.sum(grad_active * value, 0, keepdims=True)
    active = (value * opened).astype(LOW)
    point(2)
    total[...] += nt(grad_unit, left[0])
    point(3)
    inner_out[0] = tn(middle_low[...], grad_unit).astype(LOW)
    point(4)
    outer_out[0] = tn(feed[...], active).astype(LOW)
    point(5)

    @pl.when(r == groups - 1)
    def _():
        grad_before, grad_gain, grad_shift, grad_bias = norm_backward(
            before_one[...], vec[base + GAIN_ONE : base + GAIN_ONE + 1, :], total[...]
        )
        vec_out[BIAS_ONE : BIAS_ONE + 1, :] = grad_bias
        vec_out[GAIN_ONE : GAIN_ONE + 1, :] = grad_gain
        vec_out[SHIFT_ONE : SHIFT_ONE + 1, :] = grad_shift
        grad_out[...] = grad_before
        attn_out[...] = grad_before.astype(LOW)

    point(6)


def attention_backward(size, layer, first, point, *refs):
    seqs, seq_len, heads, head_size = size
    refs = list(refs)
    attn, grad_before, xwin, query_in, kv, ctx, lse, gated, small, lengths, left, right = refs[:12]
    refs = refs[12:]
    extra = None if first else refs.pop(0)
    left_out, right_out, grad_out, head_vec = refs[:4]
    (grad_kv, grad_q, kv_all, q_all, spread, mine, pair_low, pair_got, mid_low, mid_got, pair_sems, mid_sems) = refs[4:]
    step, groups = pl.program_id(0), pl.num_programs(0) // 2
    width = heads * head_size
    rows = mine.shape[0]
    group_count = mine.shape[1] // width
    window = Window(size, rows, group_count)
    block, mid_rows = window.block, window.mid_rows
    blocks = rows // block
    offset = window.base if first else 0
    here = window.at(offset + window.own, rows)
    row = small[0, 4 * layer + 2 : 4 * layer + 3, :]
    to_pair = remote(pair_low, pair_got, pair_sems, window.to_pair)
    to_mid = remote(mid_low, mid_got, mid_sems, window.to_mid)
    ahead, behind = range(group_count), range(group_count, 2 * group_count)

    @pl.when(step < groups)
    def _():
        point(0, ahead)
        opened = row[:, width : 2 * width]
        grad_gated = nn(attn[...], right[0, :, width:])
        shared = grad_gated * ctx[0]
        grad_ctx = (grad_gated * opened).astype(LOW)
        pulled = shared * opened
        scaled = query_in[0] * jnp.asarray(0.125, LOW)
        grad_kv[...] = jnp.zeros_like(grad_kv)
        for piece in range(blocks):
            part = slice(piece * block, (piece + 1) * block)
            keys = window.keys(piece)
            usable = lax.broadcasted_iota(jnp.int32, (block, seq_len), 1) < lengths[window.loc(piece)]
            for head in range(heads):
                lanes = slice(head * head_size, (head + 1) * head_size)
                later = slice(width + head * head_size, width + (head + 1) * head_size)
                key = kv[0, keys, lanes]
                scores = nt(scaled[part, lanes], key)
                chances = jnp.where(usable, jnp.exp(scores - lse[0, part, head : head + 1]), 0.0)
                grad_chances = nt(grad_ctx[part, lanes], kv[0, keys, later])
                delta = jnp.sum(pulled[part, lanes], -1, keepdims=True)
                grad_scores = (chances * (grad_chances - delta)).astype(LOW)
                grad_q[part, lanes] = nn(grad_scores, key) * 0.125
                grad_kv[keys, lanes] += tn(grad_scores, scaled[part, lanes])
                grad_kv[keys, later] += tn(chances.astype(LOW), grad_ctx[part, lanes])
                point(1 + piece * heads + head, ahead)
        query_low = grad_q[...].astype(LOW)
        kv_low = grad_kv[...].astype(LOW)
        q_all[step] = query_low
        kv_all[step] = kv_low
        head_vec[0, 0:1, :width] = jnp.sum(query_low.astype(F32), 0, keepdims=True)
        head_vec[0, 0:1, 2 * width :] = jnp.sum(kv_low.astype(F32), 0, keepdims=True)
        shared_sum = jnp.sum(shared, 0, keepdims=True)
        lane = lax.broadcasted_iota(jnp.int32, (1, 128), 1)
        by_head = jnp.zeros((1, 128), F32)
        for head in range(heads):
            one = jnp.sum(shared_sum[:, head * head_size : (head + 1) * head_size], 1, keepdims=True)
            by_head = jnp.where(lane == head, one, by_head)
        head_vec[0, 1:2, :128] = by_head

        @pl.when(step == 0)
        def _():
            spread[...] = jnp.zeros_like(spread)
            mine[...] = grad_before[...] if first else grad_before[...] + extra[0]

        spread[...] += nt(kv_low, left[0])
        mine[...] += nt(query_low, right[0, :, :width])
        point(1 + blocks * heads, ahead)

        @pl.when(step == groups - 1)
        def _():
            pair_low[...] = spread[window.at(window.pair, rows), :].astype(LOW)
            to_pair.start()

            @pl.when(window.middle)
            def _():
                mid_low[...] = spread[window.at(window.mid, mid_rows), :].astype(LOW)
                to_mid.start()

    @pl.when(step >= groups)
    def _():
        for spot in range(1 + blocks * heads):
            if spot % 3 == 0:
                point(spot, behind)
        r = step - groups
        left_out[0] = tn(xwin[window.at(offset, 2 * seq_len), :], kv_all[r]).astype(LOW)
        for spot in range(1 + blocks * heads):
            if spot % 3 == 1:
                point(spot, behind)
        right_out[0, :, :width] = tn(xwin[here, :], q_all[r]).astype(LOW)
        for spot in range(1 + blocks * heads):
            if spot % 3 == 2:
                point(spot, behind)
        right_out[0, :, width:] = tn(attn[...], gated[0]).astype(LOW)

        @pl.when(step == 2 * groups - 1)
        def _():
            to_pair.wait()
            mine[...] += spread[window.at(window.own, rows), :] + pair_got[...].astype(F32)

            @pl.when(window.middle)
            def _():
                to_mid.wait()
                mine[window.at(window.mid_row, mid_rows), :] += mid_got[...].astype(F32)

            grad_out[...] = mine[...].astype(grad_out.dtype)

        point(1 + blocks * heads, behind)


def on_device(
    ndp,
    groups,
    hidden_in,
    seq_lengths,
    layer_map,
    teacher_states,
    out_cotangent,
    query_weight,
    key_weight,
    value_weight,
    query_value_bias,
    output_weight,
    branch_bias,
    norm_gain,
    norm_shift,
    inner_weight,
    inner_bias,
    outer_weight,
    head_alpha,
    head_noise,
    unit_alpha,
    unit_noise,
    map_weight,
):
    tokens_dev, model = hidden_in.shape
    seqs_dev = seq_lengths.shape[0]
    seq_len = tokens_dev // seqs_dev
    width = query_weight.shape[2]
    units = inner_weight.shape[2]
    layers, heads = head_alpha.shape
    head_size = width // heads
    rows = tokens_dev // groups
    feats = model // ndp
    geo = Geometry(ndp, groups)
    size = (seqs_dev, seq_len, heads, head_size)
    window = Window(size, rows, groups)
    blocks = rows // window.block
    dp = lax.axis_index("dp")

    def slices(array):
        return array.reshape(array.shape[0], geo.size_y, geo.size_x, 2, feats, array.shape[-1])

    def matrices(arrays):
        return [(array.reshape(groups, model, array.shape[-1]), "group") for array in arrays]

    def pairs(cols, steps, m=0):
        out, begin = [], 0
        for step in steps:
            out.append([(m, begin, step, False), (m + 1, begin, step, True)])
            begin += step
        return out if begin == cols else [[(m, 0, cols, False), (m + 1, 0, cols, True)]]

    key_value = slices(jnp.concatenate([key_weight, value_weight], 2))
    query_output = slices(jnp.concatenate([query_weight, jnp.swapaxes(output_weight, 1, 2)], 2))
    inner, outer = slices(inner_weight), slices(outer_weight)

    open_unit, unit_back = jax.vjp(partial(gate_open, unit_noise), unit_alpha)
    open_head, head_back = jax.vjp(partial(gate_open, head_noise), head_alpha)
    (unit_slope,) = unit_back(jnp.ones_like(open_unit))
    (head_slope,) = head_back(jnp.ones_like(open_head))
    mixed = jnp.concatenate(
        [
            query_value_bias[:, 0],
            jnp.repeat(open_head, head_size, axis=1),
            jnp.zeros((layers, width), F32),
            query_value_bias[:, 1],
        ],
        1,
    )
    small = jnp.stack([open_unit, inner_bias, mixed, mixed], 1).reshape(4 * layers, units)
    vec = jnp.concatenate([branch_bias, norm_gain, norm_shift], 1).reshape(6 * layers, model)
    lengths = lax.dynamic_slice(seq_lengths, (window.first,), (2,))
    spot = jnp.arange(tokens_dev)
    row_ok = (spot % seq_len < jnp.repeat(seq_lengths, seq_len, total_repeat_length=tokens_dev)).astype(F32)
    row_ok = lax.dynamic_slice(row_ok, (window.h * rows,), (rows,))
    row_ok = jnp.broadcast_to(row_ok[:, None], (rows, 128))
    count = jnp.broadcast_to(jnp.sum(seq_lengths).astype(F32), (8, 128))
    chosen = jnp.take(teacher_states, layer_map, axis=0)

    row_block = pltpu.VMEM((rows, model), F32)
    low_block = pltpu.VMEM((rows, model), LOW)
    mid_block = pltpu.VMEM((window.mid_rows, model), LOW)
    two = pltpu.SemaphoreType.DMA((2,))
    owns, chunks = [], []
    for layer in range(layers):
        for arrays, cuts in (((key_value, query_output), ATTN_CUTS), ((inner, outer), FEED_CUTS)):
            chunks += pairs(arrays[0].shape[-1], cuts, len(owns))
            owns += [(array, layer) for array in arrays]
    chunks.append([(len(owns), 0, width, False)])
    map_slices = slices(map_weight[None])
    owns.append((map_slices, 0))
    gather = Gather(geo, owns, chunks)
    outputs = []
    for layer in range(layers):
        attn_step = lambda s, layer=layer: jnp.clip(s - 2 * layer * groups, 0, groups - 1)
        feed_step = lambda s, layer=layer: jnp.clip(s - (2 * layer + 1) * groups, 0, groups - 1)
        outputs += [
            ((groups, 2 * seq_len, 2 * width), LOW, attn_step),
            ((groups, rows, width), LOW, attn_step),
            ((groups, rows, width), F32, attn_step),
            ((groups, rows, 128), F32, attn_step),
            ((groups, rows, width), LOW, attn_step),
            ((rows, model), F32, "full"),
            ((rows, model), LOW, "full"),
            ((groups, rows, units), LOW, feed_step),
            ((rows, model), F32, "full"),
            ((rows, model), LOW, "full"),
        ]
    saves = len(outputs) // layers
    outputs += [((2 * seq_len, model), LOW, "any"), ((groups,) + small.shape, F32, "any")]
    attn_buf = pltpu.VMEM((2,) + key_value.shape[1:], LOW)
    feed_buf = pltpu.VMEM((2,) + inner.shape[1:], LOW)
    others = pltpu.SemaphoreType.DMA((groups - 1,))
    got = run(
        partial(forward, size, layers, geo, gather),
        2 * layers * groups,
        [
            (hidden_in, "full"),
            (small, "full"),
            (vec, "full"),
            (lengths, "smem"),
            (key_value, "any"),
            (query_output, "any"),
            (inner, "any"),
            (outer, "any"),
            (map_slices, "any"),
        ],
        outputs,
        [
            attn_buf,
            attn_buf,
            feed_buf,
            feed_buf,
            pltpu.SemaphoreType.DMA((2, 2, 2)),
            pltpu.SemaphoreType.DMA((2, 2)),
            row_block,
            row_block,
            row_block,
            low_block,
            pltpu.VMEM((2 * seq_len, model), LOW),
            pltpu.VMEM((groups,) + small.shape, F32),
            others,
            others,
            pltpu.VMEM(map_slices.shape[1:], LOW),
            two,
            two,
            pltpu.SemaphoreType.DMA((5,)),
        ],
        30e9,
        "forward",
        [gather, Spread(geo, count, plane=True), Deal(geo, chosen), Lend(geo, gather)],
        1,
        1,
        True,
    )
    records = [got[layer * saves : (layer + 1) * saves] for layer in range(layers)]
    xwins, small = [hidden_in, got[layers * saves]], got[layers * saves + 1]
    *weights, counts, target = got[layers * saves + 2 :]
    weights = matrices(weights)
    lows = [record[-1] for record in records]
    spread, loss, grad_map = run(
        partial(match_teacher, layers, float(tokens_dev * ndp)),
        groups,
        [(low, "full") for low in lows]
        + [(target, lambda r: jnp.maximum(r - 1, 0)), (chosen, "full"), (row_ok, "full"), (counts, "full")]
        + weights[-1:],
        [
            ((layers, rows, model), F32, "full"),
            ((8, 128), F32, "full"),
            ((groups, model, width), LOW, "group"),
        ],
        [],
        4e9,
        "match_teacher",
    )

    def parts(grad):
        return slices(grad)

    grads = [(out_cotangent, "full"), (spread[layers - 1 :], "full")]
    results = [{} for _ in range(layers)]
    riders, waiting = [], []
    shares = [lows[-1][: rows // 2], lows[-1][rows // 2 :]]
    number = 2

    def settle(got):
        for (layer, name), value in zip(waiting, got):
            results[layer][name] = value

    early, late = (lambda s: jnp.minimum(s, groups - 1)), (lambda s: jnp.maximum(s - groups, 0))
    for layer in reversed(range(layers)):
        kv, query, ctx, lse, gated, before_one, middle_low, unit_in, before_two, _ = records[layer]
        xwin = xwins[layer]
        attn_weights, feed_weights = weights[4 * layer : 4 * layer + 2], weights[4 * layer + 2 : 4 * layer + 4]
        inner_grad, outer_grad, attn, grad_before, vec_out, unit_vec, *got = run(
            partial(feed_backward, layer, layer == layers - 1),
            groups,
            [
                (before_two, "full"),
                (before_one, "full"),
                (middle_low, "full"),
                (unit_in, "group"),
                (small, "group"),
                (vec, "full"),
            ]
            + feed_weights
            + grads,
            [((groups, model, units), LOW, "group")] * 2
            + [
                ((rows, model), LOW, "full"),
                ((rows, model), F32, "full"),
                ((8, model), F32, "full"),
                ((groups, 8, units), F32, "group"),
            ],
            [row_block, low_block],
            10e9,
            "feed_backward",
            riders,
            7,
            number,
        )
        number += 1
        settle(got)
        riders = [Scatter(geo, [parts(inner_grad), parts(outer_grad)], pairs(units, BACK_CUTS))]
        waiting = [(layer, "inner"), (layer, "outer")]
        if layer in (0, layers - 1):
            half = 0 if layer else 1
            riders.append(Spread(geo, shares[half]))
            waiting.append((half, "block_out"))
        if layer == layers - 1:
            riders.append(Scatter(geo, [parts(grad_map)], [[(0, 0, width, False)]]))
            waiting.append((0, "map"))
        left, right, grad, head_vec, *got = run(
            partial(attention_backward, size, layer, layer == 0),
            2 * groups,
            [
                (attn, "full"),
                (grad_before, "full"),
                (xwin, "full"),
                (query, early),
                (kv, early),
                (ctx, early),
                (lse, early),
                (gated, late),
                (small, early),
                (lengths, "smem"),
            ]
            + [(array, early) for array, _ in attn_weights]
            + ([(spread[layer - 1 : layer], "full")] if layer else []),
            [((groups, model, 2 * width), LOW, late)] * 2
            + [
                ((rows, model), F32 if layer else LOW, "full"),
                ((groups, 8, units), F32, early),
            ],
            [
                pltpu.VMEM((2 * seq_len, 2 * width), F32),
                pltpu.VMEM((rows, width), F32),
                pltpu.VMEM((groups, 2 * seq_len, 2 * width), LOW),
                pltpu.VMEM((groups, rows, width), LOW),
                pltpu.VMEM((2 * seq_len, model), F32),
                row_block,
                low_block,
                low_block,
                mid_block,
                mid_block,
                two,
                two,
            ],
            12e9,
            "attention_backward",
            riders,
            2 + blocks * heads,
            number,
        )
        number += 1
        settle(got)
        riders = [Scatter(geo, [parts(left), parts(right)], pairs(2 * width, LAST_CUTS if layer == 0 else ATTN_CUTS))]
        waiting = [(layer, "kv"), (layer, "qo")]
        grads = [(grad, "full")]
        results[layer].update(vec=vec_out, unit=unit_vec, head=head_vec)

    everywhere = (0, feats, feats)
    unit_count, qv_cols = units // ndp, width // ndp
    items = [(results[layer]["vec"], False, (0, 6), everywhere) for layer in range(layers)]
    items += [(results[layer]["unit"], True, (0, 2), (0, unit_count, unit_count)) for layer in range(layers)]
    for layer in range(layers):
        items += [(results[layer]["head"], True, (0, 1), (0, qv_cols, qv_cols))]
        items += [(results[layer]["head"], True, (0, 1), (3 * width, qv_cols, qv_cols))]
    items += [(results[layer]["head"], True, (1, 2), (0, 0, 128)) for layer in range(layers)]
    items += [(loss, False, (0, 1), (0, 0, 128))]
    riders += [Fold(geo, items), Spread(geo, grad)]
    waiting += [(0, "sums"), (0, "grad_hidden")]
    settle(run(only_move, 1, [], [], [], 0, "scatter_last", riders, 1, number))
    sums = results[0]["sums"]
    by_feature = sums[: 6 * layers, :feats].reshape(layers, 3, 2, feats)
    by_unit = sums[6 * layers : 8 * layers, :unit_count].reshape(layers, 2, unit_count)
    by_column = sums[8 * layers : 10 * layers, :qv_cols].reshape(layers, 2, qv_cols)
    by_head = sums[10 * layers : 11 * layers, :heads]
    distill_loss = sums[11 * layers, 0] / (jnp.sum(counts[:, 0, 0]) * model * layers)
    own_slope = lax.dynamic_slice(unit_slope, (0, dp * unit_count), (layers, unit_count))

    def stacked(member, cols, turned=False):
        arrays = [results[layer][member][:, cols] for layer in range(layers)]
        return jnp.stack([array.T if turned else array for array in arrays])

    front, rear, whole = slice(0, width), slice(width, 2 * width), slice(None)
    return (
        jnp.concatenate([results[0]["block_out"], results[1]["block_out"]], 1).reshape(tokens_dev, model),
        results[0]["grad_hidden"].reshape(tokens_dev, model).astype(F32),
        distill_loss,
        stacked("qo", front),
        stacked("kv", front),
        stacked("kv", rear),
        by_column,
        stacked("qo", rear, True),
        by_feature[:, 0],
        by_feature[:, 1],
        by_feature[:, 2],
        stacked("inner", whole),
        by_unit[:, 0],
        stacked("outer", whole, True),
        by_head * head_slope,
        by_unit[:, 1] * own_slope,
        results[0]["map"],
    )


def solution(mesh):
    in_specs = (
        P("dp", None),
        P("dp"),
        P(),
        P(None, "dp", "head"),
        P("dp", None),
        P(None, None, "head"),
        P(None, None, "head"),
        P(None, None, "head"),
        P(None, None, "head"),
        P(None, "head", None),
        P(),
        P(),
        P(),
        P(None, None, "head"),
        P(None, "head"),
        P(None, "head", None),
        P(None, "head"),
        P(None, "head"),
        P(None, "head"),
        P(None, "head"),
        P(None, "head"),
    )
    out_specs = (
        P("dp", None),
        P("dp", None),
        P(),
        P(None, "dp", "head"),
        P(None, "dp", "head"),
        P(None, "dp", "head"),
        P(None, None, ("head", "dp")),
        P(None, "head", "dp"),
        P(None, None, "dp"),
        P(None, None, "dp"),
        P(None, None, "dp"),
        P(None, "dp", "head"),
        P(None, ("head", "dp")),
        P(None, "head", "dp"),
        P(None, "head"),
        P(None, ("head", "dp")),
        P("dp", "head"),
    )
    return jax.shard_map(
        partial(on_device, mesh.shape["dp"], mesh.shape["head"]),
        mesh=mesh,
        in_specs=in_specs,
        out_specs=out_specs,
        check_vma=False,
    )
```

```python
from functools import partial

import jax
import jax.numpy as jnp
from jax import lax
from jax.experimental import pallas as pl
from jax.experimental.pallas import tpu as pltpu
from jax.sharding import PartitionSpec as P

BETA = 2.0 / 3.0
EPS = 1e-05
LOW = jnp.bfloat16
F32 = jnp.float32
GELU_C = 0.7978845608028654
GELU_K = 0.044715
VMEM_LIMIT = 56 * 1024 * 1024
LARGE_LIMIT = 62 * 1024 * 1024
ATTN_CUTS = (128, 256)
FEED_CUTS = (128, 128, 256, 256)
BACK_CUTS = (384, 384)
LAST_CUTS = (128, 128, 128)
ORDER = (1, 3, 2, 0)
TIMES_LAST = (9.5, 5.1, 6.5, 5.5)
TIMES = (12.0, 6.5, 8.0, 7.0)
MESH = pl.DeviceIdType.MESH


def gate_open(noise, alpha):
    return jnp.clip(jax.nn.sigmoid((noise + alpha) / BETA) * 1.2 - 0.1, 0.0, 1.0)


def product(left, right, dims):
    return lax.dot_general(left, right, ((dims[:1], dims[1:]), ((), ())), preferred_element_type=F32)


def nn(left, right):
    return product(left, right, (1, 0))


def nt(left, right):
    return product(left, right, (1, 1))


def tn(left, right):
    return product(left, right, (0, 0))


def factor_pair(count):
    side = 1
    for trial in range(1, count + 1):
        if count % trial == 0 and trial * trial <= count:
            side = trial
    return side, count // side


def block_of(shape, place):
    if place == "once":
        return pl.BlockSpec(shape, lambda r: (0,) * len(shape), pipeline_mode=pl.Buffered(1))
    if place == "full":
        return pl.BlockSpec(shape, lambda r: (0,) * len(shape))
    return pl.BlockSpec((1,) + tuple(shape[1:]), lambda r: (place(r),) + (0,) * (len(shape) - 1))


def spec_of(array, kind):
    if kind == "any":
        return pl.BlockSpec(memory_space=pl.ANY)
    if kind == "smem":
        return pl.BlockSpec(memory_space=pltpu.SMEM)
    if kind == "group":
        return block_of(array.shape, lambda r: r)
    return block_of(array.shape, kind)


class Plan:
    def __init__(self, spots):
        self.spots = spots
        self.slots = [(step, spot) for step, count in enumerate(spots) for spot in range(count)]
        self.chosen = {slot: [] for slot in self.slots}

    def slot(self, step, spot):
        return self.slots.index((step, spot % self.spots[step]))

    def spread(self, tasks, first, last):
        for share, _, task in sorted(tasks, key=lambda item: item[:2]):
            self.chosen[self.slots[first + round(share * (last - first))]].append(task)

    def even(self, tasks, first, last):
        count = len(tasks)
        self.spread([((index + 1) / count, index, task) for index, task in enumerate(tasks)], first, last)

    def timed(self, lengths, tasks):
        times, now = [], 0.0
        for length, count in zip(lengths, self.spots):
            times += [now + length * spot / count for spot in range(count)]
            now += length
        for time, task in sorted(tasks, key=lambda item: item[0]):
            later = [number for number, at in enumerate(times) if at >= time]
            self.chosen[self.slots[later[0] if later else len(times) - 1]].append(task)

    def point(self, r, spot, span):
        for step in span:
            tasks = self.chosen.get((step, spot), ())
            if tasks:

                @pl.when(r == step)
                def _(tasks=tasks):
                    for task in tasks:
                        task()


def run(body, steps, inputs, outputs, scratch, flops, name, riders=(), points=1, number=None, placed=False, limit=VMEM_LIMIT):
    inputs, outputs, scratch = list(inputs), list(outputs), list(scratch)
    at = [len(inputs), len(outputs), len(scratch)]
    starts, sizes = [], []
    for rider in riders:
        starts.append((len(inputs), len(outputs), len(scratch)))
        inputs += rider.inputs
        outputs += rider.outputs
        scratch += rider.scratch
        sizes.append((len(rider.inputs), len(rider.outputs), len(rider.scratch)))
    out_shape = [jax.ShapeDtypeStruct(shape, dtype) for shape, dtype, _ in outputs]
    moved = sum(a.size * a.dtype.itemsize for a, kind in inputs if kind != "any")
    n_in, n_out = len(inputs), len(outputs)
    peers = []
    for rider in riders:
        peers += [peer for peer in rider.peers if peer not in peers]

    def whole(*refs):
        kinds = refs[:n_in], refs[n_in : n_in + n_out], refs[n_in + n_out :]
        own = [ref for part, n in zip(kinds, at) for ref in part[:n]]
        lists = [
            rider.tasks(*[part[i : i + n] for part, i, n in zip(kinds, start, size)])
            for rider, start, size in zip(riders, starts, sizes)
        ]
        r = pl.program_id(0)
        if riders:

            @pl.when(r == 0)
            def _():
                riders[0].geo.greet(peers)

        if placed:
            body(lists, *own)
            return
        plan = Plan([points] * steps)
        listed = []
        for number, tasks in enumerate(lists):
            for index, task in enumerate(tasks):
                listed.append((index / max(1, len(tasks) - 1), (number, index), task))
        plan.spread(listed, 0, len(plan.slots) - 1)
        body(lambda spot, span=range(steps): plan.point(r, spot, span), *own)

    params = {"vmem_limit_bytes": limit}
    if riders:
        params.update(collective_id=number, has_side_effects=True)
    return pl.pallas_call(
        whole,
        name=name,
        grid=(steps,),
        in_specs=[spec_of(a, kind) for a, kind in inputs],
        out_specs=[spec_of(o, kind) for o, (_, _, kind) in zip(out_shape, outputs)],
        scratch_shapes=scratch,
        out_shape=out_shape,
        compiler_params=pltpu.CompilerParams(**params),
        cost_estimate=pl.CostEstimate(flops=int(flops), bytes_accessed=int(moved), transcendentals=0),
    )(*[a for a, _ in inputs])


def only_move(point):
    point(0)


class Geometry:
    def __init__(self, ndp, groups):
        self.ndp, self.groups = ndp, groups
        self.size_y, self.size_x = factor_pair(ndp // 2)

    def here(self):
        dp, h = lax.axis_index("dp"), lax.axis_index("head")
        return lax.rem(dp, 2), lax.rem(lax.div(dp, 2), self.size_x), lax.div(dp, 2 * self.size_x), h

    def place(self, c=0, y=0, x=0, z=0):
        core, ix, iy, h = self.here()
        core = 1 - core if c else core
        iy = lax.rem(iy + (y + self.size_y), self.size_y) if y else iy
        ix = lax.rem(ix + (x + self.size_x), self.size_x) if x else ix
        h = lax.rem(h + (z + self.groups), self.groups) if z else h
        return iy, ix, core, h

    def device(self, **to):
        iy, ix, core, h = self.place(**to)
        return ((iy * self.size_x + ix) * 2 + core, h)

    def axes(self):
        out = [dict(c=1)]
        out += [dict(y=y) for y in range(1, self.size_y)]
        out += [dict(x=x) for x in range(1, self.size_x)]
        return out + self.column()

    def column(self):
        return [dict(z=z) for z in range(1, self.groups)]

    def plane(self):
        out = []
        for c in range(2):
            for y in range(self.size_y):
                for x in range(self.size_x):
                    to = {key: value for key, value in (("c", c), ("y", y), ("x", x)) if value}
                    if to:
                        out.append(to)
        return out

    def greet(self, peers):
        barrier = pltpu.get_barrier_semaphore()
        for peer in peers:
            pl.semaphore_signal(barrier, inc=1, device_id=self.device(**peer), device_id_type=MESH)
        pl.semaphore_wait(barrier, len(peers))


class Mover:
    def __init__(self, geo, send, recv):
        self.geo, self.send, self.recv, self.ids = geo, send, recv, {}

    def __call__(self, key, src, dst, **to):
        index = self.ids.setdefault(key, len(self.ids))
        return pltpu.make_async_remote_copy(
            src_ref=src,
            dst_ref=dst,
            send_sem=self.send.at[index],
            recv_sem=self.recv.at[index],
            device_id=self.geo.device(**to),
            device_id_type=MESH,
        )


def back(to):
    return {key: value if key == "c" else -value for key, value in to.items()}


def start(copies):
    for copy in copies:
        copy.start()


def arrive(copies):
    for copy in copies:
        copy.wait_recv()


def leave(copies):
    for copy in copies:
        copy.wait_send()


class Column:
    def __init__(self, geo, block, slot, send, recv, base, absolute=False):
        self.absolute = absolute
        self.geo, self.slot, self.send, self.recv, self.base = geo, slot, send, recv, base
        self.h = geo.here()[3]
        self.block = block

    def copy(self, r):
        return pltpu.make_async_remote_copy(
            src_ref=self.block,
            dst_ref=self.slot(0 if self.absolute else r),
            send_sem=self.send.at[self.base + r],
            recv_sem=self.recv.at[self.base + r],
            device_id=self.geo.device(z=-r),
            device_id_type=MESH,
        )

    def begin(self):
        self.copy(2).start()
        pl.when(self.h != 0)(lambda: self.copy(1).start())
        pl.when(self.h != 3)(lambda: self.copy(3).start())

    def by_middle(self, act):
        @pl.when((self.h > 0) & (self.h < 3))
        def _():
            there = 1 + 2 * lax.rem(self.h, 2)
            dp, _ = self.geo.device()
            act(
                pltpu.make_async_remote_copy(
                    src_ref=self.slot(2),
                    dst_ref=self.slot(2 if self.absolute else there),
                    send_sem=self.send.at[self.base],
                    recv_sem=self.recv.at[self.base + there],
                    device_id=(dp, self.h + 1 - 2 * lax.rem(self.h, 2)),
                    device_id_type=MESH,
                )
            )

    def relay(self):
        self.copy(2).wait_recv()
        self.by_middle(lambda copy: copy.start())

    def arrive(self):
        self.copy(1).wait_recv()
        self.copy(3).wait_recv()

    def leave(self):
        self.copy(2).wait_send()
        pl.when(self.h != 0)(lambda: self.copy(1).wait_send())
        pl.when(self.h != 3)(lambda: self.copy(3).wait_send())
        self.by_middle(lambda copy: copy.wait_send())


class Delivery:
    def __init__(self, geo, block, slot, merged, send, recv, base):
        self.h, self.block, self.slot, self.merged = geo.here()[3], block, slot, merged

        def copy(r, dst, index, z):
            return pltpu.make_async_remote_copy(
                src_ref=block(r),
                dst_ref=dst,
                send_sem=send.at[base + r],
                recv_sem=recv.at[base + index],
                device_id=geo.device(z=z),
                device_id_type=MESH,
            )

        self.copy = lambda r: copy(r, slot(r), r, r)
        self.last_to_middle = lambda: copy(1, merged, 0, -1)
        self.first_to_middle = lambda: copy(3, merged, 0, 1)

    def begin(self, r):
        if r == 1:
            pl.when(self.h != 3)(lambda: self.copy(1).start())
            pl.when(self.h == 3)(lambda: self.last_to_middle().start())

            @pl.when(self.h == 0)
            def _():
                self.slot(1)[...] = jnp.zeros_like(self.slot(1))

        if r == 3:
            pl.when(self.h != 0)(lambda: self.copy(3).start())
            pl.when(self.h == 0)(lambda: self.first_to_middle().start())

            @pl.when(self.h == 3)
            def _():
                self.slot(3)[...] = jnp.zeros_like(self.slot(3))

    def merge(self):
        @pl.when((self.h > 0) & (self.h < 3))
        def _():
            self.last_to_middle().wait_recv()
            mine = self.block(2)
            mine[...] = (mine[...].astype(F32) + self.merged[...].astype(F32)).astype(LOW)

        self.copy(2).start()

    def arrive(self):
        self.copy(2).wait_recv()
        pl.when(self.h != 0)(lambda: self.copy(1).wait_recv())
        pl.when(self.h != 3)(lambda: self.copy(3).wait_recv())

    def leave(self):
        for r in (1, 2, 3):
            self.copy(r).wait_send()


class Gather:
    def __init__(self, geo, owns, chunks):
        self.geo, self.chunks, self.peers = geo, chunks, geo.axes()
        self.layers = [layer for _, layer in owns]
        self.inputs = [(own, "any") for own, _ in owns]
        self.outputs = [((geo.groups,) + own.shape[1:], LOW, "any") for own, _ in owns]
        halves = sum(len(chunk) for chunk in chunks)
        sems = pltpu.SemaphoreType.DMA((halves * 2 * geo.size_x * geo.size_y,))
        ends = pltpu.SemaphoreType.DMA((halves * geo.groups,))
        self.scratch = [sems, sems, ends, ends]

    def tasks(self, owns, outs, scratch):
        self.outs = outs
        geo = self.geo
        move = Mover(geo, *scratch[:2])
        groups, sx, sy = geo.groups, geo.size_x, geo.size_y
        bases = {}
        for chunk, parts in enumerate(self.chunks):
            for half in range(len(parts)):
                bases[chunk, half] = groups * len(bases)
        others = pl.ds(1, groups - 1)
        owns = [own.at[layer] for own, layer in zip(owns, self.layers)]

        def columns(chunk, half):
            m, col, cols, _ = self.chunks[chunk][half]
            return m, pl.ds(col, cols)

        def along(chunk, half):
            m, cols = columns(chunk, half)
            iy, ix, core, _ = geo.place()
            return Column(
                geo,
                owns[m].at[iy, ix, core, :, cols],
                lambda r: outs[m].at[r, iy, ix, core, :, cols],
                *scratch[2:],
                bases[chunk, half],
            )

        def hop(chunk, half, block, to):
            m, cols = columns(chunk, half)
            iy, ix, core, _ = geo.place(**block)
            part = outs[m].at[others, iy, ix, core, :, cols]
            return move(("p", chunk, half, str(block), str(to)), part, part, **back(to))

        ways_x = [dict(x=x) for x in range(1, sx)]
        ways_y = [dict(y=y) for y in range(1, sy)]
        corners = [dict(x=x, y=y) for x in range(1, sx) for y in range(1, sy)]

        def halves(chunk):
            return range(len(self.chunks[chunk]))

        def alongs(chunk):
            return [along(chunk, half) for half in halves(chunk)]

        def firsts(chunk):
            return [hop(chunk, half, {}, to) for half in halves(chunk) for to in ways_x + ways_y]

        def seconds(chunk):
            out = []
            for half in halves(chunk):
                near, far = (ways_y, ways_x) if self.chunks[chunk][half][3] else (ways_x, ways_y)
                out += [hop(chunk, half, block, to) for block in near for to in far]
            return out

        def cores(chunk, blocks):
            return [hop(chunk, half, block, dict(c=1)) for half in halves(chunk) for block in blocks]

        count = len(self.chunks)

        def begin():
            for chunk in range(min(2, count)):
                for column in alongs(chunk):
                    column.begin()

        def level_zero(chunk):
            for column in alongs(chunk):
                column.relay()
            if chunk + 2 < count:
                for column in alongs(chunk + 2):
                    column.begin()

        def level_one(chunk):
            for column in alongs(chunk):
                column.arrive()
            start(firsts(chunk))
            start(cores(chunk, [{}]))

        def level_two(chunk):
            arrive(firsts(chunk))
            start(seconds(chunk))
            start(cores(chunk, ways_x + ways_y))

        def level_three(chunk):
            arrive(seconds(chunk))
            start(cores(chunk, corners))

        def level_four(chunk):
            arrive(cores(chunk, [{}] + ways_x + ways_y + corners))

        def end():
            for chunk in range(count):
                for column in alongs(chunk):
                    column.leave()
                leave(firsts(chunk) + seconds(chunk) + cores(chunk, [{}] + ways_x + ways_y + corners))

        out = [begin]
        self.done = []
        for time in range(count + 4):
            for level, late in ((level_zero, 0), (level_one, 1), (level_two, 2), (level_three, 3), (level_four, 4)):
                if 0 <= time - late < count:
                    out.append(partial(level, time - late))
            if time >= 4:
                self.done.append(len(out))
        return out + [end]


class Lend:
    def __init__(self, geo, rider):
        self.geo, self.rider, self.peers = geo, rider, []
        self.inputs, self.outputs, self.scratch = [], [], []

    def tasks(self, owns, outs, scratch):
        return [self.rider.outs]


class Timed:
    def __init__(self, rider, finish):
        self.geo, self.peers, self.inputs, self.outputs, self.scratch = (
            rider.geo,
            rider.peers,
            rider.inputs,
            rider.outputs,
            rider.scratch,
        )
        self.rider, self.finish = rider, finish

    def tasks(self, inputs, outs, scratch):
        return self.finish, self.rider.tasks(inputs, outs, scratch)


class Scatter:
    def __init__(self, geo, grads, chunks):
        self.geo, self.chunks, self.peers = geo, chunks, geo.axes()
        self.inputs = [(grad, "any") for grad in grads]
        self.outputs = [(grad.shape[4:], F32, "full") for grad in grads]
        feats = grads[0].shape[4]
        halves = [half for chunk in chunks for half in chunk]
        each = 1 + (geo.size_x - 1) + (geo.size_y - 1)
        sems = pltpu.SemaphoreType.DMA((len(halves) * each,))
        ends = pltpu.SemaphoreType.DMA((len(halves) * geo.groups,))
        self.scratch = [sems, sems, ends, ends, pltpu.SemaphoreType.DMA((len(halves),))]
        for _, _, cols, y_first in halves:
            near, far = (geo.size_y, geo.size_x) if y_first else (geo.size_x, geo.size_y)
            self.scratch += [
                pltpu.VMEM(shape, LOW)
                for shape in (
                    (geo.groups, geo.size_y, geo.size_x, feats, cols),
                    (geo.groups, geo.size_y, geo.size_x, feats, cols),
                    (near - 1, geo.groups, far, feats, cols),
                    (far - 1, geo.groups, feats, cols),
                    (geo.groups, feats, cols),
                )
            ]

    def tasks(self, grads, outs, scratch):
        geo, (send, recv, end_send, end_recv, local), buffers = self.geo, scratch[:5], scratch[5:]
        move = Mover(geo, send, recv)
        groups, sx, sy = geo.groups, geo.size_x, geo.size_y
        index = {}
        for chunk, halves in enumerate(self.chunks):
            for half in range(len(halves)):
                index[chunk, half] = len(index)

        def parts(chunk, half):
            m, col, cols, y_first = self.chunks[chunk][half]
            number = index[chunk, half]
            return grads[m], pl.ds(col, cols), y_first, buffers[5 * number : 5 * number + 5]

        def load(chunk, half):
            grad, cols, _, bufs = parts(chunk, half)
            _, _, core, _ = geo.place()
            return pltpu.make_async_copy(
                grad.at[:, :, :, core, :, cols], bufs[0], local.at[index[chunk, half]]
            )

        def cross(chunk, half):
            grad, cols, _, bufs = parts(chunk, half)
            _, _, core, _ = geo.place(c=1)
            return move(("c", chunk, half), grad.at[:, :, :, core, :, cols], bufs[1], c=1)

        def near(chunk, half):
            _, _, y_first, bufs = parts(chunk, half)
            out = []
            for step in range(1, sy if y_first else sx):
                to = dict(y=step) if y_first else dict(x=step)
                iy, ix, _, _ = geo.place(**to)
                part = bufs[0].at[:, iy] if y_first else bufs[0].at[:, :, ix]
                out.append(move(("n", chunk, half, step), part, bufs[2].at[step - 1], **to))
            return out

        def far(chunk, half):
            _, _, y_first, bufs = parts(chunk, half)
            out = []
            for step in range(1, sx if y_first else sy):
                to = dict(x=step) if y_first else dict(y=step)
                iy, ix, _, _ = geo.place(**to)
                out.append(move(("f", chunk, half, step), bufs[0].at[:, iy, ix], bufs[3].at[step - 1], **to))
            return out

        def along(chunk, half):
            _, _, _, bufs = parts(chunk, half)
            iy, ix, _, _ = geo.place()
            return Delivery(
                geo,
                lambda r: bufs[0].at[r, iy, ix],
                lambda r: bufs[4].at[r],
                bufs[4].at[0],
                end_send,
                end_recv,
                groups * index[chunk, half],
            )

        def each(chunk):
            return range(len(self.chunks[chunk]))

        def begin_one(chunk):
            for half in each(chunk):
                cross(chunk, half).start()
                load(chunk, half).start()

        count = len(self.chunks)

        def begin():
            for chunk in range(min(2, count)):
                begin_one(chunk)

        def level_one(chunk):
            for half in each(chunk):
                _, _, _, bufs = parts(chunk, half)
                load(chunk, half).wait()
                cross(chunk, half).wait_recv()
                for r in range(groups):
                    bufs[0][r] = (bufs[0][r].astype(F32) + bufs[1][r].astype(F32)).astype(LOW)
                start(near(chunk, half))
            if chunk + 2 < count:
                begin_one(chunk + 2)

        def level_two(chunk):
            iy, ix, _, _ = geo.place()
            for half in each(chunk):
                _, _, y_first, bufs = parts(chunk, half)
                arrive(near(chunk, half))
                for r in range(groups):
                    total = (bufs[0][r, iy] if y_first else bufs[0][r, :, ix]).astype(F32)
                    for other in range(bufs[2].shape[0]):
                        total = total + bufs[2][other, r].astype(F32)
                    if y_first:
                        bufs[0][r, iy] = total.astype(LOW)
                    else:
                        bufs[0][r, :, ix] = total.astype(LOW)
                start(far(chunk, half))

        def level_three(chunk):
            iy, ix, _, _ = geo.place()
            for half in each(chunk):
                _, _, _, bufs = parts(chunk, half)
                arrive(far(chunk, half))
                for r in range(groups):
                    total = bufs[0][r, iy, ix].astype(F32)
                    for other in range(bufs[3].shape[0]):
                        total = total + bufs[3][other, r].astype(F32)
                    bufs[0][r, iy, ix] = total.astype(LOW)
                for r in (1, 3):
                    along(chunk, half).begin(r)

        def level_merge(chunk):
            for half in each(chunk):
                along(chunk, half).merge()

        def level_four(chunk):
            iy, ix, _, _ = geo.place()
            for half in each(chunk):
                m, col, cols, _ = self.chunks[chunk][half]
                _, _, _, bufs = parts(chunk, half)
                along(chunk, half).arrive()
                total = bufs[0][0, iy, ix].astype(F32)
                for r in range(1, groups):
                    total = total + bufs[4][r].astype(F32)
                outs[m][:, col : col + cols] = total

        def end():
            for chunk in range(count):
                for half in each(chunk):
                    leave([cross(chunk, half)] + near(chunk, half) + far(chunk, half))
                    along(chunk, half).leave()

        out = [begin]
        levels = (level_one, level_two, level_three, level_merge, level_four)
        for time in range(count + 4):
            for late, level in enumerate(levels):
                if 0 <= time - late < count:
                    out.append(partial(level, time - late))
        return out + [end]


class Reduce:
    def __init__(self, geo, shapes, cuts):
        self.geo, self.peers = geo, geo.axes()
        self.count = len(shapes)
        self.inputs = []
        self.outputs = [(shape, F32, "full") for shape in shapes]
        self.cuts, begin = [], 0
        for cut in cuts:
            self.cuts.append((begin, cut))
            begin += cut
        if begin != shapes[0][1]:
            self.cuts = [(0, shapes[0][1])]
        self.chunks = [(r, cut) for r in ORDER for cut in range(len(self.cuts))]
        each = 1 + (geo.size_x - 1) + (geo.size_y - 1)
        sems = pltpu.SemaphoreType.DMA((self.count * len(self.chunks) * each,))
        ends = pltpu.SemaphoreType.DMA((self.count * len(self.cuts) * geo.groups,))
        self.scratch = [sems, sems, ends, ends, pltpu.SemaphoreType.REGULAR]
        for m, (feats, n) in enumerate(shapes):
            near, far = (geo.size_y, geo.size_x) if m % 2 else (geo.size_x, geo.size_y)
            self.scratch += [
                pltpu.VMEM(shape, LOW)
                for shape in (
                    (geo.groups, geo.size_y, geo.size_x, 2, feats, n),
                    (2, geo.size_y, geo.size_x, feats, n),
                    (near - 1, geo.groups, far, feats, n),
                    (far - 1, geo.groups, feats, n),
                    (geo.groups, feats, n),
                )
            ]

    def tasks(self, inputs, outs, scratch):
        geo, (send, recv, end_send, end_recv, free), buffers = self.geo, scratch[:5], scratch[5:]
        move = Mover(geo, send, recv)
        groups, sx, sy = geo.groups, geo.size_x, geo.size_y
        mats = range(self.count)
        self.grads = [buffers[5 * m] for m in mats]
        ring = self.ring = 2 * len(self.cuts)

        def parts(k, m):
            r, cut = self.chunks[k]
            begin, count = self.cuts[cut]
            return r, pl.ds(begin, count), buffers[5 * m : 5 * m + 5]

        def cross(k, m):
            r, cols, bufs = parts(k, m)
            _, _, core, _ = geo.place(c=1)
            return move(("c", k, m), bufs[0].at[r, :, :, core, :, cols], bufs[1].at[k // len(self.cuts) % 2, :, :, :, cols], c=1)

        def near(k, m):
            r, cols, bufs = parts(k, m)
            out = []
            for step in range(1, sy if m % 2 else sx):
                to = dict(y=step) if m % 2 else dict(x=step)
                iy, ix, core, _ = geo.place(**to)
                part = bufs[0].at[r, iy, :, core, :, cols] if m % 2 else bufs[0].at[r, :, ix, core, :, cols]
                out.append(move(("n", k, m, step), part, bufs[2].at[step - 1, r, :, :, cols], **to))
            return out

        def far(k, m):
            r, cols, bufs = parts(k, m)
            out = []
            for step in range(1, sx if m % 2 else sy):
                to = dict(x=step) if m % 2 else dict(y=step)
                iy, ix, core, _ = geo.place(**to)
                out.append(
                    move(
                        ("f", k, m, step),
                        bufs[0].at[r, iy, ix, core, :, cols],
                        bufs[3].at[step - 1, r, :, cols],
                        **to,
                    )
                )
            return out

        def along(cut, m):
            begin, count = self.cuts[cut]
            cols, bufs = pl.ds(begin, count), buffers[5 * m : 5 * m + 5]
            iy, ix, core, _ = geo.place()
            return Delivery(
                geo,
                lambda r: bufs[0].at[r, iy, ix, core, :, cols],
                lambda r: bufs[4].at[r, :, cols],
                bufs[4].at[0, :, cols],
                end_send,
                end_recv,
                groups * (self.count * cut + m),
            )

        def begin(k):
            if k >= ring:
                pl.semaphore_wait(free, 1)
            for m in mats:
                cross(k, m).start()

        def level_one(k):
            _, _, core, _ = geo.place()
            for m in mats:
                r, cols, bufs = parts(k, m)
                cross(k, m).wait_recv()
                total = bufs[0][r, :, :, core, :, cols].astype(F32) + bufs[1][k // len(self.cuts) % 2, :, :, :, cols].astype(F32)
                bufs[0][r, :, :, core, :, cols] = total.astype(LOW)
                start(near(k, m))
            if k + ring < len(self.chunks):
                pl.semaphore_signal(free, inc=1, device_id=geo.device(c=1), device_id_type=MESH)

        def level_two(k):
            iy, ix, core, _ = geo.place()
            for m in mats:
                r, cols, bufs = parts(k, m)
                arrive(near(k, m))
                part = bufs[0][r, iy, :, core, :, cols] if m % 2 else bufs[0][r, :, ix, core, :, cols]
                total = part.astype(F32)
                for other in range(bufs[2].shape[0]):
                    total = total + bufs[2][other, r, :, :, cols].astype(F32)
                if m % 2:
                    bufs[0][r, iy, :, core, :, cols] = total.astype(LOW)
                else:
                    bufs[0][r, :, ix, core, :, cols] = total.astype(LOW)
                start(far(k, m))

        def level_three(k):
            iy, ix, core, _ = geo.place()
            for m in mats:
                r, cols, bufs = parts(k, m)
                arrive(far(k, m))
                total = bufs[0][r, iy, ix, core, :, cols].astype(F32)
                for other in range(bufs[3].shape[0]):
                    total = total + bufs[3][other, r, :, cols].astype(F32)
                bufs[0][r, iy, ix, core, :, cols] = total.astype(LOW)
                delivery = along(self.chunks[k][1], m)
                if r == 2:
                    delivery.merge()
                elif r:
                    delivery.begin(r)

        def final(cut):
            iy, ix, core, _ = geo.place()
            begin, count = self.cuts[cut]
            cols = pl.ds(begin, count)
            for m in mats:
                bufs = buffers[5 * m : 5 * m + 5]
                along(cut, m).arrive()
                total = bufs[0][0, iy, ix, core, :, cols].astype(F32)
                for r in range(1, groups):
                    total = total + bufs[4][r, :, cols].astype(F32)
                outs[m][:, cols] = total

        def end():
            for m in mats:
                for k in range(len(self.chunks)):
                    leave([cross(k, m)] + near(k, m) + far(k, m))
                for cut in range(len(self.cuts)):
                    along(cut, m).leave()

        count = range(len(self.chunks))
        return dict(
            begin=[partial(begin, k) for k in count],
            one=[partial(level_one, k) for k in count],
            two=[partial(level_two, k) for k in count],
            three=[partial(level_three, k) for k in count],
            final=[partial(final, cut) for cut in range(len(self.cuts))],
            end=[end],
        )


class Spread:
    def __init__(self, geo, value, plane=False, absolute=True):
        self.geo, self.plane, self.absolute = geo, plane, absolute
        self.peers = geo.plane() if plane else geo.column()
        self.inputs = [(value, "full")]
        self.outputs = [((len(self.peers) + 1,) + value.shape, value.dtype, "any")]
        sems = pltpu.SemaphoreType.DMA((len(self.peers) + 1,))
        self.scratch = [sems, sems, pltpu.SemaphoreType.DMA]

    def tasks(self, values, outs, scratch):
        geo, (value,), (out,), (send, recv, local) = self.geo, values, outs, scratch
        move = Mover(geo, send, recv)
        own = 0
        mine = None
        if not self.plane:
            h = geo.here()[3]
            own = h if self.absolute else 0
            slot = lambda r: out.at[lax.rem(h + r, geo.groups) if self.absolute else r]
            column = Column(geo, value, slot, send, recv, 0, self.absolute)
            mine = pltpu.make_async_copy(value, out.at[own], local)

            def begin_column():
                column.begin()
                mine.start()

            def end_column():
                mine.wait()
                column.arrive()
                column.leave()

            return [begin_column, column.relay, end_column]
        if self.absolute:
            own = geo.device()[0] if self.plane else geo.device()[1]
        copies = []
        for to in self.peers:
            slot = own if self.absolute else to["z"]
            copies.append(move(str(to), value, out.at[slot], **back(to)))
        mine = pltpu.make_async_copy(value, out.at[own], local)

        def begin():
            start(copies)
            mine.start()

        def end():
            mine.wait()
            arrive(copies)
            leave(copies)

        return [begin, end]


class Deal:
    def __init__(self, geo, value):
        self.geo, self.peers = geo, geo.column()
        self.rows = value.shape[1] // geo.groups
        self.inputs = [(value, "any")]
        shape = (geo.groups - 1, value.shape[0], self.rows, value.shape[2])
        self.outputs = [(shape, value.dtype, "any")]
        sems = pltpu.SemaphoreType.DMA((geo.groups - 1,))
        self.scratch = [sems, sems]

    def tasks(self, values, outs, scratch):
        geo = self.geo
        move = Mover(geo, *scratch)
        copies = []
        for r in range(1, geo.groups):
            first = pl.multiple_of(geo.place(z=-r)[3] * self.rows, self.rows)
            copies.append(move(r, values[0].at[:, pl.ds(first, self.rows), :], outs[0].at[r - 1], z=-r))

        def end():
            arrive(copies)
            leave(copies)

        return [lambda: start(copies), end]


class Fold:
    def __init__(self, geo, items):
        self.geo, self.peers = geo, geo.plane() + geo.column()
        self.inputs = [(item[0], "full") for item in items]
        self.picks = [item[1:] for item in items]
        rows = sum(stop - first for _, (first, stop), _ in self.picks)
        self.rows = -(-rows // 8) * 8
        self.outputs = [((self.rows, 128), F32, "full")]
        near, far = pltpu.SemaphoreType.DMA((geo.ndp - 1,)), pltpu.SemaphoreType.DMA((geo.groups - 1,))
        wide = pltpu.VMEM((geo.ndp, geo.groups, self.rows, 128), F32)
        slim = pltpu.VMEM((geo.groups, self.rows, 128), F32)
        self.scratch = [near, near, far, far, wide, wide, slim, slim]

    def tasks(self, values, outs, scratch):
        geo = self.geo
        near_send, near_recv, far_send, far_recv, packed, landed, middle, last = scratch
        groups, ndp = geo.groups, geo.ndp
        to_plane, to_column = Mover(geo, near_send, near_recv), Mover(geo, far_send, far_recv)
        dp, h = geo.device()
        near, far = [], []
        for to in geo.plane():
            there, _ = geo.device(**to)
            near.append(to_plane(str(to), packed.at[there], landed.at[dp], **to))
        for r in range(1, groups):
            far.append(to_column(r, middle.at[r], last.at[h], z=r))

        def begin():
            packed[...] = jnp.zeros_like(packed)
            row = 0
            for value, (grouped, (low, high), (first, stride, cols)) in zip(values, self.picks):
                for r in range(groups):
                    for d in range(ndp):
                        lanes = slice(first + d * stride, first + d * stride + cols)
                        part = value[r, low:high, lanes] if grouped else value[low:high, lanes]
                        packed[d, r, row : row + high - low, :cols] = part
                row += high - low
            start(near)

        def fold():
            landed[dp] = packed[dp]
            arrive(near)
            total = landed[0]
            for d in range(1, ndp):
                total = total + landed[d]
            middle[...] = total
            start(far)

        def end():
            last[h] = middle[0]
            arrive(far)
            total = last[0]
            for z in range(1, groups):
                total = total + last[z]
            outs[0][...] = total
            leave(near)
            leave(far)

        return [begin, fold, end]


def norm_forward(before, gain, shift):
    center = before - jnp.mean(before, -1, keepdims=True)
    spread = jnp.mean(center * center, -1, keepdims=True)
    return center * lax.rsqrt(spread + EPS) * gain + shift


def norm_backward(before, gain, grad):
    center = before - jnp.mean(before, -1, keepdims=True)
    rate = lax.rsqrt(jnp.mean(center * center, -1, keepdims=True) + EPS)
    hat = center * rate
    grad_hat = grad * gain
    mean_one = jnp.mean(grad_hat, -1, keepdims=True)
    mean_two = jnp.mean(grad_hat * hat, -1, keepdims=True)
    grad_before = rate * (grad_hat - mean_one - hat * mean_two)
    return (
        grad_before,
        jnp.sum(grad * hat, 0, keepdims=True),
        jnp.sum(grad, 0, keepdims=True),
        jnp.sum(grad_before, 0, keepdims=True),
    )


BIAS_ONE, BIAS_TWO, GAIN_ONE, GAIN_TWO, SHIFT_ONE, SHIFT_TWO = range(6)


class Window:
    def __init__(self, size, rows, groups):
        self.seqs, self.seq_len, self.heads, self.head_size = size
        self.rows, self.groups = rows, groups
        self.block = self.seq_len // groups
        self.mid_rows = 2 * self.block
        h = lax.axis_index("head")
        self.h = h
        self.first = lax.div(h * (self.seqs - 1), groups)
        self.base = self.first * self.seq_len
        self.own = h * rows - self.base
        pair = h + 1 - 2 * lax.rem(h, 2)
        self.pair = pair * rows - self.base
        self.mid = lax.rem(h, 2) * (2 * rows)
        self.mid_row = lax.rem(h, 2) * self.block
        self.middle = (h > 0) & (h < groups - 1)
        dp = lax.axis_index("dp")
        self.to_pair = (dp, pair)
        self.to_mid = (dp, groups - 1 - h)

    def at(self, begin, rows):
        return pl.ds(pl.multiple_of(begin, self.block), rows)

    def loc(self, piece):
        return lax.div((self.h * (self.rows // self.block) + piece) * self.block, self.seq_len) - self.first

    def keys(self, piece):
        return pl.ds(pl.multiple_of(self.loc(piece) * self.seq_len, self.seq_len), self.seq_len)


def remote(src, dst, sems, to):
    return pltpu.make_async_remote_copy(
        src_ref=src, dst_ref=dst, send_sem=sems.at[0], recv_sem=sems.at[1], device_id=to, device_id_type=MESH
    )


def add_up(r, total, part):
    @pl.when(r == 0)
    def _():
        total[...] = part

    @pl.when(r > 0)
    def _():
        total[...] += part


def gelu_parts(unit):
    square = unit * unit
    bent = jnp.tanh(GELU_C * unit * (1.0 + GELU_K * square))
    half = 0.5 * (1.0 + bent)
    slope = half + 0.5 * unit * (1.0 - bent * bent) * (GELU_C * (1.0 + 3.0 * GELU_K * square))
    return unit * half, slope


def vector(vec, layer, which):
    return vec[6 * layer + which : 6 * layer + which + 1, :]


def attend(window, layer, xin, offset, row, lengths, left, right, outs, total, r, point):
    kv_out, q_out, ctx_out, lse_out, gated_out = outs
    seq_len, heads, head_size, block, rows = (
        window.seq_len,
        window.heads,
        window.head_size,
        window.block,
        window.rows,
    )
    width = heads * head_size
    point(0)
    kv = nn(xin[window.at(offset, 2 * seq_len), :], left) + row[:, 2 * width :]
    kv_out[0] = kv.astype(LOW)
    query = (nn(xin[window.at(offset + window.own, rows), :], right[:, :width]) + row[:, :width]).astype(LOW)
    q_out[0] = query
    scaled = query * jnp.asarray(0.125, LOW)
    for piece in range(rows // block):
        mine = slice(piece * block, (piece + 1) * block)
        keys = window.keys(piece)
        usable = lax.broadcasted_iota(jnp.int32, (block, seq_len), 1) < lengths[window.loc(piece)]
        for head in range(heads):
            lanes = slice(head * head_size, (head + 1) * head_size)
            scores = nt(scaled[mine, lanes], kv_out[0, keys, lanes])
            scores = jnp.where(usable, scores, -1e30)
            largest = jnp.max(scores, -1, keepdims=True)
            powers = jnp.exp(scores - largest)
            sums = jnp.sum(powers, -1, keepdims=True)
            value = kv_out[0, keys, width + head * head_size : width + (head + 1) * head_size]
            context = nn(powers.astype(LOW), value) / sums
            ctx_out[0, mine, lanes] = context
            lse_out[0, mine, head : head + 1] = largest + jnp.log(sums)
            point(1 + piece * heads + head)
    gated = (ctx_out[0] * row[:, width : 2 * width]).astype(LOW)
    gated_out[0] = gated
    add_up(r, total, nt(gated, right[:, width:]))


def forward(size, layers, geo, gather, lists, *refs):
    seqs, seq_len, heads, head_size = size
    refs = list(refs)
    take = lambda n: [refs.pop(0) for _ in range(n)]
    hidden, small_own, vec, lengths, key_value, query_output, inner, outer, map_own = take(9)
    saved = [take(10) for _ in range(layers)]
    win_out, small_out = take(2)
    left_buf, right_buf, inner_buf, outer_buf, load_sems, back_sems = take(6)
    total, middle, current, low, xwin, small, small_send, small_recv, map_stage = take(9)
    pair_sems, mid_sems, local = take(3)
    gather_tasks, count_tasks, deal_tasks, (weights,) = lists
    groups = geo.groups
    rows, model = total.shape
    window = Window(size, rows, groups)
    mid_rows, width = window.mid_rows, heads * head_size
    s = pl.program_id(0)
    r = lax.rem(s, groups)
    slot = lax.rem(r, 2)
    spots_attn, spots_feed = 2 + rows // window.block * heads, 4
    plan = Plan(([spots_attn] * groups + [spots_feed] * groups) * layers)

    small_column = Column(geo, small_own, lambda i: small.at[i], small_send, small_recv, 0)
    keep_small = pltpu.make_async_copy(small, small_out, local.at[2])

    def small_begin():
        small_column.begin()

    def small_end():
        small_column.relay()
        small_column.arrive()
        small_column.leave()
        keep_small.start()

    into_stage = pltpu.make_async_copy(map_own.at[0], map_stage, local.at[3])
    out_of_stage = pltpu.make_async_copy(map_stage, weights[-1].at[0], local.at[4])

    def stage_begin():
        into_stage.start()

    def stage_end():
        into_stage.wait()
        out_of_stage.start()

    phases = 2 * layers
    plan.even([small_begin] + [count_tasks[0]], 0, 0)
    ends, done = [], 0
    for phase in range(phases):
        for chunk, halves in enumerate(gather.chunks):
            if halves[0][0] // 2 == phase:
                done = gather.done[chunk]
        ends.append(done)
    first, begun = 0, 0
    for phase in range(phases):
        last = plan.slot(phase * groups, -1)
        plan.even(gather_tasks[begun : ends[phase]], first, last)
        first, begun = last, ends[phase]
        if phase == 0:
            plan.even([small_end, stage_begin], last, last)
            plan.even([count_tasks[1]], plan.slot(groups, 0), plan.slot(groups, 0))
            plan.even([stage_end], plan.slot(groups, 1), plan.slot(groups, 1))
        if phase == 2:
            plan.even([deal_tasks[0]], last, last)
    closing = len(plan.slots) - 1
    plan.even(gather_tasks[begun:], first, closing)
    plan.even([deal_tasks[1]], closing, closing)

    kinds = [(left_buf, right_buf), (inner_buf, outer_buf)]
    sources = [(key_value, query_output), (inner, outer)]

    def own_loads(phase):
        layer, kind = phase // 2, phase % 2
        return [
            pltpu.make_async_copy(src.at[layer], buf.at[0], load_sems.at[kind, side, 0])
            for side, (src, buf) in enumerate(zip(sources[kind], kinds[kind]))
        ]

    def own_backs(phase):
        kind = phase % 2
        return [
            pltpu.make_async_copy(buf.at[0], weights[2 * phase + side].at[0], back_sems.at[kind, side])
            for side, buf in enumerate(kinds[kind])
        ]

    def loads(phase, group, into):
        kind = phase % 2
        return [
            pltpu.make_async_copy(weights[2 * phase + side].at[group], buf.at[into], load_sems.at[kind, side, into])
            for side, buf in enumerate(kinds[kind])
        ]

    @pl.when(s == 0)
    def _():
        small[0] = small_own[...]
        start(own_loads(0))

    def before(phase):
        @pl.when(r == 0)
        def _():
            if phase + 1 < phases:
                start(own_loads(phase + 1))
            for copy in own_loads(phase):
                copy.wait()
            start(own_backs(phase))

        @pl.when(r > 0)
        def _():
            for copy in loads(phase, r, slot):
                copy.wait()

        @pl.when((r > 0) & (r < groups - 1))
        def _():
            start(loads(phase, r + 1, 1 - slot))

    def behind(phase):
        @pl.when(r == 0)
        def _():
            for copy in own_backs(phase):
                copy.wait()
            start(loads(phase, 1, 1))

    def flat(buf):
        value = buf[slot]
        return value.reshape(model, value.shape[-1])

    own_place = xwin.at[window.at(window.own, rows)]
    to_pair = remote(low, own_place, pair_sems, window.to_pair)
    to_mid = remote(
        low.at[window.at(window.mid_row, mid_rows)],
        xwin.at[window.at((1 - lax.rem(window.h, 2)) * 2 * rows, mid_rows)],
        mid_sems,
        window.to_mid,
    )
    keep_win = pltpu.make_async_copy(xwin, win_out, local.at[0])

    for phase in range(phases):
        layer, kind = phase // 2, phase % 2
        kv_out, q_out, ctx_out, lse_out, gated_out, before_one, middle_low, unit_out, before_two, low_out = saved[layer]
        span = range(phase * groups, (phase + 1) * groups)

        def point(spot, span=span):
            plan.point(s, spot, span)

        @pl.when(lax.div(s, groups) == phase)
        def _():
            if kind == 0:
                if layer:

                    @pl.when(r == 0)
                    def _():
                        to_pair.wait()

                        @pl.when(window.middle)
                        def _():
                            to_mid.wait()

                        keep_win.start()

                before(phase)
                xin, offset = (xwin, 0) if layer else (hidden, window.base)
                row = small[r, 4 * layer + 2 : 4 * layer + 3, :]
                outs = (kv_out, q_out, ctx_out, lse_out, gated_out)
                attend(window, layer, xin, offset, row, lengths, flat(left_buf), flat(right_buf), outs, total, r, point)

                @pl.when(r == groups - 1)
                def _():
                    if layer:
                        resid = current[...]
                    else:
                        resid = hidden[window.at(offset + window.own, rows), :].astype(F32)
                    value = resid + total[...] + vector(vec, layer, BIAS_ONE)
                    normed = norm_forward(value, vector(vec, layer, GAIN_ONE), vector(vec, layer, SHIFT_ONE))
                    before_one[...] = value
                    middle[...] = normed
                    middle_low[...] = normed.astype(LOW)

                point(spots_attn - 1)
                behind(phase)
            else:
                before(phase)
                point(0)
                unit = nn(middle_low[...], flat(inner_buf)) + small[r, 4 * layer + 1 : 4 * layer + 2, :]
                unit_out[0] = unit.astype(LOW)
                point(1)
                bent = jnp.tanh(GELU_C * unit * (1.0 + GELU_K * (unit * unit)))
                active = (0.5 * unit * (1.0 + bent) * small[r, 4 * layer : 4 * layer + 1, :]).astype(LOW)
                point(2)
                add_up(r, total, nn(active, flat(outer_buf)))

                @pl.when(r == groups - 1)
                def _():
                    value = middle[...] + total[...] + vector(vec, layer, BIAS_TWO)
                    normed = norm_forward(value, vector(vec, layer, GAIN_TWO), vector(vec, layer, SHIFT_TWO))
                    before_two[...] = value
                    low_out[...] = normed.astype(LOW)
                    if layer + 1 < layers:
                        current[...] = normed
                        low[...] = normed.astype(LOW)
                        to_pair.start()

                        @pl.when(window.middle)
                        def _():
                            to_mid.start()

                        xwin[window.at(window.own, rows), :] = normed.astype(LOW)

                        @pl.when(jnp.logical_not(window.middle))
                        def _():
                            empty = window.at(lax.rem(window.h + 1, 2) * 2 * rows, mid_rows)
                            xwin[empty, :] = jnp.zeros((mid_rows, model), LOW)

                point(spots_feed - 1)
                behind(phase)

    @pl.when(s == phases * groups - 1)
    def _():
        keep_win.wait()
        keep_small.wait()
        out_of_stage.wait()


def match_teacher(layers, tokens, point, *refs):
    refs = list(refs)
    states = [refs.pop(0) for _ in range(layers)]
    target, chosen, row_ok, counts, weight = refs[:5]
    back_out, loss_out, grad_out = refs[5:]
    r = pl.program_id(0)
    rows = states[0].shape[0]

    @pl.when(r == 0)
    def _():
        loss_out[...] = jnp.zeros_like(loss_out)
        back_out[...] = jnp.zeros_like(back_out)

    count = jnp.sum(counts[...][:, 0:1, 0:1], 0)
    factor = tokens / count
    mine = pl.ds(pl.multiple_of(lax.axis_index("head") * rows, rows), rows)
    total = None
    for layer in range(layers):
        goal = jnp.where(r == 0, chosen[layer, mine, :], target[0, layer]).astype(F32)
        miss = (nn(states[layer][...], weight[0]) - goal) * row_ok[:, :1]
        loss_out[:1, :1] += jnp.sum(jnp.sum(miss * miss, 0, keepdims=True), 1, keepdims=True)
        low = (factor * miss).astype(LOW)
        back_out[layer] += nt(low, weight[0])
        grad = tn(states[layer][...], low)
        total = grad if total is None else total + grad
    grad_out[0] = total.astype(LOW)


FEED_STEP, ATTN_STEP, WEIGHT_STEP = 5.0, 6.5, 3.0


def in_order(s):
    place = jnp.clip(s, 0, len(ORDER) - 1)
    group = 0
    for index, value in enumerate(ORDER):
        group = jnp.where(place == index, value, group)
    return group


def layer_backward(size, layer, first, last, geo, reduce, times, lists, *refs):
    seqs, seq_len, heads, head_size = size
    refs = list(refs)
    take = lambda n: [refs.pop(0) for _ in range(n)]
    before_two, before_one, middle_low, unit_in, small, vec, inner, outer = take(8)
    grad_refs = take(2 if last else 1)
    xwin, query_in, kv, ctx, lse, gated, lengths, left, right = take(9)
    extra = None if first else refs.pop(0)
    left_out, right_out, grad_out, head_vec, vec_out, unit_vec = take(6)
    (mine, feed, attn, grad_kv, grad_q, kv_all, q_all, spread, pair_low, pair_got, mid_low, mid_got) = take(12)
    pair_sems, mid_sems = take(2)
    work, riders = lists[0], lists[1:]
    groups = geo.groups
    s = pl.program_id(0)
    r = lax.rem(s, groups)
    part = lax.div(s, groups)
    width = heads * head_size
    rows, model = mine.shape
    window = Window(size, rows, groups)
    block, mid_rows = window.block, window.mid_rows
    blocks = rows // block
    offset = window.base if first else 0
    here = window.at(offset + window.own, rows)
    to_pair = remote(pair_low, pair_got, pair_sems, window.to_pair)
    to_mid = remote(mid_low, mid_got, mid_sems, window.to_mid)

    spots = [7] * groups + [2 + blocks * heads] * groups + [4] * groups
    lengths_us = [FEED_STEP] * groups + [ATTN_STEP] * groups + [WEIGHT_STEP] * groups
    plan = Plan(spots)
    whole = sum(lengths_us)
    cuts = len(reduce.cuts)
    timed = []
    first_one, pace, second, third = times
    ones = [
        max(FEED_STEP * (k // cuts + 1) + 4.5, first_one + pace * k) + 0.01 * (k % cuts)
        for k in range(len(reduce.chunks))
    ]
    for k in range(len(reduce.chunks)):
        made = FEED_STEP * (k // cuts + 1) - 0.5 + 0.01 * (k % cuts)
        if k >= reduce.ring:
            made = max(made, ones[k - reduce.ring] + 0.1)
        timed.append((made, work["begin"][k]))
        timed.append((max(ones[k], made + 3.0), work["one"][k]))
        timed.append((ones[k] + second, work["two"][k]))
        timed.append((ones[k] + second + third, work["three"][k]))
    timed += [(1e6, task) for task in work["final"] + work["end"]]
    for finish, tasks in riders:
        count = max(1, len(tasks) - 1)
        timed += [(finish * whole * index / count, task) for index, task in enumerate(tasks)]
    plan.timed(lengths_us, timed)

    def points(span):
        return lambda spot: plan.point(s, spot, span)

    point_feed = points(range(groups))
    point_attn = points(range(groups, 2 * groups))
    point_weight = points(range(2 * groups, 3 * groups))

    def feeding():
        point_feed(0)
        unit = in_order(s)

        @pl.when(r == 0)
        def _():
            if last:
                cotangent, back = grad_refs
                grad = cotangent[...].astype(F32) + back[0]
            else:
                grad = grad_refs[0][...]
            grad_before, grad_gain, grad_shift, grad_bias = norm_backward(
                before_two[...], vector(vec, layer, GAIN_TWO), grad
            )
            vec_out[BIAS_TWO : BIAS_TWO + 1, :] = grad_bias
            vec_out[GAIN_TWO : GAIN_TWO + 1, :] = grad_gain
            vec_out[SHIFT_TWO : SHIFT_TWO + 1, :] = grad_shift
            feed[...] = grad_before.astype(LOW)
            mine[...] = grad_before

        grad_active = nt(feed[...], outer[0])
        point_feed(1)
        value, slope = gelu_parts(unit_in[0].astype(F32))
        opened = small[0, 4 * layer : 4 * layer + 1, :]
        grad_unit = (grad_active * (slope * opened)).astype(LOW)
        unit_vec[0, 0:1, :] = jnp.sum(grad_unit.astype(F32), 0, keepdims=True)
        unit_vec[0, 1:2, :] = jnp.sum(grad_active * value, 0, keepdims=True)
        active = (value * opened).astype(LOW)
        point_feed(2)
        mine[...] += nt(grad_unit, inner[0])
        point_feed(3)
        shape = reduce.grads[0].shape[1:]
        reduce.grads[0][unit] = tn(middle_low[...], grad_unit).astype(LOW).reshape(shape)
        point_feed(4)
        reduce.grads[1][unit] = tn(feed[...], active).astype(LOW).reshape(shape)
        point_feed(5)

        @pl.when(r == groups - 1)
        def _():
            grad_before, grad_gain, grad_shift, grad_bias = norm_backward(
                before_one[...], vector(vec, layer, GAIN_ONE), mine[...]
            )
            vec_out[BIAS_ONE : BIAS_ONE + 1, :] = grad_bias
            vec_out[GAIN_ONE : GAIN_ONE + 1, :] = grad_gain
            vec_out[SHIFT_ONE : SHIFT_ONE + 1, :] = grad_shift
            mine[...] = grad_before if first else grad_before + extra[0]
            attn[...] = grad_before.astype(LOW)
            spread[...] = jnp.zeros_like(spread)

        point_feed(6)

    def attending():
        point_attn(0)
        row = small[0, 4 * layer + 2 : 4 * layer + 3, :]
        opened = row[:, width : 2 * width]
        grad_gated = nn(attn[...], right[0, :, width:])
        shared = grad_gated * ctx[0]
        grad_ctx = (grad_gated * opened).astype(LOW)
        pulled = shared * opened
        scaled = query_in[0] * jnp.asarray(0.125, LOW)
        grad_kv[...] = jnp.zeros_like(grad_kv)
        for piece in range(blocks):
            rows_of = slice(piece * block, (piece + 1) * block)
            keys = window.keys(piece)
            usable = lax.broadcasted_iota(jnp.int32, (block, seq_len), 1) < lengths[window.loc(piece)]
            for head in range(heads):
                lanes = slice(head * head_size, (head + 1) * head_size)
                later = slice(width + head * head_size, width + (head + 1) * head_size)
                key = kv[0, keys, lanes]
                scores = nt(scaled[rows_of, lanes], key)
                chances = jnp.where(usable, jnp.exp(scores - lse[0, rows_of, head : head + 1]), 0.0)
                grad_chances = nt(grad_ctx[rows_of, lanes], kv[0, keys, later])
                delta = jnp.sum(pulled[rows_of, lanes], -1, keepdims=True)
                grad_scores = (chances * (grad_chances - delta)).astype(LOW)
                grad_q[rows_of, lanes] = nn(grad_scores, key) * 0.125
                grad_kv[keys, lanes] += tn(grad_scores, scaled[rows_of, lanes])
                grad_kv[keys, later] += tn(chances.astype(LOW), grad_ctx[rows_of, lanes])
                point_attn(1 + piece * heads + head)
        query_low = grad_q[...].astype(LOW)
        kv_low = grad_kv[...].astype(LOW)
        q_all[r] = query_low
        kv_all[r] = kv_low
        head_vec[0, 0:1, :width] = jnp.sum(query_low.astype(F32), 0, keepdims=True)
        head_vec[0, 0:1, 2 * width :] = jnp.sum(kv_low.astype(F32), 0, keepdims=True)
        shared_sum = jnp.sum(shared, 0, keepdims=True)
        lane = lax.broadcasted_iota(jnp.int32, (1, 128), 1)
        by_head = jnp.zeros((1, 128), F32)
        for head in range(heads):
            one = jnp.sum(shared_sum[:, head * head_size : (head + 1) * head_size], 1, keepdims=True)
            by_head = jnp.where(lane == head, one, by_head)
        head_vec[0, 1:2, :128] = by_head
        spread[...] += nt(kv_low, left[0])
        mine[...] += nt(query_low, right[0, :, :width])

        @pl.when(r == groups - 1)
        def _():
            pair_low[...] = spread[window.at(window.pair, rows), :].astype(LOW)
            to_pair.start()

            @pl.when(window.middle)
            def _():
                mid_low[...] = spread[window.at(window.mid, mid_rows), :].astype(LOW)
                to_mid.start()

        point_attn(1 + blocks * heads)

    def weighing():
        point_weight(0)
        left_out[0] = tn(xwin[window.at(offset, 2 * seq_len), :], kv_all[r]).astype(LOW)
        point_weight(1)
        right_out[0, :, :width] = tn(xwin[here, :], q_all[r]).astype(LOW)
        point_weight(2)
        right_out[0, :, width:] = tn(attn[...], gated[0]).astype(LOW)

        @pl.when(r == groups - 1)
        def _():
            to_pair.wait()
            mine[...] += spread[window.at(window.own, rows), :] + pair_got[...].astype(F32)

            @pl.when(window.middle)
            def _():
                to_mid.wait()
                mine[window.at(window.mid_row, mid_rows), :] += mid_got[...].astype(F32)

            grad_out[...] = mine[...].astype(grad_out.dtype)

        point_weight(3)

    pl.when(part == 0)(feeding)
    pl.when(part == 1)(attending)
    pl.when(part == 2)(weighing)


def on_device(
    ndp,
    groups,
    hidden_in,
    seq_lengths,
    layer_map,
    teacher_states,
    out_cotangent,
    query_weight,
    key_weight,
    value_weight,
    query_value_bias,
    output_weight,
    branch_bias,
    norm_gain,
    norm_shift,
    inner_weight,
    inner_bias,
    outer_weight,
    head_alpha,
    head_noise,
    unit_alpha,
    unit_noise,
    map_weight,
):
    tokens_dev, model = hidden_in.shape
    seqs_dev = seq_lengths.shape[0]
    seq_len = tokens_dev // seqs_dev
    width = query_weight.shape[2]
    units = inner_weight.shape[2]
    layers, heads = head_alpha.shape
    head_size = width // heads
    rows = tokens_dev // groups
    feats = model // ndp
    geo = Geometry(ndp, groups)
    size = (seqs_dev, seq_len, heads, head_size)
    window = Window(size, rows, groups)
    blocks = rows // window.block
    dp = lax.axis_index("dp")

    def slices(array):
        return array.reshape(array.shape[0], geo.size_y, geo.size_x, 2, feats, array.shape[-1])

    def matrices(arrays):
        return [(array.reshape(groups, model, array.shape[-1]), "group") for array in arrays]

    def pairs(cols, steps, m=0):
        out, begin = [], 0
        for step in steps:
            out.append([(m, begin, step, False), (m + 1, begin, step, True)])
            begin += step
        return out if begin == cols else [[(m, 0, cols, False), (m + 1, 0, cols, True)]]

    key_value = slices(jnp.concatenate([key_weight, value_weight], 2))
    query_output = slices(jnp.concatenate([query_weight, jnp.swapaxes(output_weight, 1, 2)], 2))
    inner, outer = slices(inner_weight), slices(outer_weight)

    open_unit, unit_back = jax.vjp(partial(gate_open, unit_noise), unit_alpha)
    open_head, head_back = jax.vjp(partial(gate_open, head_noise), head_alpha)
    (unit_slope,) = unit_back(jnp.ones_like(open_unit))
    (head_slope,) = head_back(jnp.ones_like(open_head))
    mixed = jnp.concatenate(
        [
            query_value_bias[:, 0],
            jnp.repeat(open_head, head_size, axis=1),
            jnp.zeros((layers, width), F32),
            query_value_bias[:, 1],
        ],
        1,
    )
    small = jnp.stack([open_unit, inner_bias, mixed, mixed], 1).reshape(4 * layers, units)
    vec = jnp.concatenate([branch_bias, norm_gain, norm_shift], 1).reshape(6 * layers, model)
    lengths = lax.dynamic_slice(seq_lengths, (window.first,), (2,))
    spot = jnp.arange(tokens_dev)
    row_ok = (spot % seq_len < jnp.repeat(seq_lengths, seq_len, total_repeat_length=tokens_dev)).astype(F32)
    row_ok = lax.dynamic_slice(row_ok, (window.h * rows,), (rows,))
    row_ok = jnp.broadcast_to(row_ok[:, None], (rows, 128))
    count = jnp.broadcast_to(jnp.sum(seq_lengths).astype(F32), (8, 128))
    chosen = jnp.take(teacher_states, layer_map, axis=0)

    row_block = pltpu.VMEM((rows, model), F32)
    low_block = pltpu.VMEM((rows, model), LOW)
    mid_block = pltpu.VMEM((window.mid_rows, model), LOW)
    two = pltpu.SemaphoreType.DMA((2,))
    owns, chunks = [], []
    for layer in range(layers):
        for arrays, cuts in (((key_value, query_output), ATTN_CUTS), ((inner, outer), FEED_CUTS)):
            chunks += pairs(arrays[0].shape[-1], cuts, len(owns))
            owns += [(array, layer) for array in arrays]
    chunks.append([(len(owns), 0, width, False)])
    map_slices = slices(map_weight[None])
    owns.append((map_slices, 0))
    gather = Gather(geo, owns, chunks)
    outputs = []
    for layer in range(layers):
        attn_step = lambda s, layer=layer: jnp.clip(s - 2 * layer * groups, 0, groups - 1)
        feed_step = lambda s, layer=layer: jnp.clip(s - (2 * layer + 1) * groups, 0, groups - 1)
        outputs += [
            ((groups, 2 * seq_len, 2 * width), LOW, attn_step),
            ((groups, rows, width), LOW, attn_step),
            ((groups, rows, width), F32, attn_step),
            ((groups, rows, 128), F32, attn_step),
            ((groups, rows, width), LOW, attn_step),
            ((rows, model), F32, "full"),
            ((rows, model), LOW, "full"),
            ((groups, rows, units), LOW, feed_step),
            ((rows, model), F32, "full"),
            ((rows, model), LOW, "full"),
        ]
    saves = len(outputs) // layers
    outputs += [((2 * seq_len, model), LOW, "any"), ((groups,) + small.shape, F32, "any")]
    attn_buf = pltpu.VMEM((2,) + key_value.shape[1:], LOW)
    feed_buf = pltpu.VMEM((2,) + inner.shape[1:], LOW)
    others = pltpu.SemaphoreType.DMA((groups,))
    got = run(
        partial(forward, size, layers, geo, gather),
        2 * layers * groups,
        [
            (hidden_in, "full"),
            (small, "full"),
            (vec, "full"),
            (lengths, "smem"),
            (key_value, "any"),
            (query_output, "any"),
            (inner, "any"),
            (outer, "any"),
            (map_slices, "any"),
        ],
        outputs,
        [
            attn_buf,
            attn_buf,
            feed_buf,
            feed_buf,
            pltpu.SemaphoreType.DMA((2, 2, 2)),
            pltpu.SemaphoreType.DMA((2, 2)),
            row_block,
            row_block,
            row_block,
            low_block,
            pltpu.VMEM((2 * seq_len, model), LOW),
            pltpu.VMEM((groups,) + small.shape, F32),
            others,
            others,
            pltpu.VMEM(map_slices.shape[1:], LOW),
            two,
            two,
            pltpu.SemaphoreType.DMA((5,)),
        ],
        30e9,
        "forward",
        [gather, Spread(geo, count, plane=True), Deal(geo, chosen), Lend(geo, gather)],
        1,
        1,
        True,
    )
    records = [got[layer * saves : (layer + 1) * saves] for layer in range(layers)]
    xwins, small = [hidden_in, got[layers * saves]], got[layers * saves + 1]
    *weights, counts, target = got[layers * saves + 2 :]
    weights = matrices(weights)
    lows = [record[-1] for record in records]
    spread, loss, grad_map = run(
        partial(match_teacher, layers, float(tokens_dev * ndp)),
        groups,
        [(low, "full") for low in lows]
        + [(target, lambda r: jnp.maximum(r - 1, 0)), (chosen, "full"), (row_ok, "full"), (counts, "full")]
        + weights[-1:],
        [
            ((layers, rows, model), F32, "full"),
            ((8, 128), F32, "full"),
            ((groups, model, width), LOW, "group"),
        ],
        [],
        4e9,
        "match_teacher",
    )

    cotangent = lax.dynamic_slice(out_cotangent, (window.h * rows, 0), (rows, model))
    grads = [(cotangent, "once"), (spread[layers - 1 :], "once")]
    results = [{} for _ in range(layers)]
    riders, waiting, finishes = [], [], []

    def settle(got):
        for (layer, name), value in zip(waiting, got):
            results[layer][name] = value

    def clipped(part):
        return lambda s: jnp.clip(s - part * groups, 0, groups - 1)

    shares = [lows[-1][: rows // 2], lows[-1][rows // 2 :]]
    riders = [Scatter(geo, [slices(grad_map)], [[(0, 0, width, False)]])]
    waiting, finishes = [(0, "map")], [0.7]
    for layer in reversed(range(layers)):
        kv, query, ctx, lse, gated, before_one, middle_low, unit_in, before_two, _ = records[layer]
        attn_weights, feed_weights = weights[4 * layer : 4 * layer + 2], weights[4 * layer + 2 : 4 * layer + 4]
        if layer < 2:
            riders.append(Spread(geo, shares[layer]))
            waiting.append((layer, "block_out"))
            finishes.append(1.0)
        reduce = Reduce(geo, [(feats, units)] * 2, BACK_CUTS)
        left, right, grad, head_vec, vec_out, unit_vec, *got = run(
            partial(
                layer_backward,
                size,
                layer,
                layer == 0,
                layer == layers - 1,
                geo,
                reduce,
                TIMES_LAST if layer == layers - 1 else TIMES,
            ),
            3 * groups,
            [
                (before_two, "once"),
                (before_one, "once"),
                (middle_low, "once"),
                (unit_in, in_order),
                (small, lambda s: jnp.where(s < groups, in_order(s), lax.rem(s, groups))),
                (vec, "once"),
            ]
            + [(array, in_order) for array, _ in feed_weights]
            + grads
            + [
                (xwins[layer], "once"),
                (query, clipped(1)),
                (kv, clipped(1)),
                (ctx, clipped(1)),
                (lse, clipped(1)),
                (gated, clipped(2)),
                (lengths, "smem"),
            ]
            + [(array, clipped(1)) for array, _ in attn_weights]
            + ([(spread[layer - 1 : layer], "once")] if layer else []),
            [((groups, model, 2 * width), LOW, clipped(2))] * 2
            + [
                ((rows, model), F32 if layer else LOW, "full"),
                ((groups, 8, units), F32, clipped(1)),
                ((8, model), F32, "full"),
                ((groups, 8, units), F32, in_order),
            ],
            [
                row_block,
                low_block,
                low_block,
                pltpu.VMEM((2 * seq_len, 2 * width), F32),
                pltpu.VMEM((rows, width), F32),
                pltpu.VMEM((groups, 2 * seq_len, 2 * width), LOW),
                pltpu.VMEM((groups, rows, width), LOW),
                pltpu.VMEM((2 * seq_len, model), F32),
                low_block,
                low_block,
                mid_block,
                mid_block,
                two,
                two,
            ],
            25e9,
            "layer_backward",
            [reduce] + [Timed(rider, finish) for rider, finish in zip(riders, finishes)],
            1,
            2 + layers - 1 - layer,
            True,
            LARGE_LIMIT,
        )
        results[layer]["inner"], results[layer]["outer"] = got[:2]
        settle(got[2:])
        riders = [Scatter(geo, [slices(left), slices(right)], pairs(2 * width, LAST_CUTS if layer == 0 else ATTN_CUTS))]
        waiting, finishes = [(layer, "kv"), (layer, "qo")], [0.75]
        grads = [(grad, "once")]
        results[layer].update(vec=vec_out, unit=unit_vec, head=head_vec)

    everywhere = (0, feats, feats)
    unit_count, qv_cols = units // ndp, width // ndp
    items = [(results[layer]["vec"], False, (0, 6), everywhere) for layer in range(layers)]
    items += [(results[layer]["unit"], True, (0, 2), (0, unit_count, unit_count)) for layer in range(layers)]
    for layer in range(layers):
        items += [(results[layer]["head"], True, (0, 1), (0, qv_cols, qv_cols))]
        items += [(results[layer]["head"], True, (0, 1), (3 * width, qv_cols, qv_cols))]
    items += [(results[layer]["head"], True, (1, 2), (0, 0, 128)) for layer in range(layers)]
    items += [(loss, False, (0, 1), (0, 0, 128))]
    riders += [Fold(geo, items), Spread(geo, grad)]
    waiting += [(0, "sums"), (0, "grad_hidden")]
    settle(run(only_move, 1, [], [], [], 0, "scatter_last", riders, 1, 2 + layers))
    sums = results[0]["sums"]
    by_feature = sums[: 6 * layers, :feats].reshape(layers, 3, 2, feats)
    by_unit = sums[6 * layers : 8 * layers, :unit_count].reshape(layers, 2, unit_count)
    by_column = sums[8 * layers : 10 * layers, :qv_cols].reshape(layers, 2, qv_cols)
    by_head = sums[10 * layers : 11 * layers, :heads]
    distill_loss = sums[11 * layers, 0] / (jnp.sum(counts[:, 0, 0]) * model * layers)
    own_slope = lax.dynamic_slice(unit_slope, (0, dp * unit_count), (layers, unit_count))

    def stacked(member, cols, turned=False):
        arrays = [results[layer][member][:, cols] for layer in range(layers)]
        return jnp.stack([array.T if turned else array for array in arrays])

    front, rear, whole = slice(0, width), slice(width, 2 * width), slice(None)
    return (
        jnp.concatenate([results[0]["block_out"], results[1]["block_out"]], 1).reshape(tokens_dev, model),
        results[0]["grad_hidden"].reshape(tokens_dev, model).astype(F32),
        distill_loss,
        stacked("qo", front),
        stacked("kv", front),
        stacked("kv", rear),
        by_column,
        stacked("qo", rear, True),
        by_feature[:, 0],
        by_feature[:, 1],
        by_feature[:, 2],
        stacked("inner", whole),
        by_unit[:, 0],
        stacked("outer", whole, True),
        by_head * head_slope,
        by_unit[:, 1] * own_slope,
        results[0]["map"],
    )


def solution(mesh):
    in_specs = (
        P("dp", None),
        P("dp"),
        P(),
        P(None, "dp", "head"),
        P("dp", None),
        P(None, None, "head"),
        P(None, None, "head"),
        P(None, None, "head"),
        P(None, None, "head"),
        P(None, "head", None),
        P(),
        P(),
        P(),
        P(None, None, "head"),
        P(None, "head"),
        P(None, "head", None),
        P(None, "head"),
        P(None, "head"),
        P(None, "head"),
        P(None, "head"),
        P(None, "head"),
    )
    out_specs = (
        P("dp", None),
        P("dp", None),
        P(),
        P(None, "dp", "head"),
        P(None, "dp", "head"),
        P(None, "dp", "head"),
        P(None, None, ("head", "dp")),
        P(None, "head", "dp"),
        P(None, None, "dp"),
        P(None, None, "dp"),
        P(None, None, "dp"),
        P(None, "dp", "head"),
        P(None, ("head", "dp")),
        P(None, "head", "dp"),
        P(None, "head"),
        P(None, ("head", "dp")),
        P("dp", "head"),
    )
    return jax.shard_map(
        partial(on_device, mesh.shape["dp"], mesh.shape["head"]),
        mesh=mesh,
        in_specs=in_specs,
        out_specs=out_specs,
        check_vma=False,
    )
```

```python
from functools import partial

import jax
import jax.numpy as jnp
from jax import lax
from jax.experimental import pallas as pl
from jax.experimental.pallas import tpu as pltpu
from jax.sharding import PartitionSpec as P

BETA = 2.0 / 3.0
EPS = 1e-05
LOW = jnp.bfloat16
F32 = jnp.float32
GELU_C = 0.7978845608028654
GELU_K = 0.044715
VMEM_LIMIT = 56 * 1024 * 1024
LARGE_LIMIT = 62 * 1024 * 1024
ATTN_CUTS = (128, 256)
FEED_CUTS = (256, 256, 256)
BACK_CUTS = (384, 384)
LAST_CUTS = (128, 128, 128)
ORDER = (1, 3, 2, 0)
TIMES_LAST = (9.5, 5.1, 6.5, 5.5)
TIMES = (12.0, 6.5, 8.0, 7.0)
MESH = pl.DeviceIdType.MESH


def gate_open(noise, alpha):
    return jnp.clip(jax.nn.sigmoid((noise + alpha) / BETA) * 1.2 - 0.1, 0.0, 1.0)


def product(left, right, dims):
    return lax.dot_general(left, right, ((dims[:1], dims[1:]), ((), ())), preferred_element_type=F32)


def nn(left, right):
    return product(left, right, (1, 0))


def nt(left, right):
    return product(left, right, (1, 1))


def tn(left, right):
    return product(left, right, (0, 0))


def factor_pair(count):
    side = 1
    for trial in range(1, count + 1):
        if count % trial == 0 and trial * trial <= count:
            side = trial
    return side, count // side


def block_of(shape, place):
    if place == "once":
        return pl.BlockSpec(shape, lambda r: (0,) * len(shape), pipeline_mode=pl.Buffered(1))
    if place == "full":
        return pl.BlockSpec(shape, lambda r: (0,) * len(shape))
    return pl.BlockSpec((1,) + tuple(shape[1:]), lambda r: (place(r),) + (0,) * (len(shape) - 1))


def spec_of(array, kind):
    if kind == "any":
        return pl.BlockSpec(memory_space=pl.ANY)
    if kind == "smem":
        return pl.BlockSpec(memory_space=pltpu.SMEM)
    if kind == "group":
        return block_of(array.shape, lambda r: r)
    return block_of(array.shape, kind)


class Plan:
    def __init__(self, spots):
        self.spots = spots
        self.slots = [(step, spot) for step, count in enumerate(spots) for spot in range(count)]
        self.chosen = {slot: [] for slot in self.slots}

    def slot(self, step, spot):
        return self.slots.index((step, spot % self.spots[step]))

    def spread(self, tasks, first, last):
        for share, _, task in sorted(tasks, key=lambda item: item[:2]):
            self.chosen[self.slots[first + round(share * (last - first))]].append(task)

    def even(self, tasks, first, last):
        count = len(tasks)
        self.spread([((index + 1) / count, index, task) for index, task in enumerate(tasks)], first, last)

    def timed(self, lengths, tasks):
        times, now = [], 0.0
        for length, count in zip(lengths, self.spots):
            times += [now + length * spot / count for spot in range(count)]
            now += length
        for time, task in sorted(tasks, key=lambda item: item[0]):
            later = [number for number, at in enumerate(times) if at >= time]
            self.chosen[self.slots[later[0] if later else len(times) - 1]].append(task)

    def point(self, r, spot, span):
        for step in span:
            tasks = self.chosen.get((step, spot), ())
            if tasks:

                @pl.when(r == step)
                def _(tasks=tasks):
                    for task in tasks:
                        task()


def run(body, steps, inputs, outputs, scratch, flops, name, riders=(), points=1, number=None, placed=False, limit=VMEM_LIMIT):
    inputs, outputs, scratch = list(inputs), list(outputs), list(scratch)
    at = [len(inputs), len(outputs), len(scratch)]
    starts, sizes = [], []
    for rider in riders:
        starts.append((len(inputs), len(outputs), len(scratch)))
        inputs += rider.inputs
        outputs += rider.outputs
        scratch += rider.scratch
        sizes.append((len(rider.inputs), len(rider.outputs), len(rider.scratch)))
    out_shape = [jax.ShapeDtypeStruct(shape, dtype) for shape, dtype, _ in outputs]
    moved = sum(a.size * a.dtype.itemsize for a, kind in inputs if kind != "any")
    n_in, n_out = len(inputs), len(outputs)
    aliases = {}
    for rider, begin in zip(riders, starts):
        aliases.update({begin[0] + i: begin[1] + o for i, o in getattr(rider, "aliases", {}).items()})
    peers = []
    for rider in riders:
        peers += [peer for peer in rider.peers if peer not in peers]

    def whole(*refs):
        kinds = refs[:n_in], refs[n_in : n_in + n_out], refs[n_in + n_out :]
        own = [ref for part, n in zip(kinds, at) for ref in part[:n]]
        lists = [
            rider.tasks(*[part[i : i + n] for part, i, n in zip(kinds, start, size)])
            for rider, start, size in zip(riders, starts, sizes)
        ]
        r = pl.program_id(0)
        if riders:

            @pl.when(r == 0)
            def _():
                riders[0].geo.greet(peers)

        if placed:
            body(lists, *own)
            return
        plan = Plan([points] * steps)
        listed = []
        for number, tasks in enumerate(lists):
            for index, task in enumerate(tasks):
                listed.append((index / max(1, len(tasks) - 1), (number, index), task))
        plan.spread(listed, 0, len(plan.slots) - 1)
        body(lambda spot, span=range(steps): plan.point(r, spot, span), *own)

    params = {"vmem_limit_bytes": limit}
    if riders:
        params.update(collective_id=number, has_side_effects=True)
    return pl.pallas_call(
        whole,
        name=name,
        grid=(steps,),
        in_specs=[spec_of(a, kind) for a, kind in inputs],
        out_specs=[spec_of(o, kind) for o, (_, _, kind) in zip(out_shape, outputs)],
        scratch_shapes=scratch,
        out_shape=out_shape,
        input_output_aliases=aliases,
        compiler_params=pltpu.CompilerParams(**params),
        cost_estimate=pl.CostEstimate(flops=int(flops), bytes_accessed=int(moved), transcendentals=0),
    )(*[a for a, _ in inputs])


def only_move(point):
    point(0)


class Geometry:
    def __init__(self, ndp, groups):
        self.ndp, self.groups = ndp, groups
        self.size_y, self.size_x = factor_pair(ndp // 2)

    def here(self):
        dp, h = lax.axis_index("dp"), lax.axis_index("head")
        return lax.rem(dp, 2), lax.rem(lax.div(dp, 2), self.size_x), lax.div(dp, 2 * self.size_x), h

    def place(self, c=0, y=0, x=0, z=0):
        core, ix, iy, h = self.here()
        core = 1 - core if c else core
        iy = lax.rem(iy + (y + self.size_y), self.size_y) if y else iy
        ix = lax.rem(ix + (x + self.size_x), self.size_x) if x else ix
        h = lax.rem(h + (z + self.groups), self.groups) if z else h
        return iy, ix, core, h

    def device(self, **to):
        iy, ix, core, h = self.place(**to)
        return ((iy * self.size_x + ix) * 2 + core, h)

    def axes(self):
        out = [dict(c=1)]
        out += [dict(y=y) for y in range(1, self.size_y)]
        out += [dict(x=x) for x in range(1, self.size_x)]
        return out + self.column()

    def column(self):
        return [dict(z=z) for z in range(1, self.groups)]

    def plane(self):
        out = []
        for c in range(2):
            for y in range(self.size_y):
                for x in range(self.size_x):
                    to = {key: value for key, value in (("c", c), ("y", y), ("x", x)) if value}
                    if to:
                        out.append(to)
        return out

    def greet(self, peers):
        barrier = pltpu.get_barrier_semaphore()
        for peer in peers:
            pl.semaphore_signal(barrier, inc=1, device_id=self.device(**peer), device_id_type=MESH)
        pl.semaphore_wait(barrier, len(peers))


class Mover:
    def __init__(self, geo, send, recv):
        self.geo, self.send, self.recv, self.ids = geo, send, recv, {}

    def __call__(self, key, src, dst, **to):
        index = self.ids.setdefault(key, len(self.ids))
        return pltpu.make_async_remote_copy(
            src_ref=src,
            dst_ref=dst,
            send_sem=self.send.at[index],
            recv_sem=self.recv.at[index],
            device_id=self.geo.device(**to),
            device_id_type=MESH,
        )


def back(to):
    return {key: value if key == "c" else -value for key, value in to.items()}


def start(copies):
    for copy in copies:
        copy.start()


def arrive(copies):
    for copy in copies:
        copy.wait_recv()


def leave(copies):
    for copy in copies:
        copy.wait_send()


class Column:
    def __init__(self, geo, block, slot, send, recv, base, absolute=False):
        self.absolute = absolute
        self.geo, self.slot, self.send, self.recv, self.base = geo, slot, send, recv, base
        self.h = geo.here()[3]
        self.block = block

    def copy(self, r):
        return pltpu.make_async_remote_copy(
            src_ref=self.block,
            dst_ref=self.slot(0 if self.absolute else r),
            send_sem=self.send.at[self.base + r],
            recv_sem=self.recv.at[self.base + r],
            device_id=self.geo.device(z=-r),
            device_id_type=MESH,
        )

    def begin(self):
        self.copy(2).start()
        pl.when(self.h != 0)(lambda: self.copy(1).start())
        pl.when(self.h != 3)(lambda: self.copy(3).start())

    def by_middle(self, act):
        @pl.when((self.h > 0) & (self.h < 3))
        def _():
            there = 1 + 2 * lax.rem(self.h, 2)
            dp, _ = self.geo.device()
            act(
                pltpu.make_async_remote_copy(
                    src_ref=self.slot(2),
                    dst_ref=self.slot(2 if self.absolute else there),
                    send_sem=self.send.at[self.base],
                    recv_sem=self.recv.at[self.base + there],
                    device_id=(dp, self.h + 1 - 2 * lax.rem(self.h, 2)),
                    device_id_type=MESH,
                )
            )

    def relay(self):
        self.copy(2).wait_recv()
        self.by_middle(lambda copy: copy.start())

    def arrive(self):
        self.copy(1).wait_recv()
        self.copy(3).wait_recv()

    def leave(self):
        self.copy(2).wait_send()
        pl.when(self.h != 0)(lambda: self.copy(1).wait_send())
        pl.when(self.h != 3)(lambda: self.copy(3).wait_send())
        self.by_middle(lambda copy: copy.wait_send())


class Delivery:
    def __init__(self, geo, block, slot, merged, send, recv, base):
        self.h, self.block, self.slot, self.merged = geo.here()[3], block, slot, merged

        def copy(r, dst, index, z):
            return pltpu.make_async_remote_copy(
                src_ref=block(r),
                dst_ref=dst,
                send_sem=send.at[base + r],
                recv_sem=recv.at[base + index],
                device_id=geo.device(z=z),
                device_id_type=MESH,
            )

        self.copy = lambda r: copy(r, slot(r), r, r)
        self.last_to_middle = lambda: copy(1, merged, 0, -1)
        self.first_to_middle = lambda: copy(3, merged, 0, 1)

    def begin(self, r):
        if r == 1:
            pl.when(self.h != 3)(lambda: self.copy(1).start())
            pl.when(self.h == 3)(lambda: self.last_to_middle().start())

            @pl.when(self.h == 0)
            def _():
                self.slot(1)[...] = jnp.zeros_like(self.slot(1))

        if r == 3:
            pl.when(self.h != 0)(lambda: self.copy(3).start())
            pl.when(self.h == 0)(lambda: self.first_to_middle().start())

            @pl.when(self.h == 3)
            def _():
                self.slot(3)[...] = jnp.zeros_like(self.slot(3))

    def merge(self):
        @pl.when((self.h > 0) & (self.h < 3))
        def _():
            self.last_to_middle().wait_recv()
            mine = self.block(2)
            mine[...] = (mine[...].astype(F32) + self.merged[...].astype(F32)).astype(LOW)

        self.copy(2).start()

    def arrive(self):
        self.copy(2).wait_recv()
        pl.when(self.h != 0)(lambda: self.copy(1).wait_recv())
        pl.when(self.h != 3)(lambda: self.copy(3).wait_recv())

    def leave(self):
        for r in (1, 2, 3):
            self.copy(r).wait_send()


class Gather:
    def __init__(self, geo, owns, chunks):
        self.geo, self.chunks, self.peers = geo, chunks, geo.axes()
        self.layers = [layer for _, layer in owns]
        self.inputs = [(own, "any") for own, _ in owns]
        self.outputs = [((geo.groups,) + own.shape[1:], LOW, "any") for own, _ in owns]
        halves = sum(len(chunk) for chunk in chunks)
        sems = pltpu.SemaphoreType.DMA((halves * 2 * geo.size_x * geo.size_y,))
        ends = pltpu.SemaphoreType.DMA((halves * geo.groups,))
        self.scratch = [sems, sems, ends, ends]

    def tasks(self, owns, outs, scratch):
        self.outs = outs
        geo = self.geo
        move = Mover(geo, *scratch[:2])
        groups, sx, sy = geo.groups, geo.size_x, geo.size_y
        bases = {}
        for chunk, parts in enumerate(self.chunks):
            for half in range(len(parts)):
                bases[chunk, half] = groups * len(bases)
        others = pl.ds(1, groups - 1)
        owns = [own.at[layer] for own, layer in zip(owns, self.layers)]

        def columns(chunk, half):
            m, col, cols, _ = self.chunks[chunk][half]
            return m, pl.ds(col, cols)

        def along(chunk, half):
            m, cols = columns(chunk, half)
            iy, ix, core, _ = geo.place()
            return Column(
                geo,
                owns[m].at[iy, ix, core, :, cols],
                lambda r: outs[m].at[r, iy, ix, core, :, cols],
                *scratch[2:],
                bases[chunk, half],
            )

        def hop(chunk, half, block, to):
            m, cols = columns(chunk, half)
            iy, ix, core, _ = geo.place(**block)
            part = outs[m].at[others, iy, ix, core, :, cols]
            return move(("p", chunk, half, str(block), str(to)), part, part, **back(to))

        ways_x = [dict(x=x) for x in range(1, sx)]
        ways_y = [dict(y=y) for y in range(1, sy)]
        corners = [dict(x=x, y=y) for x in range(1, sx) for y in range(1, sy)]

        def halves(chunk):
            return range(len(self.chunks[chunk]))

        def alongs(chunk):
            return [along(chunk, half) for half in halves(chunk)]

        def firsts(chunk):
            return [hop(chunk, half, {}, to) for half in halves(chunk) for to in ways_x + ways_y]

        def seconds(chunk):
            out = []
            for half in halves(chunk):
                near, far = (ways_y, ways_x) if self.chunks[chunk][half][3] else (ways_x, ways_y)
                out += [hop(chunk, half, block, to) for block in near for to in far]
            return out

        def cores(chunk, blocks):
            return [hop(chunk, half, block, dict(c=1)) for half in halves(chunk) for block in blocks]

        count = len(self.chunks)

        def begin():
            for chunk in range(min(2, count)):
                for column in alongs(chunk):
                    column.begin()

        def level_zero(chunk):
            for column in alongs(chunk):
                column.relay()
            if chunk + 2 < count:
                for column in alongs(chunk + 2):
                    column.begin()

        def level_one(chunk):
            for column in alongs(chunk):
                column.arrive()
            start(firsts(chunk))
            start(cores(chunk, [{}]))

        def level_two(chunk):
            arrive(firsts(chunk))
            start(seconds(chunk))
            start(cores(chunk, ways_x + ways_y))

        def level_three(chunk):
            arrive(seconds(chunk))
            start(cores(chunk, corners))

        def level_four(chunk):
            arrive(cores(chunk, [{}] + ways_x + ways_y + corners))

        def end():
            for chunk in range(count):
                for column in alongs(chunk):
                    column.leave()
                leave(firsts(chunk) + seconds(chunk) + cores(chunk, [{}] + ways_x + ways_y + corners))

        out = [begin]
        self.done = []
        for time in range(count + 4):
            for level, late in ((level_zero, 0), (level_one, 1), (level_two, 2), (level_three, 3), (level_four, 4)):
                if 0 <= time - late < count:
                    out.append(partial(level, time - late))
            if time >= 4:
                self.done.append(len(out))
        return out + [end]


class Lend:
    def __init__(self, geo, rider):
        self.geo, self.rider, self.peers = geo, rider, []
        self.inputs, self.outputs, self.scratch = [], [], []

    def tasks(self, owns, outs, scratch):
        return [self.rider.outs]


class Timed:
    def __init__(self, rider, finish):
        self.geo, self.peers, self.inputs, self.outputs, self.scratch = (
            rider.geo,
            rider.peers,
            rider.inputs,
            rider.outputs,
            rider.scratch,
        )
        self.rider, self.finish, self.aliases = rider, finish, getattr(rider, "aliases", {})

    def tasks(self, inputs, outs, scratch):
        return self.finish, self.rider.tasks(inputs, outs, scratch)


class Scatter:
    def __init__(self, geo, grads, chunks):
        self.geo, self.chunks, self.peers = geo, chunks, geo.axes()
        self.inputs = [(grad, "any") for grad in grads]
        self.outputs = [(grad.shape[4:], F32, "full") for grad in grads]
        feats = grads[0].shape[4]
        halves = [half for chunk in chunks for half in chunk]
        each = 1 + (geo.size_x - 1) + (geo.size_y - 1)
        sems = pltpu.SemaphoreType.DMA((len(halves) * each,))
        ends = pltpu.SemaphoreType.DMA((len(halves) * geo.groups,))
        self.scratch = [sems, sems, ends, ends, pltpu.SemaphoreType.DMA((len(halves),))]
        for _, _, cols, y_first in halves:
            near, far = (geo.size_y, geo.size_x) if y_first else (geo.size_x, geo.size_y)
            self.scratch += [
                pltpu.VMEM(shape, LOW)
                for shape in (
                    (geo.groups, geo.size_y, geo.size_x, feats, cols),
                    (geo.groups, geo.size_y, geo.size_x, feats, cols),
                    (near - 1, geo.groups, far, feats, cols),
                    (far - 1, geo.groups, feats, cols),
                    (geo.groups, feats, cols),
                )
            ]

    def tasks(self, grads, outs, scratch):
        geo, (send, recv, end_send, end_recv, local), buffers = self.geo, scratch[:5], scratch[5:]
        move = Mover(geo, send, recv)
        groups, sx, sy = geo.groups, geo.size_x, geo.size_y
        index = {}
        for chunk, halves in enumerate(self.chunks):
            for half in range(len(halves)):
                index[chunk, half] = len(index)

        def parts(chunk, half):
            m, col, cols, y_first = self.chunks[chunk][half]
            number = index[chunk, half]
            return grads[m], pl.ds(col, cols), y_first, buffers[5 * number : 5 * number + 5]

        def load(chunk, half):
            grad, cols, _, bufs = parts(chunk, half)
            _, _, core, _ = geo.place()
            return pltpu.make_async_copy(
                grad.at[:, :, :, core, :, cols], bufs[0], local.at[index[chunk, half]]
            )

        def cross(chunk, half):
            grad, cols, _, bufs = parts(chunk, half)
            _, _, core, _ = geo.place(c=1)
            return move(("c", chunk, half), grad.at[:, :, :, core, :, cols], bufs[1], c=1)

        def near(chunk, half):
            _, _, y_first, bufs = parts(chunk, half)
            out = []
            for step in range(1, sy if y_first else sx):
                to = dict(y=step) if y_first else dict(x=step)
                iy, ix, _, _ = geo.place(**to)
                part = bufs[0].at[:, iy] if y_first else bufs[0].at[:, :, ix]
                out.append(move(("n", chunk, half, step), part, bufs[2].at[step - 1], **to))
            return out

        def far(chunk, half):
            _, _, y_first, bufs = parts(chunk, half)
            out = []
            for step in range(1, sx if y_first else sy):
                to = dict(x=step) if y_first else dict(y=step)
                iy, ix, _, _ = geo.place(**to)
                out.append(move(("f", chunk, half, step), bufs[0].at[:, iy, ix], bufs[3].at[step - 1], **to))
            return out

        def along(chunk, half):
            _, _, _, bufs = parts(chunk, half)
            iy, ix, _, _ = geo.place()
            return Delivery(
                geo,
                lambda r: bufs[0].at[r, iy, ix],
                lambda r: bufs[4].at[r],
                bufs[4].at[0],
                end_send,
                end_recv,
                groups * index[chunk, half],
            )

        def each(chunk):
            return range(len(self.chunks[chunk]))

        def begin_one(chunk):
            for half in each(chunk):
                cross(chunk, half).start()
                load(chunk, half).start()

        count = len(self.chunks)

        def begin():
            for chunk in range(min(2, count)):
                begin_one(chunk)

        def level_one(chunk):
            for half in each(chunk):
                _, _, _, bufs = parts(chunk, half)
                load(chunk, half).wait()
                cross(chunk, half).wait_recv()
                for r in range(groups):
                    bufs[0][r] = (bufs[0][r].astype(F32) + bufs[1][r].astype(F32)).astype(LOW)
                start(near(chunk, half))
            if chunk + 2 < count:
                begin_one(chunk + 2)

        def level_two(chunk):
            iy, ix, _, _ = geo.place()
            for half in each(chunk):
                _, _, y_first, bufs = parts(chunk, half)
                arrive(near(chunk, half))
                for r in range(groups):
                    total = (bufs[0][r, iy] if y_first else bufs[0][r, :, ix]).astype(F32)
                    for other in range(bufs[2].shape[0]):
                        total = total + bufs[2][other, r].astype(F32)
                    if y_first:
                        bufs[0][r, iy] = total.astype(LOW)
                    else:
                        bufs[0][r, :, ix] = total.astype(LOW)
                start(far(chunk, half))

        def level_three(chunk):
            iy, ix, _, _ = geo.place()
            for half in each(chunk):
                _, _, _, bufs = parts(chunk, half)
                arrive(far(chunk, half))
                for r in range(groups):
                    total = bufs[0][r, iy, ix].astype(F32)
                    for other in range(bufs[3].shape[0]):
                        total = total + bufs[3][other, r].astype(F32)
                    bufs[0][r, iy, ix] = total.astype(LOW)
                for r in (1, 3):
                    along(chunk, half).begin(r)

        def level_merge(chunk):
            for half in each(chunk):
                along(chunk, half).merge()

        def level_four(chunk):
            iy, ix, _, _ = geo.place()
            for half in each(chunk):
                m, col, cols, _ = self.chunks[chunk][half]
                _, _, _, bufs = parts(chunk, half)
                along(chunk, half).arrive()
                total = bufs[0][0, iy, ix].astype(F32)
                for r in range(1, groups):
                    total = total + bufs[4][r].astype(F32)
                outs[m][:, col : col + cols] = total

        def end():
            for chunk in range(count):
                for half in each(chunk):
                    leave([cross(chunk, half)] + near(chunk, half) + far(chunk, half))
                    along(chunk, half).leave()

        out = [begin]
        levels = (level_one, level_two, level_three, level_merge, level_four)
        for time in range(count + 4):
            for late, level in enumerate(levels):
                if 0 <= time - late < count:
                    out.append(partial(level, time - late))
        return out + [end]


class Reduce:
    def __init__(self, geo, shapes, cuts):
        self.geo, self.peers = geo, geo.axes()
        self.count = len(shapes)
        self.inputs = []
        self.outputs = [(shape, F32, "full") for shape in shapes]
        self.cuts, begin = [], 0
        for cut in cuts:
            self.cuts.append((begin, cut))
            begin += cut
        if begin != shapes[0][1]:
            self.cuts = [(0, shapes[0][1])]
        self.chunks = [(r, cut) for r in ORDER for cut in range(len(self.cuts))]
        each = 1 + (geo.size_x - 1) + (geo.size_y - 1)
        sems = pltpu.SemaphoreType.DMA((self.count * len(self.chunks) * each,))
        ends = pltpu.SemaphoreType.DMA((self.count * len(self.cuts) * geo.groups,))
        self.scratch = [sems, sems, ends, ends, pltpu.SemaphoreType.REGULAR]
        for m, (feats, n) in enumerate(shapes):
            near, far = (geo.size_y, geo.size_x) if m % 2 else (geo.size_x, geo.size_y)
            self.scratch += [
                pltpu.VMEM(shape, LOW)
                for shape in (
                    (geo.groups, geo.size_y, geo.size_x, 2, feats, n),
                    (2, geo.size_y, geo.size_x, feats, n),
                    (near - 1, geo.groups, far, feats, n),
                    (far - 1, geo.groups, feats, n),
                    (geo.groups, feats, n),
                )
            ]

    def tasks(self, inputs, outs, scratch):
        geo, (send, recv, end_send, end_recv, free), buffers = self.geo, scratch[:5], scratch[5:]
        move = Mover(geo, send, recv)
        groups, sx, sy = geo.groups, geo.size_x, geo.size_y
        mats = range(self.count)
        self.grads = [buffers[5 * m] for m in mats]
        ring = self.ring = 2 * len(self.cuts)

        def parts(k, m):
            r, cut = self.chunks[k]
            begin, count = self.cuts[cut]
            return r, pl.ds(begin, count), buffers[5 * m : 5 * m + 5]

        def cross(k, m):
            r, cols, bufs = parts(k, m)
            _, _, core, _ = geo.place(c=1)
            return move(("c", k, m), bufs[0].at[r, :, :, core, :, cols], bufs[1].at[k // len(self.cuts) % 2, :, :, :, cols], c=1)

        def near(k, m):
            r, cols, bufs = parts(k, m)
            out = []
            for step in range(1, sy if m % 2 else sx):
                to = dict(y=step) if m % 2 else dict(x=step)
                iy, ix, core, _ = geo.place(**to)
                part = bufs[0].at[r, iy, :, core, :, cols] if m % 2 else bufs[0].at[r, :, ix, core, :, cols]
                out.append(move(("n", k, m, step), part, bufs[2].at[step - 1, r, :, :, cols], **to))
            return out

        def far(k, m):
            r, cols, bufs = parts(k, m)
            out = []
            for step in range(1, sx if m % 2 else sy):
                to = dict(x=step) if m % 2 else dict(y=step)
                iy, ix, core, _ = geo.place(**to)
                out.append(
                    move(
                        ("f", k, m, step),
                        bufs[0].at[r, iy, ix, core, :, cols],
                        bufs[3].at[step - 1, r, :, cols],
                        **to,
                    )
                )
            return out

        def along(cut, m):
            begin, count = self.cuts[cut]
            cols, bufs = pl.ds(begin, count), buffers[5 * m : 5 * m + 5]
            iy, ix, core, _ = geo.place()
            return Delivery(
                geo,
                lambda r: bufs[0].at[r, iy, ix, core, :, cols],
                lambda r: bufs[4].at[r, :, cols],
                bufs[4].at[0, :, cols],
                end_send,
                end_recv,
                groups * (self.count * cut + m),
            )

        def begin(k):
            if k >= ring:
                pl.semaphore_wait(free, 1)
            for m in mats:
                cross(k, m).start()

        def level_one(k):
            _, _, core, _ = geo.place()
            for m in mats:
                r, cols, bufs = parts(k, m)
                cross(k, m).wait_recv()
                total = bufs[0][r, :, :, core, :, cols].astype(F32) + bufs[1][k // len(self.cuts) % 2, :, :, :, cols].astype(F32)
                bufs[0][r, :, :, core, :, cols] = total.astype(LOW)
                start(near(k, m))
            if k + ring < len(self.chunks):
                pl.semaphore_signal(free, inc=1, device_id=geo.device(c=1), device_id_type=MESH)

        def level_two(k):
            iy, ix, core, _ = geo.place()
            for m in mats:
                r, cols, bufs = parts(k, m)
                arrive(near(k, m))
                part = bufs[0][r, iy, :, core, :, cols] if m % 2 else bufs[0][r, :, ix, core, :, cols]
                total = part.astype(F32)
                for other in range(bufs[2].shape[0]):
                    total = total + bufs[2][other, r, :, :, cols].astype(F32)
                if m % 2:
                    bufs[0][r, iy, :, core, :, cols] = total.astype(LOW)
                else:
                    bufs[0][r, :, ix, core, :, cols] = total.astype(LOW)
                start(far(k, m))

        def level_three(k):
            iy, ix, core, _ = geo.place()
            for m in mats:
                r, cols, bufs = parts(k, m)
                arrive(far(k, m))
                total = bufs[0][r, iy, ix, core, :, cols].astype(F32)
                for other in range(bufs[3].shape[0]):
                    total = total + bufs[3][other, r, :, cols].astype(F32)
                bufs[0][r, iy, ix, core, :, cols] = total.astype(LOW)
                delivery = along(self.chunks[k][1], m)
                if r == 2:
                    delivery.merge()
                elif r:
                    delivery.begin(r)

        def final(cut):
            iy, ix, core, _ = geo.place()
            begin, count = self.cuts[cut]
            cols = pl.ds(begin, count)
            for m in mats:
                bufs = buffers[5 * m : 5 * m + 5]
                along(cut, m).arrive()
                total = bufs[0][0, iy, ix, core, :, cols].astype(F32)
                for r in range(1, groups):
                    total = total + bufs[4][r, :, cols].astype(F32)
                outs[m][:, cols] = total

        def end():
            for m in mats:
                for k in range(len(self.chunks)):
                    leave([cross(k, m)] + near(k, m) + far(k, m))
                for cut in range(len(self.cuts)):
                    along(cut, m).leave()

        count = range(len(self.chunks))
        return dict(
            begin=[partial(begin, k) for k in count],
            one=[partial(level_one, k) for k in count],
            two=[partial(level_two, k) for k in count],
            three=[partial(level_three, k) for k in count],
            final=[partial(final, cut) for cut in range(len(self.cuts))],
            end=[end],
        )


class Spread:
    def __init__(self, geo, value, plane=False, part=None, into=None):
        self.geo, self.plane, self.part = geo, plane, part
        self.peers = geo.plane() if plane else geo.column()
        self.inputs = [] if plane else [(value, "once")]
        self.outputs = [((len(self.peers) + 1,) + value.shape, value.dtype, "any")]
        self.aliases = {}
        if into is not None:
            self.inputs.append((into, "any"))
            self.aliases = {1: 0}
        sems = pltpu.SemaphoreType.DMA((len(self.peers) + 1,))
        self.scratch = [sems, sems, pltpu.SemaphoreType.DMA]
        if plane:
            self.scratch.append(pltpu.VMEM(value.shape, value.dtype))

    def tasks(self, values, outs, scratch):
        geo, out, (send, recv, local) = self.geo, outs[0], scratch[:3]
        dp, h = geo.device()
        if self.plane:
            self.source = scratch[3]
            move = Mover(geo, send, recv)
            copies = [move(str(to), self.source, out.at[dp], **back(to)) for to in self.peers]
            mine = pltpu.make_async_copy(self.source, out.at[dp], local)

            def begin():
                start(copies)
                mine.start()

            def end():
                mine.wait()
                arrive(copies)
                leave(copies)

            return [begin, end]
        rows = pl.ds(*self.part) if self.part else pl.ds(0, out.shape[1])
        value = values[0].at[rows]
        slot = lambda r: out.at[lax.rem(h + r, geo.groups), rows]
        column = Column(geo, value, slot, send, recv, 0, True)

        def begin_column():
            column.begin()
            pltpu.make_async_copy(value, slot(0), local).start()

        def end_column():
            pltpu.make_async_copy(value, slot(0), local).wait()
            column.arrive()
            column.leave()

        return [begin_column, column.relay, end_column]


class Deal:
    def __init__(self, geo, value):
        self.geo, self.peers = geo, geo.column()
        self.rows = value.shape[1] // geo.groups
        self.inputs = [(value, "any")]
        shape = (geo.groups - 1, value.shape[0], self.rows, value.shape[2])
        self.outputs = [(shape, value.dtype, "any")]
        sems = pltpu.SemaphoreType.DMA((geo.groups - 1,))
        self.scratch = [sems, sems]

    def tasks(self, values, outs, scratch):
        geo = self.geo
        move = Mover(geo, *scratch)
        copies = []
        for r in range(1, geo.groups):
            first = pl.multiple_of(geo.place(z=-r)[3] * self.rows, self.rows)
            copies.append(move(r, values[0].at[:, pl.ds(first, self.rows), :], outs[0].at[r - 1], z=-r))

        def end():
            arrive(copies)
            leave(copies)

        return [lambda: start(copies), end]


class Fold:
    def __init__(self, geo, items):
        self.geo, self.peers = geo, geo.plane() + geo.column()
        self.inputs = [(item[0], "full") for item in items]
        self.picks = [item[1:] for item in items]
        rows = sum(stop - first for _, (first, stop), _ in self.picks)
        self.rows = -(-rows // 8) * 8
        self.outputs = [((self.rows, 128), F32, "full")]
        near, far = pltpu.SemaphoreType.DMA((geo.ndp - 1,)), pltpu.SemaphoreType.DMA((geo.groups - 1,))
        wide = pltpu.VMEM((geo.ndp, geo.groups, self.rows, 128), F32)
        slim = pltpu.VMEM((geo.groups, self.rows, 128), F32)
        self.scratch = [near, near, far, far, wide, wide, slim, slim]

    def tasks(self, values, outs, scratch):
        geo = self.geo
        near_send, near_recv, far_send, far_recv, packed, landed, middle, last = scratch
        groups, ndp = geo.groups, geo.ndp
        to_plane, to_column = Mover(geo, near_send, near_recv), Mover(geo, far_send, far_recv)
        dp, h = geo.device()
        near, far = [], []
        for to in geo.plane():
            there, _ = geo.device(**to)
            near.append(to_plane(str(to), packed.at[there], landed.at[dp], **to))
        for r in range(1, groups):
            far.append(to_column(r, middle.at[r], last.at[h], z=r))

        def begin():
            packed[...] = jnp.zeros_like(packed)
            row = 0
            for value, (grouped, (low, high), (first, stride, cols)) in zip(values, self.picks):
                for r in range(groups):
                    for d in range(ndp):
                        lanes = slice(first + d * stride, first + d * stride + cols)
                        part = value[r, low:high, lanes] if grouped else value[low:high, lanes]
                        packed[d, r, row : row + high - low, :cols] = part
                row += high - low
            start(near)

        def fold():
            landed[dp] = packed[dp]
            arrive(near)
            total = landed[0]
            for d in range(1, ndp):
                total = total + landed[d]
            middle[...] = total
            start(far)

        def end():
            last[h] = middle[0]
            arrive(far)
            total = last[0]
            for z in range(1, groups):
                total = total + last[z]
            outs[0][...] = total
            leave(near)
            leave(far)

        return [begin, fold, end]


def norm_forward(before, gain, shift):
    center = before - jnp.mean(before, -1, keepdims=True)
    spread = jnp.mean(center * center, -1, keepdims=True)
    return center * lax.rsqrt(spread + EPS) * gain + shift


def norm_backward(before, gain, grad):
    center = before - jnp.mean(before, -1, keepdims=True)
    rate = lax.rsqrt(jnp.mean(center * center, -1, keepdims=True) + EPS)
    hat = center * rate
    grad_hat = grad * gain
    mean_one = jnp.mean(grad_hat, -1, keepdims=True)
    mean_two = jnp.mean(grad_hat * hat, -1, keepdims=True)
    grad_before = rate * (grad_hat - mean_one - hat * mean_two)
    return (
        grad_before,
        jnp.sum(grad * hat, 0, keepdims=True),
        jnp.sum(grad, 0, keepdims=True),
        jnp.sum(grad_before, 0, keepdims=True),
    )


BIAS_ONE, BIAS_TWO, GAIN_ONE, GAIN_TWO, SHIFT_ONE, SHIFT_TWO = range(6)


class Window:
    def __init__(self, size, rows, groups):
        self.seqs, self.seq_len, self.heads, self.head_size = size
        self.rows, self.groups = rows, groups
        self.block = self.seq_len // groups
        self.mid_rows = 2 * self.block
        h = lax.axis_index("head")
        self.h = h
        self.first = lax.div(h * (self.seqs - 1), groups)
        self.base = self.first * self.seq_len
        self.own = h * rows - self.base
        pair = h + 1 - 2 * lax.rem(h, 2)
        self.pair = pair * rows - self.base
        self.mid = lax.rem(h, 2) * (2 * rows)
        self.mid_row = lax.rem(h, 2) * self.block
        self.middle = (h > 0) & (h < groups - 1)
        dp = lax.axis_index("dp")
        self.to_pair = (dp, pair)
        self.to_mid = (dp, groups - 1 - h)

    def at(self, begin, rows):
        return pl.ds(pl.multiple_of(begin, self.block), rows)

    def loc(self, piece):
        return lax.div((self.h * (self.rows // self.block) + piece) * self.block, self.seq_len) - self.first

    def keys(self, piece):
        return pl.ds(pl.multiple_of(self.loc(piece) * self.seq_len, self.seq_len), self.seq_len)


def remote(src, dst, sems, to):
    return pltpu.make_async_remote_copy(
        src_ref=src, dst_ref=dst, send_sem=sems.at[0], recv_sem=sems.at[1], device_id=to, device_id_type=MESH
    )


def add_up(r, total, part):
    @pl.when(r == 0)
    def _():
        total[...] = part

    @pl.when(r > 0)
    def _():
        total[...] += part


def gelu_parts(unit):
    square = unit * unit
    bent = jnp.tanh(GELU_C * unit * (1.0 + GELU_K * square))
    half = 0.5 * (1.0 + bent)
    slope = half + 0.5 * unit * (1.0 - bent * bent) * (GELU_C * (1.0 + 3.0 * GELU_K * square))
    return unit * half, slope


def vector(vecs, layer, which):
    row = 2 * layer + which % 2
    return vecs[which // 2][row : row + 1, :]


def row_mask(window, lengths):
    block, parts = window.block, []
    for piece in range(window.rows // block):
        place = lax.rem((window.h * (window.rows // block) + piece) * block, window.seq_len)
        inside = lax.broadcasted_iota(jnp.int32, (block, 1), 0) + place < lengths[window.first + window.loc(piece)]
        parts.append(jnp.where(inside, 1.0, 0.0))
    return jnp.concatenate(parts, 0)


def attend(window, layer, xin, offset, row, lengths, left, right, outs, turned, total, r, point):
    kv_out, q_out, ctx_out, lse_out, gated_out = outs
    seq_len, heads, head_size, block, rows = (
        window.seq_len,
        window.heads,
        window.head_size,
        window.block,
        window.rows,
    )
    width = heads * head_size
    point(0)
    kv = nn(xin[window.at(offset, 2 * seq_len), :], left) + row[:, 2 * width :]
    kv_out[0] = kv.astype(LOW)
    query = (nn(xin[window.at(offset + window.own, rows), :], right[:, :width]) + row[:, :width]).astype(LOW)
    q_out[0] = query
    scaled = query * jnp.asarray(0.125, LOW)
    for piece in range(rows // block):
        mine = slice(piece * block, (piece + 1) * block)
        keys = window.keys(piece)
        length = lengths[window.first + window.loc(piece)]
        unused = jnp.where(lax.broadcasted_iota(jnp.int32, (seq_len, block), 0) < length, 0.0, -1e30)
        for head in range(heads):
            lanes = slice(head * head_size, (head + 1) * head_size)
            scores = nt(kv_out[0, keys, lanes], scaled[mine, lanes]) + unused
            largest = jnp.max(scores, 0, keepdims=True)
            powers = jnp.exp(scores - largest)
            sums = jnp.sum(powers, 0, keepdims=True)
            value = kv_out[0, keys, width + head * head_size : width + (head + 1) * head_size]
            turned[lanes, mine] = tn(value, powers.astype(LOW)) / sums
            lse_out[0, head : head + 1, mine] = largest + jnp.log(sums)
            point(1 + piece * heads + head)
    context = turned[...].T
    ctx_out[0] = context
    gated = (context * row[:, width : 2 * width]).astype(LOW)
    gated_out[0] = gated
    add_up(r, total, nt(gated, right[:, width:]))


def forward(size, layers, geo, gather, counter, lists, *refs):
    seqs, seq_len, heads, head_size = size
    refs = list(refs)
    take = lambda n: [refs.pop(0) for _ in range(n)]
    hidden = refs.pop(0)
    vec = take(3)
    lengths, unit_noise, unit_alpha, head_noise, head_alpha, inner_bias, qv_bias = take(7)
    key_value, query_output, inner, outer, map_own = take(5)
    saved = [take(10) for _ in range(layers)]
    win_out, small_out = take(2)
    left_buf, right_buf, inner_buf, outer_buf, load_sems, back_sems = take(6)
    total, middle, current, low, xwin, small, small_own, small_send, small_recv, map_stage, turned = take(11)
    pair_sems, mid_sems, local = take(3)
    gather_tasks, count_tasks, deal_tasks, (weights,) = lists
    groups = geo.groups
    rows, model = total.shape
    window = Window(size, rows, groups)
    mid_rows, width = window.mid_rows, heads * head_size
    s = pl.program_id(0)
    r = lax.rem(s, groups)
    slot = lax.rem(r, 2)
    spots_attn, spots_feed = 2 + rows // window.block * heads, 4
    plan = Plan(([spots_attn] * groups + [spots_feed] * groups) * layers)

    small_column = Column(geo, small_own, lambda i: small.at[i], small_send, small_recv, 0)
    keep_small = pltpu.make_async_copy(small, small_out, local.at[2])

    def small_begin():
        small_column.begin()

    def small_end():
        small_column.relay()
        small_column.arrive()
        small_column.leave()
        keep_small.start()

    into_stage = pltpu.make_async_copy(map_own.at[0], map_stage, local.at[3])
    out_of_stage = pltpu.make_async_copy(map_stage, weights[-1].at[0], local.at[4])

    def stage_begin():
        into_stage.start()

    def stage_end():
        into_stage.wait()
        out_of_stage.start()

    phases = 2 * layers
    plan.even([small_begin] + [count_tasks[0]], 0, 0)
    ends, done = [], 0
    for phase in range(phases):
        for chunk, halves in enumerate(gather.chunks):
            if halves[0][0] // 2 == phase:
                done = gather.done[chunk]
        ends.append(done)
    first, begun = 0, 0
    for phase in range(phases):
        last = plan.slot(phase * groups, -1)
        plan.even(gather_tasks[begun : ends[phase]], first, last)
        first, begun = last, ends[phase]
        if phase == 0:
            plan.even([small_end, stage_begin], last, last)
            plan.even([count_tasks[1]], plan.slot(groups, 0), plan.slot(groups, 0))
            plan.even([stage_end], plan.slot(groups, 1), plan.slot(groups, 1))
        if phase == 2:
            plan.even([deal_tasks[0]], last, last)
    closing = len(plan.slots) - 1
    plan.even(gather_tasks[begun:], first, closing)
    plan.even([deal_tasks[1]], closing, closing)

    kinds = [(left_buf, right_buf), (inner_buf, outer_buf)]
    sources = [(key_value, query_output), (inner, outer)]

    def own_loads(phase):
        layer, kind = phase // 2, phase % 2
        return [
            pltpu.make_async_copy(src.at[layer], buf.at[0], load_sems.at[kind, side, 0])
            for side, (src, buf) in enumerate(zip(sources[kind], kinds[kind]))
        ]

    def own_backs(phase):
        kind = phase % 2
        return [
            pltpu.make_async_copy(buf.at[0], weights[2 * phase + side].at[0], back_sems.at[kind, side])
            for side, buf in enumerate(kinds[kind])
        ]

    def loads(phase, group, into):
        kind = phase % 2
        return [
            pltpu.make_async_copy(weights[2 * phase + side].at[group], buf.at[into], load_sems.at[kind, side, into])
            for side, buf in enumerate(kinds[kind])
        ]

    @pl.when(s == 0)
    def _():
        start(own_loads(0))
        total_length = lengths[0]
        for index in range(1, seqs):
            total_length = total_length + lengths[index]
        counter.source[...] = jnp.full(counter.source.shape, total_length, jnp.int32).astype(F32)
        small_own[...] = jnp.zeros_like(small_own)
        open_unit = gate_open(unit_noise[...], unit_alpha[...])
        open_head = gate_open(head_noise[...], head_alpha[...])
        for layer in range(layers):
            own = slice(layer, layer + 1)
            place = slice(4 * layer, 4 * layer + 1)
            small_own[place, :] = open_unit[own]
            small_own[4 * layer + 1 : 4 * layer + 2, :] = inner_bias[own, :]
            place = slice(4 * layer + 2, 4 * layer + 3)
            small_own[place, :width] = qv_bias[2 * layer : 2 * layer + 1, :]
            for head in range(heads):
                begin = width + head * head_size
                small_own[place, begin : begin + head_size] = jnp.broadcast_to(
                    open_head[own, head : head + 1], (1, head_size)
                )
            small_own[place, 3 * width :] = qv_bias[2 * layer + 1 : 2 * layer + 2, :]
        small[0] = small_own[...]

    def before(phase):
        @pl.when(r == 0)
        def _():
            if phase + 1 < phases:
                start(own_loads(phase + 1))
            for copy in own_loads(phase):
                copy.wait()
            start(own_backs(phase))

        @pl.when(r > 0)
        def _():
            for copy in loads(phase, r, slot):
                copy.wait()

        @pl.when((r > 0) & (r < groups - 1))
        def _():
            start(loads(phase, r + 1, 1 - slot))

    def behind(phase):
        @pl.when(r == 0)
        def _():
            for copy in own_backs(phase):
                copy.wait()
            start(loads(phase, 1, 1))

    def flat(buf):
        value = buf[slot]
        return value.reshape(model, value.shape[-1])

    own_place = xwin.at[window.at(window.own, rows)]
    to_pair = remote(low, own_place, pair_sems, window.to_pair)
    to_mid = remote(
        low.at[window.at(window.mid_row, mid_rows)],
        xwin.at[window.at((1 - lax.rem(window.h, 2)) * 2 * rows, mid_rows)],
        mid_sems,
        window.to_mid,
    )
    keep_win = pltpu.make_async_copy(xwin, win_out, local.at[0])

    for phase in range(phases):
        layer, kind = phase // 2, phase % 2
        kv_out, q_out, ctx_out, lse_out, gated_out, before_one, middle_low, unit_out, before_two, low_out = saved[layer]
        span = range(phase * groups, (phase + 1) * groups)

        def point(spot, span=span):
            plan.point(s, spot, span)

        @pl.when(lax.div(s, groups) == phase)
        def _():
            if kind == 0:
                if layer:

                    @pl.when(r == 0)
                    def _():
                        to_pair.wait()

                        @pl.when(window.middle)
                        def _():
                            to_mid.wait()

                        keep_win.start()

                before(phase)
                xin, offset = (xwin, 0) if layer else (hidden, window.base)
                row = small[r, 4 * layer + 2 : 4 * layer + 3, :]
                outs = (kv_out, q_out, ctx_out, lse_out, gated_out)
                attend(
                    window,
                    layer,
                    xin,
                    offset,
                    row,
                    lengths,
                    flat(left_buf),
                    flat(right_buf),
                    outs,
                    turned,
                    total,
                    r,
                    point,
                )

                @pl.when(r == groups - 1)
                def _():
                    if layer:
                        resid = current[...]
                    else:
                        resid = hidden[window.at(offset + window.own, rows), :].astype(F32)
                    value = resid + total[...] + vector(vec, layer, BIAS_ONE)
                    normed = norm_forward(value, vector(vec, layer, GAIN_ONE), vector(vec, layer, SHIFT_ONE))
                    before_one[...] = value
                    middle[...] = normed
                    middle_low[...] = normed.astype(LOW)

                point(spots_attn - 1)
                behind(phase)
            else:
                before(phase)
                point(0)
                unit = nn(middle_low[...], flat(inner_buf)) + small[r, 4 * layer + 1 : 4 * layer + 2, :]
                unit_out[0] = unit.astype(LOW)
                point(1)
                bent = jnp.tanh(GELU_C * unit * (1.0 + GELU_K * (unit * unit)))
                active = (0.5 * unit * (1.0 + bent) * small[r, 4 * layer : 4 * layer + 1, :]).astype(LOW)
                point(2)
                add_up(r, total, nn(active, flat(outer_buf)))

                @pl.when(r == groups - 1)
                def _():
                    value = middle[...] + total[...] + vector(vec, layer, BIAS_TWO)
                    normed = norm_forward(value, vector(vec, layer, GAIN_TWO), vector(vec, layer, SHIFT_TWO))
                    before_two[...] = value
                    low_out[...] = normed.astype(LOW)
                    if layer + 1 < layers:
                        current[...] = normed
                        low[...] = normed.astype(LOW)
                        to_pair.start()

                        @pl.when(window.middle)
                        def _():
                            to_mid.start()

                        xwin[window.at(window.own, rows), :] = normed.astype(LOW)

                        @pl.when(jnp.logical_not(window.middle))
                        def _():
                            empty = window.at(lax.rem(window.h + 1, 2) * 2 * rows, mid_rows)
                            xwin[empty, :] = jnp.zeros((mid_rows, model), LOW)

                point(spots_feed - 1)
                behind(phase)

    @pl.when(s == phases * groups - 1)
    def _():
        keep_win.wait()
        keep_small.wait()
        out_of_stage.wait()


def match_teacher(size, layers, tokens, point, *refs):
    refs = list(refs)
    states = [refs.pop(0) for _ in range(layers)]
    target, chosen, lengths, counts, weight = refs[:5]
    back_outs, (loss_out, grad_out) = refs[5 : 5 + layers], refs[5 + layers :]
    r = pl.program_id(0)
    rows = states[0].shape[0]

    @pl.when(r == 0)
    def _():
        loss_out[...] = jnp.zeros_like(loss_out)
        for back_out in back_outs:
            back_out[...] = jnp.zeros_like(back_out)

    count = jnp.sum(counts[...][:, 0:1, 0:1], 0)
    factor = tokens / count
    mine = pl.ds(pl.multiple_of(lax.axis_index("head") * rows, rows), rows)
    row_ok = row_mask(Window(size, rows, pl.num_programs(0)), lengths)
    total = None
    for layer in range(layers):
        goal = jnp.where(r == 0, chosen[layer, mine, :], target[0, layer]).astype(F32)
        miss = (nn(states[layer][...], weight[0]) - goal) * row_ok
        loss_out[:1, :1] += jnp.sum(jnp.sum(miss * miss, 0, keepdims=True), 1, keepdims=True)
        low = (factor * miss).astype(LOW)
        back_outs[layer][...] += nt(low, weight[0])
        grad = tn(states[layer][...], low)
        total = grad if total is None else total + grad
    grad_out[0] = total.astype(LOW)


FEED_STEP, ATTN_STEP, WEIGHT_STEP = 5.0, 6.5, 3.0


def in_order(s):
    place = jnp.clip(s, 0, len(ORDER) - 1)
    group = 0
    for index, value in enumerate(ORDER):
        group = jnp.where(place == index, value, group)
    return group


def layer_backward(size, layer, first, last, geo, reduce, times, lists, *refs):
    seqs, seq_len, heads, head_size = size
    refs = list(refs)
    take = lambda n: [refs.pop(0) for _ in range(n)]
    before_two, before_one, middle_low, unit_in, small = take(5)
    vec = take(3)
    inner, outer = take(2)
    grad_refs = take(2 if last else 1)
    xwin, query_in, kv, ctx, lse, gated, lengths, left, right = take(9)
    extra = None if first else refs.pop(0)
    left_out, right_out, grad_out, head_vec, vec_out, unit_vec = take(6)
    (mine, feed, attn, grad_kv, turned, kv_all, q_all, spread, pair_low, pair_got, mid_low, mid_got) = take(12)
    pair_sems, mid_sems, local = take(3)
    work, riders = lists[0], lists[1:]
    groups = geo.groups
    s = pl.program_id(0)
    r = lax.rem(s, groups)
    part = lax.div(s, groups)
    width = heads * head_size
    rows, model = mine.shape
    window = Window(size, rows, groups)
    block, mid_rows = window.block, window.mid_rows
    blocks = rows // block
    offset = window.base if first else 0
    here = window.at(offset + window.own, rows)
    to_pair = remote(pair_low, pair_got, pair_sems, window.to_pair)
    to_mid = remote(mid_low, mid_got, mid_sems, window.to_mid)

    spots = [7] * groups + [2 + blocks * heads] * groups + [4] * groups
    lengths_us = [FEED_STEP] * groups + [ATTN_STEP] * groups + [WEIGHT_STEP] * groups
    plan = Plan(spots)
    whole = sum(lengths_us)
    cuts = len(reduce.cuts)
    timed = []
    first_one, pace, second, third = times
    ones = [
        max(FEED_STEP * (k // cuts + 1) + 4.5, first_one + pace * k) + 0.01 * (k % cuts)
        for k in range(len(reduce.chunks))
    ]
    for k in range(len(reduce.chunks)):
        made = FEED_STEP * (k // cuts + 1) - 0.5 + 0.01 * (k % cuts)
        if k >= reduce.ring:
            made = max(made, ones[k - reduce.ring] + 0.1)
        timed.append((made, work["begin"][k]))
        timed.append((max(ones[k], made + 3.0), work["one"][k]))
        timed.append((ones[k] + second, work["two"][k]))
        timed.append((ones[k] + second + third, work["three"][k]))
    timed += [(1e6, task) for task in work["final"] + work["end"]]
    for finish, tasks in riders:
        count = max(1, len(tasks) - 1)
        timed += [(finish * whole * index / count, task) for index, task in enumerate(tasks)]
    plan.timed(lengths_us, timed)

    def points(span):
        return lambda spot: plan.point(s, spot, span)

    point_feed = points(range(groups))
    point_attn = points(range(groups, 2 * groups))
    point_weight = points(range(2 * groups, 3 * groups))

    def feeding():
        point_feed(0)
        unit = in_order(s)

        @pl.when(r == 0)
        def _():
            if last:
                cotangent, back = grad_refs
                own = pl.ds(pl.multiple_of(window.h * rows, rows), rows)
                fetch = pltpu.make_async_copy(cotangent.at[own], pair_low, local)
                fetch.start()
                fetch.wait()
                grad = pair_low[...].astype(F32) + back[...]
            else:
                grad = grad_refs[0][...]
            grad_before, grad_gain, grad_shift, grad_bias = norm_backward(
                before_two[...], vector(vec, layer, GAIN_TWO), grad
            )
            vec_out[BIAS_TWO : BIAS_TWO + 1, :] = grad_bias
            vec_out[GAIN_TWO : GAIN_TWO + 1, :] = grad_gain
            vec_out[SHIFT_TWO : SHIFT_TWO + 1, :] = grad_shift
            feed[...] = grad_before.astype(LOW)
            mine[...] = grad_before

        grad_active = nt(feed[...], outer[0])
        point_feed(1)
        value, slope = gelu_parts(unit_in[0].astype(F32))
        opened = small[0, 4 * layer : 4 * layer + 1, :]
        grad_unit = (grad_active * (slope * opened)).astype(LOW)
        unit_vec[0, 0:1, :] = jnp.sum(grad_unit.astype(F32), 0, keepdims=True)
        unit_vec[0, 1:2, :] = jnp.sum(grad_active * value, 0, keepdims=True)
        active = (value * opened).astype(LOW)
        point_feed(2)
        mine[...] += nt(grad_unit, inner[0])
        point_feed(3)
        shape = reduce.grads[0].shape[1:]
        reduce.grads[0][unit] = tn(middle_low[...], grad_unit).astype(LOW).reshape(shape)
        point_feed(4)
        reduce.grads[1][unit] = tn(feed[...], active).astype(LOW).reshape(shape)
        point_feed(5)

        @pl.when(r == groups - 1)
        def _():
            grad_before, grad_gain, grad_shift, grad_bias = norm_backward(
                before_one[...], vector(vec, layer, GAIN_ONE), mine[...]
            )
            vec_out[BIAS_ONE : BIAS_ONE + 1, :] = grad_bias
            vec_out[GAIN_ONE : GAIN_ONE + 1, :] = grad_gain
            vec_out[SHIFT_ONE : SHIFT_ONE + 1, :] = grad_shift
            mine[...] = grad_before if first else grad_before + extra[...]
            attn[...] = grad_before.astype(LOW)
            spread[...] = jnp.zeros_like(spread)

        point_feed(6)

    def attending():
        point_attn(0)
        row = small[0, 4 * layer + 2 : 4 * layer + 3, :]
        opened = row[:, width : 2 * width]
        grad_gated = nn(attn[...], right[0, :, width:])
        shared = grad_gated * ctx[0]
        grad_ctx = (grad_gated * opened).astype(LOW)
        pulled = shared * opened
        scaled = query_in[0] * jnp.asarray(0.125, LOW)
        grad_kv[...] = jnp.zeros_like(grad_kv)
        pulled_turned = pulled.T
        for piece in range(blocks):
            rows_of = slice(piece * block, (piece + 1) * block)
            keys = window.keys(piece)
            length = lengths[window.first + window.loc(piece)]
            unused = jnp.where(lax.broadcasted_iota(jnp.int32, (seq_len, block), 0) < length, 0.0, -1e30)
            for head in range(heads):
                lanes = slice(head * head_size, (head + 1) * head_size)
                later = slice(width + head * head_size, width + (head + 1) * head_size)
                key = kv[0, keys, lanes]
                scores = nt(key, scaled[rows_of, lanes]) + unused
                chances = jnp.exp(scores - lse[0, head : head + 1, rows_of])
                grad_chances = nt(kv[0, keys, later], grad_ctx[rows_of, lanes])
                delta = jnp.sum(pulled_turned[lanes, rows_of], 0, keepdims=True)
                grad_scores = (chances * (grad_chances - delta)).astype(LOW)
                turned[lanes, rows_of] = tn(key, grad_scores)
                grad_kv[keys, lanes] += nn(grad_scores, scaled[rows_of, lanes])
                grad_kv[keys, later] += nn(chances.astype(LOW), grad_ctx[rows_of, lanes])
                point_attn(1 + piece * heads + head)
        query_low = (turned[...].T * 0.125).astype(LOW)
        kv_low = grad_kv[...].astype(LOW)
        q_all[r] = query_low
        kv_all[r] = kv_low
        head_vec[0, 0:1, :width] = jnp.sum(query_low.astype(F32), 0, keepdims=True)
        head_vec[0, 0:1, 2 * width :] = jnp.sum(kv_low.astype(F32), 0, keepdims=True)
        shared_sum = jnp.sum(shared, 0, keepdims=True)
        lane = lax.broadcasted_iota(jnp.int32, (1, 128), 1)
        by_head = jnp.zeros((1, 128), F32)
        for head in range(heads):
            one = jnp.sum(shared_sum[:, head * head_size : (head + 1) * head_size], 1, keepdims=True)
            by_head = jnp.where(lane == head, one, by_head)
        head_vec[0, 1:2, :128] = by_head
        spread[...] += nt(kv_low, left[0])
        mine[...] += nt(query_low, right[0, :, :width])

        @pl.when(r == groups - 1)
        def _():
            pair_low[...] = spread[window.at(window.pair, rows), :].astype(LOW)
            to_pair.start()

            @pl.when(window.middle)
            def _():
                mid_low[...] = spread[window.at(window.mid, mid_rows), :].astype(LOW)
                to_mid.start()

        point_attn(1 + blocks * heads)

    def weighing():
        point_weight(0)
        left_out[0] = tn(xwin[window.at(offset, 2 * seq_len), :], kv_all[r]).astype(LOW)
        point_weight(1)
        right_out[0, :, :width] = tn(xwin[here, :], q_all[r]).astype(LOW)
        point_weight(2)
        right_out[0, :, width:] = tn(attn[...], gated[0]).astype(LOW)

        @pl.when(r == groups - 1)
        def _():
            to_pair.wait()
            mine[...] += spread[window.at(window.own, rows), :] + pair_got[...].astype(F32)

            @pl.when(window.middle)
            def _():
                to_mid.wait()
                mine[window.at(window.mid_row, mid_rows), :] += mid_got[...].astype(F32)

            grad_out[...] = mine[...].astype(grad_out.dtype)

        point_weight(3)

    pl.when(part == 0)(feeding)
    pl.when(part == 1)(attending)
    pl.when(part == 2)(weighing)


def on_device(
    ndp,
    groups,
    hidden_in,
    seq_lengths,
    layer_map,
    teacher_states,
    out_cotangent,
    query_weight,
    key_weight,
    value_weight,
    query_value_bias,
    output_weight,
    branch_bias,
    norm_gain,
    norm_shift,
    inner_weight,
    inner_bias,
    outer_weight,
    head_alpha,
    head_noise,
    unit_alpha,
    unit_noise,
    map_weight,
):
    tokens_dev, model = hidden_in.shape
    seqs_dev = seq_lengths.shape[0]
    seq_len = tokens_dev // seqs_dev
    width = query_weight.shape[2]
    units = inner_weight.shape[2]
    layers, heads = head_alpha.shape
    head_size = width // heads
    rows = tokens_dev // groups
    feats = model // ndp
    geo = Geometry(ndp, groups)
    size = (seqs_dev, seq_len, heads, head_size)
    window = Window(size, rows, groups)
    blocks = rows // window.block
    dp = lax.axis_index("dp")

    def slices(array):
        return array.reshape(array.shape[0], geo.size_y, geo.size_x, 2, feats, array.shape[-1])

    def matrices(arrays):
        return [(array.reshape(groups, model, array.shape[-1]), "group") for array in arrays]

    def pairs(cols, steps, m=0):
        out, begin = [], 0
        for step in steps:
            out.append([(m, begin, step, False), (m + 1, begin, step, True)])
            begin += step
        return out if begin == cols else [[(m, 0, cols, False), (m + 1, 0, cols, True)]]

    key_value = slices(jnp.concatenate([key_weight, value_weight], 2))
    query_output = slices(jnp.concatenate([query_weight, jnp.swapaxes(output_weight, 1, 2)], 2))
    inner, outer = slices(inner_weight), slices(outer_weight)

    _, unit_back = jax.vjp(partial(gate_open, unit_noise), unit_alpha)
    _, head_back = jax.vjp(partial(gate_open, head_noise), head_alpha)
    (unit_slope,) = unit_back(jnp.ones_like(unit_alpha))
    (head_slope,) = head_back(jnp.ones_like(head_alpha))
    small = jax.ShapeDtypeStruct((4 * layers, units), F32)
    vec = [(array.reshape(2 * layers, model), "once") for array in (branch_bias, norm_gain, norm_shift)]
    count = jax.ShapeDtypeStruct((8, 128), F32)
    chosen = jnp.stack(
        [lax.dynamic_index_in_dim(teacher_states, layer_map[layer], 0, keepdims=False) for layer in range(layers)]
    )

    row_block = pltpu.VMEM((rows, model), F32)
    low_block = pltpu.VMEM((rows, model), LOW)
    mid_block = pltpu.VMEM((window.mid_rows, model), LOW)
    two = pltpu.SemaphoreType.DMA((2,))
    owns, chunks = [], []
    for layer in range(layers):
        for arrays, cuts in (((key_value, query_output), ATTN_CUTS), ((inner, outer), FEED_CUTS)):
            chunks += pairs(arrays[0].shape[-1], cuts, len(owns))
            owns += [(array, layer) for array in arrays]
    chunks.append([(len(owns), 0, width, False)])
    map_slices = slices(map_weight[None])
    owns.append((map_slices, 0))
    gather = Gather(geo, owns, chunks)
    counter = Spread(geo, count, plane=True)
    outputs = []
    for layer in range(layers):
        attn_step = lambda s, layer=layer: jnp.clip(s - 2 * layer * groups, 0, groups - 1)
        feed_step = lambda s, layer=layer: jnp.clip(s - (2 * layer + 1) * groups, 0, groups - 1)
        outputs += [
            ((groups, 2 * seq_len, 2 * width), LOW, attn_step),
            ((groups, rows, width), LOW, attn_step),
            ((groups, rows, width), F32, attn_step),
            ((groups, 8, rows), F32, attn_step),
            ((groups, rows, width), LOW, attn_step),
            ((rows, model), F32, "full"),
            ((rows, model), LOW, "full"),
            ((groups, rows, units), LOW, feed_step),
            ((rows, model), F32, "full"),
            ((rows, model), LOW, "full"),
        ]
    saves = len(outputs) // layers
    outputs += [((2 * seq_len, model), LOW, "any"), ((groups,) + small.shape, F32, "any")]
    attn_buf = pltpu.VMEM((2,) + key_value.shape[1:], LOW)
    feed_buf = pltpu.VMEM((2,) + inner.shape[1:], LOW)
    others = pltpu.SemaphoreType.DMA((groups,))
    got = run(
        partial(forward, size, layers, geo, gather, counter),
        2 * layers * groups,
        [
            (hidden_in, "once"),
            *vec,
            (seq_lengths, "smem"),
            (unit_noise, "once"),
            (unit_alpha, "once"),
            (head_noise, "once"),
            (head_alpha, "once"),
            (inner_bias, "once"),
            (query_value_bias.reshape(2 * layers, width), "once"),
            (key_value, "any"),
            (query_output, "any"),
            (inner, "any"),
            (outer, "any"),
            (map_slices, "any"),
        ],
        outputs,
        [
            attn_buf,
            attn_buf,
            feed_buf,
            feed_buf,
            pltpu.SemaphoreType.DMA((2, 2, 2)),
            pltpu.SemaphoreType.DMA((2, 2)),
            row_block,
            row_block,
            row_block,
            low_block,
            pltpu.VMEM((2 * seq_len, model), LOW),
            pltpu.VMEM((groups,) + small.shape, F32),
            pltpu.VMEM(small.shape, F32),
            others,
            others,
            pltpu.VMEM(map_slices.shape[1:], LOW),
            pltpu.VMEM((width, rows), F32),
            two,
            two,
            pltpu.SemaphoreType.DMA((5,)),
        ],
        30e9,
        "forward",
        [gather, counter, Deal(geo, chosen), Lend(geo, gather)],
        1,
        1,
        True,
    )
    records = [got[layer * saves : (layer + 1) * saves] for layer in range(layers)]
    xwins, small = [hidden_in, got[layers * saves]], got[layers * saves + 1]
    *weights, counts, target = got[layers * saves + 2 :]
    weights = matrices(weights)
    lows = [record[-1] for record in records]
    *spread, loss, grad_map = run(
        partial(match_teacher, size, layers, float(tokens_dev * ndp)),
        groups,
        [(low, "full") for low in lows]
        + [(target, lambda r: jnp.maximum(r - 1, 0)), (chosen, "full"), (seq_lengths, "smem"), (counts, "full")]
        + weights[-1:],
        [
            *[((rows, model), F32, "full")] * layers,
            ((8, 128), F32, "full"),
            ((groups, model, width), LOW, "group"),
        ],
        [],
        4e9,
        "match_teacher",
    )

    grads = [(out_cotangent, "any"), (spread[-1], "once")]
    results = [{} for _ in range(layers)]
    riders, waiting, finishes = [], [], []

    def settle(got):
        for (layer, name), value in zip(waiting, got):
            results[layer][name] = value

    def clipped(part):
        return lambda s: jnp.clip(s - part * groups, 0, groups - 1)

    block_out = None
    riders = [Scatter(geo, [slices(grad_map)], [[(0, 0, width, False)]])]
    waiting, finishes = [(0, "map")], [0.7]
    for layer in reversed(range(layers)):
        kv, query, ctx, lse, gated, before_one, middle_low, unit_in, before_two, _ = records[layer]
        attn_weights, feed_weights = weights[4 * layer : 4 * layer + 2], weights[4 * layer + 2 : 4 * layer + 4]
        if layer in (0, layers - 1):
            part = (0, rows // 2) if layer else (rows // 2, rows // 2)
            riders.append(Spread(geo, lows[-1], part=part, into=block_out))
            waiting.append((0, "block_out"))
            finishes.append(1.0)
        reduce = Reduce(geo, [(feats, units)] * 2, BACK_CUTS)
        left, right, grad, head_vec, vec_out, unit_vec, *got = run(
            partial(
                layer_backward,
                size,
                layer,
                layer == 0,
                layer == layers - 1,
                geo,
                reduce,
                TIMES_LAST if layer == layers - 1 else TIMES,
            ),
            3 * groups,
            [
                (before_two, "once"),
                (before_one, "once"),
                (middle_low, "once"),
                (unit_in, in_order),
                (small, lambda s: jnp.where(s < groups, in_order(s), lax.rem(s, groups))),
                *vec,
            ]
            + [(array, in_order) for array, _ in feed_weights]
            + grads
            + [
                (xwins[layer], "once"),
                (query, clipped(1)),
                (kv, clipped(1)),
                (ctx, clipped(1)),
                (lse, clipped(1)),
                (gated, clipped(2)),
                (seq_lengths, "smem"),
            ]
            + [(array, clipped(1)) for array, _ in attn_weights]
            + ([(spread[layer - 1], "once")] if layer else []),
            [((groups, model, 2 * width), LOW, clipped(2))] * 2
            + [
                ((rows, model), F32 if layer else LOW, "full"),
                ((groups, 8, units), F32, clipped(1)),
                ((8, model), F32, "full"),
                ((groups, 8, units), F32, in_order),
            ],
            [
                row_block,
                low_block,
                low_block,
                pltpu.VMEM((2 * seq_len, 2 * width), F32),
                pltpu.VMEM((width, rows), F32),
                pltpu.VMEM((groups, 2 * seq_len, 2 * width), LOW),
                pltpu.VMEM((groups, rows, width), LOW),
                pltpu.VMEM((2 * seq_len, model), F32),
                low_block,
                low_block,
                mid_block,
                mid_block,
                two,
                two,
                pltpu.SemaphoreType.DMA,
            ],
            25e9,
            "layer_backward",
            [reduce] + [Timed(rider, finish) for rider, finish in zip(riders, finishes)],
            1,
            2 + layers - 1 - layer,
            True,
            LARGE_LIMIT,
        )
        results[layer]["inner"], results[layer]["outer"] = got[:2]
        settle(got[2:])
        block_out = results[0]["block_out"]
        riders = [Scatter(geo, [slices(left), slices(right)], pairs(2 * width, LAST_CUTS if layer == 0 else ATTN_CUTS))]
        waiting, finishes = [(layer, "kv"), (layer, "qo")], [0.75]
        grads = [(grad, "once")]
        results[layer].update(vec=vec_out, unit=unit_vec, head=head_vec)

    everywhere = (0, feats, feats)
    unit_count, qv_cols = units // ndp, width // ndp
    items = [(results[layer]["vec"], False, (0, 6), everywhere) for layer in range(layers)]
    items += [(results[layer]["unit"], True, (0, 2), (0, unit_count, unit_count)) for layer in range(layers)]
    for layer in range(layers):
        items += [(results[layer]["head"], True, (0, 1), (0, qv_cols, qv_cols))]
        items += [(results[layer]["head"], True, (0, 1), (3 * width, qv_cols, qv_cols))]
    items += [(results[layer]["head"], True, (1, 2), (0, 0, 128)) for layer in range(layers)]
    items += [(loss, False, (0, 1), (0, 0, 128))]
    riders += [Fold(geo, items), Spread(geo, grad)]
    waiting += [(0, "sums"), (0, "grad_hidden")]
    settle(run(only_move, 1, [], [], [], 0, "scatter_last", riders, 1, 2 + layers))
    sums = results[0]["sums"]
    by_feature = sums[: 6 * layers, :feats].reshape(layers, 3, 2, feats)
    by_unit = sums[6 * layers : 8 * layers, :unit_count].reshape(layers, 2, unit_count)
    by_column = sums[8 * layers : 10 * layers, :qv_cols].reshape(layers, 2, qv_cols)
    by_head = sums[10 * layers : 11 * layers, :heads]
    distill_loss = sums[11 * layers, 0] / (jnp.sum(counts[:, 0, 0]) * model * layers)
    own_slope = lax.dynamic_slice(unit_slope, (0, dp * unit_count), (layers, unit_count))

    def stacked(member, cols, turned=False):
        arrays = [results[layer][member][:, cols] for layer in range(layers)]
        return jnp.stack([array.T if turned else array for array in arrays])

    front, rear, whole = slice(0, width), slice(width, 2 * width), slice(None)
    return (
        block_out.reshape(tokens_dev, model),
        results[0]["grad_hidden"].reshape(tokens_dev, model).astype(F32),
        distill_loss,
        stacked("qo", front),
        stacked("kv", front),
        stacked("kv", rear),
        by_column,
        stacked("qo", rear, True),
        by_feature[:, 0],
        by_feature[:, 1],
        by_feature[:, 2],
        stacked("inner", whole),
        by_unit[:, 0],
        stacked("outer", whole, True),
        by_head * head_slope,
        by_unit[:, 1] * own_slope,
        results[0]["map"],
    )


def solution(mesh):
    in_specs = (
        P("dp", None),
        P("dp"),
        P(),
        P(None, "dp", "head"),
        P("dp", None),
        P(None, None, "head"),
        P(None, None, "head"),
        P(None, None, "head"),
        P(None, None, "head"),
        P(None, "head", None),
        P(),
        P(),
        P(),
        P(None, None, "head"),
        P(None, "head"),
        P(None, "head", None),
        P(None, "head"),
        P(None, "head"),
        P(None, "head"),
        P(None, "head"),
        P(None, "head"),
    )
    out_specs = (
        P("dp", None),
        P("dp", None),
        P(),
        P(None, "dp", "head"),
        P(None, "dp", "head"),
        P(None, "dp", "head"),
        P(None, None, ("head", "dp")),
        P(None, "head", "dp"),
        P(None, None, "dp"),
        P(None, None, "dp"),
        P(None, None, "dp"),
        P(None, "dp", "head"),
        P(None, ("head", "dp")),
        P(None, "head", "dp"),
        P(None, "head"),
        P(None, ("head", "dp")),
        P("dp", "head"),
    )
    return jax.shard_map(
        partial(on_device, mesh.shape["dp"], mesh.shape["head"]),
        mesh=mesh,
        in_specs=in_specs,
        out_specs=out_specs,
        check_vma=False,
    )
```

```python
from functools import partial

import jax
import jax.numpy as jnp
from jax import lax
from jax.experimental import pallas as pl
from jax.experimental.pallas import tpu as pltpu
from jax.sharding import PartitionSpec as P

BETA = 2.0 / 3.0
EPS = 1e-05
LOW = jnp.bfloat16
F32 = jnp.float32
GELU_C = 0.7978845608028654
GELU_K = 0.044715
VMEM_LIMIT = 56 * 1024 * 1024
LARGE_LIMIT = 62 * 1024 * 1024
ATTN_CUTS = (128, 256)
FEED_CUTS = (256, 256, 256)
BACK_CUTS = (384, 384)
LAST_CUTS = (128, 128, 128)
ORDER = (1, 3, 2, 0)
TIMES_LAST = (8.0, 3.6, 6.0, 8.0)
TIMES = (9.0, 5.0, 7.0, 8.0)
FORWARD_ATTN_STEP, FORWARD_FEED_STEP, HALO_WAIT = 4.5, 3.2, 14.0
MESH = pl.DeviceIdType.MESH


def gate_open(noise, alpha):
    return jnp.clip(jax.nn.sigmoid((noise + alpha) / BETA) * 1.2 - 0.1, 0.0, 1.0)


def product(left, right, dims):
    return lax.dot_general(left, right, ((dims[:1], dims[1:]), ((), ())), preferred_element_type=F32)


def nn(left, right):
    return product(left, right, (1, 0))


def nt(left, right):
    return product(left, right, (1, 1))


def tn(left, right):
    return product(left, right, (0, 0))


def factor_pair(count):
    side = 1
    for trial in range(1, count + 1):
        if count % trial == 0 and trial * trial <= count:
            side = trial
    return side, count // side


def block_of(shape, place):
    if place == "once":
        return pl.BlockSpec(shape, lambda r: (0,) * len(shape), pipeline_mode=pl.Buffered(1))
    if place == "full":
        return pl.BlockSpec(shape, lambda r: (0,) * len(shape))
    return pl.BlockSpec((1,) + tuple(shape[1:]), lambda r: (place(r),) + (0,) * (len(shape) - 1))


def spec_of(array, kind):
    if kind == "any":
        return pl.BlockSpec(memory_space=pl.ANY)
    if kind == "smem":
        return pl.BlockSpec(memory_space=pltpu.SMEM)
    if kind == "group":
        return block_of(array.shape, lambda r: r)
    return block_of(array.shape, kind)


class Plan:
    def __init__(self, spots):
        self.spots = spots
        self.slots = [(step, spot) for step, count in enumerate(spots) for spot in range(count)]
        self.chosen = {slot: [] for slot in self.slots}

    def slot(self, step, spot):
        return self.slots.index((step, spot % self.spots[step]))

    def spread(self, tasks, first, last):
        for share, _, task in sorted(tasks, key=lambda item: item[:2]):
            self.chosen[self.slots[first + round(share * (last - first))]].append(task)

    def even(self, tasks, first, last):
        count = len(tasks)
        self.spread([((index + 1) / count, index, task) for index, task in enumerate(tasks)], first, last)

    def paced(self, lengths, waits, tasks, first, finish, count, due):
        times, now = [], 0.0
        for length, number in zip(lengths, self.spots):
            for _ in range(number):
                now += waits.get(len(times), 0.0)
                times.append(now)
                now += length / number
        pace = (times[finish] - times[first]) / count
        for index, task in enumerate(tasks):
            later = [slot for slot, at in enumerate(times) if at >= times[first] + pace * (index + 1)]
            place = min([later[0] if later else len(times) - 1] + [slot for number, slot in due if index < number])
            self.chosen[self.slots[place]].append(task)

    def timed(self, lengths, tasks):
        times, now = [], 0.0
        for length, count in zip(lengths, self.spots):
            times += [now + length * spot / count for spot in range(count)]
            now += length
        for time, task in sorted(tasks, key=lambda item: item[0]):
            later = [number for number, at in enumerate(times) if at >= time]
            self.chosen[self.slots[later[0] if later else len(times) - 1]].append(task)

    def point(self, r, spot, span):
        for step in span:
            tasks = self.chosen.get((step, spot), ())
            if tasks:

                @pl.when(r == step)
                def _(tasks=tasks):
                    for task in tasks:
                        task()


def run(body, steps, inputs, outputs, scratch, flops, name, riders=(), points=1, number=None, placed=False, limit=VMEM_LIMIT):
    inputs, outputs, scratch = list(inputs), list(outputs), list(scratch)
    at = [len(inputs), len(outputs), len(scratch)]
    starts, sizes = [], []
    for rider in riders:
        starts.append((len(inputs), len(outputs), len(scratch)))
        inputs += rider.inputs
        outputs += rider.outputs
        scratch += rider.scratch
        sizes.append((len(rider.inputs), len(rider.outputs), len(rider.scratch)))
    out_shape = [jax.ShapeDtypeStruct(shape, dtype) for shape, dtype, _ in outputs]
    moved = sum(a.size * a.dtype.itemsize for a, kind in inputs if kind != "any")
    n_in, n_out = len(inputs), len(outputs)
    aliases = {}
    for rider, begin in zip(riders, starts):
        aliases.update({begin[0] + i: begin[1] + o for i, o in getattr(rider, "aliases", {}).items()})
    peers = []
    for rider in riders:
        peers += [peer for peer in rider.peers if peer not in peers]

    def whole(*refs):
        kinds = refs[:n_in], refs[n_in : n_in + n_out], refs[n_in + n_out :]
        own = [ref for part, n in zip(kinds, at) for ref in part[:n]]
        lists = [
            rider.tasks(*[part[i : i + n] for part, i, n in zip(kinds, start, size)])
            for rider, start, size in zip(riders, starts, sizes)
        ]
        r = pl.program_id(0)
        if riders:

            @pl.when(r == 0)
            def _():
                riders[0].geo.greet(peers)

        if placed:
            body(lists, *own)
            return
        plan = Plan([points] * steps)
        listed = []
        for number, tasks in enumerate(lists):
            for index, task in enumerate(tasks):
                listed.append((index / max(1, len(tasks) - 1), (number, index), task))
        plan.spread(listed, 0, len(plan.slots) - 1)
        body(lambda spot, span=range(steps): plan.point(r, spot, span), *own)

    params = {"vmem_limit_bytes": limit}
    if riders:
        params.update(collective_id=number, has_side_effects=True)
    return pl.pallas_call(
        whole,
        name=name,
        grid=(steps,),
        in_specs=[spec_of(a, kind) for a, kind in inputs],
        out_specs=[spec_of(o, kind) for o, (_, _, kind) in zip(out_shape, outputs)],
        scratch_shapes=scratch,
        out_shape=out_shape,
        input_output_aliases=aliases,
        compiler_params=pltpu.CompilerParams(**params),
        cost_estimate=pl.CostEstimate(flops=int(flops), bytes_accessed=int(moved), transcendentals=0),
    )(*[a for a, _ in inputs])


def only_move(point):
    point(0)


class Geometry:
    def __init__(self, ndp, groups):
        self.ndp, self.groups = ndp, groups
        self.size_y, self.size_x = factor_pair(ndp // 2)

    def here(self):
        dp, h = lax.axis_index("dp"), lax.axis_index("head")
        return lax.rem(dp, 2), lax.rem(lax.div(dp, 2), self.size_x), lax.div(dp, 2 * self.size_x), h

    def place(self, c=0, y=0, x=0, z=0):
        core, ix, iy, h = self.here()
        core = 1 - core if c else core
        iy = lax.rem(iy + (y + self.size_y), self.size_y) if y else iy
        ix = lax.rem(ix + (x + self.size_x), self.size_x) if x else ix
        h = lax.rem(h + (z + self.groups), self.groups) if z else h
        return iy, ix, core, h

    def device(self, **to):
        iy, ix, core, h = self.place(**to)
        return ((iy * self.size_x + ix) * 2 + core, h)

    def axes(self):
        out = [dict(c=1)]
        out += [dict(y=y) for y in range(1, self.size_y)]
        out += [dict(x=x) for x in range(1, self.size_x)]
        return out + self.column()

    def column(self):
        return [dict(z=z) for z in range(1, self.groups)]

    def plane(self):
        out = []
        for c in range(2):
            for y in range(self.size_y):
                for x in range(self.size_x):
                    to = {key: value for key, value in (("c", c), ("y", y), ("x", x)) if value}
                    if to:
                        out.append(to)
        return out

    def greet(self, peers):
        barrier = pltpu.get_barrier_semaphore()
        for peer in peers:
            pl.semaphore_signal(barrier, inc=1, device_id=self.device(**peer), device_id_type=MESH)
        pl.semaphore_wait(barrier, len(peers))


class Mover:
    def __init__(self, geo, send, recv):
        self.geo, self.send, self.recv, self.ids = geo, send, recv, {}

    def __call__(self, key, src, dst, **to):
        index = self.ids.setdefault(key, len(self.ids))
        return pltpu.make_async_remote_copy(
            src_ref=src,
            dst_ref=dst,
            send_sem=self.send.at[index],
            recv_sem=self.recv.at[index],
            device_id=self.geo.device(**to),
            device_id_type=MESH,
        )


def back(to):
    return {key: value if key == "c" else -value for key, value in to.items()}


def start(copies):
    for copy in copies:
        copy.start()


def arrive(copies):
    for copy in copies:
        copy.wait_recv()


def leave(copies):
    for copy in copies:
        copy.wait_send()


class Column:
    def __init__(self, geo, block, slot, send, recv, base, absolute=False):
        self.absolute = absolute
        self.geo, self.slot, self.send, self.recv, self.base = geo, slot, send, recv, base
        self.h = geo.here()[3]
        self.block = block

    def copy(self, r):
        return pltpu.make_async_remote_copy(
            src_ref=self.block,
            dst_ref=self.slot(0 if self.absolute else r),
            send_sem=self.send.at[self.base + r],
            recv_sem=self.recv.at[self.base + r],
            device_id=self.geo.device(z=-r),
            device_id_type=MESH,
        )

    def begin(self):
        self.copy(2).start()
        pl.when(self.h != 0)(lambda: self.copy(1).start())
        pl.when(self.h != 3)(lambda: self.copy(3).start())

    def by_middle(self, act):
        @pl.when((self.h > 0) & (self.h < 3))
        def _():
            there = 1 + 2 * lax.rem(self.h, 2)
            dp, _ = self.geo.device()
            act(
                pltpu.make_async_remote_copy(
                    src_ref=self.slot(2),
                    dst_ref=self.slot(2 if self.absolute else there),
                    send_sem=self.send.at[self.base],
                    recv_sem=self.recv.at[self.base + there],
                    device_id=(dp, self.h + 1 - 2 * lax.rem(self.h, 2)),
                    device_id_type=MESH,
                )
            )

    def relay(self):
        self.copy(2).wait_recv()
        self.by_middle(lambda copy: copy.start())

    def arrive(self):
        self.copy(1).wait_recv()
        self.copy(3).wait_recv()

    def leave(self):
        self.copy(2).wait_send()
        pl.when(self.h != 0)(lambda: self.copy(1).wait_send())
        pl.when(self.h != 3)(lambda: self.copy(3).wait_send())
        self.by_middle(lambda copy: copy.wait_send())


class Delivery:
    def __init__(self, geo, block, slot, merged, send, recv, base):
        self.h, self.block, self.slot, self.merged = geo.here()[3], block, slot, merged

        def copy(r, dst, index, z):
            return pltpu.make_async_remote_copy(
                src_ref=block(r),
                dst_ref=dst,
                send_sem=send.at[base + r],
                recv_sem=recv.at[base + index],
                device_id=geo.device(z=z),
                device_id_type=MESH,
            )

        self.copy = lambda r: copy(r, slot(r), r, r)
        self.last_to_middle = lambda: copy(1, merged, 0, -1)
        self.first_to_middle = lambda: copy(3, merged, 0, 1)

    def begin(self, r):
        if r == 1:
            pl.when(self.h != 3)(lambda: self.copy(1).start())
            pl.when(self.h == 3)(lambda: self.last_to_middle().start())

            @pl.when(self.h == 0)
            def _():
                self.slot(1)[...] = jnp.zeros_like(self.slot(1))

        if r == 3:
            pl.when(self.h != 0)(lambda: self.copy(3).start())
            pl.when(self.h == 0)(lambda: self.first_to_middle().start())

            @pl.when(self.h == 3)
            def _():
                self.slot(3)[...] = jnp.zeros_like(self.slot(3))

    def merge(self):
        @pl.when((self.h > 0) & (self.h < 3))
        def _():
            self.last_to_middle().wait_recv()
            mine = self.block(2)
            mine[...] = (mine[...].astype(F32) + self.merged[...].astype(F32)).astype(LOW)

        self.copy(2).start()

    def arrive(self):
        self.copy(2).wait_recv()
        pl.when(self.h != 0)(lambda: self.copy(1).wait_recv())
        pl.when(self.h != 3)(lambda: self.copy(3).wait_recv())

    def leave(self):
        for r in (1, 2, 3):
            self.copy(r).wait_send()


class Gather:
    def __init__(self, geo, owns, chunks):
        self.geo, self.chunks, self.peers = geo, chunks, geo.axes()
        self.layers = [layer for _, layer in owns]
        self.inputs = [(own, "any") for own, _ in owns]
        self.outputs = [((geo.groups,) + own.shape[1:], LOW, "any") for own, _ in owns]
        halves = sum(len(chunk) for chunk in chunks)
        sems = pltpu.SemaphoreType.DMA((halves * 2 * geo.size_x * geo.size_y,))
        ends = pltpu.SemaphoreType.DMA((halves * geo.groups,))
        self.scratch = [sems, sems, ends, ends]

    def tasks(self, owns, outs, scratch):
        self.outs = outs
        geo = self.geo
        move = Mover(geo, *scratch[:2])
        groups, sx, sy = geo.groups, geo.size_x, geo.size_y
        bases = {}
        for chunk, parts in enumerate(self.chunks):
            for half in range(len(parts)):
                bases[chunk, half] = groups * len(bases)
        others = pl.ds(1, groups - 1)
        owns = [own.at[layer] for own, layer in zip(owns, self.layers)]

        def columns(chunk, half):
            m, col, cols, _ = self.chunks[chunk][half]
            return m, pl.ds(col, cols)

        def along(chunk, half):
            m, cols = columns(chunk, half)
            iy, ix, core, _ = geo.place()
            return Column(
                geo,
                owns[m].at[iy, ix, core, :, cols],
                lambda r: outs[m].at[r, iy, ix, core, :, cols],
                *scratch[2:],
                bases[chunk, half],
            )

        def hop(chunk, half, block, to):
            m, cols = columns(chunk, half)
            iy, ix, core, _ = geo.place(**block)
            part = outs[m].at[others, iy, ix, core, :, cols]
            return move(("p", chunk, half, str(block), str(to)), part, part, **back(to))

        ways_x = [dict(x=x) for x in range(1, sx)]
        ways_y = [dict(y=y) for y in range(1, sy)]
        corners = [dict(x=x, y=y) for x in range(1, sx) for y in range(1, sy)]

        def halves(chunk):
            return range(len(self.chunks[chunk]))

        def alongs(chunk):
            return [along(chunk, half) for half in halves(chunk)]

        def firsts(chunk):
            return [hop(chunk, half, {}, to) for half in halves(chunk) for to in ways_x + ways_y]

        def seconds(chunk):
            out = []
            for half in halves(chunk):
                near, far = (ways_y, ways_x) if self.chunks[chunk][half][3] else (ways_x, ways_y)
                out += [hop(chunk, half, block, to) for block in near for to in far]
            return out

        def cores(chunk, blocks):
            return [hop(chunk, half, block, dict(c=1)) for half in halves(chunk) for block in blocks]

        count = len(self.chunks)

        def begin():
            for chunk in range(min(2, count)):
                for column in alongs(chunk):
                    column.begin()

        def level_zero(chunk):
            for column in alongs(chunk):
                column.relay()
            if chunk + 2 < count:
                for column in alongs(chunk + 2):
                    column.begin()

        def level_one(chunk):
            for column in alongs(chunk):
                column.arrive()
            start(firsts(chunk))
            start(cores(chunk, [{}]))

        def level_two(chunk):
            arrive(firsts(chunk))
            start(seconds(chunk))
            start(cores(chunk, ways_x + ways_y))

        def level_three(chunk):
            arrive(seconds(chunk))
            start(cores(chunk, corners))

        def level_four(chunk):
            arrive(cores(chunk, [{}] + ways_x + ways_y + corners))

        def end():
            for chunk in range(count):
                for column in alongs(chunk):
                    column.leave()
                leave(firsts(chunk) + seconds(chunk) + cores(chunk, [{}] + ways_x + ways_y + corners))

        out = [begin]
        self.done = []
        for time in range(count + 4):
            for level, late in ((level_zero, 0), (level_one, 1), (level_two, 2), (level_three, 3), (level_four, 4)):
                if 0 <= time - late < count:
                    out.append(partial(level, time - late))
            if time >= 4:
                self.done.append(len(out))
        return out + [end]


class Lend:
    def __init__(self, geo, rider):
        self.geo, self.rider, self.peers = geo, rider, []
        self.inputs, self.outputs, self.scratch = [], [], []

    def tasks(self, owns, outs, scratch):
        return [self.rider.outs]


class Timed:
    def __init__(self, rider, finish):
        self.geo, self.peers, self.inputs, self.outputs, self.scratch = (
            rider.geo,
            rider.peers,
            rider.inputs,
            rider.outputs,
            rider.scratch,
        )
        self.rider, self.finish, self.aliases = rider, finish, getattr(rider, "aliases", {})

    def tasks(self, inputs, outs, scratch):
        return self.finish, self.rider.tasks(inputs, outs, scratch)


class Scatter:
    def __init__(self, geo, grads, chunks):
        self.geo, self.chunks, self.peers = geo, chunks, geo.axes()
        self.inputs = [(grad, "any") for grad in grads]
        self.outputs = [(grad.shape[4:], F32, "full") for grad in grads]
        feats = grads[0].shape[4]
        halves = [half for chunk in chunks for half in chunk]
        each = 1 + (geo.size_x - 1) + (geo.size_y - 1)
        sems = pltpu.SemaphoreType.DMA((len(halves) * each,))
        ends = pltpu.SemaphoreType.DMA((len(halves) * geo.groups,))
        self.scratch = [sems, sems, ends, ends, pltpu.SemaphoreType.DMA((len(halves),))]
        for _, _, cols, y_first in halves:
            near, far = (geo.size_y, geo.size_x) if y_first else (geo.size_x, geo.size_y)
            self.scratch += [
                pltpu.VMEM(shape, LOW)
                for shape in (
                    (geo.groups, geo.size_y, geo.size_x, feats, cols),
                    (geo.groups, geo.size_y, geo.size_x, feats, cols),
                    (near - 1, geo.groups, far, feats, cols),
                    (far - 1, geo.groups, feats, cols),
                    (geo.groups, feats, cols),
                )
            ]

    def tasks(self, grads, outs, scratch):
        geo, (send, recv, end_send, end_recv, local), buffers = self.geo, scratch[:5], scratch[5:]
        move = Mover(geo, send, recv)
        groups, sx, sy = geo.groups, geo.size_x, geo.size_y
        index = {}
        for chunk, halves in enumerate(self.chunks):
            for half in range(len(halves)):
                index[chunk, half] = len(index)

        def parts(chunk, half):
            m, col, cols, y_first = self.chunks[chunk][half]
            number = index[chunk, half]
            return grads[m], pl.ds(col, cols), y_first, buffers[5 * number : 5 * number + 5]

        def load(chunk, half):
            grad, cols, _, bufs = parts(chunk, half)
            _, _, core, _ = geo.place()
            return pltpu.make_async_copy(
                grad.at[:, :, :, core, :, cols], bufs[0], local.at[index[chunk, half]]
            )

        def cross(chunk, half):
            grad, cols, _, bufs = parts(chunk, half)
            _, _, core, _ = geo.place(c=1)
            return move(("c", chunk, half), grad.at[:, :, :, core, :, cols], bufs[1], c=1)

        def near(chunk, half):
            _, _, y_first, bufs = parts(chunk, half)
            out = []
            for step in range(1, sy if y_first else sx):
                to = dict(y=step) if y_first else dict(x=step)
                iy, ix, _, _ = geo.place(**to)
                part = bufs[0].at[:, iy] if y_first else bufs[0].at[:, :, ix]
                out.append(move(("n", chunk, half, step), part, bufs[2].at[step - 1], **to))
            return out

        def far(chunk, half):
            _, _, y_first, bufs = parts(chunk, half)
            out = []
            for step in range(1, sx if y_first else sy):
                to = dict(x=step) if y_first else dict(y=step)
                iy, ix, _, _ = geo.place(**to)
                out.append(move(("f", chunk, half, step), bufs[0].at[:, iy, ix], bufs[3].at[step - 1], **to))
            return out

        def along(chunk, half):
            _, _, _, bufs = parts(chunk, half)
            iy, ix, _, _ = geo.place()
            return Delivery(
                geo,
                lambda r: bufs[0].at[r, iy, ix],
                lambda r: bufs[4].at[r],
                bufs[4].at[0],
                end_send,
                end_recv,
                groups * index[chunk, half],
            )

        def each(chunk):
            return range(len(self.chunks[chunk]))

        def begin_one(chunk):
            for half in each(chunk):
                cross(chunk, half).start()
                load(chunk, half).start()

        count = len(self.chunks)

        def begin():
            for chunk in range(min(2, count)):
                begin_one(chunk)

        def level_one(chunk):
            for half in each(chunk):
                _, _, _, bufs = parts(chunk, half)
                load(chunk, half).wait()
                cross(chunk, half).wait_recv()
                for r in range(groups):
                    bufs[0][r] = (bufs[0][r].astype(F32) + bufs[1][r].astype(F32)).astype(LOW)
                start(near(chunk, half))
            if chunk + 2 < count:
                begin_one(chunk + 2)

        def level_two(chunk):
            iy, ix, _, _ = geo.place()
            for half in each(chunk):
                _, _, y_first, bufs = parts(chunk, half)
                arrive(near(chunk, half))
                for r in range(groups):
                    total = (bufs[0][r, iy] if y_first else bufs[0][r, :, ix]).astype(F32)
                    for other in range(bufs[2].shape[0]):
                        total = total + bufs[2][other, r].astype(F32)
                    if y_first:
                        bufs[0][r, iy] = total.astype(LOW)
                    else:
                        bufs[0][r, :, ix] = total.astype(LOW)
                start(far(chunk, half))

        def level_three(chunk):
            iy, ix, _, _ = geo.place()
            for half in each(chunk):
                _, _, _, bufs = parts(chunk, half)
                arrive(far(chunk, half))
                for r in range(groups):
                    total = bufs[0][r, iy, ix].astype(F32)
                    for other in range(bufs[3].shape[0]):
                        total = total + bufs[3][other, r].astype(F32)
                    bufs[0][r, iy, ix] = total.astype(LOW)
                for r in (1, 3):
                    along(chunk, half).begin(r)

        def level_merge(chunk):
            for half in each(chunk):
                along(chunk, half).merge()

        def level_four(chunk):
            iy, ix, _, _ = geo.place()
            for half in each(chunk):
                m, col, cols, _ = self.chunks[chunk][half]
                _, _, _, bufs = parts(chunk, half)
                along(chunk, half).arrive()
                total = bufs[0][0, iy, ix].astype(F32)
                for r in range(1, groups):
                    total = total + bufs[4][r].astype(F32)
                outs[m][:, col : col + cols] = total

        def end():
            for chunk in range(count):
                for half in each(chunk):
                    leave([cross(chunk, half)] + near(chunk, half) + far(chunk, half))
                    along(chunk, half).leave()

        out = [begin]
        levels = (level_one, level_two, level_three, level_merge, level_four)
        for time in range(count + 4):
            for late, level in enumerate(levels):
                if 0 <= time - late < count:
                    out.append(partial(level, time - late))
        return out + [end]


class Reduce:
    def __init__(self, geo, shapes, cuts):
        self.geo, self.peers = geo, geo.axes()
        self.count = len(shapes)
        self.inputs = []
        self.outputs = [(shape, F32, "full") for shape in shapes]
        self.cuts, begin = [], 0
        for cut in cuts:
            self.cuts.append((begin, cut))
            begin += cut
        if begin != shapes[0][1]:
            self.cuts = [(0, shapes[0][1])]
        self.chunks = [(r, cut) for r in ORDER for cut in range(len(self.cuts))]
        each = 1 + (geo.size_x - 1) + (geo.size_y - 1)
        sems = pltpu.SemaphoreType.DMA((self.count * len(self.chunks) * each,))
        ends = pltpu.SemaphoreType.DMA((self.count * len(self.cuts) * geo.groups,))
        self.scratch = [sems, sems, ends, ends, pltpu.SemaphoreType.REGULAR]
        for m, (feats, n) in enumerate(shapes):
            near, far = (geo.size_y, geo.size_x) if m % 2 else (geo.size_x, geo.size_y)
            self.scratch += [
                pltpu.VMEM(shape, LOW)
                for shape in (
                    (geo.groups, geo.size_y, geo.size_x, 2, feats, n),
                    (2, geo.size_y, geo.size_x, feats, n),
                    (near - 1, geo.groups, far, feats, n),
                    (far - 1, geo.groups, feats, n),
                    (geo.groups, feats, n),
                )
            ]

    def tasks(self, inputs, outs, scratch):
        geo, (send, recv, end_send, end_recv, free), buffers = self.geo, scratch[:5], scratch[5:]
        move = Mover(geo, send, recv)
        groups, sx, sy = geo.groups, geo.size_x, geo.size_y
        mats = range(self.count)
        self.grads = [buffers[5 * m] for m in mats]
        ring = self.ring = 2 * len(self.cuts)

        def parts(k, m):
            r, cut = self.chunks[k]
            begin, count = self.cuts[cut]
            return r, pl.ds(begin, count), buffers[5 * m : 5 * m + 5]

        def cross(k, m):
            r, cols, bufs = parts(k, m)
            _, _, core, _ = geo.place(c=1)
            return move(("c", k, m), bufs[0].at[r, :, :, core, :, cols], bufs[1].at[k // len(self.cuts) % 2, :, :, :, cols], c=1)

        def near(k, m):
            r, cols, bufs = parts(k, m)
            out = []
            for step in range(1, sy if m % 2 else sx):
                to = dict(y=step) if m % 2 else dict(x=step)
                iy, ix, core, _ = geo.place(**to)
                part = bufs[0].at[r, iy, :, core, :, cols] if m % 2 else bufs[0].at[r, :, ix, core, :, cols]
                out.append(move(("n", k, m, step), part, bufs[2].at[step - 1, r, :, :, cols], **to))
            return out

        def far(k, m):
            r, cols, bufs = parts(k, m)
            out = []
            for step in range(1, sx if m % 2 else sy):
                to = dict(x=step) if m % 2 else dict(y=step)
                iy, ix, core, _ = geo.place(**to)
                out.append(
                    move(
                        ("f", k, m, step),
                        bufs[0].at[r, iy, ix, core, :, cols],
                        bufs[3].at[step - 1, r, :, cols],
                        **to,
                    )
                )
            return out

        def along(cut, m):
            begin, count = self.cuts[cut]
            cols, bufs = pl.ds(begin, count), buffers[5 * m : 5 * m + 5]
            iy, ix, core, _ = geo.place()
            return Delivery(
                geo,
                lambda r: bufs[0].at[r, iy, ix, core, :, cols],
                lambda r: bufs[4].at[r, :, cols],
                bufs[4].at[0, :, cols],
                end_send,
                end_recv,
                groups * (self.count * cut + m),
            )

        def begin(k):
            if k >= ring:
                pl.semaphore_wait(free, 1)
            for m in mats:
                cross(k, m).start()

        def level_one(k):
            _, _, core, _ = geo.place()
            for m in mats:
                r, cols, bufs = parts(k, m)
                cross(k, m).wait_recv()
                total = bufs[0][r, :, :, core, :, cols].astype(F32) + bufs[1][k // len(self.cuts) % 2, :, :, :, cols].astype(F32)
                bufs[0][r, :, :, core, :, cols] = total.astype(LOW)
                start(near(k, m))
            if k + ring < len(self.chunks):
                pl.semaphore_signal(free, inc=1, device_id=geo.device(c=1), device_id_type=MESH)

        def level_two(k):
            iy, ix, core, _ = geo.place()
            for m in mats:
                r, cols, bufs = parts(k, m)
                arrive(near(k, m))
                part = bufs[0][r, iy, :, core, :, cols] if m % 2 else bufs[0][r, :, ix, core, :, cols]
                total = part.astype(F32)
                for other in range(bufs[2].shape[0]):
                    total = total + bufs[2][other, r, :, :, cols].astype(F32)
                if m % 2:
                    bufs[0][r, iy, :, core, :, cols] = total.astype(LOW)
                else:
                    bufs[0][r, :, ix, core, :, cols] = total.astype(LOW)
                start(far(k, m))

        def level_three(k):
            iy, ix, core, _ = geo.place()
            for m in mats:
                r, cols, bufs = parts(k, m)
                arrive(far(k, m))
                total = bufs[0][r, iy, ix, core, :, cols].astype(F32)
                for other in range(bufs[3].shape[0]):
                    total = total + bufs[3][other, r, :, cols].astype(F32)
                bufs[0][r, iy, ix, core, :, cols] = total.astype(LOW)
                delivery = along(self.chunks[k][1], m)
                if r == 2:
                    delivery.merge()
                elif r:
                    delivery.begin(r)

        def final(cut):
            iy, ix, core, _ = geo.place()
            begin, count = self.cuts[cut]
            cols = pl.ds(begin, count)
            for m in mats:
                bufs = buffers[5 * m : 5 * m + 5]
                along(cut, m).arrive()
                total = bufs[0][0, iy, ix, core, :, cols].astype(F32)
                for r in range(1, groups):
                    total = total + bufs[4][r, :, cols].astype(F32)
                outs[m][:, cols] = total

        def end():
            for m in mats:
                for k in range(len(self.chunks)):
                    leave([cross(k, m)] + near(k, m) + far(k, m))
                for cut in range(len(self.cuts)):
                    along(cut, m).leave()

        count = range(len(self.chunks))
        return dict(
            begin=[partial(begin, k) for k in count],
            one=[partial(level_one, k) for k in count],
            two=[partial(level_two, k) for k in count],
            three=[partial(level_three, k) for k in count],
            final=[partial(final, cut) for cut in range(len(self.cuts))],
            end=[end],
        )


class Spread:
    def __init__(self, geo, value, plane=False, part=None, into=None):
        self.geo, self.plane, self.part = geo, plane, part
        self.peers = geo.plane() if plane else geo.column()
        self.inputs = [] if plane else [(value, "once")]
        self.outputs = [((len(self.peers) + 1,) + value.shape, value.dtype, "any")]
        self.aliases = {}
        if into is not None:
            self.inputs.append((into, "any"))
            self.aliases = {1: 0}
        sems = pltpu.SemaphoreType.DMA((len(self.peers) + 1,))
        self.scratch = [sems, sems, pltpu.SemaphoreType.DMA]
        if plane:
            self.scratch.append(pltpu.VMEM(value.shape, value.dtype))

    def tasks(self, values, outs, scratch):
        geo, out, (send, recv, local) = self.geo, outs[0], scratch[:3]
        dp, h = geo.device()
        if self.plane:
            self.source = scratch[3]
            move = Mover(geo, send, recv)
            copies = [move(str(to), self.source, out.at[dp], **back(to)) for to in self.peers]
            mine = pltpu.make_async_copy(self.source, out.at[dp], local)

            def begin():
                start(copies)
                mine.start()

            def end():
                mine.wait()
                arrive(copies)
                leave(copies)

            return [begin, end]
        rows = pl.ds(*self.part) if self.part else pl.ds(0, out.shape[1])
        value = values[0].at[rows]
        slot = lambda r: out.at[lax.rem(h + r, geo.groups), rows]
        column = Column(geo, value, slot, send, recv, 0, True)

        def begin_column():
            column.begin()
            pltpu.make_async_copy(value, slot(0), local).start()

        def end_column():
            pltpu.make_async_copy(value, slot(0), local).wait()
            column.arrive()
            column.leave()

        return [begin_column, column.relay, end_column]


class Deal:
    def __init__(self, geo, value):
        self.geo, self.peers = geo, geo.column()
        self.rows = value.shape[1] // geo.groups
        self.inputs = [(value, "any")]
        shape = (geo.groups - 1, value.shape[0], self.rows, value.shape[2])
        self.outputs = [(shape, value.dtype, "any")]
        sems = pltpu.SemaphoreType.DMA((geo.groups - 1,))
        self.scratch = [sems, sems]

    def tasks(self, values, outs, scratch):
        geo = self.geo
        move = Mover(geo, *scratch)
        copies = []
        for r in range(1, geo.groups):
            first = pl.multiple_of(geo.place(z=-r)[3] * self.rows, self.rows)
            copies.append(move(r, values[0].at[:, pl.ds(first, self.rows), :], outs[0].at[r - 1], z=-r))

        def end():
            arrive(copies)
            leave(copies)

        return [lambda: start(copies), end]


class Fold:
    def __init__(self, geo, items):
        self.geo, self.peers = geo, geo.plane() + geo.column()
        self.inputs = [(item[0], "full") for item in items]
        self.picks = [item[1:] for item in items]
        rows = sum(stop - first for _, (first, stop), _ in self.picks)
        self.rows = -(-rows // 8) * 8
        self.outputs = [((self.rows, 128), F32, "full")]
        near, far = pltpu.SemaphoreType.DMA((geo.ndp - 1,)), pltpu.SemaphoreType.DMA((geo.groups - 1,))
        wide = pltpu.VMEM((geo.ndp, geo.groups, self.rows, 128), F32)
        slim = pltpu.VMEM((geo.groups, self.rows, 128), F32)
        self.scratch = [near, near, far, far, wide, wide, slim, slim]

    def tasks(self, values, outs, scratch):
        geo = self.geo
        near_send, near_recv, far_send, far_recv, packed, landed, middle, last = scratch
        groups, ndp = geo.groups, geo.ndp
        to_plane, to_column = Mover(geo, near_send, near_recv), Mover(geo, far_send, far_recv)
        dp, h = geo.device()
        near, far = [], []
        for to in geo.plane():
            there, _ = geo.device(**to)
            near.append(to_plane(str(to), packed.at[there], landed.at[dp], **to))
        for r in range(1, groups):
            far.append(to_column(r, middle.at[r], last.at[h], z=r))

        def begin():
            packed[...] = jnp.zeros_like(packed)
            row = 0
            for value, (grouped, (low, high), (first, stride, cols)) in zip(values, self.picks):
                for r in range(groups):
                    for d in range(ndp):
                        lanes = slice(first + d * stride, first + d * stride + cols)
                        part = value[r, low:high, lanes] if grouped else value[low:high, lanes]
                        packed[d, r, row : row + high - low, :cols] = part
                row += high - low
            start(near)

        def fold():
            landed[dp] = packed[dp]
            arrive(near)
            total = landed[0]
            for d in range(1, ndp):
                total = total + landed[d]
            middle[...] = total
            start(far)

        def end():
            last[h] = middle[0]
            arrive(far)
            total = last[0]
            for z in range(1, groups):
                total = total + last[z]
            outs[0][...] = total
            leave(near)
            leave(far)

        return [begin, fold, end]


def norm_forward(before, gain, shift):
    center = before - jnp.mean(before, -1, keepdims=True)
    spread = jnp.mean(center * center, -1, keepdims=True)
    return center * lax.rsqrt(spread + EPS) * gain + shift


def norm_backward(before, gain, grad):
    center = before - jnp.mean(before, -1, keepdims=True)
    rate = lax.rsqrt(jnp.mean(center * center, -1, keepdims=True) + EPS)
    hat = center * rate
    grad_hat = grad * gain
    mean_one = jnp.mean(grad_hat, -1, keepdims=True)
    mean_two = jnp.mean(grad_hat * hat, -1, keepdims=True)
    grad_before = rate * (grad_hat - mean_one - hat * mean_two)
    return (
        grad_before,
        jnp.sum(grad * hat, 0, keepdims=True),
        jnp.sum(grad, 0, keepdims=True),
        jnp.sum(grad_before, 0, keepdims=True),
    )


BIAS_ONE, BIAS_TWO, GAIN_ONE, GAIN_TWO, SHIFT_ONE, SHIFT_TWO = range(6)


class Window:
    def __init__(self, size, rows, groups):
        self.seqs, self.seq_len, self.heads, self.head_size = size
        self.rows, self.groups = rows, groups
        self.block = self.seq_len // groups
        self.mid_rows = 2 * self.block
        h = lax.axis_index("head")
        self.h = h
        self.first = lax.div(h * (self.seqs - 1), groups)
        self.base = self.first * self.seq_len
        self.own = h * rows - self.base
        pair = h + 1 - 2 * lax.rem(h, 2)
        self.pair = pair * rows - self.base
        self.mid = lax.rem(h, 2) * (2 * rows)
        self.mid_row = lax.rem(h, 2) * self.block
        self.middle = (h > 0) & (h < groups - 1)
        dp = lax.axis_index("dp")
        self.to_pair = (dp, pair)
        self.to_mid = (dp, groups - 1 - h)

    def at(self, begin, rows):
        return pl.ds(pl.multiple_of(begin, self.block), rows)

    def loc(self, piece):
        return lax.div((self.h * (self.rows // self.block) + piece) * self.block, self.seq_len) - self.first

    def keys(self, piece):
        return pl.ds(pl.multiple_of(self.loc(piece) * self.seq_len, self.seq_len), self.seq_len)


def remote(src, dst, sems, to):
    return pltpu.make_async_remote_copy(
        src_ref=src, dst_ref=dst, send_sem=sems.at[0], recv_sem=sems.at[1], device_id=to, device_id_type=MESH
    )


def add_up(r, total, part):
    @pl.when(r == 0)
    def _():
        total[...] = part

    @pl.when(r > 0)
    def _():
        total[...] += part


def gelu_parts(unit):
    square = unit * unit
    bent = jnp.tanh(GELU_C * unit * (1.0 + GELU_K * square))
    half = 0.5 * (1.0 + bent)
    slope = half + 0.5 * unit * (1.0 - bent * bent) * (GELU_C * (1.0 + 3.0 * GELU_K * square))
    return unit * half, slope


def vector(vecs, layer, which):
    return vecs[which // 2][layer, which % 2 : which % 2 + 1, :]


def row_mask(window, lengths):
    block, parts = window.block, []
    for piece in range(window.rows // block):
        place = lax.rem((window.h * (window.rows // block) + piece) * block, window.seq_len)
        inside = lax.broadcasted_iota(jnp.int32, (block, 1), 0) + place < lengths[window.first + window.loc(piece)]
        parts.append(jnp.where(inside, 1.0, 0.0))
    return jnp.concatenate(parts, 0)


def attend(window, layer, xin, offset, row, lengths, left, right, outs, turned, total, r, point):
    kv_out, q_out, ctx_out, lse_out, gated_out = outs
    seq_len, heads, head_size, block, rows = (
        window.seq_len,
        window.heads,
        window.head_size,
        window.block,
        window.rows,
    )
    width = heads * head_size
    point(0)
    kv = nn(xin[window.at(offset, 2 * seq_len), :], left) + row[:, 2 * width :]
    kv_out[0] = kv.astype(LOW)
    query = (nn(xin[window.at(offset + window.own, rows), :], right[:, :width]) + row[:, :width]).astype(LOW)
    q_out[0] = query
    scaled = query * jnp.asarray(0.125, LOW)
    for piece in range(rows // block):
        mine = slice(piece * block, (piece + 1) * block)
        keys = window.keys(piece)
        length = lengths[window.first + window.loc(piece)]
        unused = jnp.where(lax.broadcasted_iota(jnp.int32, (seq_len, block), 0) < length, 0.0, -1e30)
        for head in range(heads):
            lanes = slice(head * head_size, (head + 1) * head_size)
            scores = nt(kv_out[0, keys, lanes], scaled[mine, lanes]) + unused
            largest = jnp.max(scores, 0, keepdims=True)
            powers = jnp.exp(scores - largest)
            sums = jnp.sum(powers, 0, keepdims=True)
            value = kv_out[0, keys, width + head * head_size : width + (head + 1) * head_size]
            turned[lanes, mine] = tn(value, powers.astype(LOW)) / sums
            lse_out[0, head : head + 1, mine] = largest + jnp.log(sums)
            point(1 + piece * heads + head)
    context = turned[...].T
    ctx_out[0] = context
    gated = (context * row[:, width : 2 * width]).astype(LOW)
    gated_out[0] = gated
    add_up(r, total, nt(gated, right[:, width:]))


def forward(size, layers, geo, gather, counter, lists, *refs):
    seqs, seq_len, heads, head_size = size
    refs = list(refs)
    take = lambda n: [refs.pop(0) for _ in range(n)]
    hidden = refs.pop(0)
    vec = take(3)
    lengths, unit_noise, unit_alpha, head_noise, head_alpha, inner_bias, qv_bias = take(7)
    key_value, query_output, inner, outer, map_own = take(5)
    saved = [take(10) for _ in range(layers)]
    win_out, small_out = take(2)
    left_buf, right_buf, inner_buf, outer_buf, load_sems, back_sems = take(6)
    total, middle, current, low, xwin, small, small_own, small_send, small_recv, map_stage, turned = take(11)
    pair_sems, mid_sems, local = take(3)
    gather_tasks, count_tasks, deal_tasks, (weights,) = lists
    groups = geo.groups
    rows, model = total.shape
    window = Window(size, rows, groups)
    mid_rows, width = window.mid_rows, heads * head_size
    s = pl.program_id(0)
    r = lax.rem(s, groups)
    slot = lax.rem(r, 2)
    spots_attn, spots_feed = 2 + rows // window.block * heads, 4
    plan = Plan(([spots_attn] * groups + [spots_feed] * groups) * layers)

    small_column = Column(geo, small_own, lambda i: small.at[i], small_send, small_recv, 0)
    keep_small = pltpu.make_async_copy(small, small_out, local.at[2])

    def small_begin():
        small_column.begin()

    def small_end():
        small_column.relay()
        small_column.arrive()
        small_column.leave()
        keep_small.start()

    into_stage = pltpu.make_async_copy(map_own.at[0], map_stage, local.at[3])
    out_of_stage = pltpu.make_async_copy(map_stage, weights[-1].at[0], local.at[4])

    def stage_begin():
        into_stage.start()

    def stage_end():
        into_stage.wait()
        out_of_stage.start()

    phases = 2 * layers
    plan.even([small_begin] + [count_tasks[0]], 0, 0)
    ends, done = [], 0
    for phase in range(phases):
        for chunk, halves in enumerate(gather.chunks):
            if halves[0][0] // 2 == phase:
                done = gather.done[chunk]
        ends.append(done)
    lengths_us = ([FORWARD_ATTN_STEP] * groups + [FORWARD_FEED_STEP] * groups) * layers
    first, begun = 0, 0
    for phase in range(phases):
        last = plan.slot(phase * groups, -1)
        if phase < 2:
            plan.even(gather_tasks[begun : ends[phase]], first, last)
            first, begun = last, ends[phase]
        if phase == 0:
            plan.even([small_end, stage_begin], last, last)
            plan.even([count_tasks[1]], plan.slot(groups, 0), plan.slot(groups, 0))
            plan.even([stage_end], plan.slot(groups, 1), plan.slot(groups, 1))
        if phase == 2:
            plan.even([deal_tasks[0]], last, last)
    closing = len(plan.slots) - 1
    waits = {plan.slot(phase * groups - 1, -1): HALO_WAIT for phase in range(2, phases, 2)}
    due = [(ends[phase] - begun, plan.slot(phase * groups, -1)) for phase in range(2, phases)]
    plan.paced(lengths_us, waits, gather_tasks[begun:], first, due[-1][1], due[-1][0], due)
    plan.even([deal_tasks[1]], closing, closing)

    kinds = [(left_buf, right_buf), (inner_buf, outer_buf)]
    sources = [(key_value, query_output), (inner, outer)]

    def own_loads(phase):
        layer, kind = phase // 2, phase % 2
        return [
            pltpu.make_async_copy(src.at[layer], buf.at[0], load_sems.at[kind, side, 0])
            for side, (src, buf) in enumerate(zip(sources[kind], kinds[kind]))
        ]

    def own_backs(phase):
        kind = phase % 2
        return [
            pltpu.make_async_copy(buf.at[0], weights[2 * phase + side].at[0], back_sems.at[kind, side])
            for side, buf in enumerate(kinds[kind])
        ]

    def loads(phase, group, into):
        kind = phase % 2
        return [
            pltpu.make_async_copy(weights[2 * phase + side].at[group], buf.at[into], load_sems.at[kind, side, into])
            for side, buf in enumerate(kinds[kind])
        ]

    @pl.when(s == 0)
    def _():
        start(own_loads(0))
        total_length = lengths[0]
        for index in range(1, seqs):
            total_length = total_length + lengths[index]
        counter.source[...] = jnp.full(counter.source.shape, total_length, jnp.int32).astype(F32)
        small_own[...] = jnp.zeros_like(small_own)
        open_unit = gate_open(unit_noise[...], unit_alpha[...])
        open_head = gate_open(head_noise[...], head_alpha[...])
        for layer in range(layers):
            own = slice(layer, layer + 1)
            place = slice(4 * layer, 4 * layer + 1)
            small_own[place, :] = open_unit[own]
            small_own[4 * layer + 1 : 4 * layer + 2, :] = inner_bias[own, :]
            place = slice(4 * layer + 2, 4 * layer + 3)
            small_own[place, :width] = qv_bias[layer, 0:1, :]
            for head in range(heads):
                begin = width + head * head_size
                small_own[place, begin : begin + head_size] = jnp.broadcast_to(
                    open_head[own, head : head + 1], (1, head_size)
                )
            small_own[place, 3 * width :] = qv_bias[layer, 1:2, :]
        small[0] = small_own[...]

    def before(phase):
        @pl.when(r == 0)
        def _():
            if phase + 1 < phases:
                start(own_loads(phase + 1))
            for copy in own_loads(phase):
                copy.wait()
            start(own_backs(phase))

        @pl.when(r > 0)
        def _():
            for copy in loads(phase, r, slot):
                copy.wait()

        @pl.when((r > 0) & (r < groups - 1))
        def _():
            start(loads(phase, r + 1, 1 - slot))

    def behind(phase):
        @pl.when(r == 0)
        def _():
            for copy in own_backs(phase):
                copy.wait()
            start(loads(phase, 1, 1))

    def flat(buf):
        value = buf[slot]
        return value.reshape(model, value.shape[-1])

    own_place = xwin.at[window.at(window.own, rows)]
    to_pair = remote(low, own_place, pair_sems, window.to_pair)
    to_mid = remote(
        low.at[window.at(window.mid_row, mid_rows)],
        xwin.at[window.at((1 - lax.rem(window.h, 2)) * 2 * rows, mid_rows)],
        mid_sems,
        window.to_mid,
    )
    keep_win = pltpu.make_async_copy(xwin, win_out, local.at[0])

    for phase in range(phases):
        layer, kind = phase // 2, phase % 2
        kv_out, q_out, ctx_out, lse_out, gated_out, before_one, middle_low, unit_out, before_two, low_out = saved[layer]
        span = range(phase * groups, (phase + 1) * groups)

        def point(spot, span=span):
            plan.point(s, spot, span)

        @pl.when(lax.div(s, groups) == phase)
        def _():
            if kind == 0:
                if layer:

                    @pl.when(r == 0)
                    def _():
                        to_pair.wait()

                        @pl.when(window.middle)
                        def _():
                            to_mid.wait()

                        keep_win.start()

                before(phase)
                xin, offset = (xwin, 0) if layer else (hidden, window.base)
                row = small[r, 4 * layer + 2 : 4 * layer + 3, :]
                outs = (kv_out, q_out, ctx_out, lse_out, gated_out)
                attend(
                    window,
                    layer,
                    xin,
                    offset,
                    row,
                    lengths,
                    flat(left_buf),
                    flat(right_buf),
                    outs,
                    turned,
                    total,
                    r,
                    point,
                )

                @pl.when(r == groups - 1)
                def _():
                    if layer:
                        resid = current[...]
                    else:
                        resid = hidden[window.at(offset + window.own, rows), :].astype(F32)
                    value = resid + total[...] + vector(vec, layer, BIAS_ONE)
                    normed = norm_forward(value, vector(vec, layer, GAIN_ONE), vector(vec, layer, SHIFT_ONE))
                    before_one[...] = value
                    middle[...] = normed
                    middle_low[...] = normed.astype(LOW)

                point(spots_attn - 1)
                behind(phase)
            else:
                before(phase)
                point(0)
                unit = nn(middle_low[...], flat(inner_buf)) + small[r, 4 * layer + 1 : 4 * layer + 2, :]
                unit_out[0] = unit.astype(LOW)
                point(1)
                bent = jnp.tanh(GELU_C * unit * (1.0 + GELU_K * (unit * unit)))
                active = (0.5 * unit * (1.0 + bent) * small[r, 4 * layer : 4 * layer + 1, :]).astype(LOW)
                point(2)
                add_up(r, total, nn(active, flat(outer_buf)))

                @pl.when(r == groups - 1)
                def _():
                    value = middle[...] + total[...] + vector(vec, layer, BIAS_TWO)
                    normed = norm_forward(value, vector(vec, layer, GAIN_TWO), vector(vec, layer, SHIFT_TWO))
                    before_two[...] = value
                    low_out[...] = normed.astype(LOW)
                    if layer + 1 < layers:
                        current[...] = normed
                        low[...] = normed.astype(LOW)
                        to_pair.start()

                        @pl.when(window.middle)
                        def _():
                            to_mid.start()

                        xwin[window.at(window.own, rows), :] = normed.astype(LOW)

                        @pl.when(jnp.logical_not(window.middle))
                        def _():
                            empty = window.at(lax.rem(window.h + 1, 2) * 2 * rows, mid_rows)
                            xwin[empty, :] = jnp.zeros((mid_rows, model), LOW)

                point(spots_feed - 1)
                behind(phase)

    @pl.when(s == phases * groups - 1)
    def _():
        keep_win.wait()
        keep_small.wait()
        out_of_stage.wait()


def match_teacher(size, layers, tokens, point, *refs):
    refs = list(refs)
    states = [refs.pop(0) for _ in range(layers)]
    target, chosen, lengths, counts, weight = refs[:5]
    back_outs, (loss_out, grad_out) = refs[5 : 5 + layers], refs[5 + layers :]
    r = pl.program_id(0)
    rows = states[0].shape[0]

    @pl.when(r == 0)
    def _():
        loss_out[...] = jnp.zeros_like(loss_out)
        for back_out in back_outs:
            back_out[...] = jnp.zeros_like(back_out)
        loss_out[0:1, 1:2] = jnp.sum(counts[...][:, 0:1, 0:1], 0)

    count = jnp.sum(counts[...][:, 0:1, 0:1], 0)
    factor = tokens / count
    mine = pl.ds(pl.multiple_of(lax.axis_index("head") * rows, rows), rows)
    row_ok = row_mask(Window(size, rows, pl.num_programs(0)), lengths)
    total = None
    for layer in range(layers):
        goal = jnp.where(r == 0, chosen[layer, mine, :], target[0, layer]).astype(F32)
        miss = (nn(states[layer][...], weight[0]) - goal) * row_ok
        loss_out[:1, :1] += jnp.sum(jnp.sum(miss * miss, 0, keepdims=True), 1, keepdims=True)
        low = (factor * miss).astype(LOW)
        back_outs[layer][...] += nt(low, weight[0])
        grad = tn(states[layer][...], low)
        total = grad if total is None else total + grad
    grad_out[0] = total.astype(LOW)


FEED_STEP, ATTN_STEP, WEIGHT_STEP = 5.0, 6.5, 3.0


def in_order(s):
    place = jnp.clip(s, 0, len(ORDER) - 1)
    group = 0
    for index, value in enumerate(ORDER):
        group = jnp.where(place == index, value, group)
    return group


def layer_backward(size, layer, first, last, geo, reduce, times, lists, *refs):
    seqs, seq_len, heads, head_size = size
    refs = list(refs)
    take = lambda n: [refs.pop(0) for _ in range(n)]
    before_two, before_one, middle_low, unit_in, small = take(5)
    vec = take(3)
    inner, outer = take(2)
    grad_refs = take(2 if last else 1)
    xwin, query_in, kv, ctx, lse, gated, lengths, left, right = take(9)
    extra = None if first else refs.pop(0)
    left_out, right_out, grad_out, head_vec, vec_out, unit_vec = take(6)
    (mine, feed, attn, grad_kv, turned, kv_all, q_all, spread, pair_low, pair_got, mid_low, mid_got) = take(12)
    pair_sems, mid_sems, local = take(3)
    work, riders = lists[0], lists[1:]
    groups = geo.groups
    s = pl.program_id(0)
    r = lax.rem(s, groups)
    part = lax.div(s, groups)
    width = heads * head_size
    rows, model = mine.shape
    window = Window(size, rows, groups)
    block, mid_rows = window.block, window.mid_rows
    blocks = rows // block
    offset = window.base if first else 0
    here = window.at(offset + window.own, rows)
    to_pair = remote(pair_low, pair_got, pair_sems, window.to_pair)
    to_mid = remote(mid_low, mid_got, mid_sems, window.to_mid)

    spots = [7] * groups + [2 + blocks * heads] * groups + [4] * groups
    lengths_us = [FEED_STEP] * groups + [ATTN_STEP] * groups + [WEIGHT_STEP] * groups
    plan = Plan(spots)
    whole = sum(lengths_us)
    cuts = len(reduce.cuts)
    timed = []
    first_one, pace, second, third = times
    ones = [
        max(FEED_STEP * (k // cuts + 1) + 4.5, first_one + pace * k) + 0.01 * (k % cuts)
        for k in range(len(reduce.chunks))
    ]
    for k in range(len(reduce.chunks)):
        made = FEED_STEP * (k // cuts + 1) - 0.5 + 0.01 * (k % cuts)
        if k >= reduce.ring:
            made = max(made, ones[k - reduce.ring] + 0.1)
        timed.append((made, work["begin"][k]))
        timed.append((max(ones[k], made + 3.0), work["one"][k]))
        timed.append((ones[k] + second, work["two"][k]))
        timed.append((ones[k] + second + third, work["three"][k]))
    timed += [(1e6, task) for task in work["final"] + work["end"]]
    for finish, tasks in riders:
        count = max(1, len(tasks) - 1)
        timed += [(finish * whole * index / count, task) for index, task in enumerate(tasks)]
    plan.timed(lengths_us, timed)

    def points(span):
        return lambda spot: plan.point(s, spot, span)

    point_feed = points(range(groups))
    point_attn = points(range(groups, 2 * groups))
    point_weight = points(range(2 * groups, 3 * groups))

    def feeding():
        point_feed(0)
        unit = in_order(s)

        @pl.when(r == 0)
        def _():
            if last:
                cotangent, back = grad_refs
                own = pl.ds(pl.multiple_of(window.h * rows, rows), rows)
                fetch = pltpu.make_async_copy(cotangent.at[own], pair_low, local)
                fetch.start()
                fetch.wait()
                grad = pair_low[...].astype(F32) + back[...]
            else:
                grad = grad_refs[0][...]
            grad_before, grad_gain, grad_shift, grad_bias = norm_backward(
                before_two[...], vector(vec, layer, GAIN_TWO), grad
            )
            vec_out[BIAS_TWO : BIAS_TWO + 1, :] = grad_bias
            vec_out[GAIN_TWO : GAIN_TWO + 1, :] = grad_gain
            vec_out[SHIFT_TWO : SHIFT_TWO + 1, :] = grad_shift
            feed[...] = grad_before.astype(LOW)
            mine[...] = grad_before

        grad_active = nt(feed[...], outer[0])
        point_feed(1)
        value, slope = gelu_parts(unit_in[0].astype(F32))
        opened = small[0, 4 * layer : 4 * layer + 1, :]
        grad_unit = (grad_active * (slope * opened)).astype(LOW)
        unit_vec[0, 0:1, :] = jnp.sum(grad_unit.astype(F32), 0, keepdims=True)
        unit_vec[0, 1:2, :] = jnp.sum(grad_active * value, 0, keepdims=True)
        active = (value * opened).astype(LOW)
        point_feed(2)
        mine[...] += nt(grad_unit, inner[0])
        point_feed(3)
        shape = reduce.grads[0].shape[1:]
        reduce.grads[0][unit] = tn(middle_low[...], grad_unit).astype(LOW).reshape(shape)
        point_feed(4)
        reduce.grads[1][unit] = tn(feed[...], active).astype(LOW).reshape(shape)
        point_feed(5)

        @pl.when(r == groups - 1)
        def _():
            grad_before, grad_gain, grad_shift, grad_bias = norm_backward(
                before_one[...], vector(vec, layer, GAIN_ONE), mine[...]
            )
            vec_out[BIAS_ONE : BIAS_ONE + 1, :] = grad_bias
            vec_out[GAIN_ONE : GAIN_ONE + 1, :] = grad_gain
            vec_out[SHIFT_ONE : SHIFT_ONE + 1, :] = grad_shift
            mine[...] = grad_before if first else grad_before + extra[...]
            attn[...] = grad_before.astype(LOW)
            spread[...] = jnp.zeros_like(spread)

        point_feed(6)

    def attending():
        point_attn(0)
        row = small[0, 4 * layer + 2 : 4 * layer + 3, :]
        opened = row[:, width : 2 * width]
        grad_gated = nn(attn[...], right[0, :, width:])
        shared = grad_gated * ctx[0]
        grad_ctx = (grad_gated * opened).astype(LOW)
        pulled = shared * opened
        scaled = query_in[0] * jnp.asarray(0.125, LOW)
        grad_kv[...] = jnp.zeros_like(grad_kv)
        pulled_turned = pulled.T
        for piece in range(blocks):
            rows_of = slice(piece * block, (piece + 1) * block)
            keys = window.keys(piece)
            length = lengths[window.first + window.loc(piece)]
            unused = jnp.where(lax.broadcasted_iota(jnp.int32, (seq_len, block), 0) < length, 0.0, -1e30)
            for head in range(heads):
                lanes = slice(head * head_size, (head + 1) * head_size)
                later = slice(width + head * head_size, width + (head + 1) * head_size)
                key = kv[0, keys, lanes]
                scores = nt(key, scaled[rows_of, lanes]) + unused
                chances = jnp.exp(scores - lse[0, head : head + 1, rows_of])
                grad_chances = nt(kv[0, keys, later], grad_ctx[rows_of, lanes])
                delta = jnp.sum(pulled_turned[lanes, rows_of], 0, keepdims=True)
                grad_scores = (chances * (grad_chances - delta)).astype(LOW)
                turned[lanes, rows_of] = tn(key, grad_scores)
                grad_kv[keys, lanes] += nn(grad_scores, scaled[rows_of, lanes])
                grad_kv[keys, later] += nn(chances.astype(LOW), grad_ctx[rows_of, lanes])
                point_attn(1 + piece * heads + head)
        query_low = (turned[...].T * 0.125).astype(LOW)
        kv_low = grad_kv[...].astype(LOW)
        q_all[r] = query_low
        kv_all[r] = kv_low
        head_vec[0, 0:1, :width] = jnp.sum(query_low.astype(F32), 0, keepdims=True)
        head_vec[0, 0:1, 2 * width :] = jnp.sum(kv_low.astype(F32), 0, keepdims=True)
        shared_sum = jnp.sum(shared, 0, keepdims=True)
        lane = lax.broadcasted_iota(jnp.int32, (1, 128), 1)
        by_head = jnp.zeros((1, 128), F32)
        for head in range(heads):
            one = jnp.sum(shared_sum[:, head * head_size : (head + 1) * head_size], 1, keepdims=True)
            by_head = jnp.where(lane == head, one, by_head)
        head_vec[0, 1:2, :128] = by_head
        spread[...] += nt(kv_low, left[0])
        mine[...] += nt(query_low, right[0, :, :width])

        @pl.when(r == groups - 1)
        def _():
            pair_low[...] = spread[window.at(window.pair, rows), :].astype(LOW)
            to_pair.start()

            @pl.when(window.middle)
            def _():
                mid_low[...] = spread[window.at(window.mid, mid_rows), :].astype(LOW)
                to_mid.start()

        point_attn(1 + blocks * heads)

    def weighing():
        point_weight(0)
        left_out[0] = tn(xwin[window.at(offset, 2 * seq_len), :], kv_all[r]).astype(LOW)
        point_weight(1)
        right_out[0, :, :width] = tn(xwin[here, :], q_all[r]).astype(LOW)
        point_weight(2)
        right_out[0, :, width:] = tn(attn[...], gated[0]).astype(LOW)

        @pl.when(r == groups - 1)
        def _():
            to_pair.wait()
            mine[...] += spread[window.at(window.own, rows), :] + pair_got[...].astype(F32)

            @pl.when(window.middle)
            def _():
                to_mid.wait()
                mine[window.at(window.mid_row, mid_rows), :] += mid_got[...].astype(F32)

            grad_out[...] = mine[...].astype(grad_out.dtype)

        point_weight(3)

    pl.when(part == 0)(feeding)
    pl.when(part == 1)(attending)
    pl.when(part == 2)(weighing)


def on_device(
    ndp,
    groups,
    hidden_in,
    seq_lengths,
    layer_map,
    teacher_states,
    out_cotangent,
    query_weight,
    key_weight,
    value_weight,
    query_value_bias,
    output_weight,
    branch_bias,
    norm_gain,
    norm_shift,
    inner_weight,
    inner_bias,
    outer_weight,
    head_alpha,
    head_noise,
    unit_alpha,
    unit_noise,
    map_weight,
):
    tokens_dev, model = hidden_in.shape
    seqs_dev = seq_lengths.shape[0]
    seq_len = tokens_dev // seqs_dev
    width = query_weight.shape[2]
    units = inner_weight.shape[2]
    layers, heads = head_alpha.shape
    head_size = width // heads
    rows = tokens_dev // groups
    feats = model // ndp
    geo = Geometry(ndp, groups)
    size = (seqs_dev, seq_len, heads, head_size)
    window = Window(size, rows, groups)
    blocks = rows // window.block
    dp = lax.axis_index("dp")

    def slices(array):
        return array.reshape(array.shape[0], geo.size_y, geo.size_x, 2, feats, array.shape[-1])

    def matrices(arrays):
        return [(array.reshape(groups, model, array.shape[-1]), "group") for array in arrays]

    def pairs(cols, steps, m=0):
        out, begin = [], 0
        for step in steps:
            out.append([(m, begin, step, False), (m + 1, begin, step, True)])
            begin += step
        return out if begin == cols else [[(m, 0, cols, False), (m + 1, 0, cols, True)]]

    key_value = slices(jnp.concatenate([key_weight, value_weight], 2))
    query_output = slices(jnp.concatenate([query_weight, jnp.swapaxes(output_weight, 1, 2)], 2))
    inner, outer = slices(inner_weight), slices(outer_weight)

    _, unit_back = jax.vjp(partial(gate_open, unit_noise), unit_alpha)
    _, head_back = jax.vjp(partial(gate_open, head_noise), head_alpha)
    (unit_slope,) = unit_back(jnp.ones_like(unit_alpha))
    (head_slope,) = head_back(jnp.ones_like(head_alpha))
    small = jax.ShapeDtypeStruct((4 * layers, units), F32)
    vec = [(array, "once") for array in (branch_bias, norm_gain, norm_shift)]
    count = jax.ShapeDtypeStruct((8, 128), F32)
    chosen = jnp.stack(
        [lax.dynamic_index_in_dim(teacher_states, layer_map[layer], 0, keepdims=False) for layer in range(layers)]
    )

    row_block = pltpu.VMEM((rows, model), F32)
    low_block = pltpu.VMEM((rows, model), LOW)
    mid_block = pltpu.VMEM((window.mid_rows, model), LOW)
    two = pltpu.SemaphoreType.DMA((2,))
    owns, chunks = [], []
    for layer in range(layers):
        for arrays, cuts in (((key_value, query_output), ATTN_CUTS), ((inner, outer), FEED_CUTS)):
            chunks += pairs(arrays[0].shape[-1], cuts, len(owns))
            owns += [(array, layer) for array in arrays]
    chunks.append([(len(owns), 0, width, False)])
    map_slices = slices(map_weight[None])
    owns.append((map_slices, 0))
    gather = Gather(geo, owns, chunks)
    counter = Spread(geo, count, plane=True)
    outputs = []
    for layer in range(layers):
        attn_step = lambda s, layer=layer: jnp.clip(s - 2 * layer * groups, 0, groups - 1)
        feed_step = lambda s, layer=layer: jnp.clip(s - (2 * layer + 1) * groups, 0, groups - 1)
        outputs += [
            ((groups, 2 * seq_len, 2 * width), LOW, attn_step),
            ((groups, rows, width), LOW, attn_step),
            ((groups, rows, width), F32, attn_step),
            ((groups, 8, rows), F32, attn_step),
            ((groups, rows, width), LOW, attn_step),
            ((rows, model), F32, "full"),
            ((rows, model), LOW, "full"),
            ((groups, rows, units), LOW, feed_step),
            ((rows, model), F32, "full"),
            ((rows, model), LOW, "full"),
        ]
    saves = len(outputs) // layers
    outputs += [((2 * seq_len, model), LOW, "any"), ((groups,) + small.shape, F32, "any")]
    attn_buf = pltpu.VMEM((2,) + key_value.shape[1:], LOW)
    feed_buf = pltpu.VMEM((2,) + inner.shape[1:], LOW)
    others = pltpu.SemaphoreType.DMA((groups,))
    got = run(
        partial(forward, size, layers, geo, gather, counter),
        2 * layers * groups,
        [
            (hidden_in, "once"),
            *vec,
            (seq_lengths, "smem"),
            (unit_noise, "once"),
            (unit_alpha, "once"),
            (head_noise, "once"),
            (head_alpha, "once"),
            (inner_bias, "once"),
            (query_value_bias, "once"),
            (key_value, "any"),
            (query_output, "any"),
            (inner, "any"),
            (outer, "any"),
            (map_slices, "any"),
        ],
        outputs,
        [
            attn_buf,
            attn_buf,
            feed_buf,
            feed_buf,
            pltpu.SemaphoreType.DMA((2, 2, 2)),
            pltpu.SemaphoreType.DMA((2, 2)),
            row_block,
            row_block,
            row_block,
            low_block,
            pltpu.VMEM((2 * seq_len, model), LOW),
            pltpu.VMEM((groups,) + small.shape, F32),
            pltpu.VMEM(small.shape, F32),
            others,
            others,
            pltpu.VMEM(map_slices.shape[1:], LOW),
            pltpu.VMEM((width, rows), F32),
            two,
            two,
            pltpu.SemaphoreType.DMA((5,)),
        ],
        30e9,
        "forward",
        [gather, counter, Deal(geo, chosen), Lend(geo, gather)],
        1,
        1,
        True,
    )
    records = [got[layer * saves : (layer + 1) * saves] for layer in range(layers)]
    xwins, small = [hidden_in, got[layers * saves]], got[layers * saves + 1]
    *weights, counts, target = got[layers * saves + 2 :]
    weights = matrices(weights)
    lows = [record[-1] for record in records]
    *spread, loss, grad_map = run(
        partial(match_teacher, size, layers, float(tokens_dev * ndp)),
        groups,
        [(low, "full") for low in lows]
        + [(target, lambda r: jnp.maximum(r - 1, 0)), (chosen, "full"), (seq_lengths, "smem"), (counts, "full")]
        + weights[-1:],
        [
            *[((rows, model), F32, "full")] * layers,
            ((8, 128), F32, "full"),
            ((groups, model, width), LOW, "group"),
        ],
        [],
        4e9,
        "match_teacher",
    )

    grads = [(out_cotangent, "any"), (spread[-1], "once")]
    results = [{} for _ in range(layers)]
    riders, waiting, finishes = [], [], []

    def settle(got):
        for (layer, name), value in zip(waiting, got):
            results[layer][name] = value

    def clipped(part):
        return lambda s: jnp.clip(s - part * groups, 0, groups - 1)

    block_out = None
    riders = [Scatter(geo, [slices(grad_map)], [[(0, 0, width, False)]])]
    waiting, finishes = [(0, "map")], [0.7]
    for layer in reversed(range(layers)):
        kv, query, ctx, lse, gated, before_one, middle_low, unit_in, before_two, _ = records[layer]
        attn_weights, feed_weights = weights[4 * layer : 4 * layer + 2], weights[4 * layer + 2 : 4 * layer + 4]
        if layer in (0, layers - 1):
            part = (0, rows // 2) if layer else (rows // 2, rows // 2)
            riders.append(Spread(geo, lows[-1], part=part, into=block_out))
            waiting.append((0, "block_out"))
            finishes.append(1.0)
        reduce = Reduce(geo, [(feats, units)] * 2, BACK_CUTS)
        left, right, grad, head_vec, vec_out, unit_vec, *got = run(
            partial(
                layer_backward,
                size,
                layer,
                layer == 0,
                layer == layers - 1,
                geo,
                reduce,
                TIMES_LAST if layer == layers - 1 else TIMES,
            ),
            3 * groups,
            [
                (before_two, "once"),
                (before_one, "once"),
                (middle_low, "once"),
                (unit_in, in_order),
                (small, lambda s: jnp.where(s < groups, in_order(s), lax.rem(s, groups))),
                *vec,
            ]
            + [(array, in_order) for array, _ in feed_weights]
            + grads
            + [
                (xwins[layer], "once"),
                (query, clipped(1)),
                (kv, clipped(1)),
                (ctx, clipped(1)),
                (lse, clipped(1)),
                (gated, clipped(2)),
                (seq_lengths, "smem"),
            ]
            + [(array, clipped(1)) for array, _ in attn_weights]
            + ([(spread[layer - 1], "once")] if layer else []),
            [((groups, model, 2 * width), LOW, clipped(2))] * 2
            + [
                ((rows, model), F32 if layer else LOW, "full"),
                ((groups, 8, units), F32, clipped(1)),
                ((8, model), F32, "full"),
                ((groups, 8, units), F32, in_order),
            ],
            [
                row_block,
                low_block,
                low_block,
                pltpu.VMEM((2 * seq_len, 2 * width), F32),
                pltpu.VMEM((width, rows), F32),
                pltpu.VMEM((groups, 2 * seq_len, 2 * width), LOW),
                pltpu.VMEM((groups, rows, width), LOW),
                pltpu.VMEM((2 * seq_len, model), F32),
                low_block,
                low_block,
                mid_block,
                mid_block,
                two,
                two,
                pltpu.SemaphoreType.DMA,
            ],
            25e9,
            "layer_backward",
            [reduce] + [Timed(rider, finish) for rider, finish in zip(riders, finishes)],
            1,
            2 + layers - 1 - layer,
            True,
            LARGE_LIMIT,
        )
        results[layer]["inner"], results[layer]["outer"] = got[:2]
        settle(got[2:])
        block_out = results[0]["block_out"]
        riders = [Scatter(geo, [slices(left), slices(right)], pairs(2 * width, LAST_CUTS if layer == 0 else ATTN_CUTS))]
        waiting, finishes = [(layer, "kv"), (layer, "qo")], [0.75]
        grads = [(grad, "once")]
        results[layer].update(vec=vec_out, unit=unit_vec, head=head_vec)

    everywhere = (0, feats, feats)
    unit_count, qv_cols = units // ndp, width // ndp
    items = [(results[layer]["vec"], False, (0, 6), everywhere) for layer in range(layers)]
    items += [(results[layer]["unit"], True, (0, 2), (0, unit_count, unit_count)) for layer in range(layers)]
    for layer in range(layers):
        items += [(results[layer]["head"], True, (0, 1), (0, qv_cols, qv_cols))]
        items += [(results[layer]["head"], True, (0, 1), (3 * width, qv_cols, qv_cols))]
    items += [(results[layer]["head"], True, (1, 2), (0, 0, 128)) for layer in range(layers)]
    items += [(loss, False, (0, 1), (0, 0, 128))]
    riders += [Fold(geo, items), Spread(geo, grad)]
    waiting += [(0, "sums"), (0, "grad_hidden")]
    settle(run(only_move, 1, [], [], [], 0, "scatter_last", riders, 1, 2 + layers))
    sums = results[0]["sums"]
    by_feature = sums[: 6 * layers, :feats].reshape(layers, 3, 2, feats)
    by_unit = sums[6 * layers : 8 * layers, :unit_count].reshape(layers, 2, unit_count)
    by_column = sums[8 * layers : 10 * layers, :qv_cols].reshape(layers, 2, qv_cols)
    by_head = sums[10 * layers : 11 * layers, :heads]
    loss_sums = sums[11 * layers, :2]
    distill_loss = loss_sums[0] / (loss_sums[1] / (ndp * groups) * model * layers)
    own_slope = lax.dynamic_slice(unit_slope, (0, dp * unit_count), (layers, unit_count))

    def stacked(member, cols, turned=False):
        arrays = [results[layer][member][:, cols] for layer in range(layers)]
        return jnp.stack([array.T if turned else array for array in arrays])

    front, rear, whole = slice(0, width), slice(width, 2 * width), slice(None)
    return (
        block_out.reshape(tokens_dev, model),
        results[0]["grad_hidden"].reshape(tokens_dev, model).astype(F32),
        distill_loss,
        stacked("qo", front),
        stacked("kv", front),
        stacked("kv", rear),
        by_column,
        stacked("qo", rear, True),
        by_feature[:, 0],
        by_feature[:, 1],
        by_feature[:, 2],
        stacked("inner", whole),
        by_unit[:, 0],
        stacked("outer", whole, True),
        by_head * head_slope,
        by_unit[:, 1] * own_slope,
        results[0]["map"],
    )


def solution(mesh):
    in_specs = (
        P("dp", None),
        P("dp"),
        P(),
        P(None, "dp", "head"),
        P("dp", None),
        P(None, None, "head"),
        P(None, None, "head"),
        P(None, None, "head"),
        P(None, None, "head"),
        P(None, "head", None),
        P(),
        P(),
        P(),
        P(None, None, "head"),
        P(None, "head"),
        P(None, "head", None),
        P(None, "head"),
        P(None, "head"),
        P(None, "head"),
        P(None, "head"),
        P(None, "head"),
    )
    out_specs = (
        P("dp", None),
        P("dp", None),
        P(),
        P(None, "dp", "head"),
        P(None, "dp", "head"),
        P(None, "dp", "head"),
        P(None, None, ("head", "dp")),
        P(None, "head", "dp"),
        P(None, None, "dp"),
        P(None, None, "dp"),
        P(None, None, "dp"),
        P(None, "dp", "head"),
        P(None, ("head", "dp")),
        P(None, "head", "dp"),
        P(None, "head"),
        P(None, ("head", "dp")),
        P("dp", "head"),
    )
    return jax.shard_map(
        partial(on_device, mesh.shape["dp"], mesh.shape["head"]),
        mesh=mesh,
        in_specs=in_specs,
        out_specs=out_specs,
        check_vma=False,
    )
```

```python
from functools import partial

import jax
import jax.numpy as jnp
from jax import lax
from jax.experimental import pallas as pl
from jax.experimental.pallas import tpu as pltpu
from jax.sharding import PartitionSpec as P

BETA = 2.0 / 3.0
EPS = 1e-05
LOW = jnp.bfloat16
F32 = jnp.float32
GELU_C = 0.7978845608028654
GELU_K = 0.044715
VMEM_LIMIT = 56 * 1024 * 1024
LARGE_LIMIT = 62 * 1024 * 1024
ATTN_CUTS = (128, 256)
FEED_CUTS = (256, 256, 256)
BACK_CUTS = (384, 384)
LAST_CUTS = (128, 128, 128)
ORDER = (1, 3, 2, 0)
TIMES_LAST = (8.0, 3.6, 6.0, 8.0)
TIMES = (9.0, 5.0, 7.0, 8.0)
FORWARD_ATTN_STEP, FORWARD_FEED_STEP, HALO_WAIT = 4.5, 3.2, 14.0
MESH = pl.DeviceIdType.MESH


def gate_open(noise, alpha):
    return jnp.clip(jax.nn.sigmoid((noise + alpha) / BETA) * 1.2 - 0.1, 0.0, 1.0)


def product(left, right, dims):
    return lax.dot_general(left, right, ((dims[:1], dims[1:]), ((), ())), preferred_element_type=F32)


def nn(left, right):
    return product(left, right, (1, 0))


def nt(left, right):
    return product(left, right, (1, 1))


def tn(left, right):
    return product(left, right, (0, 0))


def factor_pair(count):
    side = 1
    for trial in range(1, count + 1):
        if count % trial == 0 and trial * trial <= count:
            side = trial
    return side, count // side


def block_of(shape, place):
    if place == "once":
        return pl.BlockSpec(shape, lambda r: (0,) * len(shape), pipeline_mode=pl.Buffered(1))
    if place == "full":
        return pl.BlockSpec(shape, lambda r: (0,) * len(shape))
    return pl.BlockSpec((1,) + tuple(shape[1:]), lambda r: (place(r),) + (0,) * (len(shape) - 1))


def spec_of(array, kind):
    if kind == "any":
        return pl.BlockSpec(memory_space=pl.ANY)
    if kind == "smem":
        return pl.BlockSpec(memory_space=pltpu.SMEM)
    if kind == "group":
        return block_of(array.shape, lambda r: r)
    return block_of(array.shape, kind)


class Plan:
    def __init__(self, spots):
        self.spots = spots
        self.slots = [(step, spot) for step, count in enumerate(spots) for spot in range(count)]
        self.chosen = {slot: [] for slot in self.slots}

    def slot(self, step, spot):
        return self.slots.index((step, spot % self.spots[step]))

    def spread(self, tasks, first, last):
        for share, _, task in sorted(tasks, key=lambda item: item[:2]):
            self.chosen[self.slots[first + round(share * (last - first))]].append(task)

    def even(self, tasks, first, last):
        count = len(tasks)
        self.spread([((index + 1) / count, index, task) for index, task in enumerate(tasks)], first, last)

    def paced(self, lengths, waits, tasks, first, finish, count, due):
        times, now = [], 0.0
        for length, number in zip(lengths, self.spots):
            for _ in range(number):
                now += waits.get(len(times), 0.0)
                times.append(now)
                now += length / number
        pace = (times[finish] - times[first]) / count
        for index, task in enumerate(tasks):
            later = [slot for slot, at in enumerate(times) if at >= times[first] + pace * (index + 1)]
            place = min([later[0] if later else len(times) - 1] + [slot for number, slot in due if index < number])
            self.chosen[self.slots[place]].append(task)

    def timed(self, lengths, tasks):
        times, now = [], 0.0
        for length, count in zip(lengths, self.spots):
            times += [now + length * spot / count for spot in range(count)]
            now += length
        for time, task in sorted(tasks, key=lambda item: item[0]):
            later = [number for number, at in enumerate(times) if at >= time]
            self.chosen[self.slots[later[0] if later else len(times) - 1]].append(task)

    def point(self, r, spot, span):
        for step in span:
            tasks = self.chosen.get((step, spot), ())
            if tasks:

                @pl.when(r == step)
                def _(tasks=tasks):
                    for task in tasks:
                        task()


def run(body, steps, inputs, outputs, scratch, flops, name, riders=(), points=1, number=None, placed=False, limit=VMEM_LIMIT):
    inputs, outputs, scratch = list(inputs), list(outputs), list(scratch)
    at = [len(inputs), len(outputs), len(scratch)]
    starts, sizes = [], []
    for rider in riders:
        starts.append((len(inputs), len(outputs), len(scratch)))
        inputs += rider.inputs
        outputs += rider.outputs
        scratch += rider.scratch
        sizes.append((len(rider.inputs), len(rider.outputs), len(rider.scratch)))
    out_shape = [jax.ShapeDtypeStruct(shape, dtype) for shape, dtype, _ in outputs]
    moved = sum(a.size * a.dtype.itemsize for a, kind in inputs if kind != "any")
    n_in, n_out = len(inputs), len(outputs)
    aliases = {}
    for rider, begin in zip(riders, starts):
        aliases.update({begin[0] + i: begin[1] + o for i, o in getattr(rider, "aliases", {}).items()})
    peers = []
    for rider in riders:
        peers += [peer for peer in rider.peers if peer not in peers]

    def whole(*refs):
        kinds = refs[:n_in], refs[n_in : n_in + n_out], refs[n_in + n_out :]
        own = [ref for part, n in zip(kinds, at) for ref in part[:n]]
        lists = [
            rider.tasks(*[part[i : i + n] for part, i, n in zip(kinds, start, size)])
            for rider, start, size in zip(riders, starts, sizes)
        ]
        r = pl.program_id(0)
        if riders:

            @pl.when(r == 0)
            def _():
                riders[0].geo.greet(peers)

        if placed:
            body(lists, *own)
            return
        plan = Plan([points] * steps)
        listed = []
        for number, tasks in enumerate(lists):
            for index, task in enumerate(tasks):
                listed.append((index / max(1, len(tasks) - 1), (number, index), task))
        plan.spread(listed, 0, len(plan.slots) - 1)
        body(lambda spot, span=range(steps): plan.point(r, spot, span), *own)

    params = {"vmem_limit_bytes": limit}
    if riders:
        params.update(collective_id=number, has_side_effects=True)
    return pl.pallas_call(
        whole,
        name=name,
        grid=(steps,),
        in_specs=[spec_of(a, kind) for a, kind in inputs],
        out_specs=[spec_of(o, kind) for o, (_, _, kind) in zip(out_shape, outputs)],
        scratch_shapes=scratch,
        out_shape=out_shape,
        input_output_aliases=aliases,
        compiler_params=pltpu.CompilerParams(**params),
        cost_estimate=pl.CostEstimate(flops=int(flops), bytes_accessed=int(moved), transcendentals=0),
    )(*[a for a, _ in inputs])


def only_move(point):
    point(0)


class Geometry:
    def __init__(self, ndp, groups):
        self.ndp, self.groups = ndp, groups
        self.size_y, self.size_x = factor_pair(ndp // 2)

    def here(self):
        dp, h = lax.axis_index("dp"), lax.axis_index("head")
        return lax.rem(dp, 2), lax.rem(lax.div(dp, 2), self.size_x), lax.div(dp, 2 * self.size_x), h

    def place(self, c=0, y=0, x=0, z=0):
        core, ix, iy, h = self.here()
        core = 1 - core if c else core
        iy = lax.rem(iy + (y + self.size_y), self.size_y) if y else iy
        ix = lax.rem(ix + (x + self.size_x), self.size_x) if x else ix
        h = lax.rem(h + (z + self.groups), self.groups) if z else h
        return iy, ix, core, h

    def device(self, **to):
        iy, ix, core, h = self.place(**to)
        return ((iy * self.size_x + ix) * 2 + core, h)

    def axes(self):
        out = [dict(c=1)]
        out += [dict(y=y) for y in range(1, self.size_y)]
        out += [dict(x=x) for x in range(1, self.size_x)]
        return out + self.column()

    def column(self):
        return [dict(z=z) for z in range(1, self.groups)]

    def plane(self):
        out = []
        for c in range(2):
            for y in range(self.size_y):
                for x in range(self.size_x):
                    to = {key: value for key, value in (("c", c), ("y", y), ("x", x)) if value}
                    if to:
                        out.append(to)
        return out

    def greet(self, peers):
        barrier = pltpu.get_barrier_semaphore()
        for peer in peers:
            pl.semaphore_signal(barrier, inc=1, device_id=self.device(**peer), device_id_type=MESH)
        pl.semaphore_wait(barrier, len(peers))


class Mover:
    def __init__(self, geo, send, recv):
        self.geo, self.send, self.recv, self.ids = geo, send, recv, {}

    def __call__(self, key, src, dst, **to):
        index = self.ids.setdefault(key, len(self.ids))
        return pltpu.make_async_remote_copy(
            src_ref=src,
            dst_ref=dst,
            send_sem=self.send.at[index],
            recv_sem=self.recv.at[index],
            device_id=self.geo.device(**to),
            device_id_type=MESH,
        )


def back(to):
    return {key: value if key == "c" else -value for key, value in to.items()}


def start(copies):
    for copy in copies:
        copy.start()


def arrive(copies):
    for copy in copies:
        copy.wait_recv()


def leave(copies):
    for copy in copies:
        copy.wait_send()


class Column:
    def __init__(self, geo, block, slot, send, recv, base, absolute=False):
        self.absolute = absolute
        self.geo, self.slot, self.send, self.recv, self.base = geo, slot, send, recv, base
        self.h = geo.here()[3]
        self.block = block

    def copy(self, r):
        return pltpu.make_async_remote_copy(
            src_ref=self.block,
            dst_ref=self.slot(0 if self.absolute else r),
            send_sem=self.send.at[self.base + r],
            recv_sem=self.recv.at[self.base + r],
            device_id=self.geo.device(z=-r),
            device_id_type=MESH,
        )

    def begin(self):
        self.copy(2).start()
        pl.when(self.h != 0)(lambda: self.copy(1).start())
        pl.when(self.h != 3)(lambda: self.copy(3).start())

    def by_middle(self, act):
        @pl.when((self.h > 0) & (self.h < 3))
        def _():
            there = 1 + 2 * lax.rem(self.h, 2)
            dp, _ = self.geo.device()
            act(
                pltpu.make_async_remote_copy(
                    src_ref=self.slot(2),
                    dst_ref=self.slot(2 if self.absolute else there),
                    send_sem=self.send.at[self.base],
                    recv_sem=self.recv.at[self.base + there],
                    device_id=(dp, self.h + 1 - 2 * lax.rem(self.h, 2)),
                    device_id_type=MESH,
                )
            )

    def relay(self):
        self.copy(2).wait_recv()
        self.by_middle(lambda copy: copy.start())

    def arrive(self):
        self.copy(1).wait_recv()
        self.copy(3).wait_recv()

    def leave(self):
        self.copy(2).wait_send()
        pl.when(self.h != 0)(lambda: self.copy(1).wait_send())
        pl.when(self.h != 3)(lambda: self.copy(3).wait_send())
        self.by_middle(lambda copy: copy.wait_send())


class Delivery:
    def __init__(self, geo, block, slot, merged, send, recv, base):
        self.h, self.block, self.slot, self.merged = geo.here()[3], block, slot, merged

        def copy(r, dst, index, z):
            return pltpu.make_async_remote_copy(
                src_ref=block(r),
                dst_ref=dst,
                send_sem=send.at[base + r],
                recv_sem=recv.at[base + index],
                device_id=geo.device(z=z),
                device_id_type=MESH,
            )

        self.copy = lambda r: copy(r, slot(r), r, r)
        self.last_to_middle = lambda: copy(1, merged, 0, -1)
        self.first_to_middle = lambda: copy(3, merged, 0, 1)

    def begin(self, r):
        if r == 1:
            pl.when(self.h != 3)(lambda: self.copy(1).start())
            pl.when(self.h == 3)(lambda: self.last_to_middle().start())

            @pl.when(self.h == 0)
            def _():
                self.slot(1)[...] = jnp.zeros_like(self.slot(1))

        if r == 3:
            pl.when(self.h != 0)(lambda: self.copy(3).start())
            pl.when(self.h == 0)(lambda: self.first_to_middle().start())

            @pl.when(self.h == 3)
            def _():
                self.slot(3)[...] = jnp.zeros_like(self.slot(3))

    def merge(self):
        @pl.when((self.h > 0) & (self.h < 3))
        def _():
            self.last_to_middle().wait_recv()
            mine = self.block(2)
            mine[...] = (mine[...].astype(F32) + self.merged[...].astype(F32)).astype(LOW)

        self.copy(2).start()

    def arrive(self):
        self.copy(2).wait_recv()
        pl.when(self.h != 0)(lambda: self.copy(1).wait_recv())
        pl.when(self.h != 3)(lambda: self.copy(3).wait_recv())

    def leave(self):
        for r in (1, 2, 3):
            self.copy(r).wait_send()


class Gather:
    def __init__(self, geo, owns, chunks):
        self.geo, self.chunks, self.peers = geo, chunks, geo.axes()
        self.layers = [layer for _, layer in owns]
        self.inputs = [(own, "any") for own, _ in owns]
        self.outputs = [((geo.groups,) + own.shape[1:], LOW, "any") for own, _ in owns]
        halves = sum(len(chunk) for chunk in chunks)
        sems = pltpu.SemaphoreType.DMA((halves * 2 * geo.size_x * geo.size_y,))
        ends = pltpu.SemaphoreType.DMA((halves * geo.groups,))
        self.scratch = [sems, sems, ends, ends]

    def tasks(self, owns, outs, scratch):
        self.outs = outs
        geo = self.geo
        move = Mover(geo, *scratch[:2])
        groups, sx, sy = geo.groups, geo.size_x, geo.size_y
        bases = {}
        for chunk, parts in enumerate(self.chunks):
            for half in range(len(parts)):
                bases[chunk, half] = groups * len(bases)
        others = pl.ds(1, groups - 1)
        owns = [own.at[layer] for own, layer in zip(owns, self.layers)]

        def columns(chunk, half):
            m, col, cols, _ = self.chunks[chunk][half]
            return m, pl.ds(col, cols)

        def along(chunk, half):
            m, cols = columns(chunk, half)
            iy, ix, core, _ = geo.place()
            return Column(
                geo,
                owns[m].at[iy, ix, core, :, cols],
                lambda r: outs[m].at[r, iy, ix, core, :, cols],
                *scratch[2:],
                bases[chunk, half],
            )

        def hop(chunk, half, block, to):
            m, cols = columns(chunk, half)
            iy, ix, core, _ = geo.place(**block)
            part = outs[m].at[others, iy, ix, core, :, cols]
            return move(("p", chunk, half, str(block), str(to)), part, part, **back(to))

        ways_x = [dict(x=x) for x in range(1, sx)]
        ways_y = [dict(y=y) for y in range(1, sy)]
        corners = [dict(x=x, y=y) for x in range(1, sx) for y in range(1, sy)]

        def halves(chunk):
            return range(len(self.chunks[chunk]))

        def alongs(chunk):
            return [along(chunk, half) for half in halves(chunk)]

        def firsts(chunk):
            return [hop(chunk, half, {}, to) for half in halves(chunk) for to in ways_x + ways_y]

        def seconds(chunk):
            out = []
            for half in halves(chunk):
                near, far = (ways_y, ways_x) if self.chunks[chunk][half][3] else (ways_x, ways_y)
                out += [hop(chunk, half, block, to) for block in near for to in far]
            return out

        def cores(chunk, blocks):
            return [hop(chunk, half, block, dict(c=1)) for half in halves(chunk) for block in blocks]

        count = len(self.chunks)

        def begin():
            for chunk in range(min(2, count)):
                for column in alongs(chunk):
                    column.begin()

        def level_zero(chunk):
            for column in alongs(chunk):
                column.relay()
            if chunk + 2 < count:
                for column in alongs(chunk + 2):
                    column.begin()

        def level_one(chunk):
            for column in alongs(chunk):
                column.arrive()
            start(firsts(chunk))
            start(cores(chunk, [{}]))

        def level_two(chunk):
            arrive(firsts(chunk))
            start(seconds(chunk))
            start(cores(chunk, ways_x + ways_y))

        def level_three(chunk):
            arrive(seconds(chunk))
            start(cores(chunk, corners))

        def level_four(chunk):
            arrive(cores(chunk, [{}] + ways_x + ways_y + corners))

        def end():
            for chunk in range(count):
                for column in alongs(chunk):
                    column.leave()
                leave(firsts(chunk) + seconds(chunk) + cores(chunk, [{}] + ways_x + ways_y + corners))

        out = [begin]
        self.done = []
        for time in range(count + 4):
            for level, late in ((level_zero, 0), (level_one, 1), (level_two, 2), (level_three, 3), (level_four, 4)):
                if 0 <= time - late < count:
                    out.append(partial(level, time - late))
            if time >= 4:
                self.done.append(len(out))
        return out + [end]


class Lend:
    def __init__(self, geo, rider):
        self.geo, self.rider, self.peers = geo, rider, []
        self.inputs, self.outputs, self.scratch = [], [], []

    def tasks(self, owns, outs, scratch):
        return [self.rider.outs]


class Timed:
    def __init__(self, rider, finish):
        self.geo, self.peers, self.inputs, self.outputs, self.scratch = (
            rider.geo,
            rider.peers,
            rider.inputs,
            rider.outputs,
            rider.scratch,
        )
        self.rider, self.finish, self.aliases = rider, finish, getattr(rider, "aliases", {})

    def tasks(self, inputs, outs, scratch):
        return self.finish, self.rider.tasks(inputs, outs, scratch)


class Scatter:
    def __init__(self, geo, grads, chunks):
        self.geo, self.chunks, self.peers = geo, chunks, geo.axes()
        self.inputs = [(grad, "any") for grad in grads]
        self.outputs = [(grad.shape[4:], F32, "full") for grad in grads]
        feats = grads[0].shape[4]
        halves = [half for chunk in chunks for half in chunk]
        each = 1 + (geo.size_x - 1) + (geo.size_y - 1)
        sems = pltpu.SemaphoreType.DMA((len(halves) * each,))
        ends = pltpu.SemaphoreType.DMA((len(halves) * geo.groups,))
        self.scratch = [sems, sems, ends, ends, pltpu.SemaphoreType.DMA((len(halves),))]
        for _, _, cols, y_first in halves:
            near, far = (geo.size_y, geo.size_x) if y_first else (geo.size_x, geo.size_y)
            self.scratch += [
                pltpu.VMEM(shape, LOW)
                for shape in (
                    (geo.groups, geo.size_y, geo.size_x, feats, cols),
                    (geo.groups, geo.size_y, geo.size_x, feats, cols),
                    (near - 1, geo.groups, far, feats, cols),
                    (far - 1, geo.groups, feats, cols),
                    (geo.groups, feats, cols),
                )
            ]

    def tasks(self, grads, outs, scratch):
        geo, (send, recv, end_send, end_recv, local), buffers = self.geo, scratch[:5], scratch[5:]
        move = Mover(geo, send, recv)
        groups, sx, sy = geo.groups, geo.size_x, geo.size_y
        index = {}
        for chunk, halves in enumerate(self.chunks):
            for half in range(len(halves)):
                index[chunk, half] = len(index)

        def parts(chunk, half):
            m, col, cols, y_first = self.chunks[chunk][half]
            number = index[chunk, half]
            return grads[m], pl.ds(col, cols), y_first, buffers[5 * number : 5 * number + 5]

        def load(chunk, half):
            grad, cols, _, bufs = parts(chunk, half)
            _, _, core, _ = geo.place()
            return pltpu.make_async_copy(
                grad.at[:, :, :, core, :, cols], bufs[0], local.at[index[chunk, half]]
            )

        def cross(chunk, half):
            grad, cols, _, bufs = parts(chunk, half)
            _, _, core, _ = geo.place(c=1)
            return move(("c", chunk, half), grad.at[:, :, :, core, :, cols], bufs[1], c=1)

        def near(chunk, half):
            _, _, y_first, bufs = parts(chunk, half)
            out = []
            for step in range(1, sy if y_first else sx):
                to = dict(y=step) if y_first else dict(x=step)
                iy, ix, _, _ = geo.place(**to)
                part = bufs[0].at[:, iy] if y_first else bufs[0].at[:, :, ix]
                out.append(move(("n", chunk, half, step), part, bufs[2].at[step - 1], **to))
            return out

        def far(chunk, half):
            _, _, y_first, bufs = parts(chunk, half)
            out = []
            for step in range(1, sx if y_first else sy):
                to = dict(x=step) if y_first else dict(y=step)
                iy, ix, _, _ = geo.place(**to)
                out.append(move(("f", chunk, half, step), bufs[0].at[:, iy, ix], bufs[3].at[step - 1], **to))
            return out

        def along(chunk, half):
            _, _, _, bufs = parts(chunk, half)
            iy, ix, _, _ = geo.place()
            return Delivery(
                geo,
                lambda r: bufs[0].at[r, iy, ix],
                lambda r: bufs[4].at[r],
                bufs[4].at[0],
                end_send,
                end_recv,
                groups * index[chunk, half],
            )

        def each(chunk):
            return range(len(self.chunks[chunk]))

        def begin_one(chunk):
            for half in each(chunk):
                cross(chunk, half).start()
                load(chunk, half).start()

        count = len(self.chunks)

        def begin():
            for chunk in range(min(2, count)):
                begin_one(chunk)

        def level_one(chunk):
            for half in each(chunk):
                _, _, _, bufs = parts(chunk, half)
                load(chunk, half).wait()
                cross(chunk, half).wait_recv()
                for r in range(groups):
                    bufs[0][r] = (bufs[0][r].astype(F32) + bufs[1][r].astype(F32)).astype(LOW)
                start(near(chunk, half))
            if chunk + 2 < count:
                begin_one(chunk + 2)

        def level_two(chunk):
            iy, ix, _, _ = geo.place()
            for half in each(chunk):
                _, _, y_first, bufs = parts(chunk, half)
                arrive(near(chunk, half))
                for r in range(groups):
                    total = (bufs[0][r, iy] if y_first else bufs[0][r, :, ix]).astype(F32)
                    for other in range(bufs[2].shape[0]):
                        total = total + bufs[2][other, r].astype(F32)
                    if y_first:
                        bufs[0][r, iy] = total.astype(LOW)
                    else:
                        bufs[0][r, :, ix] = total.astype(LOW)
                start(far(chunk, half))

        def level_three(chunk):
            iy, ix, _, _ = geo.place()
            for half in each(chunk):
                _, _, _, bufs = parts(chunk, half)
                arrive(far(chunk, half))
                for r in range(groups):
                    total = bufs[0][r, iy, ix].astype(F32)
                    for other in range(bufs[3].shape[0]):
                        total = total + bufs[3][other, r].astype(F32)
                    bufs[0][r, iy, ix] = total.astype(LOW)
                for r in (1, 3):
                    along(chunk, half).begin(r)

        def level_merge(chunk):
            for half in each(chunk):
                along(chunk, half).merge()

        def level_four(chunk):
            iy, ix, _, _ = geo.place()
            for half in each(chunk):
                m, col, cols, _ = self.chunks[chunk][half]
                _, _, _, bufs = parts(chunk, half)
                along(chunk, half).arrive()
                total = bufs[0][0, iy, ix].astype(F32)
                for r in range(1, groups):
                    total = total + bufs[4][r].astype(F32)
                outs[m][:, col : col + cols] = total

        def end():
            for chunk in range(count):
                for half in each(chunk):
                    leave([cross(chunk, half)] + near(chunk, half) + far(chunk, half))
                    along(chunk, half).leave()

        out = [begin]
        levels = (level_one, level_two, level_three, level_merge, level_four)
        for time in range(count + 4):
            for late, level in enumerate(levels):
                if 0 <= time - late < count:
                    out.append(partial(level, time - late))
        return out + [end]


class Reduce:
    def __init__(self, geo, shapes, cuts):
        self.geo, self.peers = geo, geo.axes()
        self.count = len(shapes)
        self.inputs = []
        self.outputs = [(shape, F32, "full") for shape in shapes]
        self.cuts, begin = [], 0
        for cut in cuts:
            self.cuts.append((begin, cut))
            begin += cut
        if begin != shapes[0][1]:
            self.cuts = [(0, shapes[0][1])]
        self.chunks = [(r, cut) for r in ORDER for cut in range(len(self.cuts))]
        each = 1 + (geo.size_x - 1) + (geo.size_y - 1)
        sems = pltpu.SemaphoreType.DMA((self.count * len(self.chunks) * each,))
        ends = pltpu.SemaphoreType.DMA((self.count * len(self.cuts) * geo.groups,))
        self.scratch = [sems, sems, ends, ends, pltpu.SemaphoreType.REGULAR]
        for m, (feats, n) in enumerate(shapes):
            near, far = (geo.size_y, geo.size_x) if m % 2 else (geo.size_x, geo.size_y)
            self.scratch += [
                pltpu.VMEM(shape, LOW)
                for shape in (
                    (geo.groups, geo.size_y, geo.size_x, 2, feats, n),
                    (2, geo.size_y, geo.size_x, feats, n),
                    (near - 1, geo.groups, far, feats, n),
                    (far - 1, geo.groups, feats, n),
                    (geo.groups, feats, n),
                )
            ]

    def tasks(self, inputs, outs, scratch):
        geo, (send, recv, end_send, end_recv, free), buffers = self.geo, scratch[:5], scratch[5:]
        move = Mover(geo, send, recv)
        groups, sx, sy = geo.groups, geo.size_x, geo.size_y
        mats = range(self.count)
        self.grads = [buffers[5 * m] for m in mats]
        ring = self.ring = 2 * len(self.cuts)

        def parts(k, m):
            r, cut = self.chunks[k]
            begin, count = self.cuts[cut]
            return r, pl.ds(begin, count), buffers[5 * m : 5 * m + 5]

        def cross(k, m):
            r, cols, bufs = parts(k, m)
            _, _, core, _ = geo.place(c=1)
            return move(("c", k, m), bufs[0].at[r, :, :, core, :, cols], bufs[1].at[k // len(self.cuts) % 2, :, :, :, cols], c=1)

        def near(k, m):
            r, cols, bufs = parts(k, m)
            out = []
            for step in range(1, sy if m % 2 else sx):
                to = dict(y=step) if m % 2 else dict(x=step)
                iy, ix, core, _ = geo.place(**to)
                part = bufs[0].at[r, iy, :, core, :, cols] if m % 2 else bufs[0].at[r, :, ix, core, :, cols]
                out.append(move(("n", k, m, step), part, bufs[2].at[step - 1, r, :, :, cols], **to))
            return out

        def far(k, m):
            r, cols, bufs = parts(k, m)
            out = []
            for step in range(1, sx if m % 2 else sy):
                to = dict(x=step) if m % 2 else dict(y=step)
                iy, ix, core, _ = geo.place(**to)
                out.append(
                    move(
                        ("f", k, m, step),
                        bufs[0].at[r, iy, ix, core, :, cols],
                        bufs[3].at[step - 1, r, :, cols],
                        **to,
                    )
                )
            return out

        def along(cut, m):
            begin, count = self.cuts[cut]
            cols, bufs = pl.ds(begin, count), buffers[5 * m : 5 * m + 5]
            iy, ix, core, _ = geo.place()
            return Delivery(
                geo,
                lambda r: bufs[0].at[r, iy, ix, core, :, cols],
                lambda r: bufs[4].at[r, :, cols],
                bufs[4].at[0, :, cols],
                end_send,
                end_recv,
                groups * (self.count * cut + m),
            )

        def begin(k):
            if k >= ring:
                pl.semaphore_wait(free, 1)
            for m in mats:
                cross(k, m).start()

        def level_one(k):
            _, _, core, _ = geo.place()
            for m in mats:
                r, cols, bufs = parts(k, m)
                cross(k, m).wait_recv()
                total = bufs[0][r, :, :, core, :, cols].astype(F32) + bufs[1][k // len(self.cuts) % 2, :, :, :, cols].astype(F32)
                bufs[0][r, :, :, core, :, cols] = total.astype(LOW)
                start(near(k, m))
            if k + ring < len(self.chunks):
                pl.semaphore_signal(free, inc=1, device_id=geo.device(c=1), device_id_type=MESH)

        def level_two(k):
            iy, ix, core, _ = geo.place()
            for m in mats:
                r, cols, bufs = parts(k, m)
                arrive(near(k, m))
                part = bufs[0][r, iy, :, core, :, cols] if m % 2 else bufs[0][r, :, ix, core, :, cols]
                total = part.astype(F32)
                for other in range(bufs[2].shape[0]):
                    total = total + bufs[2][other, r, :, :, cols].astype(F32)
                if m % 2:
                    bufs[0][r, iy, :, core, :, cols] = total.astype(LOW)
                else:
                    bufs[0][r, :, ix, core, :, cols] = total.astype(LOW)
                start(far(k, m))

        def level_three(k):
            iy, ix, core, _ = geo.place()
            for m in mats:
                r, cols, bufs = parts(k, m)
                arrive(far(k, m))
                total = bufs[0][r, iy, ix, core, :, cols].astype(F32)
                for other in range(bufs[3].shape[0]):
                    total = total + bufs[3][other, r, :, cols].astype(F32)
                bufs[0][r, iy, ix, core, :, cols] = total.astype(LOW)
                delivery = along(self.chunks[k][1], m)
                if r == 2:
                    delivery.merge()
                elif r:
                    delivery.begin(r)

        def final(cut):
            iy, ix, core, _ = geo.place()
            begin, count = self.cuts[cut]
            cols = pl.ds(begin, count)
            for m in mats:
                bufs = buffers[5 * m : 5 * m + 5]
                along(cut, m).arrive()
                total = bufs[0][0, iy, ix, core, :, cols].astype(F32)
                for r in range(1, groups):
                    total = total + bufs[4][r, :, cols].astype(F32)
                outs[m][:, cols] = total

        def end():
            for m in mats:
                for k in range(len(self.chunks)):
                    leave([cross(k, m)] + near(k, m) + far(k, m))
                for cut in range(len(self.cuts)):
                    along(cut, m).leave()

        count = range(len(self.chunks))
        return dict(
            begin=[partial(begin, k) for k in count],
            one=[partial(level_one, k) for k in count],
            two=[partial(level_two, k) for k in count],
            three=[partial(level_three, k) for k in count],
            final=[partial(final, cut) for cut in range(len(self.cuts))],
            end=[end],
        )


class Spread:
    def __init__(self, geo, value, plane=False, part=None, into=None):
        self.geo, self.plane, self.part = geo, plane, part
        self.peers = geo.plane() if plane else geo.column()
        self.inputs = [] if plane else [(value, "once")]
        self.outputs = [((len(self.peers) + 1,) + value.shape, value.dtype, "any")]
        self.aliases = {}
        if into is not None:
            self.inputs.append((into, "any"))
            self.aliases = {1: 0}
        sems = pltpu.SemaphoreType.DMA((len(self.peers) + 1,))
        self.scratch = [sems, sems, pltpu.SemaphoreType.DMA]
        if plane:
            self.scratch.append(pltpu.VMEM(value.shape, value.dtype))

    def tasks(self, values, outs, scratch):
        geo, out, (send, recv, local) = self.geo, outs[0], scratch[:3]
        dp, h = geo.device()
        if self.plane:
            self.source = scratch[3]
            move = Mover(geo, send, recv)
            copies = [move(str(to), self.source, out.at[dp], **back(to)) for to in self.peers]
            mine = pltpu.make_async_copy(self.source, out.at[dp], local)

            def begin():
                start(copies)
                mine.start()

            def end():
                mine.wait()
                arrive(copies)
                leave(copies)

            return [begin, end]
        rows = pl.ds(*self.part) if self.part else pl.ds(0, out.shape[1])
        value = values[0].at[rows]
        slot = lambda r: out.at[lax.rem(h + r, geo.groups), rows]
        column = Column(geo, value, slot, send, recv, 0, True)

        def begin_column():
            column.begin()
            pltpu.make_async_copy(value, slot(0), local).start()

        def end_column():
            pltpu.make_async_copy(value, slot(0), local).wait()
            column.arrive()
            column.leave()

        return [begin_column, column.relay, end_column]


class Deal:
    def __init__(self, geo, values):
        self.geo, self.peers = geo, geo.column()
        tokens, cols = values[0].shape
        self.rows = tokens // geo.groups
        self.inputs = [(value, "any") for value in values]
        self.outputs = [((geo.groups - 1, len(values), self.rows, cols), values[0].dtype, "any")]
        sems = pltpu.SemaphoreType.DMA(((geo.groups - 1) * len(values),))
        self.scratch = [sems, sems]

    def tasks(self, values, outs, scratch):
        geo = self.geo
        move = Mover(geo, *scratch)
        copies = []
        for r in range(1, geo.groups):
            first = pl.multiple_of(geo.place(z=-r)[3] * self.rows, self.rows)
            for layer, value in enumerate(values):
                copies.append(move((r, layer), value.at[pl.ds(first, self.rows), :], outs[0].at[r - 1, layer], z=-r))

        def end():
            arrive(copies)
            leave(copies)

        return [lambda: start(copies), end]


class Fold:
    def __init__(self, geo, items):
        self.geo, self.peers = geo, geo.plane() + geo.column()
        self.inputs = [(item[0], "full") for item in items]
        self.picks = [item[1:] for item in items]
        rows = sum(stop - first for _, (first, stop), _ in self.picks)
        self.rows = -(-rows // 8) * 8
        self.outputs = [((self.rows, 128), F32, "full")]
        near, far = pltpu.SemaphoreType.DMA((geo.ndp - 1,)), pltpu.SemaphoreType.DMA((geo.groups - 1,))
        wide = pltpu.VMEM((geo.ndp, geo.groups, self.rows, 128), F32)
        slim = pltpu.VMEM((geo.groups, self.rows, 128), F32)
        self.scratch = [near, near, far, far, wide, wide, slim, slim]

    def tasks(self, values, outs, scratch):
        geo = self.geo
        near_send, near_recv, far_send, far_recv, packed, landed, middle, last = scratch
        groups, ndp = geo.groups, geo.ndp
        to_plane, to_column = Mover(geo, near_send, near_recv), Mover(geo, far_send, far_recv)
        dp, h = geo.device()
        near, far = [], []
        for to in geo.plane():
            there, _ = geo.device(**to)
            near.append(to_plane(str(to), packed.at[there], landed.at[dp], **to))
        for r in range(1, groups):
            far.append(to_column(r, middle.at[r], last.at[h], z=r))

        def begin():
            packed[...] = jnp.zeros_like(packed)
            row = 0
            for value, (grouped, (low, high), (first, stride, cols)) in zip(values, self.picks):
                for r in range(groups):
                    for d in range(ndp):
                        lanes = slice(first + d * stride, first + d * stride + cols)
                        part = value[r, low:high, lanes] if grouped else value[low:high, lanes]
                        packed[d, r, row : row + high - low, :cols] = part
                row += high - low
            start(near)

        def fold():
            landed[dp] = packed[dp]
            arrive(near)
            total = landed[0]
            for d in range(1, ndp):
                total = total + landed[d]
            middle[...] = total
            start(far)

        def end():
            last[h] = middle[0]
            arrive(far)
            total = last[0]
            for z in range(1, groups):
                total = total + last[z]
            outs[0][...] = total
            leave(near)
            leave(far)

        return [begin, fold, end]


def norm_forward(before, gain, shift):
    center = before - jnp.mean(before, -1, keepdims=True)
    spread = jnp.mean(center * center, -1, keepdims=True)
    return center * lax.rsqrt(spread + EPS) * gain + shift


def norm_backward(before, gain, grad):
    center = before - jnp.mean(before, -1, keepdims=True)
    rate = lax.rsqrt(jnp.mean(center * center, -1, keepdims=True) + EPS)
    hat = center * rate
    grad_hat = grad * gain
    mean_one = jnp.mean(grad_hat, -1, keepdims=True)
    mean_two = jnp.mean(grad_hat * hat, -1, keepdims=True)
    grad_before = rate * (grad_hat - mean_one - hat * mean_two)
    return (
        grad_before,
        jnp.sum(grad * hat, 0, keepdims=True),
        jnp.sum(grad, 0, keepdims=True),
        jnp.sum(grad_before, 0, keepdims=True),
    )


BIAS_ONE, BIAS_TWO, GAIN_ONE, GAIN_TWO, SHIFT_ONE, SHIFT_TWO = range(6)


class Window:
    def __init__(self, size, rows, groups):
        self.seqs, self.seq_len, self.heads, self.head_size = size
        self.rows, self.groups = rows, groups
        self.block = self.seq_len // groups
        self.mid_rows = 2 * self.block
        h = lax.axis_index("head")
        self.h = h
        self.first = lax.div(h * (self.seqs - 1), groups)
        self.base = self.first * self.seq_len
        self.own = h * rows - self.base
        pair = h + 1 - 2 * lax.rem(h, 2)
        self.pair = pair * rows - self.base
        self.mid = lax.rem(h, 2) * (2 * rows)
        self.mid_row = lax.rem(h, 2) * self.block
        self.middle = (h > 0) & (h < groups - 1)
        dp = lax.axis_index("dp")
        self.to_pair = (dp, pair)
        self.to_mid = (dp, groups - 1 - h)

    def at(self, begin, rows):
        return pl.ds(pl.multiple_of(begin, self.block), rows)

    def loc(self, piece):
        return lax.div((self.h * (self.rows // self.block) + piece) * self.block, self.seq_len) - self.first

    def keys(self, piece):
        return pl.ds(pl.multiple_of(self.loc(piece) * self.seq_len, self.seq_len), self.seq_len)


def remote(src, dst, sems, to):
    return pltpu.make_async_remote_copy(
        src_ref=src, dst_ref=dst, send_sem=sems.at[0], recv_sem=sems.at[1], device_id=to, device_id_type=MESH
    )


def add_up(r, total, part):
    @pl.when(r == 0)
    def _():
        total[...] = part

    @pl.when(r > 0)
    def _():
        total[...] += part


def gelu_parts(unit):
    square = unit * unit
    bent = jnp.tanh(GELU_C * unit * (1.0 + GELU_K * square))
    half = 0.5 * (1.0 + bent)
    slope = half + 0.5 * unit * (1.0 - bent * bent) * (GELU_C * (1.0 + 3.0 * GELU_K * square))
    return unit * half, slope


def vector(vecs, layer, which):
    return vecs[which // 2][layer, which % 2 : which % 2 + 1, :]


def row_mask(window, lengths):
    block, parts = window.block, []
    for piece in range(window.rows // block):
        place = lax.rem((window.h * (window.rows // block) + piece) * block, window.seq_len)
        inside = lax.broadcasted_iota(jnp.int32, (block, 1), 0) + place < lengths[window.first + window.loc(piece)]
        parts.append(jnp.where(inside, 1.0, 0.0))
    return jnp.concatenate(parts, 0)


def attend(window, layer, xin, offset, row, lengths, left, right, outs, turned, total, r, point):
    kv_out, q_out, ctx_out, lse_out, gated_out = outs
    seq_len, heads, head_size, block, rows = (
        window.seq_len,
        window.heads,
        window.head_size,
        window.block,
        window.rows,
    )
    width = heads * head_size
    point(0)
    kv = nn(xin[window.at(offset, 2 * seq_len), :], left) + row[:, 2 * width :]
    kv_out[0] = kv.astype(LOW)
    query = (nn(xin[window.at(offset + window.own, rows), :], right[:, :width]) + row[:, :width]).astype(LOW)
    q_out[0] = query
    scaled = query * jnp.asarray(0.125, LOW)
    for piece in range(rows // block):
        mine = slice(piece * block, (piece + 1) * block)
        keys = window.keys(piece)
        length = lengths[window.first + window.loc(piece)]
        unused = jnp.where(lax.broadcasted_iota(jnp.int32, (seq_len, block), 0) < length, 0.0, -1e30)
        for head in range(heads):
            lanes = slice(head * head_size, (head + 1) * head_size)
            scores = nt(kv_out[0, keys, lanes], scaled[mine, lanes]) + unused
            largest = jnp.max(scores, 0, keepdims=True)
            powers = jnp.exp(scores - largest)
            sums = jnp.sum(powers, 0, keepdims=True)
            value = kv_out[0, keys, width + head * head_size : width + (head + 1) * head_size]
            turned[lanes, mine] = tn(value, powers.astype(LOW)) / sums
            lse_out[0, head : head + 1, mine] = largest + jnp.log(sums)
            point(1 + piece * heads + head)
    context = turned[...].T
    ctx_out[0] = context
    gated = (context * row[:, width : 2 * width]).astype(LOW)
    gated_out[0] = gated
    add_up(r, total, nt(gated, right[:, width:]))


def forward(size, layers, geo, gather, counter, lists, *refs):
    seqs, seq_len, heads, head_size = size
    refs = list(refs)
    take = lambda n: [refs.pop(0) for _ in range(n)]
    hidden = refs.pop(0)
    vec = take(3)
    lengths, unit_noise, unit_alpha, head_noise, head_alpha, inner_bias, qv_bias = take(7)
    key_value, query_output, inner, outer, map_own = take(5)
    saved = [take(10) for _ in range(layers)]
    win_out, small_out = take(2)
    left_buf, right_buf, inner_buf, outer_buf, load_sems, back_sems = take(6)
    total, middle, current, low, xwin, small, small_own, small_send, small_recv, map_stage, turned = take(11)
    pair_sems, mid_sems, local = take(3)
    gather_tasks, count_tasks, deal_tasks, (weights,) = lists
    groups = geo.groups
    rows, model = total.shape
    window = Window(size, rows, groups)
    mid_rows, width = window.mid_rows, heads * head_size
    s = pl.program_id(0)
    r = lax.rem(s, groups)
    slot = lax.rem(r, 2)
    spots_attn, spots_feed = 2 + rows // window.block * heads, 4
    plan = Plan(([spots_attn] * groups + [spots_feed] * groups) * layers)

    small_column = Column(geo, small_own, lambda i: small.at[i], small_send, small_recv, 0)
    keep_small = pltpu.make_async_copy(small, small_out, local.at[2])

    def small_begin():
        small_column.begin()

    def small_end():
        small_column.relay()
        small_column.arrive()
        small_column.leave()
        keep_small.start()

    into_stage = pltpu.make_async_copy(map_own.at[0], map_stage, local.at[3])
    out_of_stage = pltpu.make_async_copy(map_stage, weights[-1].at[0], local.at[4])

    def stage_begin():
        into_stage.start()

    def stage_end():
        into_stage.wait()
        out_of_stage.start()

    phases = 2 * layers
    plan.even([small_begin] + [count_tasks[0]], 0, 0)
    ends, done = [], 0
    for phase in range(phases):
        for chunk, halves in enumerate(gather.chunks):
            if halves[0][0] // 2 == phase:
                done = gather.done[chunk]
        ends.append(done)
    lengths_us = ([FORWARD_ATTN_STEP] * groups + [FORWARD_FEED_STEP] * groups) * layers
    first, begun = 0, 0
    for phase in range(phases):
        last = plan.slot(phase * groups, -1)
        if phase < 2:
            plan.even(gather_tasks[begun : ends[phase]], first, last)
            first, begun = last, ends[phase]
        if phase == 0:
            plan.even([small_end, stage_begin], last, last)
            plan.even([count_tasks[1]], plan.slot(groups, 0), plan.slot(groups, 0))
            plan.even([stage_end], plan.slot(groups, 1), plan.slot(groups, 1))
        if phase == 2:
            plan.even([deal_tasks[0]], last, last)
    closing = len(plan.slots) - 1
    waits = {plan.slot(phase * groups - 1, -1): HALO_WAIT for phase in range(2, phases, 2)}
    due = [(ends[phase] - begun, plan.slot(phase * groups, -1)) for phase in range(2, phases)]
    plan.paced(lengths_us, waits, gather_tasks[begun:], first, due[-1][1], due[-1][0], due)
    plan.even([deal_tasks[1]], closing, closing)

    kinds = [(left_buf, right_buf), (inner_buf, outer_buf)]
    sources = [(key_value, query_output), (inner, outer)]

    def own_loads(phase):
        layer, kind = phase // 2, phase % 2
        return [
            pltpu.make_async_copy(src.at[layer], buf.at[0], load_sems.at[kind, side, 0])
            for side, (src, buf) in enumerate(zip(sources[kind], kinds[kind]))
        ]

    def own_backs(phase):
        kind = phase % 2
        return [
            pltpu.make_async_copy(buf.at[0], weights[2 * phase + side].at[0], back_sems.at[kind, side])
            for side, buf in enumerate(kinds[kind])
        ]

    def loads(phase, group, into):
        kind = phase % 2
        return [
            pltpu.make_async_copy(weights[2 * phase + side].at[group], buf.at[into], load_sems.at[kind, side, into])
            for side, buf in enumerate(kinds[kind])
        ]

    @pl.when(s == 0)
    def _():
        start(own_loads(0))
        total_length = lengths[0]
        for index in range(1, seqs):
            total_length = total_length + lengths[index]
        counter.source[...] = jnp.full(counter.source.shape, total_length, jnp.int32).astype(F32)
        small_own[...] = jnp.zeros_like(small_own)
        open_unit = gate_open(unit_noise[...], unit_alpha[...])
        open_head = gate_open(head_noise[...], head_alpha[...])
        for layer in range(layers):
            own = slice(layer, layer + 1)
            place = slice(4 * layer, 4 * layer + 1)
            small_own[place, :] = open_unit[own]
            small_own[4 * layer + 1 : 4 * layer + 2, :] = inner_bias[own, :]
            place = slice(4 * layer + 2, 4 * layer + 3)
            small_own[place, :width] = qv_bias[layer, 0:1, :]
            for head in range(heads):
                begin = width + head * head_size
                small_own[place, begin : begin + head_size] = jnp.broadcast_to(
                    open_head[own, head : head + 1], (1, head_size)
                )
            small_own[place, 3 * width :] = qv_bias[layer, 1:2, :]
        small[0] = small_own[...]

    def before(phase):
        @pl.when(r == 0)
        def _():
            if phase + 1 < phases:
                start(own_loads(phase + 1))
            for copy in own_loads(phase):
                copy.wait()
            start(own_backs(phase))

        @pl.when(r > 0)
        def _():
            for copy in loads(phase, r, slot):
                copy.wait()

        @pl.when((r > 0) & (r < groups - 1))
        def _():
            start(loads(phase, r + 1, 1 - slot))

    def behind(phase):
        @pl.when(r == 0)
        def _():
            for copy in own_backs(phase):
                copy.wait()
            start(loads(phase, 1, 1))

    def flat(buf):
        value = buf[slot]
        return value.reshape(model, value.shape[-1])

    own_place = xwin.at[window.at(window.own, rows)]
    to_pair = remote(low, own_place, pair_sems, window.to_pair)
    to_mid = remote(
        low.at[window.at(window.mid_row, mid_rows)],
        xwin.at[window.at((1 - lax.rem(window.h, 2)) * 2 * rows, mid_rows)],
        mid_sems,
        window.to_mid,
    )
    keep_win = pltpu.make_async_copy(xwin, win_out, local.at[0])

    for phase in range(phases):
        layer, kind = phase // 2, phase % 2
        kv_out, q_out, ctx_out, lse_out, gated_out, before_one, middle_low, unit_out, before_two, low_out = saved[layer]
        span = range(phase * groups, (phase + 1) * groups)

        def point(spot, span=span):
            plan.point(s, spot, span)

        @pl.when(lax.div(s, groups) == phase)
        def _():
            if kind == 0:
                if layer:

                    @pl.when(r == 0)
                    def _():
                        to_pair.wait()

                        @pl.when(window.middle)
                        def _():
                            to_mid.wait()

                        keep_win.start()

                before(phase)
                xin, offset = (xwin, 0) if layer else (hidden, window.base)
                row = small[r, 4 * layer + 2 : 4 * layer + 3, :]
                outs = (kv_out, q_out, ctx_out, lse_out, gated_out)
                attend(
                    window,
                    layer,
                    xin,
                    offset,
                    row,
                    lengths,
                    flat(left_buf),
                    flat(right_buf),
                    outs,
                    turned,
                    total,
                    r,
                    point,
                )

                @pl.when(r == groups - 1)
                def _():
                    if layer:
                        resid = current[...]
                    else:
                        resid = hidden[window.at(offset + window.own, rows), :].astype(F32)
                    value = resid + total[...] + vector(vec, layer, BIAS_ONE)
                    normed = norm_forward(value, vector(vec, layer, GAIN_ONE), vector(vec, layer, SHIFT_ONE))
                    before_one[...] = value
                    middle[...] = normed
                    middle_low[...] = normed.astype(LOW)

                point(spots_attn - 1)
                behind(phase)
            else:
                before(phase)
                point(0)
                unit = nn(middle_low[...], flat(inner_buf)) + small[r, 4 * layer + 1 : 4 * layer + 2, :]
                unit_out[0] = unit.astype(LOW)
                point(1)
                bent = jnp.tanh(GELU_C * unit * (1.0 + GELU_K * (unit * unit)))
                active = (0.5 * unit * (1.0 + bent) * small[r, 4 * layer : 4 * layer + 1, :]).astype(LOW)
                point(2)
                add_up(r, total, nn(active, flat(outer_buf)))

                @pl.when(r == groups - 1)
                def _():
                    value = middle[...] + total[...] + vector(vec, layer, BIAS_TWO)
                    normed = norm_forward(value, vector(vec, layer, GAIN_TWO), vector(vec, layer, SHIFT_TWO))
                    before_two[...] = value
                    low_out[...] = normed.astype(LOW)
                    if layer + 1 < layers:
                        current[...] = normed
                        low[...] = normed.astype(LOW)
                        to_pair.start()

                        @pl.when(window.middle)
                        def _():
                            to_mid.start()

                        xwin[window.at(window.own, rows), :] = normed.astype(LOW)

                        @pl.when(jnp.logical_not(window.middle))
                        def _():
                            empty = window.at(lax.rem(window.h + 1, 2) * 2 * rows, mid_rows)
                            xwin[empty, :] = jnp.zeros((mid_rows, model), LOW)

                point(spots_feed - 1)
                behind(phase)

    @pl.when(s == phases * groups - 1)
    def _():
        keep_win.wait()
        keep_small.wait()
        out_of_stage.wait()


def match_teacher(size, layers, tokens, point, *refs):
    refs = list(refs)
    states = [refs.pop(0) for _ in range(layers)]
    chosen = [refs.pop(0) for _ in range(layers)]
    target, lengths, counts, weight = refs[:4]
    back_outs, (loss_out, grad_out) = refs[4 : 4 + layers], refs[4 + layers :]
    r = pl.program_id(0)
    rows = states[0].shape[0]

    @pl.when(r == 0)
    def _():
        loss_out[...] = jnp.zeros_like(loss_out)
        for back_out in back_outs:
            back_out[...] = jnp.zeros_like(back_out)
        loss_out[0:1, 1:2] = jnp.sum(counts[...][:, 0:1, 0:1], 0)

    count = jnp.sum(counts[...][:, 0:1, 0:1], 0)
    factor = tokens / count
    mine = pl.ds(pl.multiple_of(lax.axis_index("head") * rows, rows), rows)
    row_ok = row_mask(Window(size, rows, pl.num_programs(0)), lengths)
    total = None
    for layer in range(layers):
        goal = jnp.where(r == 0, chosen[layer][mine, :], target[0, layer]).astype(F32)
        miss = (nn(states[layer][...], weight[0]) - goal) * row_ok
        loss_out[:1, :1] += jnp.sum(jnp.sum(miss * miss, 0, keepdims=True), 1, keepdims=True)
        low = (factor * miss).astype(LOW)
        back_outs[layer][...] += nt(low, weight[0])
        grad = tn(states[layer][...], low)
        total = grad if total is None else total + grad
    grad_out[0] = total.astype(LOW)


FEED_STEP, ATTN_STEP, WEIGHT_STEP = 5.0, 6.5, 3.0


def in_order(s):
    place = jnp.clip(s, 0, len(ORDER) - 1)
    group = 0
    for index, value in enumerate(ORDER):
        group = jnp.where(place == index, value, group)
    return group


def layer_backward(size, layer, first, last, geo, reduce, times, lists, *refs):
    seqs, seq_len, heads, head_size = size
    refs = list(refs)
    take = lambda n: [refs.pop(0) for _ in range(n)]
    before_two, before_one, middle_low, unit_in, small = take(5)
    vec = take(3)
    inner, outer = take(2)
    grad_refs = take(2 if last else 1)
    xwin, query_in, kv, ctx, lse, gated, lengths, left, right = take(9)
    extra = None if first else refs.pop(0)
    left_out, right_out, grad_out, head_vec, vec_out, unit_vec = take(6)
    (mine, feed, attn, grad_kv, turned, kv_all, q_all, spread, pair_low, pair_got, mid_low, mid_got) = take(12)
    pair_sems, mid_sems, local = take(3)
    work, riders = lists[0], lists[1:]
    groups = geo.groups
    s = pl.program_id(0)
    r = lax.rem(s, groups)
    part = lax.div(s, groups)
    width = heads * head_size
    rows, model = mine.shape
    window = Window(size, rows, groups)
    block, mid_rows = window.block, window.mid_rows
    blocks = rows // block
    offset = window.base if first else 0
    here = window.at(offset + window.own, rows)
    to_pair = remote(pair_low, pair_got, pair_sems, window.to_pair)
    to_mid = remote(mid_low, mid_got, mid_sems, window.to_mid)

    spots = [7] * groups + [2 + blocks * heads] * groups + [4] * groups
    lengths_us = [FEED_STEP] * groups + [ATTN_STEP] * groups + [WEIGHT_STEP] * groups
    plan = Plan(spots)
    whole = sum(lengths_us)
    cuts = len(reduce.cuts)
    timed = []
    first_one, pace, second, third = times
    ones = [
        max(FEED_STEP * (k // cuts + 1) + 4.5, first_one + pace * k) + 0.01 * (k % cuts)
        for k in range(len(reduce.chunks))
    ]
    for k in range(len(reduce.chunks)):
        made = FEED_STEP * (k // cuts + 1) - 0.5 + 0.01 * (k % cuts)
        if k >= reduce.ring:
            made = max(made, ones[k - reduce.ring] + 0.1)
        timed.append((made, work["begin"][k]))
        timed.append((max(ones[k], made + 3.0), work["one"][k]))
        timed.append((ones[k] + second, work["two"][k]))
        timed.append((ones[k] + second + third, work["three"][k]))
    timed += [(1e6, task) for task in work["final"] + work["end"]]
    for finish, tasks in riders:
        count = max(1, len(tasks) - 1)
        timed += [(finish * whole * index / count, task) for index, task in enumerate(tasks)]
    plan.timed(lengths_us, timed)

    def points(span):
        return lambda spot: plan.point(s, spot, span)

    point_feed = points(range(groups))
    point_attn = points(range(groups, 2 * groups))
    point_weight = points(range(2 * groups, 3 * groups))

    def feeding():
        point_feed(0)
        unit = in_order(s)

        @pl.when(r == 0)
        def _():
            if last:
                cotangent, back = grad_refs
                own = pl.ds(pl.multiple_of(window.h * rows, rows), rows)
                fetch = pltpu.make_async_copy(cotangent.at[own], pair_low, local)
                fetch.start()
                fetch.wait()
                grad = pair_low[...].astype(F32) + back[...]
            else:
                grad = grad_refs[0][...]
            grad_before, grad_gain, grad_shift, grad_bias = norm_backward(
                before_two[...], vector(vec, layer, GAIN_TWO), grad
            )
            vec_out[BIAS_TWO : BIAS_TWO + 1, :] = grad_bias
            vec_out[GAIN_TWO : GAIN_TWO + 1, :] = grad_gain
            vec_out[SHIFT_TWO : SHIFT_TWO + 1, :] = grad_shift
            feed[...] = grad_before.astype(LOW)
            mine[...] = grad_before

        grad_active = nt(feed[...], outer[0])
        point_feed(1)
        value, slope = gelu_parts(unit_in[0].astype(F32))
        opened = small[0, 4 * layer : 4 * layer + 1, :]
        grad_unit = (grad_active * (slope * opened)).astype(LOW)
        unit_vec[0, 0:1, :] = jnp.sum(grad_unit.astype(F32), 0, keepdims=True)
        unit_vec[0, 1:2, :] = jnp.sum(grad_active * value, 0, keepdims=True)
        active = (value * opened).astype(LOW)
        point_feed(2)
        mine[...] += nt(grad_unit, inner[0])
        point_feed(3)
        shape = reduce.grads[0].shape[1:]
        reduce.grads[0][unit] = tn(middle_low[...], grad_unit).astype(LOW).reshape(shape)
        point_feed(4)
        reduce.grads[1][unit] = tn(feed[...], active).astype(LOW).reshape(shape)
        point_feed(5)

        @pl.when(r == groups - 1)
        def _():
            grad_before, grad_gain, grad_shift, grad_bias = norm_backward(
                before_one[...], vector(vec, layer, GAIN_ONE), mine[...]
            )
            vec_out[BIAS_ONE : BIAS_ONE + 1, :] = grad_bias
            vec_out[GAIN_ONE : GAIN_ONE + 1, :] = grad_gain
            vec_out[SHIFT_ONE : SHIFT_ONE + 1, :] = grad_shift
            mine[...] = grad_before if first else grad_before + extra[...]
            attn[...] = grad_before.astype(LOW)
            spread[...] = jnp.zeros_like(spread)

        point_feed(6)

    def attending():
        point_attn(0)
        row = small[0, 4 * layer + 2 : 4 * layer + 3, :]
        opened = row[:, width : 2 * width]
        grad_gated = nn(attn[...], right[0, :, width:])
        shared = grad_gated * ctx[0]
        grad_ctx = (grad_gated * opened).astype(LOW)
        pulled = shared * opened
        scaled = query_in[0] * jnp.asarray(0.125, LOW)
        grad_kv[...] = jnp.zeros_like(grad_kv)
        pulled_turned = pulled.T
        for piece in range(blocks):
            rows_of = slice(piece * block, (piece + 1) * block)
            keys = window.keys(piece)
            length = lengths[window.first + window.loc(piece)]
            unused = jnp.where(lax.broadcasted_iota(jnp.int32, (seq_len, block), 0) < length, 0.0, -1e30)
            for head in range(heads):
                lanes = slice(head * head_size, (head + 1) * head_size)
                later = slice(width + head * head_size, width + (head + 1) * head_size)
                key = kv[0, keys, lanes]
                scores = nt(key, scaled[rows_of, lanes]) + unused
                chances = jnp.exp(scores - lse[0, head : head + 1, rows_of])
                grad_chances = nt(kv[0, keys, later], grad_ctx[rows_of, lanes])
                delta = jnp.sum(pulled_turned[lanes, rows_of], 0, keepdims=True)
                grad_scores = (chances * (grad_chances - delta)).astype(LOW)
                turned[lanes, rows_of] = tn(key, grad_scores)
                grad_kv[keys, lanes] += nn(grad_scores, scaled[rows_of, lanes])
                grad_kv[keys, later] += nn(chances.astype(LOW), grad_ctx[rows_of, lanes])
                point_attn(1 + piece * heads + head)
        query_low = (turned[...].T * 0.125).astype(LOW)
        kv_low = grad_kv[...].astype(LOW)
        q_all[r] = query_low
        kv_all[r] = kv_low
        head_vec[0, 0:1, :width] = jnp.sum(query_low.astype(F32), 0, keepdims=True)
        head_vec[0, 0:1, 2 * width :] = jnp.sum(kv_low.astype(F32), 0, keepdims=True)
        shared_sum = jnp.sum(shared, 0, keepdims=True)
        lane = lax.broadcasted_iota(jnp.int32, (1, 128), 1)
        by_head = jnp.zeros((1, 128), F32)
        for head in range(heads):
            one = jnp.sum(shared_sum[:, head * head_size : (head + 1) * head_size], 1, keepdims=True)
            by_head = jnp.where(lane == head, one, by_head)
        head_vec[0, 1:2, :128] = by_head
        spread[...] += nt(kv_low, left[0])
        mine[...] += nt(query_low, right[0, :, :width])

        @pl.when(r == groups - 1)
        def _():
            pair_low[...] = spread[window.at(window.pair, rows), :].astype(LOW)
            to_pair.start()

            @pl.when(window.middle)
            def _():
                mid_low[...] = spread[window.at(window.mid, mid_rows), :].astype(LOW)
                to_mid.start()

        point_attn(1 + blocks * heads)

    def weighing():
        point_weight(0)
        left_out[0] = tn(xwin[window.at(offset, 2 * seq_len), :], kv_all[r]).astype(LOW)
        point_weight(1)
        right_out[0, :, :width] = tn(xwin[here, :], q_all[r]).astype(LOW)
        point_weight(2)
        right_out[0, :, width:] = tn(attn[...], gated[0]).astype(LOW)

        @pl.when(r == groups - 1)
        def _():
            to_pair.wait()
            mine[...] += spread[window.at(window.own, rows), :] + pair_got[...].astype(F32)

            @pl.when(window.middle)
            def _():
                to_mid.wait()
                mine[window.at(window.mid_row, mid_rows), :] += mid_got[...].astype(F32)

            grad_out[...] = mine[...].astype(grad_out.dtype)

        point_weight(3)

    pl.when(part == 0)(feeding)
    pl.when(part == 1)(attending)
    pl.when(part == 2)(weighing)


def on_device(
    ndp,
    groups,
    hidden_in,
    seq_lengths,
    layer_map,
    teacher_states,
    out_cotangent,
    query_weight,
    key_weight,
    value_weight,
    query_value_bias,
    output_weight,
    branch_bias,
    norm_gain,
    norm_shift,
    inner_weight,
    inner_bias,
    outer_weight,
    head_alpha,
    head_noise,
    unit_alpha,
    unit_noise,
    map_weight,
):
    tokens_dev, model = hidden_in.shape
    seqs_dev = seq_lengths.shape[0]
    seq_len = tokens_dev // seqs_dev
    width = query_weight.shape[2]
    units = inner_weight.shape[2]
    layers, heads = head_alpha.shape
    head_size = width // heads
    rows = tokens_dev // groups
    feats = model // ndp
    geo = Geometry(ndp, groups)
    size = (seqs_dev, seq_len, heads, head_size)
    window = Window(size, rows, groups)
    blocks = rows // window.block
    dp = lax.axis_index("dp")

    def slices(array):
        return array.reshape(array.shape[0], geo.size_y, geo.size_x, 2, feats, array.shape[-1])

    def matrices(arrays):
        return [(array.reshape(groups, model, array.shape[-1]), "group") for array in arrays]

    def pairs(cols, steps, m=0):
        out, begin = [], 0
        for step in steps:
            out.append([(m, begin, step, False), (m + 1, begin, step, True)])
            begin += step
        return out if begin == cols else [[(m, 0, cols, False), (m + 1, 0, cols, True)]]

    key_value = slices(jnp.concatenate([key_weight, value_weight], 2))
    query_output = slices(jnp.concatenate([query_weight, jnp.swapaxes(output_weight, 1, 2)], 2))
    inner, outer = slices(inner_weight), slices(outer_weight)

    _, unit_back = jax.vjp(partial(gate_open, unit_noise), unit_alpha)
    _, head_back = jax.vjp(partial(gate_open, head_noise), head_alpha)
    (unit_slope,) = unit_back(jnp.ones_like(unit_alpha))
    (head_slope,) = head_back(jnp.ones_like(head_alpha))
    small = jax.ShapeDtypeStruct((4 * layers, units), F32)
    vec = [(array, "once") for array in (branch_bias, norm_gain, norm_shift)]
    count = jax.ShapeDtypeStruct((8, 128), F32)
    chosen = [
        lax.dynamic_index_in_dim(teacher_states, layer_map[layer], 0, keepdims=False) for layer in range(layers)
    ]

    row_block = pltpu.VMEM((rows, model), F32)
    low_block = pltpu.VMEM((rows, model), LOW)
    mid_block = pltpu.VMEM((window.mid_rows, model), LOW)
    two = pltpu.SemaphoreType.DMA((2,))
    owns, chunks = [], []
    for layer in range(layers):
        for arrays, cuts in (((key_value, query_output), ATTN_CUTS), ((inner, outer), FEED_CUTS)):
            chunks += pairs(arrays[0].shape[-1], cuts, len(owns))
            owns += [(array, layer) for array in arrays]
    chunks.append([(len(owns), 0, width, False)])
    map_slices = slices(map_weight[None])
    owns.append((map_slices, 0))
    gather = Gather(geo, owns, chunks)
    counter = Spread(geo, count, plane=True)
    outputs = []
    for layer in range(layers):
        attn_step = lambda s, layer=layer: jnp.clip(s - 2 * layer * groups, 0, groups - 1)
        feed_step = lambda s, layer=layer: jnp.clip(s - (2 * layer + 1) * groups, 0, groups - 1)
        outputs += [
            ((groups, 2 * seq_len, 2 * width), LOW, attn_step),
            ((groups, rows, width), LOW, attn_step),
            ((groups, rows, width), F32, attn_step),
            ((groups, 8, rows), F32, attn_step),
            ((groups, rows, width), LOW, attn_step),
            ((rows, model), F32, "full"),
            ((rows, model), LOW, "full"),
            ((groups, rows, units), LOW, feed_step),
            ((rows, model), F32, "full"),
            ((rows, model), LOW, "full"),
        ]
    saves = len(outputs) // layers
    outputs += [((2 * seq_len, model), LOW, "any"), ((groups,) + small.shape, F32, "any")]
    attn_buf = pltpu.VMEM((2,) + key_value.shape[1:], LOW)
    feed_buf = pltpu.VMEM((2,) + inner.shape[1:], LOW)
    others = pltpu.SemaphoreType.DMA((groups,))
    got = run(
        partial(forward, size, layers, geo, gather, counter),
        2 * layers * groups,
        [
            (hidden_in, "once"),
            *vec,
            (seq_lengths, "smem"),
            (unit_noise, "once"),
            (unit_alpha, "once"),
            (head_noise, "once"),
            (head_alpha, "once"),
            (inner_bias, "once"),
            (query_value_bias, "once"),
            (key_value, "any"),
            (query_output, "any"),
            (inner, "any"),
            (outer, "any"),
            (map_slices, "any"),
        ],
        outputs,
        [
            attn_buf,
            attn_buf,
            feed_buf,
            feed_buf,
            pltpu.SemaphoreType.DMA((2, 2, 2)),
            pltpu.SemaphoreType.DMA((2, 2)),
            row_block,
            row_block,
            row_block,
            low_block,
            pltpu.VMEM((2 * seq_len, model), LOW),
            pltpu.VMEM((groups,) + small.shape, F32),
            pltpu.VMEM(small.shape, F32),
            others,
            others,
            pltpu.VMEM(map_slices.shape[1:], LOW),
            pltpu.VMEM((width, rows), F32),
            two,
            two,
            pltpu.SemaphoreType.DMA((5,)),
        ],
        30e9,
        "forward",
        [gather, counter, Deal(geo, chosen), Lend(geo, gather)],
        1,
        1,
        True,
    )
    records = [got[layer * saves : (layer + 1) * saves] for layer in range(layers)]
    xwins, small = [hidden_in, got[layers * saves]], got[layers * saves + 1]
    *weights, counts, target = got[layers * saves + 2 :]
    weights = matrices(weights)
    lows = [record[-1] for record in records]
    *spread, loss, grad_map = run(
        partial(match_teacher, size, layers, float(tokens_dev * ndp)),
        groups,
        [(low, "full") for low in lows]
        + [(array, "full") for array in chosen]
        + [(target, lambda r: jnp.maximum(r - 1, 0)), (seq_lengths, "smem"), (counts, "full")]
        + weights[-1:],
        [
            *[((rows, model), F32, "full")] * layers,
            ((8, 128), F32, "full"),
            ((groups, model, width), LOW, "group"),
        ],
        [],
        4e9,
        "match_teacher",
    )

    grads = [(out_cotangent, "any"), (spread[-1], "once")]
    results = [{} for _ in range(layers)]
    riders, waiting, finishes = [], [], []

    def settle(got):
        for (layer, name), value in zip(waiting, got):
            results[layer][name] = value

    def clipped(part):
        return lambda s: jnp.clip(s - part * groups, 0, groups - 1)

    block_out = None
    riders = [Scatter(geo, [slices(grad_map)], [[(0, 0, width, False)]])]
    waiting, finishes = [(0, "map")], [0.7]
    for layer in reversed(range(layers)):
        kv, query, ctx, lse, gated, before_one, middle_low, unit_in, before_two, _ = records[layer]
        attn_weights, feed_weights = weights[4 * layer : 4 * layer + 2], weights[4 * layer + 2 : 4 * layer + 4]
        if layer in (0, layers - 1):
            part = (0, rows // 2) if layer else (rows // 2, rows // 2)
            riders.append(Spread(geo, lows[-1], part=part, into=block_out))
            waiting.append((0, "block_out"))
            finishes.append(1.0)
        reduce = Reduce(geo, [(feats, units)] * 2, BACK_CUTS)
        left, right, grad, head_vec, vec_out, unit_vec, *got = run(
            partial(
                layer_backward,
                size,
                layer,
                layer == 0,
                layer == layers - 1,
                geo,
                reduce,
                TIMES_LAST if layer == layers - 1 else TIMES,
            ),
            3 * groups,
            [
                (before_two, "once"),
                (before_one, "once"),
                (middle_low, "once"),
                (unit_in, in_order),
                (small, lambda s: jnp.where(s < groups, in_order(s), lax.rem(s, groups))),
                *vec,
            ]
            + [(array, in_order) for array, _ in feed_weights]
            + grads
            + [
                (xwins[layer], "once"),
                (query, clipped(1)),
                (kv, clipped(1)),
                (ctx, clipped(1)),
                (lse, clipped(1)),
                (gated, clipped(2)),
                (seq_lengths, "smem"),
            ]
            + [(array, clipped(1)) for array, _ in attn_weights]
            + ([(spread[layer - 1], "once")] if layer else []),
            [((groups, model, 2 * width), LOW, clipped(2))] * 2
            + [
                ((rows, model), F32 if layer else LOW, "full"),
                ((groups, 8, units), F32, clipped(1)),
                ((8, model), F32, "full"),
                ((groups, 8, units), F32, in_order),
            ],
            [
                row_block,
                low_block,
                low_block,
                pltpu.VMEM((2 * seq_len, 2 * width), F32),
                pltpu.VMEM((width, rows), F32),
                pltpu.VMEM((groups, 2 * seq_len, 2 * width), LOW),
                pltpu.VMEM((groups, rows, width), LOW),
                pltpu.VMEM((2 * seq_len, model), F32),
                low_block,
                low_block,
                mid_block,
                mid_block,
                two,
                two,
                pltpu.SemaphoreType.DMA,
            ],
            25e9,
            "layer_backward",
            [reduce] + [Timed(rider, finish) for rider, finish in zip(riders, finishes)],
            1,
            2 + layers - 1 - layer,
            True,
            LARGE_LIMIT,
        )
        results[layer]["inner"], results[layer]["outer"] = got[:2]
        settle(got[2:])
        block_out = results[0]["block_out"]
        riders = [Scatter(geo, [slices(left), slices(right)], pairs(2 * width, LAST_CUTS if layer == 0 else ATTN_CUTS))]
        waiting, finishes = [(layer, "kv"), (layer, "qo")], [0.75]
        grads = [(grad, "once")]
        results[layer].update(vec=vec_out, unit=unit_vec, head=head_vec)

    everywhere = (0, feats, feats)
    unit_count, qv_cols = units // ndp, width // ndp
    items = [(results[layer]["vec"], False, (0, 6), everywhere) for layer in range(layers)]
    items += [(results[layer]["unit"], True, (0, 2), (0, unit_count, unit_count)) for layer in range(layers)]
    for layer in range(layers):
        items += [(results[layer]["head"], True, (0, 1), (0, qv_cols, qv_cols))]
        items += [(results[layer]["head"], True, (0, 1), (3 * width, qv_cols, qv_cols))]
    items += [(results[layer]["head"], True, (1, 2), (0, 0, 128)) for layer in range(layers)]
    items += [(loss, False, (0, 1), (0, 0, 128))]
    riders = [Spread(geo, grad)] + riders + [Fold(geo, items)]
    waiting = [(0, "grad_hidden")] + waiting + [(0, "sums")]
    settle(run(only_move, 1, [], [], [], 0, "scatter_last", riders, 1, 2 + layers))
    sums = results[0]["sums"]
    by_feature = sums[: 6 * layers, :feats].reshape(layers, 3, 2, feats)
    by_unit = sums[6 * layers : 8 * layers, :unit_count].reshape(layers, 2, unit_count)
    by_column = sums[8 * layers : 10 * layers, :qv_cols].reshape(layers, 2, qv_cols)
    by_head = sums[10 * layers : 11 * layers, :heads]
    loss_sums = sums[11 * layers, :2]
    distill_loss = loss_sums[0] / (loss_sums[1] / (ndp * groups) * model * layers)
    own_slope = lax.dynamic_slice(unit_slope, (0, dp * unit_count), (layers, unit_count))

    def stacked(member, cols, turned=False):
        arrays = [results[layer][member][:, cols] for layer in range(layers)]
        return jnp.stack([array.T if turned else array for array in arrays])

    front, rear, whole = slice(0, width), slice(width, 2 * width), slice(None)
    return (
        block_out.reshape(tokens_dev, model),
        results[0]["grad_hidden"].reshape(tokens_dev, model).astype(F32),
        distill_loss,
        stacked("qo", front),
        stacked("kv", front),
        stacked("kv", rear),
        by_column,
        stacked("qo", rear, True),
        by_feature[:, 0],
        by_feature[:, 1],
        by_feature[:, 2],
        stacked("inner", whole),
        by_unit[:, 0],
        stacked("outer", whole, True),
        by_head * head_slope,
        by_unit[:, 1] * own_slope,
        results[0]["map"],
    )


def solution(mesh):
    in_specs = (
        P("dp", None),
        P("dp"),
        P(),
        P(None, "dp", "head"),
        P("dp", None),
        P(None, None, "head"),
        P(None, None, "head"),
        P(None, None, "head"),
        P(None, None, "head"),
        P(None, "head", None),
        P(),
        P(),
        P(),
        P(None, None, "head"),
        P(None, "head"),
        P(None, "head", None),
        P(None, "head"),
        P(None, "head"),
        P(None, "head"),
        P(None, "head"),
        P(None, "head"),
    )
    out_specs = (
        P("dp", None),
        P("dp", None),
        P(),
        P(None, "dp", "head"),
        P(None, "dp", "head"),
        P(None, "dp", "head"),
        P(None, None, ("head", "dp")),
        P(None, "head", "dp"),
        P(None, None, "dp"),
        P(None, None, "dp"),
        P(None, None, "dp"),
        P(None, "dp", "head"),
        P(None, ("head", "dp")),
        P(None, "head", "dp"),
        P(None, "head"),
        P(None, ("head", "dp")),
        P("dp", "head"),
    )
    return jax.shard_map(
        partial(on_device, mesh.shape["dp"], mesh.shape["head"]),
        mesh=mesh,
        in_specs=in_specs,
        out_specs=out_specs,
        check_vma=False,
    )
```
